128 devices in a mesh: dp: 8 (over x, core), ctx: 4 (over y), tp: 4 (over z).
Axes of the slice: x: 4, y: 4, z: 4, core: 2. Of those that a mesh axis runs over, the one named last changes fastest.
Arguments:
- tokens: float32 [8192, 2048], P(('dp', 'ctx')), may hold values from -6 to 6
- cotangent: float32 [8192, 2048], P(('dp', 'ctx')), may hold values from -6 to 6
- gain_first: float32 [2048], replicated, may hold values from 0.25 to 1.75
- gain_second: float32 [2048], replicated, may hold values from 0.25 to 1.75
- w_query: bfloat16 [2048, 2048], P(('dp', 'ctx'), 'tp'), may hold values from -0.125 to 0.125
- w_key: bfloat16 [2048, 2048], P(('dp', 'ctx'), 'tp'), may hold values from -0.125 to 0.125
- w_value: bfloat16 [2048, 4096], P(('dp', 'ctx'), 'tp'), may hold values from -0.125 to 0.125
- w_gate: bfloat16 [2048, 4096], P(('dp', 'ctx'), 'tp'), may hold values from -0.125 to 0.125
- w_output: bfloat16 [4096, 2048], P('tp', ('dp', 'ctx')), may hold values from -0.125 to 0.125
- w_hidden: bfloat16 [2048, 4096], P(('dp', 'ctx'), 'tp'), may hold values from -0.125 to 0.125
- w_linear: bfloat16 [2048, 4096], P(('dp', 'ctx'), 'tp'), may hold values from -0.125 to 0.125
- w_down: bfloat16 [4096, 2048], P('tp', ('dp', 'ctx')), may hold values from -0.125 to 0.125
- decay_scale: float32 [8], P('tp'), may hold values from 0.3 to 40
- first_length: int32 [8], P('dp'), may hold values from 769 to 1024, as said below
Outputs:
- layer_out: float32 [8192, 2048], P(('dp', 'ctx'))
- input_grad: float32 [8192, 2048], P(('dp', 'ctx'))
- gain_first_grad: float32 [2048], P(('dp', 'ctx'))
- gain_second_grad: float32 [2048], P(('dp', 'ctx'))
- query_grad: float32 [2048, 2048], P(('dp', 'ctx'), 'tp')
- key_grad: float32 [2048, 2048], P(('dp', 'ctx'), 'tp')
- value_grad: float32 [2048, 4096], P(('dp', 'ctx'), 'tp')
- gate_grad: float32 [2048, 4096], P(('dp', 'ctx'), 'tp')
- output_grad: float32 [4096, 2048], P('tp', ('dp', 'ctx'))
- hidden_grad: float32 [2048, 4096], P(('dp', 'ctx'), 'tp')
- linear_grad: float32 [2048, 4096], P(('dp', 'ctx'), 'tp')
- down_grad: float32 [4096, 2048], P('tp', ('dp', 'ctx'))
The draws below stay inside these ranges and needn't reach their ends.
Inputs may be any that keep to these rules, and one draw needn't show every extreme that they name: Rows of group g after the first first_length[g] form a second sequence; in some group it is empty.
All inputs are finite; a program needn't handle non-finite values.
Results may differ from the reference program's by a relative error of at most 0.03.
Values may be sent and summed in bfloat16 or wider, within the bound.
No kernel may reach another device: no remote copies, remote signals or barrier semaphores. Data moves between devices by JAX's collectives and lax.ppermute only.
A program may use at most 128 MiB of HBM per device.

```python
import math
import jax
import jax.numpy as jnp
from jax import lax

D = 2048
HEADS = 8
DK = 256
DV = 512
FF = 4096
TOK_DEV = 256
PACK = 1024
TOKENS = 8192
QK = 2048
VD = 4096
N_DP = 8
N_CTX = 4


def draw_decay_scale(key, part):
    key = jax.random.fold_in(key, 11)
    spread = jax.random.uniform(key, (HEADS,), jnp.float32, math.log(0.3), math.log(40.0))
    return jnp.exp(spread)


def draw_first_length(key, part):
    key = jax.random.fold_in(key, 23)
    key_lengths, key_full = jax.random.split(key)
    lengths = jax.random.randint(key_lengths, (N_DP,), 3 * TOK_DEV + 1, N_CTX * TOK_DEV + 1)
    chosen = jax.random.randint(key_full, (), 0, N_DP)
    return jnp.where(jnp.arange(N_DP) == chosen, N_CTX * TOK_DEV, lengths).astype(jnp.int32)


def strengthened(values, stream_key, source, target, parts, factor):
    owner, partner = [(jnp.arange(values.shape[dim]) // (values.shape[dim] // parts)).reshape([-1 if axis == dim else 1 for axis in range(values.ndim)]) for dim in (source, target)]
    chosen = jax.random.permutation(stream_key, parts)[partner]
    strong = (owner == chosen) | (owner == (partner + parts // 2) % parts)
    return jnp.where(strong, factor * values, values)


def level_of(key, extent, shards, smallest, high):
    level = 1.0
    for axis_at, parts in shards:
        heights = jax.random.uniform(jax.random.fold_in(jax.random.fold_in(key, 6), axis_at), (parts,), jnp.float32, smallest / len(shards), high / len(shards))
        level = level * jnp.repeat(jnp.exp(heights), extent[axis_at] // parts).reshape((-1,) + (1,) * (len(extent) - 1 - axis_at))
    return level


def gaussian(key, extent, scale, bound, cuts=(), kind=jnp.bfloat16):
    entries = jax.random.normal(key, extent, jnp.float32) * scale
    if len(cuts) > 0:
        entries = level_of(key, extent, cuts, -0.22, 0.18) * entries
    return jnp.clip(entries, min=-bound, max=bound).astype(kind)


def gaussian_with(own_key, shape, scale, reach, cuts, heavy, kind=jnp.bfloat16):
    entries = scale * jax.random.normal(own_key, shape, jnp.float32)
    if cuts:
        entries = entries * level_of(own_key, shape, cuts, -0.22, 0.18)
    return jnp.clip(strengthened(entries, jax.random.fold_in(own_key, 3), *heavy), -reach, reach).astype(kind)


def setup_inputs(seed: int = 0) -> dict:
    arg_keys = jax.random.split(jax.random.key(seed), 15)
    tokens = gaussian(arg_keys[0], (TOKENS, D), 1.0, 6.0, ((0, 32),), jnp.float32)
    cotangent = gaussian_with(arg_keys[1], (TOKENS, D), 1.0, 6.0, ((0, 32),), (0, 1, 32, 2.75), jnp.float32)
    gain_first = jnp.clip(1.0 + 0.15 * jax.random.normal(arg_keys[2], (D,), jnp.float32), 0.25, 1.75)
    gain_second = jnp.clip(1.0 + 0.15 * jax.random.normal(arg_keys[3], (D,), jnp.float32), 0.25, 1.75)
    w_query = gaussian(arg_keys[4], (D, QK), D ** -0.5, 0.125, ((0, 32), (1, 4)))
    w_key = gaussian(arg_keys[5], (D, QK), D ** -0.5, 0.125, ((0, 32), (1, 4)))
    w_value = gaussian(arg_keys[6], (D, VD), D ** -0.5, 0.125, ((0, 32), (1, 4)))
    w_gate = gaussian(arg_keys[7], (D, VD), D ** -0.5, 0.125, ((0, 32), (1, 4)))
    w_output = gaussian(arg_keys[8], (VD, D), (VD // 2) ** -0.5, 0.125, ((0, 4), (1, 32)))
    w_hidden = gaussian(arg_keys[9], (D, FF), D ** -0.5, 0.125, ((0, 32), (1, 4)))
    w_linear = gaussian(arg_keys[10], (D, FF), D ** -0.5, 0.125, ((0, 32), (1, 4)))
    w_down = gaussian(arg_keys[11], (FF, D), (FF // 2) ** -0.5, 0.125, ((0, 4), (1, 32)))
    decay_scale = draw_decay_scale(jax.random.fold_in(arg_keys[14], 71), 0)
    first_length = draw_first_length(jax.random.fold_in(arg_keys[14], 71), 0)
    return dict(tokens=tokens, cotangent=cotangent, gain_first=gain_first, gain_second=gain_second, w_query=w_query, w_key=w_key, w_value=w_value, w_gate=w_gate, w_output=w_output, w_hidden=w_hidden, w_linear=w_linear, w_down=w_down, decay_scale=decay_scale, first_length=first_length)


@jax.custom_vjp
def low(v):
    return lax.optimization_barrier(v.astype(jnp.bfloat16)).astype(jnp.float32)

@jax.custom_vjp
def low_back(v):
    return v

def low_keep(v):
    return (low(v), None)

def low_pass(kept, grad):
    return (grad,)

def back_keep(v):
    return (v, None)

def back_low(kept, grad):
    return (low(grad),)
low.defvjp(low_keep, low_pass)
low_back.defvjp(back_keep, back_low)

def product(left, right):
    return jnp.dot(left, right, precision=lax.Precision.HIGHEST)

def mean_scale(values, gain):
    factor = lax.rsqrt(lax.optimization_barrier(jnp.mean(values * values, axis=-1, keepdims=True)) + 1e-06)
    return values * factor * gain

def gate_norm(gate_pre, retained):
    row_count = retained.shape[0]
    grouped = retained.reshape(row_count, -1, DV)
    centred = grouped - lax.optimization_barrier(jnp.mean(grouped, axis=-1, keepdims=True))
    normed = centred * lax.rsqrt(lax.optimization_barrier(jnp.mean(centred * centred, axis=-1, keepdims=True)) + 1.0 * DK)
    return gate_pre * jax.nn.sigmoid(gate_pre) * normed.reshape(row_count, -1)

def gelu_gate(hidden, linear):
    return jax.nn.gelu(hidden, approximate=True) * linear

def rotate(values, positions, direction):
    half = DK // 2
    frequency = 10000.0 ** (-(jnp.arange(half).astype(values.dtype) / half))
    angles = positions[:, None] * frequency[None, :]
    cosine = jnp.cos(angles)[:, None, :]
    sine = jnp.sin(angles)[:, None, :] * direction
    shaped = values.reshape(values.shape[0], -1, DK)
    first = shaped[..., :half]
    second = shaped[..., half:]
    turned = jnp.concatenate((first * cosine - second * sine, first * sine + second * cosine), axis=-1)
    return turned.reshape(values.shape)

def layer(tokens, length, gain_first, gain_second, w_query, w_key, w_value, w_gate, w_output, w_hidden, w_linear, w_down, decay_scale):
    normed_first = low(mean_scale(tokens, gain_first))
    query = low_back(product(normed_first, w_query))
    key_proj = low_back(product(normed_first, w_key))
    value = low(low_back(product(normed_first, w_value)))
    gate_pre = low_back(product(normed_first, w_gate))
    index = jnp.arange(PACK, dtype=jnp.int32)
    positions = index.astype(tokens.dtype)
    query_rot = low(rotate(query, positions, 1.0))
    key_rot = low(rotate(key_proj, positions, 1.0))
    offsets = index[:, None] - index[None, :]
    document = (index >= length).astype(jnp.int32)
    linked = (offsets >= 0) & (document[:, None] == document[None, :])
    rates = decay_scale / PACK
    decays = jnp.exp(-rates[:, None, None] * jnp.maximum(offsets, 0).astype(tokens.dtype)[None])
    mask = jnp.where(linked[None], decays, 0.0)
    query_heads = query_rot.reshape(PACK, HEADS, DK)
    key_heads = key_rot.reshape(PACK, HEADS, DK)
    value_heads = value.reshape(PACK, HEADS, DV)
    scores = jnp.einsum('ihd,jhd->hij', query_heads, key_heads, precision=lax.Precision.HIGHEST)
    retained = jnp.einsum('hij,jhe->ihe', scores * mask, value_heads, precision=lax.Precision.HIGHEST).reshape(PACK, VD)
    mixed = low(gate_norm(gate_pre, retained))
    hidden_state = tokens + low_back(product(mixed, w_output))
    normed_second = low(mean_scale(hidden_state, gain_second))
    hidden = low_back(product(normed_second, w_hidden))
    linear = low_back(product(normed_second, w_linear))
    activated = low(gelu_gate(hidden, linear))
    return hidden_state + low_back(product(activated, w_down))

def reference(tokens, cotangent, gain_first, gain_second, w_query, w_key, w_value, w_gate, w_output, w_hidden, w_linear, w_down, decay_scale, first_length):

    def whole(tokens, gain_first, gain_second, w_query, w_key, w_value, w_gate, w_output, w_hidden, w_linear, w_down):
        grouped = tokens.reshape(N_DP, PACK, D)

        def one_group(item):
            return layer(item[0], item[1], gain_first, gain_second, w_query, w_key, w_value, w_gate, w_output, w_hidden, w_linear, w_down, decay_scale)
        return lax.map(jax.checkpoint(one_group), (grouped, first_length)).reshape(TOKENS, D)
    result, pullback = jax.vjp(whole, tokens, gain_first, gain_second, w_query.astype(jnp.float32), w_key.astype(jnp.float32), w_value.astype(jnp.float32), w_gate.astype(jnp.float32), w_output.astype(jnp.float32), w_hidden.astype(jnp.float32), w_linear.astype(jnp.float32), w_down.astype(jnp.float32))
    grads = pullback(cotangent)
    return (result, grads[0], grads[1], grads[2], grads[3], grads[4], grads[5], grads[6], grads[7], grads[8], grads[9], grads[10])
```

```python
import jax
import jax.numpy as jnp
import numpy as np
from jax import lax
from jax.sharding import Mesh, PartitionSpec as P

DK = 256
DV = 512
BF = jnp.bfloat16
F32 = jnp.float32
XY = ("x", "ctx")


def shift(value, axis, offset):
    n = lax.axis_size(axis)
    return lax.ppermute(value, axis, [(i, (i + offset) % n) for i in range(n)])


def shift_open(value, axis, offset):
    n = lax.axis_size(axis)
    return lax.ppermute(
        value, axis, [(i, i + offset) for i in range(n) if 0 <= i + offset < n]
    )


def swap(value):
    return lax.ppermute(value, "core", [(0, 1), (1, 0)])


def dot(left, right):
    return jnp.dot(left, right, preferred_element_type=F32)


def dot_t(left, right):
    return lax.dot_general(left, right, (((1,), (1,)), ((), ())), preferred_element_type=F32)


def t_dot(left, right):
    return lax.dot_general(left, right, (((0,), (0,)), ((), ())), preferred_element_type=F32)


def both(value):
    return jnp.concatenate((value, swap(value)), axis=0)


def heads_total(partial):
    rows = partial.shape[0] // 2
    low = partial[rows:].astype(BF)
    chip = partial[:rows] + swap(low).astype(F32)
    blocks = chip.astype(BF).reshape(4, rows // 4, -1)
    got = [shift(blocks[o], "tp", o) for o in (1, 2, 3)]
    mine = blocks[0].astype(F32)
    for part in got:
        mine = mine + part.astype(F32)
    mine = mine.astype(BF)
    parts = [mine] + [shift(mine, "tp", -o) for o in (1, 2, 3)]
    return jnp.concatenate(parts, axis=0).astype(F32)


def mean_scale(values, gain):
    factor = lax.rsqrt(jnp.mean(values * values, axis=-1, keepdims=True) + 1e-06)
    return values * factor * gain


def mean_scale_back(values, gain, grad):
    factor = lax.rsqrt(jnp.mean(values * values, axis=-1, keepdims=True) + 1e-06)
    unit = values * factor
    scaled = grad * gain
    out = factor * (scaled - unit * jnp.mean(scaled * unit, axis=-1, keepdims=True))
    part = jnp.sum((grad * unit).reshape(4, values.shape[0] // 4, -1), axis=1)
    return out, (part[0] + part[2]) + (part[1] + part[3])


def gate_norm(gate_pre, retained):
    centred = retained - jnp.mean(retained, axis=-1, keepdims=True)
    normed = centred * lax.rsqrt(jnp.mean(centred * centred, axis=-1, keepdims=True) + 1.0 * DK)
    return gate_pre * jax.nn.sigmoid(gate_pre) * normed


def gelu_gate(hidden, linear):
    return jax.nn.gelu(hidden, approximate=True) * linear


def rotate(values, cosine, sine):
    half = DK // 2
    first = values[:, :half]
    second = values[:, half:]
    return jnp.concatenate((first * cosine - second * sine, first * sine + second * cosine), axis=1)


def ein(spec, left, right):
    return jnp.einsum(spec, left, right, preferred_element_type=F32)


def columns_in(value):
    lead = value.shape[:-1]
    return value.reshape(*lead, 4, 2, 4, 64).swapaxes(-3, -2).reshape(*lead, 2048)


def columns_out(value):
    lead = value.shape[:-1]
    return value.reshape(*lead, 4, 4, 2, 64).swapaxes(-3, -2).reshape(*lead, 2048)


def roll_rows(value, amount):
    return lax.dynamic_slice_in_dim(jnp.concatenate((value, value), axis=0), amount, value.shape[0], 0)


def per_device(
    tokens,
    cotangent,
    gain_first,
    gain_second,
    w_query,
    w_key,
    w_value,
    w_gate,
    w_output,
    w_hidden,
    w_linear,
    w_down,
    decay_scale,
    first_length,
):
    rows = tokens.shape[0]
    core = lax.axis_index("core")
    place = lax.axis_index("ctx")
    plane = lax.axis_index("tp")

    def per_head(weight):
        return weight.reshape(weight.shape[0], 2, -1).swapaxes(0, 1)

    def gathered(weights):
        own = jnp.concatenate([per_head(w) for w in weights], axis=2)
        mine = lax.dynamic_index_in_dim(own, core, 0, False)
        theirs = swap(lax.dynamic_index_in_dim(own, 1 - core, 0, False))
        block = jnp.where(
            core == 0, jnp.concatenate((mine, theirs)), jnp.concatenate((theirs, mine))
        )
        return lax.all_gather(block, XY, axis=0, tiled=True)

    attn = gathered((w_query, w_key, w_value, w_gate))
    rest = gathered((w_output.T, w_hidden, w_linear, w_down.T))
    w_out_t = rest[:, :DV]
    w_mlp = rest[:, DV : 3 * DV]
    w_down_t = rest[:, 3 * DV :]

    tokens = columns_in(roll_rows(tokens, plane * (rows // 4)))
    cotangent = columns_in(roll_rows(cotangent, plane * (rows // 4)))
    gain_first = columns_in(gain_first)
    gain_second = columns_in(gain_second)

    rate = lax.dynamic_index_in_dim(decay_scale, core, 0, False) / 1024.0
    local = (jnp.arange(rows, dtype=jnp.int32) + plane * (rows // 4)) % rows
    index = place * rows + local
    lengths = jnp.concatenate((first_length, swap(first_length)))
    document = (index[None, :] >= lengths[:, None]).astype(jnp.int32)
    carried = (document == 0).astype(F32)
    steps = local.astype(F32)
    offsets = local[:, None] - local[None, :]
    linked = (offsets >= 0)[None] & (document[:, :, None] == document[:, None, :])
    mask = jnp.where(
        linked, jnp.exp(-rate * jnp.maximum(offsets, 0).astype(F32))[None], 0.0
    )
    enter = (carried * jnp.exp(-rate * (steps + 1.0))[None])[:, :, None]
    leave = jnp.exp(-rate * (rows - 1.0 - steps))[None, :, None]
    hop = jnp.exp(-rate * rows)
    half = DK // 2
    frequency = 10000.0 ** (-(jnp.arange(half).astype(F32) / half))
    angles = index.astype(F32)[:, None] * frequency[None, :]
    cosine = jnp.tile(jnp.cos(angles), (2, 1))
    sine = jnp.tile(jnp.sin(angles), (2, 1))

    def carry(state, way):
        low = state.astype(BF)
        near, mid, far = [shift_open(low, "ctx", way * o).astype(F32) for o in (1, 2, 3)]
        return near + hop * (mid + hop * far)

    normed_first = mean_scale(tokens, gain_first)
    x_first = both(normed_first.astype(BF))
    projected = dot(x_first, attn)
    query = rotate(projected[:, :DK], cosine, sine).astype(BF).reshape(2, rows, DK)
    key = rotate(projected[:, DK : 2 * DK], cosine, sine).astype(BF).reshape(2, rows, DK)
    value = projected[:, 2 * DK : 2 * DK + DV].astype(BF).reshape(2, rows, DV)
    gate_pre = projected[:, 2 * DK + DV :]
    key_out = (key.astype(F32) * leave).astype(BF)
    state_in = carry(ein("gjd,gje->gde", key_out, value), 1).astype(BF)
    weighted = (ein("gid,gjd->gij", query, key) * mask).astype(BF)
    inner = ein("gij,gje->gie", weighted, value)
    retained = (inner + ein("gid,gde->gie", query, state_in) * enter).reshape(2 * rows, DV)
    mixed_full, gate_back = jax.vjp(gate_norm, gate_pre, retained)
    mixed = mixed_full.astype(BF)
    hidden_state = tokens + heads_total(dot_t(mixed, w_out_t))
    normed_second = mean_scale(hidden_state, gain_second)
    x_second = both(normed_second.astype(BF))
    paired = dot(x_second, w_mlp)
    activated_full, gelu_back = jax.vjp(gelu_gate, paired[:, :DV], paired[:, DV:])
    activated = activated_full.astype(BF)
    layer_out = hidden_state + heads_total(dot_t(activated, w_down_t))
    g_out = both(cotangent.astype(BF))
    grad_hidden, grad_linear = gelu_back(dot(g_out, w_down_t))
    grad_pair = jnp.concatenate((grad_hidden, grad_linear), axis=1).astype(BF)
    grad_second = heads_total(dot_t(grad_pair, w_mlp))
    d_mlp = jnp.concatenate((t_dot(x_second, grad_pair), t_dot(g_out, activated)), axis=1).astype(BF)
    grad_state_part, gain_second_part = mean_scale_back(hidden_state, gain_second, grad_second)
    grad_state = cotangent + grad_state_part
    g_state = both(grad_state.astype(BF))
    grad_gate, grad_retained = gate_back(dot(g_state, w_out_t))
    grad_heads = grad_retained.reshape(2, rows, DV)
    grad_low = grad_heads.astype(BF)
    query_in = (query.astype(F32) * enter).astype(BF)
    state_back = carry(ein("gid,gie->gde", query_in, grad_low), -1).astype(BF)
    grad_scores = (ein("gie,gje->gij", grad_low, value) * mask).astype(BF)
    grad_query = ein("gij,gjd->gid", grad_scores, key) + enter * ein("gie,gde->gid", grad_low, state_in)
    grad_key = ein("gij,gid->gjd", grad_scores, query) + leave * ein("gje,gde->gjd", value, state_back)
    grad_value = ein("gij,gie->gje", weighted, grad_low) + ein("gjd,gde->gje", key_out, state_back)
    grad_proj = jnp.concatenate(
        (
            rotate(grad_query.reshape(2 * rows, DK), cosine, -sine),
            rotate(grad_key.reshape(2 * rows, DK), cosine, -sine),
            grad_value.reshape(2 * rows, DV),
            grad_gate,
        ),
        axis=1,
    ).astype(BF)
    d_attn = jnp.concatenate((t_dot(x_first, grad_proj), t_dot(g_state, mixed)), axis=1).astype(BF)
    grad_first = heads_total(dot_t(grad_proj, attn))
    grad_token_part, gain_first_part = mean_scale_back(tokens, gain_first, grad_first)
    input_grad = grad_state + grad_token_part

    def scattered(grad):
        block = lax.psum_scatter(grad, XY, scatter_dimension=0, tiled=True)
        block = block.reshape(2, 64, -1)
        mine = lax.dynamic_index_in_dim(block, core, 0, False)
        theirs = swap(lax.dynamic_index_in_dim(block, 1 - core, 0, False))
        return (
            jnp.where(core == 0, mine, theirs).astype(F32),
            jnp.where(core == 0, theirs, mine).astype(F32),
        )

    def wide(pair, start, stop):
        return jnp.concatenate((pair[0][:, start:stop], pair[1][:, start:stop]), axis=1)

    mlp_sum = scattered(d_mlp)
    attn_sum = scattered(d_attn)

    def gain_total(part):
        part = part + swap(part)
        for axis in XY:
            part = part + shift(part, axis, 1) + shift(part, axis, 2) + shift(part, axis, 3)
        spot = (lax.axis_index("x") * 4 + place) * 2 + core
        return lax.dynamic_slice_in_dim(part, spot * 64, 64, 0)

    gains = gain_total(jnp.stack((gain_first_part, gain_second_part)).T)

    def rows_out(value):
        return roll_rows(columns_out(value), rows - plane * (rows // 4))

    return (
        rows_out(layer_out),
        rows_out(input_grad),
        gains[:, 0],
        gains[:, 1],
        wide(attn_sum, 0, DK),
        wide(attn_sum, DK, 2 * DK),
        wide(attn_sum, 2 * DK, 2 * DK + DV),
        wide(attn_sum, 2 * DK + DV, 2 * DK + 2 * DV),
        wide(attn_sum, 2 * DK + 2 * DV, 2 * DK + 3 * DV).T,
        wide(mlp_sum, 0, DV),
        wide(mlp_sum, DV, 2 * DV),
        wide(mlp_sum, 2 * DV, 3 * DV).T,
    )


def solution(mesh):
    fine = Mesh(np.asarray(mesh.devices).reshape(4, 2, 4, 4), ("x", "core", "ctx", "tp"))
    split = ("x", "core", "ctx")
    row = P(split, None)
    win = P(split, "tp")
    wout = P("tp", split)
    in_specs = (row, row, P(), P(), win, win, win, win, wout, win, win, wout, P("tp"), P(("x", "core")))
    out_specs = (row, row, P(split), P(split), win, win, win, win, wout, win, win, wout)
    return jax.shard_map(
        per_device, mesh=fine, in_specs=in_specs, out_specs=out_specs, check_vma=False
    )
```

```python
import jax
import jax.numpy as jnp
import numpy as np
from jax import lax
from jax.experimental import pallas as pl
from jax.experimental.pallas import tpu as pltpu
from jax.sharding import Mesh, PartitionSpec as P

D = 2048
DK = 256
DV = 512
SLAB = 512
BF = jnp.bfloat16
F32 = jnp.float32
XY = ("x", "ctx")
MIB = 1 << 20


def shift(value, axis, offset):
    n = lax.axis_size(axis)
    return lax.ppermute(value, axis, [(i, (i + offset) % n) for i in range(n)])


def shift_open(value, axis, offset):
    n = lax.axis_size(axis)
    return lax.ppermute(
        value, axis, [(i, i + offset) for i in range(n) if 0 <= i + offset < n]
    )


def swap(value):
    return lax.ppermute(value, "core", [(0, 1), (1, 0)])


def after(value, *earlier):
    return lax.optimization_barrier((value, *earlier))[0]


def call(body, grid, ins, outs, shapes, scalars, operands, name, flops=0, scratch=()):
    nbytes = sum(a.size * a.dtype.itemsize for a in jax.tree.leaves((operands, shapes)))
    return pl.pallas_call(
        body,
        out_shape=shapes,
        grid_spec=pltpu.PrefetchScalarGridSpec(
            num_scalar_prefetch=1, grid=grid, in_specs=ins, out_specs=outs, scratch_shapes=scratch
        ),
        compiler_params=pltpu.CompilerParams(
            vmem_limit_bytes=48 * MIB, dimension_semantics=("arbitrary",) * len(grid)
        ),
        cost_estimate=pl.CostEstimate(flops=flops, bytes_accessed=nbytes, transcendentals=0),
        name=name,
    )(scalars, *operands)


def whole(array):
    return pl.BlockSpec(array.shape, lambda *_: (0,) * array.ndim)


def sds(shape, dtype):
    return jax.ShapeDtypeStruct(shape, dtype)


def slab_rows(ref, core):
    return jnp.concatenate(
        [ref[0, y, jnp.bitwise_xor(c, core)] for c in (0, 1) for y in range(4)], axis=0
    )


def mm_in(left, right, weight, start, width, scalars, name):
    def body(s_ref, a_ref, b_ref, w_ref, out_ref):
        step = pl.program_id(0)
        part = jnp.dot(
            jnp.concatenate((a_ref[...], b_ref[...]), axis=0),
            slab_rows(w_ref, s_ref[0]),
            preferred_element_type=F32,
        )

        @pl.when(step == 0)
        def _():
            out_ref[...] = part

        @pl.when(step > 0)
        def _():
            out_ref[...] += part

    rows = left.shape[0]
    cols = pl.BlockSpec((rows, SLAB), lambda i, s: (0, i))
    return call(
        body,
        (4,),
        [cols, cols, pl.BlockSpec((1, 4, 2, 64, width), lambda i, s: (i, 0, 0, 0, start // width))],
        pl.BlockSpec((2 * rows, width), lambda i, s: (0, 0)),
        sds((2 * rows, width), F32),
        scalars,
        (left, right, weight),
        name,
        flops=4 * rows * D * width,
    )


def mm_back(grad, weight, start, scalars, name):
    rows, width = grad.shape
    half = rows // 2

    def body(s_ref, g_ref, w_ref, own_ref, other_ref):
        out = lax.dot_general(
            g_ref[...],
            slab_rows(w_ref, s_ref[0]),
            (((1,), (1,)), ((), ())),
            preferred_element_type=F32,
        )
        own_ref[...] = out[:half]
        other_ref[...] = out[half:].astype(BF)

    cols = pl.BlockSpec((half, SLAB), lambda i, s: (0, i))
    return call(
        body,
        (4,),
        [whole(grad), pl.BlockSpec((1, 4, 2, 64, width), lambda i, s: (i, 0, 0, 0, start // width))],
        (cols, cols),
        (sds((half, D), F32), sds((half, D), BF)),
        scalars,
        (grad, weight),
        name,
        flops=2 * rows * D * width,
    )


def mm_weight(pairs, scalars, name):
    widths = [grad.shape[1] for _, grad in pairs]
    rows = pairs[0][0][0].shape[0]

    def body(s_ref, *refs):
        out_ref = refs[-1]
        at = 0
        for k, width in enumerate(widths):
            a_ref, b_ref, g_ref = refs[3 * k : 3 * k + 3]
            out = lax.dot_general(
                jnp.concatenate((a_ref[...], b_ref[...]), axis=0),
                g_ref[...],
                (((0,), (0,)), ((), ())),
                preferred_element_type=F32,
            ).astype(BF)
            for c in (0, 1):
                for y in range(4):
                    first = (c * 4 + y) * 64
                    out_ref[0, y, jnp.bitwise_xor(c, s_ref[0]), :, at : at + width] = out[
                        first : first + 64
                    ]
            at += width

    cols = pl.BlockSpec((rows, SLAB), lambda i, s: (0, i))
    specs, operands = [], []
    for (a, b), grad in pairs:
        specs += [cols, cols, whole(grad)]
        operands += [a, b, grad]
    total = sum(widths)
    return call(
        body,
        (4,),
        specs,
        pl.BlockSpec((1, 4, 2, 64, total), lambda i, s: (i, 0, 0, 0, 0)),
        sds((4, 4, 2, 64, total), BF),
        scalars,
        tuple(operands),
        name,
        flops=4 * rows * D * total,
    )


def split_heads(weights, turned, scalars, name):
    widths = [(w.shape[0] if t else w.shape[1]) // 2 for w, t in zip(weights, turned)]

    def body(s_ref, *refs):
        mine_ref, theirs_ref = refs[-2:]
        core = s_ref[0]
        for out_ref, head in ((mine_ref, core), (theirs_ref, 1 - core)):
            at = 0
            for ref, width, turn in zip(refs, widths, turned):
                if turn:
                    piece = ref[pl.ds(pl.multiple_of(head * width, width), width), :]
                    piece = piece.astype(F32).T.astype(BF)
                else:
                    piece = ref[:, pl.ds(pl.multiple_of(head * width, width), width)]
                out_ref[:, at : at + width] = piece
                at += width

    total = sum(widths)
    spec = pl.BlockSpec((64, total), lambda i, s: (0, 0))
    return call(
        body,
        (1,),
        [whole(w) for w in weights],
        (spec, spec),
        (sds((64, total), BF),) * 2,
        scalars,
        tuple(weights),
        name,
    )


def join_heads(mine, theirs, widths, turned, scalars, name):
    def body(s_ref, mine_ref, theirs_ref, *outs):
        core = s_ref[0]
        for in_ref, head in ((mine_ref, core), (theirs_ref, 1 - core)):
            at = 0
            for ref, width, turn in zip(outs, widths, turned):
                piece = in_ref[:, at : at + width].astype(F32)
                span = pl.ds(pl.multiple_of(head * width, width), width)
                if turn:
                    ref[span, :] = piece.T
                else:
                    ref[:, span] = piece
                at += width

    shapes = tuple(
        sds((2 * w, 64) if t else (64, 2 * w), F32) for w, t in zip(widths, turned)
    )
    return call(
        body,
        (1,),
        [whole(mine), whole(theirs)],
        tuple(whole(s) for s in shapes),
        shapes,
        scalars,
        (mine, theirs),
        name,
    )


def scale_of(values):
    return lax.rsqrt(jnp.mean(values * values, axis=-1, keepdims=True) + 1e-06)


def turned_spec(rows):
    return pl.BlockSpec((rows, D), lambda i, s: (lax.rem(i + s[1], 4), 0))


def plain_spec(rows):
    return pl.BlockSpec((rows, D), lambda i, s: (i, 0))


def enter_rows(tokens, cotangent, gain, scalars):
    rows = tokens.shape[0]
    block = rows // 4

    def body(s_ref, t_ref, c_ref, g_ref, t_out, c_out, n_out, l_out):
        values = t_ref[...]
        t_out[...] = values
        n_out[...] = (values * scale_of(values) * g_ref[...]).astype(BF)
        c_out[...] = c_ref[...]
        l_out[...] = c_ref[...].astype(BF)

    turn, plain = turned_spec(block), plain_spec(block)
    full = (rows, D)
    return call(
        body,
        (4,),
        [turn, turn, whole(gain)],
        (plain,) * 4,
        (sds(full, F32), sds(full, F32), sds(full, BF), sds(full, BF)),
        scalars,
        (tokens, cotangent, gain),
        "enter_rows",
    )


def each_part(refs, work):
    step = pl.program_id(0)
    for k, ref in enumerate(refs):

        @pl.when(step == k)
        def _(ref=ref):
            work(ref[...].astype(F32))


def second_norm(tokens, parts, gain, scalars):
    rows = tokens.shape[0]
    block = rows // 4

    def body(s_ref, t_ref, g_ref, *refs):
        h_out, n_out = refs[4:]

        def work(part):
            values = t_ref[...] + part
            h_out[...] = values
            n_out[...] = (values * scale_of(values) * g_ref[...]).astype(BF)

        each_part(refs[:4], work)

    plain = plain_spec(block)
    return call(
        body,
        (4,),
        [plain, whole(gain)] + [whole(p) for p in parts],
        (plain, plain),
        (sds((rows, D), F32), sds((rows, D), BF)),
        scalars,
        (tokens, gain, *parts),
        "second_norm",
    )


def leave_rows(hidden, parts, scalars):
    rows = hidden.shape[0]
    block = rows // 4

    def body(s_ref, h_ref, *refs):
        def work(part):
            refs[4][...] = h_ref[...] + part

        each_part(refs[:4], work)

    return call(
        body,
        (4,),
        [plain_spec(block)] + [whole(p) for p in parts],
        turned_spec(block),
        sds((rows, D), F32),
        scalars,
        (hidden, *parts),
        "leave_rows",
    )


def norm_back(values, upstream, parts, gain, last, scalars, name):
    rows = values.shape[0]
    block = rows // 4

    def body(s_ref, v_ref, u_ref, g_ref, *refs):
        outs = refs[4:]

        def work(part):
            values = v_ref[...]
            factor = scale_of(values)
            unit = values * factor
            scaled = part * g_ref[...]
            out = u_ref[...] + factor * (
                scaled - unit * jnp.mean(scaled * unit, axis=-1, keepdims=True)
            )
            outs[0][...] = out
            outs[1][0] = jnp.sum(part * unit, axis=0, keepdims=True)
            if not last:
                outs[2][...] = out.astype(BF)

        each_part(refs[:4], work)

    plain = plain_spec(block)
    specs = [turned_spec(block) if last else plain, pl.BlockSpec((1, 1, D), lambda i, s: (i, 0, 0))]
    shapes = [sds((rows, D), F32), sds((4, 1, D), F32)]
    if not last:
        specs.append(plain)
        shapes.append(sds((rows, D), BF))
    out = call(
        body,
        (4,),
        [plain, plain, whole(gain)] + [whole(p) for p in parts],
        tuple(specs),
        tuple(shapes),
        scalars,
        (values, upstream, gain, *parts),
        name,
    )
    gains = out[1][:, 0]
    return (out[0], (gains[0] + gains[2]) + (gains[1] + gains[3]), *out[2:])


def heads_total(own, other):
    came = swap(other)
    block = own.shape[0] // 4
    blocks = [
        (own[o * block : (o + 1) * block] + came[o * block : (o + 1) * block].astype(F32)).astype(BF)
        for o in range(4)
    ]
    got = [shift(blocks[o], "tp", o) for o in (1, 3, 2)]
    mine = blocks[0].astype(F32)
    for part in got:
        mine = mine + part.astype(F32)
    mine = mine.astype(BF)
    near, far, mid = [shift(mine, "tp", -o) for o in (1, 3, 2)]
    return (mine, near, mid, far)


def gate_norm(gate_pre, retained):
    centred = retained - jnp.mean(retained, axis=-1, keepdims=True)
    normed = centred * lax.rsqrt(jnp.mean(centred * centred, axis=-1, keepdims=True) + 1.0 * DK)
    return gate_pre * jax.nn.sigmoid(gate_pre) * normed


def gelu_gate(hidden, linear):
    return jax.nn.gelu(hidden, approximate=True) * linear


def rotate(values, cosine, sine):
    half = DK // 2
    first = values[:, :half]
    second = values[:, half:]
    return jnp.concatenate((first * cosine - second * sine, first * sine + second * cosine), axis=1)


def ein(spec, left, right):
    return jnp.einsum(spec, left, right, preferred_element_type=F32)


def per_device(
    tokens,
    cotangent,
    gain_first,
    gain_second,
    w_query,
    w_key,
    w_value,
    w_gate,
    w_output,
    w_hidden,
    w_linear,
    w_down,
    decay_scale,
    first_length,
):
    rows = tokens.shape[0]
    core = lax.axis_index("core")
    place = lax.axis_index("ctx")
    plane = lax.axis_index("tp")
    scalars = jnp.stack((core, plane)).astype(jnp.int32)

    def gathered(mine, theirs):
        block = jnp.concatenate((mine, swap(theirs)), axis=0)
        return lax.all_gather(block, XY, axis=0, tiled=True).reshape(4, 4, 2, 64, -1)

    attn_split = split_heads(
        (w_query, w_key, w_value, w_gate), (False,) * 4, scalars, "split_attn"
    )
    attn = gathered(*attn_split)
    rest = gathered(
        *split_heads(
            after((w_hidden, w_linear, w_output, w_down), attn_split[0]),
            (False, False, True, True),
            scalars,
            "split_rest",
        )
    )
    tokens, cotangent = after((tokens, cotangent), attn_split[0])
    gain_first = gain_first.reshape(1, D)
    gain_second = gain_second.reshape(1, D)
    tokens, cotangent, normed_first, cot_low = enter_rows(tokens, cotangent, gain_first, scalars)

    rate = lax.dynamic_index_in_dim(decay_scale, core, 0, False) / 1024.0
    local = (jnp.arange(rows, dtype=jnp.int32) + plane * (rows // 4)) % rows
    index = place * rows + local
    lengths = jnp.concatenate((first_length, swap(first_length)))
    document = (index[None, :] >= lengths[:, None]).astype(jnp.int32)
    carried = (document == 0).astype(F32)
    steps = local.astype(F32)
    offsets = local[:, None] - local[None, :]
    linked = (offsets >= 0)[None] & (document[:, :, None] == document[:, None, :])
    mask = jnp.where(
        linked, jnp.exp(-rate * jnp.maximum(offsets, 0).astype(F32))[None], 0.0
    )
    enter = (carried * jnp.exp(-rate * (steps + 1.0))[None])[:, :, None]
    leave = jnp.exp(-rate * (rows - 1.0 - steps))[None, :, None]
    hop = jnp.exp(-rate * rows)
    half = DK // 2
    frequency = 10000.0 ** (-(jnp.arange(half).astype(F32) / half))
    angles = index.astype(F32)[:, None] * frequency[None, :]
    cosine = jnp.tile(jnp.cos(angles), (2, 1))
    sine = jnp.tile(jnp.sin(angles), (2, 1))

    def carry(state, way):
        low = state.astype(BF)
        near, mid, far = [shift_open(low, "ctx", way * o).astype(F32) for o in (1, 2, 3)]
        return near + hop * (mid + hop * far)

    x_first = (normed_first, swap(normed_first))
    projected = mm_in(*x_first, attn, 0, 1536, scalars, "project_attn")
    query = rotate(projected[:, :DK], cosine, sine).astype(BF).reshape(2, rows, DK)
    key = rotate(projected[:, DK : 2 * DK], cosine, sine).astype(BF).reshape(2, rows, DK)
    value = projected[:, 2 * DK : 2 * DK + DV].astype(BF).reshape(2, rows, DV)
    gate_pre = projected[:, 2 * DK + DV :]
    key_out = (key.astype(F32) * leave).astype(BF)
    state_in = carry(ein("gjd,gje->gde", key_out, value), 1).astype(BF)
    weighted = (ein("gid,gjd->gij", query, key) * mask).astype(BF)
    inner = ein("gij,gje->gie", weighted, value)
    retained = (inner + ein("gid,gde->gie", query, state_in) * enter).reshape(2 * rows, DV)
    mixed_full, gate_back = jax.vjp(gate_norm, gate_pre, retained)
    mixed = mixed_full.astype(BF)
    parts = heads_total(*mm_back(mixed, rest, 2 * DV, scalars, "project_out"))
    g_out = (cot_low, swap(cot_low))
    grad_activated = mm_in(*g_out, rest, 3 * DV, DV, scalars, "back_down")
    hidden_state, normed_second = second_norm(tokens, parts, gain_second, scalars)
    x_second = (normed_second, swap(normed_second))
    paired = mm_in(*x_second, rest, 0, 2 * DV, scalars, "project_mlp")
    activated_full, gelu_back = jax.vjp(gelu_gate, paired[:, :DV], paired[:, DV:])
    activated = activated_full.astype(BF)
    grad_pair = jnp.concatenate(gelu_back(grad_activated), axis=1).astype(BF)
    parts = heads_total(*mm_back(grad_pair, rest, 0, scalars, "back_mlp"))
    layer_parts = heads_total(*mm_back(activated, rest, 3 * DV, scalars, "project_down"))
    layer_out = leave_rows(hidden_state, layer_parts, scalars)
    d_mlp = mm_weight(
        ((x_second, grad_pair), (g_out, activated)), scalars, "weight_mlp"
    )
    grad_state, gain_second_part, grad_state_low = norm_back(
        hidden_state, cotangent, parts, gain_second, False, scalars, "second_back"
    )
    g_state = (grad_state_low, swap(grad_state_low))
    grad_mixed = mm_in(*g_state, rest, 2 * DV, DV, scalars, "back_out")
    grad_gate, grad_retained = gate_back(grad_mixed)
    grad_low = grad_retained.reshape(2, rows, DV).astype(BF)
    query_in = (query.astype(F32) * enter).astype(BF)
    state_back = carry(ein("gid,gie->gde", query_in, grad_low), -1).astype(BF)
    grad_scores = (ein("gie,gje->gij", grad_low, value) * mask).astype(BF)
    grad_query = ein("gij,gjd->gid", grad_scores, key) + enter * ein("gie,gde->gid", grad_low, state_in)
    grad_key = ein("gij,gid->gjd", grad_scores, query) + leave * ein("gje,gde->gjd", value, state_back)
    grad_value = ein("gij,gie->gje", weighted, grad_low) + ein("gjd,gde->gje", key_out, state_back)
    grad_proj = jnp.concatenate(
        (
            rotate(grad_query.reshape(2 * rows, DK), cosine, -sine),
            rotate(grad_key.reshape(2 * rows, DK), cosine, -sine),
            grad_value.reshape(2 * rows, DV),
            grad_gate,
        ),
        axis=1,
    ).astype(BF)
    d_attn = mm_weight(((x_first, grad_proj), (g_state, mixed)), scalars, "weight_attn")
    parts = heads_total(*mm_back(grad_proj, attn, 0, scalars, "back_attn"))
    input_grad, gain_first_part = norm_back(
        tokens, grad_state, parts, gain_first, True, scalars, "first_back"
    )

    def scattered(grad):
        block = lax.psum_scatter(
            grad.reshape(16, 128, -1).reshape(2048, -1), XY, scatter_dimension=0, tiled=True
        )
        return block[:64], swap(block[64:])

    d_hidden, d_linear, d_down = join_heads(
        *scattered(d_mlp), (DV, DV, DV), (False, False, True), scalars, "join_mlp"
    )
    d_query, d_key, d_value, d_gate, d_output = join_heads(
        *scattered(d_attn),
        (DK, DK, DV, DV, DV),
        (False, False, False, False, True),
        scalars,
        "join_attn",
    )

    def gain_total(part):
        part = part + swap(part)
        for axis in XY:
            part = part + shift(part, axis, 1) + shift(part, axis, 2) + shift(part, axis, 3)
        spot = (lax.axis_index("x") * 2 + core) * 4 + place
        return lax.dynamic_slice_in_dim(part, spot * 64, 64, 1)

    gains = gain_total(jnp.stack((gain_first_part, gain_second_part)))
    return (
        layer_out,
        input_grad,
        gains[0],
        gains[1],
        d_query,
        d_key,
        d_value,
        d_gate,
        d_output,
        d_hidden,
        d_linear,
        d_down,
    )


def solution(mesh):
    fine = Mesh(np.asarray(mesh.devices).reshape(4, 2, 4, 4), ("x", "core", "ctx", "tp"))
    split = ("x", "core", "ctx")
    row = P(split, None)
    win = P(split, "tp")
    wout = P("tp", split)
    in_specs = (row, row, P(), P(), win, win, win, win, wout, win, win, wout, P("tp"), P(("x", "core")))
    out_specs = (row, row, P(split), P(split), win, win, win, win, wout, win, win, wout)
    return jax.shard_map(
        per_device, mesh=fine, in_specs=in_specs, out_specs=out_specs, check_vma=False
    )
```

```python
import jax
import jax.numpy as jnp
import numpy as np
from jax import lax
from jax.experimental import pallas as pl
from jax.experimental.pallas import tpu as pltpu
from jax.sharding import Mesh, PartitionSpec as P

D = 2048
DK = 256
DV = 512
SLAB = 512
BF = jnp.bfloat16
F32 = jnp.float32
XY = ("x", "ctx")
MIB = 1 << 20


def shift(value, axis, offset):
    n = lax.axis_size(axis)
    return lax.ppermute(value, axis, [(i, (i + offset) % n) for i in range(n)])


def shift_open(value, axis, offset):
    n = lax.axis_size(axis)
    return lax.ppermute(
        value, axis, [(i, i + offset) for i in range(n) if 0 <= i + offset < n]
    )


def swap(value):
    return lax.ppermute(value, "core", [(0, 1), (1, 0)])


def after(value, *earlier):
    return lax.optimization_barrier((value, *earlier))[0]


def call(body, grid, ins, outs, shapes, scalars, operands, name, flops=0, scratch=(), deps=()):
    nbytes = sum(a.size * a.dtype.itemsize for a in jax.tree.leaves((operands, shapes)))
    count = len(operands)

    def kernel(s_ref, *refs):
        body(s_ref, *refs[:count], *refs[count + len(deps) :])

    ins = [*ins, *[pl.BlockSpec(memory_space=pl.ANY)] * len(deps)]
    return pl.pallas_call(
        kernel,
        out_shape=shapes,
        grid_spec=pltpu.PrefetchScalarGridSpec(
            num_scalar_prefetch=1, grid=grid, in_specs=ins, out_specs=outs, scratch_shapes=scratch
        ),
        compiler_params=pltpu.CompilerParams(
            vmem_limit_bytes=48 * MIB, dimension_semantics=("arbitrary",) * len(grid)
        ),
        cost_estimate=pl.CostEstimate(flops=flops, bytes_accessed=nbytes, transcendentals=0),
        name=name,
    )(scalars, *operands, *deps)


def whole(array):
    return pl.BlockSpec(array.shape, lambda *_: (0,) * array.ndim)


def sds(shape, dtype):
    return jax.ShapeDtypeStruct(shape, dtype)


def slab_rows(ref, core):
    if ref.shape[1] == 2:
        return ref[0].reshape(SLAB, ref.shape[-1])
    return jnp.concatenate(
        [ref[0, y, jnp.bitwise_xor(c, core)] for c in (0, 1) for y in range(4)], axis=0
    )


def slab_spec(weight, start, width):
    return pl.BlockSpec((1, *weight.shape[1:4], width), lambda i, s: (i, 0, 0, 0, start // width))


def hop(value, first, offset):
    pairs = []
    for x in range(4):
        for core in (0, 1):
            for y in range(4):
                to = ((x + offset) % 4, y) if (core == 0) == first else (x, (y + offset) % 4)
                pairs.append(((x * 2 + core) * 4 + y, (to[0] * 2 + core) * 4 + to[1]))
    return lax.ppermute(value, ("x", "core", "ctx"), pairs)


def spread_near(block):
    near, far, mid = [hop(block, False, o) for o in (1, 3, 2)]
    return jnp.stack((block, near, mid, far)).reshape(4, 2, 64, -1)


def spread_far(stack, scalars):
    near = hop(stack, True, 1)
    far = hop(stack, True, -1)
    half_a = hop(near[:2], True, 1)
    half_b = hop(far[2:], True, -1)
    width = stack.shape[-1]

    def body(s_ref, own_ref, near_ref, a_ref, b_ref, far_ref, out_ref, sems):
        core, x0, y0 = s_ref[0], s_ref[2], s_ref[3]
        copies = []
        for j in range(4):
            for i in range(4):
                if j == 2:
                    ref, at = (a_ref, i) if i < 2 else (b_ref, i - 2)
                else:
                    ref, at = (own_ref, near_ref, None, far_ref)[j], i
                x = lax.rem(x0 + 4 - jnp.where(core == 0, j, i), 4)
                y = lax.rem(y0 + 4 - jnp.where(core == 0, i, j), 4)
                for rel in (0, 1):
                    copies.append(
                        pltpu.make_async_copy(
                            ref.at[at, rel],
                            out_ref.at[x, jnp.bitwise_xor(core, rel), y],
                            sems.at[len(copies)],
                        )
                    )
        for copy in copies:
            copy.start()
        for copy in copies:
            copy.wait()

    anywhere = pl.BlockSpec(memory_space=pl.ANY)
    return call(
        body,
        (1,),
        [anywhere] * 5,
        anywhere,
        sds((4, 2, 4, 64, width), BF),
        scalars,
        (stack, near, half_a, half_b, far),
        "arrange",
        scratch=[pltpu.SemaphoreType.DMA((32,))],
    )


def collect_far(parts):
    (own_a, own_b), (near_a, near_b), (mid_a, mid_b), (far_a, far_b) = parts
    got_near_b = hop(near_b, True, 1)
    got_far_a = hop(far_a, True, -1)
    via_near = hop(mid_a, True, 1)
    via_far = hop(mid_b, True, -1)
    got_near_a = hop((near_a.astype(F32) + via_near.astype(F32)).astype(BF), True, 1)
    got_far_b = hop((far_b.astype(F32) + via_far.astype(F32)).astype(BF), True, -1)
    sums = []
    for own, near, far in ((own_a, got_near_a, got_far_a), (own_b, got_near_b, got_far_b)):
        for j in (0, 1):
            sums.append((own[j].astype(F32) + near[j].astype(F32) + far[j].astype(F32)).astype(BF))
    return sums


def collect_near(sums):
    got = [hop(sums[j], False, j) for j in (1, 3, 2)]
    total = sums[0].astype(F32)
    for part in got:
        total = total + part.astype(F32)
    return total.astype(BF)


def mm_in(left, right, weight, start, width, scalars, name):
    def body(s_ref, a_ref, b_ref, w_ref, out_ref):
        step = pl.program_id(0)
        part = jnp.dot(
            jnp.concatenate((a_ref[...], b_ref[...]), axis=0),
            slab_rows(w_ref, s_ref[0]),
            preferred_element_type=F32,
        )

        @pl.when(step == 0)
        def _():
            out_ref[...] = part

        @pl.when(step > 0)
        def _():
            out_ref[...] += part

    rows = left.shape[0]
    cols = pl.BlockSpec((rows, SLAB), lambda i, s: (0, i))
    return call(
        body,
        (4,),
        [cols, cols, slab_spec(weight, start, width)],
        pl.BlockSpec((2 * rows, width), lambda i, s: (0, 0)),
        sds((2 * rows, width), F32),
        scalars,
        (left, right, weight),
        name,
        flops=4 * rows * D * width,
    )


def mm_back(grad, weight, start, scalars, name, deps=()):
    rows, width = grad.shape
    half = rows // 2

    def body(s_ref, g_ref, w_ref, own_ref, other_ref):
        out = lax.dot_general(
            g_ref[...],
            slab_rows(w_ref, s_ref[0]),
            (((1,), (1,)), ((), ())),
            preferred_element_type=F32,
        )
        own_ref[...] = out[:half]
        other_ref[...] = out[half:].astype(BF)

    cols = pl.BlockSpec((half, SLAB), lambda i, s: (0, i))
    return call(
        body,
        (4,),
        [whole(grad), slab_spec(weight, start, width)],
        (cols, cols),
        (sds((half, D), F32), sds((half, D), BF)),
        scalars,
        (grad, weight),
        name,
        flops=2 * rows * D * width,
        deps=deps,
    )


def mm_weight(pairs, scalars, name, apart=False, deps=()):
    widths = [grad.shape[1] for _, grad in pairs]
    rows = pairs[0][0][0].shape[0]
    count = 3 * len(pairs)
    total = sum(widths)

    def body(s_ref, *refs):
        core = s_ref[0]
        outs, held = refs[count:-1], refs[-1]
        at = 0
        for k, width in enumerate(widths):
            a_ref, b_ref, g_ref = refs[3 * k : 3 * k + 3]
            out = lax.dot_general(
                jnp.concatenate((a_ref[...], b_ref[...]), axis=0),
                g_ref[...],
                (((0,), (0,)), ((), ())),
                preferred_element_type=F32,
            ).astype(BF)
            held[:, :, at : at + width] = out.reshape(8, 64, width)
            at += width
        if not apart:
            for c in (0, 1):
                for y in range(4):
                    outs[0][0, y, jnp.bitwise_xor(c, core)] = held[c * 4 + y]
            return
        x_far = lax.rem(pl.program_id(0) + 4 - s_ref[2], 4)
        for k in range(4):

            @pl.when((core == 0) & (x_far == k))
            def _(k=k):
                for j in range(4):
                    y = lax.rem(s_ref[3] + j, 4)
                    for rel in (0, 1):
                        outs[2 * k + j // 2][j % 2, rel] = held[rel * 4 + y]

        for h in (0, 1):

            @pl.when((core == 1) & (x_far // 2 == h))
            def _(h=h):
                for k in range(4):
                    y = lax.rem(s_ref[3] + k, 4)
                    for rel in (0, 1):
                        outs[2 * k + h][lax.rem(x_far, 2), rel] = held[(1 - rel) * 4 + y]

    cols = pl.BlockSpec((rows, SLAB), lambda i, s: (0, i))
    specs, operands = [], []
    for (a, b), grad in pairs:
        specs += [cols, cols, whole(grad)]
        operands += [a, b, grad]
    if apart:
        shapes = (sds((2, 2, 64, total), BF),) * 8
        out_specs = tuple(whole(s) for s in shapes)
    else:
        shapes = sds((4, 4, 2, 64, total), BF)
        out_specs = pl.BlockSpec((1, 4, 2, 64, total), lambda i, s: (i, 0, 0, 0, 0))
    return call(
        body,
        (4,),
        specs,
        out_specs,
        shapes,
        scalars,
        tuple(operands),
        name,
        flops=4 * rows * D * total,
        scratch=[pltpu.VMEM((8, 64, total), BF)],
        deps=deps,
    )


def split_heads(weights, turned, scalars, name, deps=()):
    widths = [(w.shape[0] if t else w.shape[1]) // 2 for w, t in zip(weights, turned)]

    def body(s_ref, *refs):
        mine_ref, theirs_ref = refs[-2:]
        core = s_ref[0]
        for out_ref, head in ((mine_ref, core), (theirs_ref, 1 - core)):
            at = 0
            for ref, width, turn in zip(refs, widths, turned):
                if turn:
                    piece = ref[pl.ds(pl.multiple_of(head * width, width), width), :]
                    piece = piece.astype(F32).T.astype(BF)
                else:
                    piece = ref[:, pl.ds(pl.multiple_of(head * width, width), width)]
                out_ref[:, at : at + width] = piece
                at += width

    total = sum(widths)
    spec = pl.BlockSpec((64, total), lambda i, s: (0, 0))
    return call(
        body,
        (1,),
        [whole(w) for w in weights],
        (spec, spec),
        (sds((64, total), BF),) * 2,
        scalars,
        tuple(weights),
        name,
        deps=deps,
    )


def join_heads(mine, theirs, widths, turned, scalars, name):
    def body(s_ref, mine_ref, theirs_ref, *outs):
        core = s_ref[0]
        for in_ref, head in ((mine_ref, core), (theirs_ref, 1 - core)):
            at = 0
            for ref, width, turn in zip(outs, widths, turned):
                piece = in_ref[:, at : at + width].astype(F32)
                span = pl.ds(pl.multiple_of(head * width, width), width)
                if turn:
                    ref[span, :] = piece.T
                else:
                    ref[:, span] = piece
                at += width

    shapes = tuple(
        sds((2 * w, 64) if t else (64, 2 * w), F32) for w, t in zip(widths, turned)
    )
    return call(
        body,
        (1,),
        [whole(mine), whole(theirs)],
        tuple(whole(s) for s in shapes),
        shapes,
        scalars,
        (mine, theirs),
        name,
    )


def scale_of(values):
    return lax.rsqrt(jnp.mean(values * values, axis=-1, keepdims=True) + 1e-06)


def turned_spec(rows):
    return pl.BlockSpec((rows, D), lambda i, s: (lax.rem(i + s[1], 4), 0))


def plain_spec(rows):
    return pl.BlockSpec((rows, D), lambda i, s: (i, 0))


def enter_rows(tokens, cotangent, gain, scalars, deps=()):
    rows = tokens.shape[0]
    block = rows // 4

    def body(s_ref, t_ref, c_ref, g_ref, t_out, c_out, n_out, l_out):
        values = t_ref[...]
        t_out[...] = values
        n_out[...] = (values * scale_of(values) * g_ref[...]).astype(BF)
        c_out[...] = c_ref[...]
        l_out[...] = c_ref[...].astype(BF)

    turn, plain = turned_spec(block), plain_spec(block)
    full = (rows, D)
    return call(
        body,
        (4,),
        [turn, turn, whole(gain)],
        (plain,) * 4,
        (sds(full, F32), sds(full, F32), sds(full, BF), sds(full, BF)),
        scalars,
        (tokens, cotangent, gain),
        "enter_rows",
        deps=deps,
    )


def each_part(refs, work):
    step = pl.program_id(0)
    for k, ref in enumerate(refs):

        @pl.when(step == k)
        def _(ref=ref):
            work(ref[...].astype(F32))


def second_norm(tokens, parts, gain, scalars, deps=()):
    rows = tokens.shape[0]
    block = rows // 4

    def body(s_ref, t_ref, g_ref, *refs):
        h_out, n_out = refs[4:]

        def work(part):
            values = t_ref[...] + part
            h_out[...] = values
            n_out[...] = (values * scale_of(values) * g_ref[...]).astype(BF)

        each_part(refs[:4], work)

    plain = plain_spec(block)
    return call(
        body,
        (4,),
        [plain, whole(gain)] + [whole(p) for p in parts],
        (plain, plain),
        (sds((rows, D), F32), sds((rows, D), BF)),
        scalars,
        (tokens, gain, *parts),
        "second_norm",
        deps=deps,
    )


def leave_rows(hidden, parts, scalars):
    rows = hidden.shape[0]
    block = rows // 4

    def body(s_ref, h_ref, *refs):
        def work(part):
            refs[4][...] = h_ref[...] + part

        each_part(refs[:4], work)

    return call(
        body,
        (4,),
        [plain_spec(block)] + [whole(p) for p in parts],
        turned_spec(block),
        sds((rows, D), F32),
        scalars,
        (hidden, *parts),
        "leave_rows",
    )


def norm_back(values, upstream, parts, gain, last, scalars, name, deps=()):
    rows = values.shape[0]
    block = rows // 4

    def body(s_ref, v_ref, u_ref, g_ref, *refs):
        outs = refs[4:]

        def work(part):
            values = v_ref[...]
            factor = scale_of(values)
            unit = values * factor
            scaled = part * g_ref[...]
            out = u_ref[...] + factor * (
                scaled - unit * jnp.mean(scaled * unit, axis=-1, keepdims=True)
            )
            outs[0][...] = out
            outs[1][0] = jnp.sum(part * unit, axis=0, keepdims=True)
            if not last:
                outs[2][...] = out.astype(BF)

        each_part(refs[:4], work)

    plain = plain_spec(block)
    specs = [turned_spec(block) if last else plain, pl.BlockSpec((1, 1, D), lambda i, s: (i, 0, 0))]
    shapes = [sds((rows, D), F32), sds((4, 1, D), F32)]
    if not last:
        specs.append(plain)
        shapes.append(sds((rows, D), BF))
    out = call(
        body,
        (4,),
        [plain, plain, whole(gain)] + [whole(p) for p in parts],
        tuple(specs),
        tuple(shapes),
        scalars,
        (values, upstream, gain, *parts),
        name,
        deps=deps,
    )
    gains = out[1][:, 0]
    return (out[0], (gains[0] + gains[2]) + (gains[1] + gains[3]), *out[2:])


def heads_total(own, other):
    came = swap(other)
    block = own.shape[0] // 4
    blocks = [
        (own[o * block : (o + 1) * block] + came[o * block : (o + 1) * block].astype(F32)).astype(BF)
        for o in range(4)
    ]
    got = [shift(blocks[o], "tp", o) for o in (1, 3, 2)]
    mine = blocks[0].astype(F32)
    for part in got:
        mine = mine + part.astype(F32)
    mine = mine.astype(BF)
    near, far, mid = [shift(mine, "tp", -o) for o in (1, 3, 2)]
    return (mine, near, mid, far)


def gate_norm(gate_pre, retained):
    centred = retained - jnp.mean(retained, axis=-1, keepdims=True)
    normed = centred * lax.rsqrt(jnp.mean(centred * centred, axis=-1, keepdims=True) + 1.0 * DK)
    return gate_pre * jax.nn.sigmoid(gate_pre) * normed


def gelu_gate(hidden, linear):
    return jax.nn.gelu(hidden, approximate=True) * linear


def rotate(values, cosine, sine):
    half = DK // 2
    first = values[:, :half]
    second = values[:, half:]
    return jnp.concatenate((first * cosine - second * sine, first * sine + second * cosine), axis=1)


def ein(spec, left, right):
    return jnp.einsum(spec, left, right, preferred_element_type=F32)


def per_device(
    tokens,
    cotangent,
    gain_first,
    gain_second,
    w_query,
    w_key,
    w_value,
    w_gate,
    w_output,
    w_hidden,
    w_linear,
    w_down,
    decay_scale,
    first_length,
):
    rows = tokens.shape[0]
    core = lax.axis_index("core")
    place = lax.axis_index("ctx")
    plane = lax.axis_index("tp")
    scalars = jnp.stack((core, plane, lax.axis_index("x"), place)).astype(jnp.int32)

    mine, theirs = split_heads(
        (w_query, w_key, w_value, w_gate, w_output), (False,) * 4 + (True,), scalars, "split_attn"
    )
    attn = lax.all_gather(
        jnp.concatenate((mine, swap(theirs)), axis=0), XY, axis=0, tiled=True
    ).reshape(4, 4, 2, 64, -1)
    mine_mlp, theirs_mlp = split_heads(
        (w_hidden, w_linear, w_down), (False, False, True), scalars, "split_mlp", deps=(mine,)
    )
    stack = spread_near(jnp.concatenate((mine_mlp, swap(theirs_mlp)), axis=0))
    gain_first = gain_first.reshape(1, D)
    gain_second = gain_second.reshape(1, D)
    tokens, cotangent, normed_first, cot_low = enter_rows(tokens, cotangent, gain_first, scalars, deps=(mine_mlp,))

    rate = lax.dynamic_index_in_dim(decay_scale, core, 0, False) / 1024.0
    local = (jnp.arange(rows, dtype=jnp.int32) + plane * (rows // 4)) % rows
    index = place * rows + local
    lengths = jnp.concatenate((first_length, swap(first_length)))
    document = (index[None, :] >= lengths[:, None]).astype(jnp.int32)
    carried = (document == 0).astype(F32)
    steps = local.astype(F32)
    offsets = local[:, None] - local[None, :]
    linked = (offsets >= 0)[None] & (document[:, :, None] == document[:, None, :])
    mask = jnp.where(
        linked, jnp.exp(-rate * jnp.maximum(offsets, 0).astype(F32))[None], 0.0
    )
    enter = (carried * jnp.exp(-rate * (steps + 1.0))[None])[:, :, None]
    leave = jnp.exp(-rate * (rows - 1.0 - steps))[None, :, None]
    hop = jnp.exp(-rate * rows)
    half = DK // 2
    frequency = 10000.0 ** (-(jnp.arange(half).astype(F32) / half))
    angles = index.astype(F32)[:, None] * frequency[None, :]
    cosine = jnp.tile(jnp.cos(angles), (2, 1))
    sine = jnp.tile(jnp.sin(angles), (2, 1))

    def carry(state, way):
        low = state.astype(BF)
        near, mid, far = [shift_open(low, "ctx", way * o).astype(F32) for o in (1, 2, 3)]
        return near + hop * (mid + hop * far)

    x_first = (normed_first, swap(normed_first))
    projected = mm_in(*x_first, attn, 0, 1536, scalars, "project_attn")
    mlp = spread_far(after(stack, attn), scalars)
    query = rotate(projected[:, :DK], cosine, sine).astype(BF).reshape(2, rows, DK)
    key = rotate(projected[:, DK : 2 * DK], cosine, sine).astype(BF).reshape(2, rows, DK)
    value = projected[:, 2 * DK : 2 * DK + DV].astype(BF).reshape(2, rows, DV)
    gate_pre = projected[:, 2 * DK + DV : 2 * DK + 2 * DV]
    key_out = (key.astype(F32) * leave).astype(BF)
    state_in = carry(ein("gjd,gje->gde", key_out, value), 1).astype(BF)
    weighted = (ein("gid,gjd->gij", query, key) * mask).astype(BF)
    inner = ein("gij,gje->gie", weighted, value)
    retained = (inner + ein("gid,gde->gie", query, state_in) * enter).reshape(2 * rows, DV)
    mixed_full, gate_back = jax.vjp(gate_norm, gate_pre, retained)
    mixed = mixed_full.astype(BF)
    parts = heads_total(*mm_back(mixed, attn, 1536, scalars, "project_out"))
    g_out = (cot_low, swap(cot_low))
    grad_activated = mm_in(*g_out, mlp, 2 * DV, DV, scalars, "back_down")
    hidden_state, normed_second = second_norm(tokens, parts, gain_second, scalars, deps=(grad_activated,))
    x_second = (normed_second, swap(normed_second))
    paired = mm_in(*x_second, mlp, 0, 2 * DV, scalars, "project_mlp")
    activated_full, gelu_back = jax.vjp(gelu_gate, paired[:, :DV], paired[:, DV:])
    activated = activated_full.astype(BF)
    grad_pair = jnp.concatenate(gelu_back(grad_activated), axis=1).astype(BF)
    parts = heads_total(*mm_back(grad_pair, mlp, 0, scalars, "back_mlp"))
    down = mm_back(activated, mlp, 2 * DV, scalars, "project_down")
    d_mlp = mm_weight(
        ((x_second, grad_pair), (g_out, activated)), scalars, "weight_mlp"
    )
    grad_state, gain_second_part, grad_state_low = norm_back(
        hidden_state,
        cotangent,
        parts,
        gain_second,
        False,
        scalars,
        "second_back",
        deps=(d_mlp, down[1]),
    )
    g_state = (grad_state_low, swap(grad_state_low))
    grad_mixed = mm_in(*g_state, attn, 1536, DV, scalars, "back_out")
    grad_gate, grad_retained = gate_back(grad_mixed)
    grad_low = grad_retained.reshape(2, rows, DV).astype(BF)
    query_in = (query.astype(F32) * enter).astype(BF)
    state_back = carry(ein("gid,gie->gde", query_in, grad_low), -1).astype(BF)
    grad_scores = (ein("gie,gje->gij", grad_low, value) * mask).astype(BF)
    grad_query = ein("gij,gjd->gid", grad_scores, key) + enter * ein("gie,gde->gid", grad_low, state_in)
    grad_key = ein("gij,gid->gjd", grad_scores, query) + leave * ein("gje,gde->gjd", value, state_back)
    grad_value = ein("gij,gie->gje", weighted, grad_low) + ein("gjd,gde->gje", key_out, state_back)
    grad_proj = jnp.concatenate(
        (
            rotate(grad_query.reshape(2 * rows, DK), cosine, -sine),
            rotate(grad_key.reshape(2 * rows, DK), cosine, -sine),
            grad_value.reshape(2 * rows, DV),
            grad_gate,
        ),
        axis=1,
    ).astype(BF)
    d_attn = mm_weight(((x_first, grad_proj), (g_state, mixed)), scalars, "weight_attn", True)
    layer_parts = heads_total(down[0], after(down[1], grad_low))
    layer_out = leave_rows(hidden_state, layer_parts, scalars)
    parts = heads_total(*mm_back(grad_proj, attn, 0, scalars, "back_attn"))
    input_grad, gain_first_part = norm_back(
        tokens, grad_state, parts, gain_first, True, scalars, "first_back"
    )

    mlp_block = lax.psum_scatter(
        d_mlp.reshape(2048, -1), XY, scatter_dimension=0, tiled=True
    ).reshape(2, 64, -1)
    d_hidden, d_linear, d_down = join_heads(
        mlp_block[0], swap(mlp_block[1]), (DV, DV, DV), (False, False, True), scalars, "join_mlp"
    )
    attn_block = collect_near(collect_far([d_attn[2 * k : 2 * k + 2] for k in range(4)]))
    d_query, d_key, d_value, d_gate, d_output = join_heads(
        attn_block[0],
        swap(attn_block[1]),
        (DK, DK, DV, DV, DV),
        (False, False, False, False, True),
        scalars,
        "join_attn",
    )

    def gain_total(part):
        part = part + swap(part)
        for axis in XY:
            part = part + shift(part, axis, 1) + shift(part, axis, 2) + shift(part, axis, 3)
        spot = (lax.axis_index("x") * 2 + core) * 4 + place
        return lax.dynamic_slice_in_dim(part, spot * 64, 64, 1)

    gains = gain_total(jnp.stack((gain_first_part, gain_second_part)))
    return (
        layer_out,
        input_grad,
        gains[0],
        gains[1],
        d_query,
        d_key,
        d_value,
        d_gate,
        d_output,
        d_hidden,
        d_linear,
        d_down,
    )


def solution(mesh):
    fine = Mesh(np.asarray(mesh.devices).reshape(4, 2, 4, 4), ("x", "core", "ctx", "tp"))
    split = ("x", "core", "ctx")
    row = P(split, None)
    win = P(split, "tp")
    wout = P("tp", split)
    in_specs = (row, row, P(), P(), win, win, win, win, wout, win, win, wout, P("tp"), P(("x", "core")))
    out_specs = (row, row, P(split), P(split), win, win, win, win, wout, win, win, wout)
    return jax.shard_map(
        per_device, mesh=fine, in_specs=in_specs, out_specs=out_specs, check_vma=False
    )
```

```python
import math

import jax
import jax.numpy as jnp
import numpy as np
from jax import lax
from jax.experimental import pallas as pl
from jax.experimental.pallas import tpu as pltpu
from jax.sharding import Mesh, PartitionSpec as P

D = 2048
DK = 256
DV = 512
SLAB = 512
BF = jnp.bfloat16
F32 = jnp.float32
XY = ("x", "ctx")
MIB = 1 << 20


def shift(value, axis, offset):
    n = lax.axis_size(axis)
    return lax.ppermute(value, axis, [(i, (i + offset) % n) for i in range(n)])


def shift_open(value, axis, offset):
    n = lax.axis_size(axis)
    return lax.ppermute(
        value, axis, [(i, i + offset) for i in range(n) if 0 <= i + offset < n]
    )


def swap(value):
    return lax.ppermute(value, "core", [(0, 1), (1, 0)])


def after(value, *earlier):
    return lax.optimization_barrier((value, *earlier))[0]


def call(body, grid, ins, outs, shapes, scalars, operands, name, flops=0, scratch=(), deps=()):
    nbytes = sum(a.size * a.dtype.itemsize for a in jax.tree.leaves((operands, shapes)))
    count = len(operands)

    def kernel(s_ref, *refs):
        body(s_ref, *refs[:count], *refs[count + len(deps) :])

    ins = [*ins, *[pl.BlockSpec(memory_space=pl.ANY)] * len(deps)]
    return pl.pallas_call(
        kernel,
        out_shape=shapes,
        grid_spec=pltpu.PrefetchScalarGridSpec(
            num_scalar_prefetch=1, grid=grid, in_specs=ins, out_specs=outs, scratch_shapes=scratch
        ),
        compiler_params=pltpu.CompilerParams(
            vmem_limit_bytes=48 * MIB, dimension_semantics=("arbitrary",) * len(grid)
        ),
        cost_estimate=pl.CostEstimate(flops=flops, bytes_accessed=nbytes, transcendentals=0),
        name=name,
    )(scalars, *operands, *deps)


def whole(array):
    return pl.BlockSpec(array.shape, lambda *_: (0,) * array.ndim)


def sds(shape, dtype):
    return jax.ShapeDtypeStruct(shape, dtype)


def weight_operands(weight, start, width):
    if not isinstance(weight, tuple):
        spec = pl.BlockSpec((1, 4, 2, 64, width), lambda i, s: (i, 0, 0, 0, start // width))
        return [weight], [spec]
    piece = math.gcd(start, width) if start else width
    operands, specs = [], []
    for at in range(start, start + width, piece):
        for stack in weight:
            operands.append(stack)
            specs.append(pl.BlockSpec((4, 2, 64, piece), lambda i, s, at=at: (0, 0, 0, at // piece)))
    return operands, specs


def load_slab(s_ref, refs, held):
    core = s_ref[0]
    if len(refs) == 1:
        return jnp.concatenate(
            [refs[0][0, y, jnp.bitwise_xor(c, core)] for c in (0, 1) for y in range(4)], axis=0
        )
    x_far = lax.rem(s_ref[2] + 4 - pl.program_id(0), 4)
    at = 0
    for first in range(0, len(refs), 4):
        stacks = refs[first : first + 4]
        width = stacks[0].shape[-1]
        for j in range(4):

            @pl.when((core == 0) & (x_far == j))
            def _(j=j, at=at, width=width, stacks=stacks):
                for i in range(4):
                    y = lax.rem(s_ref[3] + 4 - i, 4)
                    for c in (0, 1):
                        held[c * 4 + y, :, at : at + width] = stacks[j][i, c]

        @pl.when(core == 1)
        def _(at=at, width=width, stacks=stacks):
            for j in range(4):
                y = lax.rem(s_ref[3] + 4 - j, 4)
                for c in (0, 1):
                    held[c * 4 + y, :, at : at + width] = stacks[j][x_far, 1 - c]

        at += width
    return held[...].reshape(SLAB, at)


def hop(value, first, offset):
    pairs = []
    for x in range(4):
        for core in (0, 1):
            for y in range(4):
                to = ((x + offset) % 4, y) if (core == 0) == first else (x, (y + offset) % 4)
                pairs.append(((x * 2 + core) * 4 + y, (to[0] * 2 + core) * 4 + to[1]))
    return lax.ppermute(value, ("x", "core", "ctx"), pairs)


def spread_near(block):
    near, far, mid = [hop(block, False, o) for o in (1, 3, 2)]
    return block, near, mid, far


def spread_far(blocks, start, stop):
    stack = jnp.stack([b[:, start:stop] for b in blocks]).reshape(4, 2, 64, stop - start)
    near, far, mid = [hop(stack, True, o) for o in (1, 3, 2)]
    return stack, near, mid, far


def collect_far(parts):
    got = [hop(parts[k], True, k) for k in (1, 3, 2)]
    sums = []
    for j in range(4):
        total = parts[0][j].astype(F32)
        for part in got:
            total = total + part[j].astype(F32)
        sums.append(total.astype(BF))
    return sums


def collect_near(sums):
    got = [hop(sums[j], False, j) for j in (1, 3, 2)]
    total = sums[0].astype(F32)
    for part in got:
        total = total + part.astype(F32)
    return total.astype(BF)


def mm_in(left, right, weight, start, width, scalars, name, deps=()):
    operands, specs = weight_operands(weight, start, width)

    def body(s_ref, a_ref, b_ref, *refs):
        out_ref = refs[len(operands)]
        step = pl.program_id(0)
        part = jnp.dot(
            jnp.concatenate((a_ref[...], b_ref[...]), axis=0),
            load_slab(s_ref, refs[: len(operands)], refs[-1]),
            preferred_element_type=F32,
        )

        @pl.when(step == 0)
        def _():
            out_ref[...] = part

        @pl.when(step > 0)
        def _():
            out_ref[...] += part

    rows = left.shape[0]
    cols = pl.BlockSpec((rows, SLAB), lambda i, s: (0, i))
    return call(
        body,
        (4,),
        [cols, cols, *specs],
        pl.BlockSpec((2 * rows, width), lambda i, s: (0, 0)),
        sds((2 * rows, width), F32),
        scalars,
        (left, right, *operands),
        name,
        flops=4 * rows * D * width,
        scratch=[pltpu.VMEM((8, 64, width), BF)],
        deps=deps,
    )


def mm_back(terms, scalars, name, deps=()):
    rows = terms[0][0].shape[0]
    half = rows // 2
    operands, specs, counts, scratch = [], [], [], []
    for grad, weight, start in terms:
        ops, sp = weight_operands(weight, start, grad.shape[1])
        operands += [grad, *ops]
        specs += [whole(grad), *sp]
        counts.append(len(ops))
        scratch.append(pltpu.VMEM((8, 64, grad.shape[1]), BF))

    def body(s_ref, *refs):
        own_ref, other_ref = refs[len(operands) : len(operands) + 2]
        at, out = 0, 0.0
        for k, count in enumerate(counts):
            slab = load_slab(s_ref, refs[at + 1 : at + 1 + count], refs[len(operands) + 2 + k])
            out += lax.dot_general(
                refs[at][...], slab, (((1,), (1,)), ((), ())), preferred_element_type=F32
            )
            at += count + 1
        own_ref[...] = out[:half]
        other_ref[...] = out[half:].astype(BF)

    cols = pl.BlockSpec((half, SLAB), lambda i, s: (0, i))
    return call(
        body,
        (4,),
        specs,
        (cols, cols),
        (sds((half, D), F32), sds((half, D), BF)),
        scalars,
        tuple(operands),
        name,
        flops=sum(2 * rows * D * grad.shape[1] for grad, _, _ in terms),
        scratch=scratch,
        deps=deps,
    )


def mm_weight(pairs, scalars, name, apart=False, deps=()):
    widths = [grad.shape[1] for _, grad in pairs]
    rows = pairs[0][0][0].shape[0]
    count = 3 * len(pairs)
    total = sum(widths)

    def body(s_ref, *refs):
        core = s_ref[0]
        outs, held = refs[count:-1], refs[-1]
        at = 0
        for k, width in enumerate(widths):
            a_ref, b_ref, g_ref = refs[3 * k : 3 * k + 3]
            out = lax.dot_general(
                jnp.concatenate((a_ref[...], b_ref[...]), axis=0),
                g_ref[...],
                (((0,), (0,)), ((), ())),
                preferred_element_type=F32,
            ).astype(BF)
            held[:, :, at : at + width] = out.reshape(8, 64, width)
            at += width
        if not apart:
            for c in (0, 1):
                for y in range(4):
                    outs[0][0, y, jnp.bitwise_xor(c, core)] = held[c * 4 + y]
            return
        x_far = lax.rem(pl.program_id(0) + 4 - s_ref[2], 4)
        for k in range(4):

            @pl.when((core == 0) & (x_far == k))
            def _(k=k):
                for j in range(4):
                    y = lax.rem(s_ref[3] + j, 4)
                    for rel in (0, 1):
                        outs[k][j, rel] = held[rel * 4 + y]

        @pl.when(core == 1)
        def _():
            for k in range(4):
                y = lax.rem(s_ref[3] + k, 4)
                for rel in (0, 1):
                    outs[k][x_far, rel] = held[(1 - rel) * 4 + y]

    cols = pl.BlockSpec((rows, SLAB), lambda i, s: (0, i))
    specs, operands = [], []
    for (a, b), grad in pairs:
        specs += [cols, cols, whole(grad)]
        operands += [a, b, grad]
    if apart:
        shapes = (sds((4, 2, 64, total), BF),) * 4
        out_specs = tuple(whole(s) for s in shapes)
    else:
        shapes = sds((4, 4, 2, 64, total), BF)
        out_specs = pl.BlockSpec((1, 4, 2, 64, total), lambda i, s: (i, 0, 0, 0, 0))
    return call(
        body,
        (4,),
        specs,
        out_specs,
        shapes,
        scalars,
        tuple(operands),
        name,
        flops=4 * rows * D * total,
        scratch=[pltpu.VMEM((8, 64, total), BF)],
        deps=deps,
    )


def split_heads(weights, scalars, name, deps=()):
    widths = [w.shape[1] // 2 for w in weights]

    def body(s_ref, *refs):
        mine_ref, theirs_ref = refs[-2:]
        core = s_ref[0]
        for out_ref, head in ((mine_ref, core), (theirs_ref, 1 - core)):
            at = 0
            for ref, width in zip(refs, widths):
                out_ref[:, at : at + width] = ref[:, pl.ds(pl.multiple_of(head * width, width), width)]
                at += width

    total = sum(widths)
    spec = pl.BlockSpec((64, total), lambda i, s: (0, 0))
    return call(
        body,
        (1,),
        [whole(w) for w in weights],
        (spec, spec),
        (sds((64, total), BF),) * 2,
        scalars,
        tuple(weights),
        name,
        deps=deps,
    )


def join_heads(mine, theirs, widths, scalars, name):
    def body(s_ref, mine_ref, theirs_ref, *outs):
        core = s_ref[0]
        for in_ref, head in ((mine_ref, core), (theirs_ref, 1 - core)):
            at = 0
            for ref, width in zip(outs, widths):
                span = pl.ds(pl.multiple_of(head * width, width), width)
                ref[:, span] = in_ref[:, at : at + width].astype(F32)
                at += width

    shapes = tuple(sds((64, 2 * w), F32) for w in widths)
    return call(
        body,
        (1,),
        [whole(mine), whole(theirs)],
        tuple(whole(s) for s in shapes),
        shapes,
        scalars,
        (mine, theirs),
        name,
    )


def scale_of(values):
    return lax.rsqrt(jnp.mean(values * values, axis=-1, keepdims=True) + 1e-06)


def turned_spec(rows):
    return pl.BlockSpec((rows, D), lambda i, s: (lax.rem(i + s[1], 4), 0))


def plain_spec(rows):
    return pl.BlockSpec((rows, D), lambda i, s: (i, 0))


def enter_rows(tokens, cotangent, gain, scalars, deps=()):
    rows = tokens.shape[0]
    block = rows // 4

    def body(s_ref, t_ref, c_ref, g_ref, t_out, c_out, n_out, l_out):
        values = t_ref[...]
        t_out[...] = values
        n_out[...] = (values * scale_of(values) * g_ref[...]).astype(BF)
        c_out[...] = c_ref[...]
        l_out[...] = c_ref[...].astype(BF)

    turn, plain = turned_spec(block), plain_spec(block)
    full = (rows, D)
    return call(
        body,
        (4,),
        [turn, turn, whole(gain)],
        (plain,) * 4,
        (sds(full, F32), sds(full, F32), sds(full, BF), sds(full, BF)),
        scalars,
        (tokens, cotangent, gain),
        "enter_rows",
        deps=deps,
    )


def each_part(refs, work):
    step = pl.program_id(0)
    for k, ref in enumerate(refs):

        @pl.when(step == k)
        def _(ref=ref):
            work(ref[...].astype(F32))


def second_norm(tokens, parts, gain, scalars, deps=()):
    rows = tokens.shape[0]
    block = rows // 4

    def body(s_ref, t_ref, g_ref, *refs):
        h_out, n_out = refs[4:]

        def work(part):
            values = t_ref[...] + part
            h_out[...] = values
            n_out[...] = (values * scale_of(values) * g_ref[...]).astype(BF)

        each_part(refs[:4], work)

    plain = plain_spec(block)
    return call(
        body,
        (4,),
        [plain, whole(gain)] + [whole(p) for p in parts],
        (plain, plain),
        (sds((rows, D), F32), sds((rows, D), BF)),
        scalars,
        (tokens, gain, *parts),
        "second_norm",
        deps=deps,
    )


def turned_total(own, came, scalars, name):
    rows = own.shape[0]
    block = rows // 4

    def body(s_ref, own_ref, came_ref, out_ref):
        out_ref[...] = (own_ref[...] + came_ref[...].astype(F32)).astype(BF)

    plain = plain_spec(block)
    return call(
        body, (4,), [plain, plain], turned_spec(block), sds((rows, D), BF), scalars, (own, came), name
    )


def leave_rows(hidden, total, scalars):
    rows = hidden.shape[0]
    block = rows // 4

    def body(s_ref, h_ref, t_ref, out_ref):
        out_ref[...] = h_ref[...] + t_ref[...].astype(F32)

    turn = turned_spec(block)
    return call(
        body,
        (4,),
        [plain_spec(block), turn],
        turn,
        sds((rows, D), F32),
        scalars,
        (hidden, total),
        "leave_rows",
    )


def gain_part(values, grad, name):
    block = grad.shape[0]

    def body(v_ref, p_ref, out_ref):
        values = v_ref[...]
        out_ref[...] = jnp.sum(
            p_ref[...].astype(F32) * (values * scale_of(values)), axis=0, keepdims=True
        )

    return pl.pallas_call(
        body,
        out_shape=sds((1, D), F32),
        grid=(1,),
        in_specs=[pl.BlockSpec((block, D), lambda i: (0, 0))] * 2,
        out_specs=pl.BlockSpec((1, D), lambda i: (0, 0)),
        name=name,
    )(values, grad)


def norm_back(values, upstream, parts, gain, last, scalars, name, deps=()):
    rows = values.shape[0]
    block = rows // 4

    def body(s_ref, v_ref, u_ref, g_ref, *refs):
        outs = refs[4:]

        def work(part):
            values = v_ref[...]
            factor = scale_of(values)
            unit = values * factor
            scaled = part * g_ref[...]
            out = u_ref[...] + factor * (
                scaled - unit * jnp.mean(scaled * unit, axis=-1, keepdims=True)
            )
            outs[0][...] = out
            if not last:
                outs[1][...] = out.astype(BF)

        each_part(refs[:4], work)

    plain = plain_spec(block)
    specs = [turned_spec(block) if last else plain]
    shapes = [sds((rows, D), F32)]
    if not last:
        specs.append(plain)
        shapes.append(sds((rows, D), BF))
    return call(
        body,
        (4,),
        [plain, plain, whole(gain)] + [whole(p) for p in parts],
        tuple(specs),
        tuple(shapes),
        scalars,
        (values, upstream, gain, *parts),
        name,
        deps=deps,
    )


def heads_total(own, other):
    came = swap(other)
    block = own.shape[0] // 4
    blocks = [
        (own[o * block : (o + 1) * block] + came[o * block : (o + 1) * block].astype(F32)).astype(BF)
        for o in range(4)
    ]
    got = [shift(blocks[o], "tp", o) for o in (1, 3, 2)]
    mine = blocks[0].astype(F32)
    for part in got:
        mine = mine + part.astype(F32)
    mine = mine.astype(BF)
    near, far, mid = [shift(mine, "tp", -o) for o in (1, 3, 2)]
    return (mine, near, mid, far)


def gate_norm(gate_pre, retained):
    centred = retained - jnp.mean(retained, axis=-1, keepdims=True)
    normed = centred * lax.rsqrt(jnp.mean(centred * centred, axis=-1, keepdims=True) + 1.0 * DK)
    return gate_pre * jax.nn.sigmoid(gate_pre) * normed


def gelu_gate(hidden, linear):
    return jax.nn.gelu(hidden, approximate=True) * linear


def rotate(values, cosine, sine):
    half = DK // 2
    first = values[:, :half]
    second = values[:, half:]
    return jnp.concatenate((first * cosine - second * sine, first * sine + second * cosine), axis=1)


def ein(spec, left, right):
    return jnp.einsum(spec, left, right, preferred_element_type=F32)


def per_device(
    tokens,
    cotangent,
    gain_first,
    gain_second,
    w_query,
    w_key,
    w_value,
    w_gate,
    w_output,
    w_hidden,
    w_linear,
    w_down,
    decay_scale,
    first_length,
):
    rows = tokens.shape[0]
    core = lax.axis_index("core")
    place = lax.axis_index("ctx")
    plane = lax.axis_index("tp")
    scalars = jnp.stack((core, plane, lax.axis_index("x"), place)).astype(jnp.int32)

    w_output = w_output.T
    w_down = w_down.T
    mine, theirs = split_heads((w_key, w_value, w_gate, w_query, w_output), scalars, "split_attn")
    blocks = spread_near(jnp.concatenate((mine, swap(theirs)), axis=0))
    w_kv = spread_far(blocks, 0, 768)
    w_gqo = spread_far(blocks, 768, 2048)
    mine_mlp, theirs_mlp = split_heads(
        (w_hidden, w_linear, w_down), scalars, "split_mlp", deps=w_kv[1:]
    )
    mlp = lax.all_gather(
        jnp.concatenate((mine_mlp, swap(theirs_mlp)), axis=0), XY, axis=0, tiled=True
    ).reshape(4, 4, 2, 64, -1)
    gain_first = gain_first.reshape(1, D)
    gain_second = gain_second.reshape(1, D)
    tokens, cotangent, normed_first, cot_low = enter_rows(tokens, cotangent, gain_first, scalars, deps=(mine,))

    rate = lax.dynamic_index_in_dim(decay_scale, core, 0, False) / 1024.0
    local = (jnp.arange(rows, dtype=jnp.int32) + plane * (rows // 4)) % rows
    index = place * rows + local
    lengths = jnp.concatenate((first_length, swap(first_length)))
    document = (index[None, :] >= lengths[:, None]).astype(jnp.int32)
    carried = (document == 0).astype(F32)
    steps = local.astype(F32)
    offsets = local[:, None] - local[None, :]
    linked = (offsets >= 0)[None] & (document[:, :, None] == document[:, None, :])
    mask = jnp.where(
        linked, jnp.exp(-rate * jnp.maximum(offsets, 0).astype(F32))[None], 0.0
    )
    enter = (carried * jnp.exp(-rate * (steps + 1.0))[None])[:, :, None]
    leave = jnp.exp(-rate * (rows - 1.0 - steps))[None, :, None]
    hop = jnp.exp(-rate * rows)
    half = DK // 2
    frequency = 10000.0 ** (-(jnp.arange(half).astype(F32) / half))
    angles = index.astype(F32)[:, None] * frequency[None, :]
    cosine = jnp.tile(jnp.cos(angles), (2, 1))
    sine = jnp.tile(jnp.sin(angles), (2, 1))

    def carry(state, way):
        low = state.astype(BF)
        near, mid, far = [shift_open(low, "ctx", way * o).astype(F32) for o in (1, 2, 3)]
        return near + hop * (mid + hop * far)

    x_first = (normed_first, swap(normed_first))
    projected = mm_in(*x_first, w_kv, 0, 768, scalars, "project_kv")
    key = rotate(projected[:, :DK], cosine, sine).astype(BF).reshape(2, rows, DK)
    value = projected[:, DK:].astype(BF).reshape(2, rows, DV)
    key_out = (key.astype(F32) * leave).astype(BF)
    state_in = carry(ein("gjd,gje->gde", key_out, value), 1).astype(BF)
    projected = mm_in(*x_first, w_gqo, 0, 768, scalars, "project_gq")
    gate_pre = projected[:, :DV]
    query = rotate(projected[:, DV:], cosine, sine).astype(BF).reshape(2, rows, DK)
    weighted = (ein("gid,gjd->gij", query, key) * mask).astype(BF)
    inner = ein("gij,gje->gie", weighted, value)
    retained = (inner + ein("gid,gde->gie", query, state_in) * enter).reshape(2 * rows, DV)
    mixed_full, gate_back = jax.vjp(gate_norm, gate_pre, retained)
    mixed = mixed_full.astype(BF)
    parts = heads_total(*mm_back([(mixed, w_gqo, 768)], scalars, "project_out"))
    g_out = (cot_low, swap(cot_low))
    grad_activated = mm_in(*g_out, mlp, 2 * DV, DV, scalars, "back_down")
    hidden_state, normed_second = second_norm(tokens, parts, gain_second, scalars, deps=(grad_activated,))
    x_second = (normed_second, swap(normed_second))
    paired = mm_in(*x_second, mlp, 0, 2 * DV, scalars, "project_mlp")
    activated_full, gelu_back = jax.vjp(gelu_gate, paired[:, :DV], paired[:, DV:])
    activated = activated_full.astype(BF)
    grad_pair = jnp.concatenate(gelu_back(grad_activated), axis=1).astype(BF)
    parts = heads_total(*mm_back([(grad_pair, mlp, 0)], scalars, "back_mlp"))
    down = mm_back([(activated, mlp, 2 * DV)], scalars, "project_down")
    d_mlp = mm_weight(
        ((x_second, grad_pair), (g_out, activated)), scalars, "weight_mlp"
    )
    gain_second_part = gain_part(hidden_state, parts[0], "gain_second")
    grad_state, grad_state_low = norm_back(
        hidden_state,
        cotangent,
        parts,
        gain_second,
        False,
        scalars,
        "second_back",
        deps=(d_mlp, down[1]),
    )
    g_state = (grad_state_low, swap(grad_state_low))
    grad_mixed = mm_in(*g_state, w_gqo, 768, DV, scalars, "back_out")
    grad_gate, grad_retained = gate_back(grad_mixed)
    grad_low = grad_retained.reshape(2, rows, DV).astype(BF)
    query_in = (query.astype(F32) * enter).astype(BF)
    state_back = carry(ein("gid,gie->gde", query_in, grad_low), -1).astype(BF)
    grad_scores = (ein("gie,gje->gij", grad_low, value) * mask).astype(BF)
    grad_query = ein("gij,gjd->gid", grad_scores, key) + enter * ein("gie,gde->gid", grad_low, state_in)
    grad_key = ein("gij,gid->gjd", grad_scores, query) + leave * ein("gje,gde->gjd", value, state_back)
    grad_value = ein("gij,gie->gje", weighted, grad_low) + ein("gjd,gde->gje", key_out, state_back)
    grad_gq = jnp.concatenate(
        (grad_gate, rotate(grad_query.reshape(2 * rows, DK), cosine, -sine)), axis=1
    ).astype(BF)
    grad_kv = jnp.concatenate(
        (rotate(grad_key.reshape(2 * rows, DK), cosine, -sine), grad_value.reshape(2 * rows, DV)),
        axis=1,
    ).astype(BF)
    d_gqo = mm_weight(((x_first, grad_gq), (g_state, mixed)), scalars, "weight_gqo", True)
    gqo_sums = collect_far(after(d_gqo, state_back))
    parts = heads_total(
        *mm_back([(grad_kv, w_kv, 0), (grad_gq, w_gqo, 0)], scalars, "back_attn")
    )
    d_kv = mm_weight(((x_first, grad_kv),), scalars, "weight_kv", True)
    kv_sums = collect_far(d_kv)
    gqo_block = collect_near(gqo_sums)
    kv_block = collect_near(kv_sums)
    gains = jnp.concatenate((gain_part(tokens, parts[0], "gain_first"), gain_second_part))
    for axis, swapped in (
        ("core", (1, 0)),
        ("tp", (1, 0, 3, 2)),
        ("tp", (3, 2, 1, 0)),
        ("ctx", (1, 0, 3, 2)),
        ("ctx", (3, 2, 1, 0)),
        ("x", (1, 0, 3, 2)),
        ("x", (3, 2, 1, 0)),
    ):
        gains = gains + lax.ppermute(gains, axis, list(enumerate(swapped)))
    spot = (lax.axis_index("x") * 2 + core) * 4 + place
    gains = lax.dynamic_slice_in_dim(gains, spot * 64, 64, 1)
    (input_grad,) = norm_back(tokens, grad_state, parts, gain_first, True, scalars, "first_back")

    mlp_block = lax.psum_scatter(
        d_mlp.reshape(2048, -1), XY, scatter_dimension=0, tiled=True
    ).reshape(2, 64, -1)
    layer_total = lax.psum(turned_total(down[0], swap(down[1]), scalars, "down_total"), "tp")
    layer_out = leave_rows(hidden_state, layer_total, scalars)
    d_hidden, d_linear, d_down = join_heads(
        mlp_block[0], swap(mlp_block[1]), (DV, DV, DV), scalars, "join_mlp"
    )
    d_gate, d_query, d_output = join_heads(
        gqo_block[0], swap(gqo_block[1]), (DV, DK, DV), scalars, "join_gqo"
    )
    d_key, d_value = join_heads(
        kv_block[0], swap(kv_block[1]), (DK, DV), scalars, "join_kv"
    )
    return (
        layer_out,
        input_grad,
        gains[0],
        gains[1],
        d_query,
        d_key,
        d_value,
        d_gate,
        d_output.T,
        d_hidden,
        d_linear,
        d_down.T,
    )


def solution(mesh):
    fine = Mesh(np.asarray(mesh.devices).reshape(4, 2, 4, 4), ("x", "core", "ctx", "tp"))
    split = ("x", "core", "ctx")
    row = P(split, None)
    win = P(split, "tp")
    wout = P("tp", split)
    in_specs = (row, row, P(), P(), win, win, win, win, wout, win, win, wout, P("tp"), P(("x", "core")))
    out_specs = (row, row, P(split), P(split), win, win, win, win, wout, win, win, wout)
    return jax.shard_map(
        per_device, mesh=fine, in_specs=in_specs, out_specs=out_specs, check_vma=False
    )
```

```python
import math

import jax
import jax.numpy as jnp
import numpy as np
from jax import lax
from jax.experimental import pallas as pl
from jax.experimental.pallas import tpu as pltpu
from jax.sharding import Mesh, PartitionSpec as P

D = 2048
DK = 256
DV = 512
SLAB = 512
BF = jnp.bfloat16
F32 = jnp.float32
XY = ("x", "ctx")
MIB = 1 << 20


def shift(value, axis, offset):
    n = lax.axis_size(axis)
    return lax.ppermute(value, axis, [(i, (i + offset) % n) for i in range(n)])


def shift_open(value, axis, offset):
    n = lax.axis_size(axis)
    return lax.ppermute(
        value, axis, [(i, i + offset) for i in range(n) if 0 <= i + offset < n]
    )


def swap(value):
    return lax.ppermute(value, "core", [(0, 1), (1, 0)])


def after(value, *earlier):
    return lax.optimization_barrier((value, *earlier))[0]


def call(body, grid, ins, outs, shapes, scalars, operands, name, flops=0, scratch=(), deps=()):
    nbytes = sum(a.size * a.dtype.itemsize for a in jax.tree.leaves((operands, shapes)))
    count = len(operands)

    def kernel(s_ref, *refs):
        body(s_ref, *refs[:count], *refs[count + len(deps) :])

    ins = [*ins, *[pl.BlockSpec(memory_space=pl.ANY)] * len(deps)]
    return pl.pallas_call(
        kernel,
        out_shape=shapes,
        grid_spec=pltpu.PrefetchScalarGridSpec(
            num_scalar_prefetch=1, grid=grid, in_specs=ins, out_specs=outs, scratch_shapes=scratch
        ),
        compiler_params=pltpu.CompilerParams(
            vmem_limit_bytes=48 * MIB, dimension_semantics=("arbitrary",) * len(grid)
        ),
        cost_estimate=pl.CostEstimate(flops=flops, bytes_accessed=nbytes, transcendentals=0),
        name=name,
    )(scalars, *operands, *deps)


def tie(values, deps):
    count = len(values)
    anywhere = pl.BlockSpec(memory_space=pl.ANY)
    return pl.pallas_call(
        lambda *refs: None,
        out_shape=tuple(sds(v.shape, v.dtype) for v in values),
        in_specs=[anywhere] * (count + len(deps)),
        out_specs=(anywhere,) * count,
        input_output_aliases={i: i for i in range(count)},
        name="tie",
    )(*values, *deps)


def whole(array):
    return pl.BlockSpec(array.shape, lambda *_: (0,) * array.ndim)


def sds(shape, dtype):
    return jax.ShapeDtypeStruct(shape, dtype)


def weight_operands(weight, start, width):
    if not isinstance(weight, tuple):
        spec = pl.BlockSpec((1, 4, 2, 64, width), lambda i, s: (i, 0, 0, 0, start // width))
        return [weight], [spec]
    piece = math.gcd(start, width) if start else width
    operands, specs = [], []
    for at in range(start, start + width, piece):
        for stack in weight:
            operands.append(stack)
            specs.append(pl.BlockSpec((4, 2, 64, piece), lambda i, s, at=at: (0, 0, 0, at // piece)))
    return operands, specs


def load_slab(s_ref, refs, held):
    core = s_ref[0]
    if len(refs) == 1:
        return jnp.concatenate(
            [refs[0][0, y, jnp.bitwise_xor(c, core)] for c in (0, 1) for y in range(4)], axis=0
        )
    x_far = lax.rem(s_ref[2] + 4 - pl.program_id(0), 4)
    at = 0
    for first in range(0, len(refs), 4):
        stacks = refs[first : first + 4]
        width = stacks[0].shape[-1]
        for j in range(4):

            @pl.when((core == 0) & (x_far == j))
            def _(j=j, at=at, width=width, stacks=stacks):
                for i in range(4):
                    y = lax.rem(s_ref[3] + 4 - i, 4)
                    for c in (0, 1):
                        held[c * 4 + y, :, at : at + width] = stacks[j][i, c]

        @pl.when(core == 1)
        def _(at=at, width=width, stacks=stacks):
            for j in range(4):
                y = lax.rem(s_ref[3] + 4 - j, 4)
                for c in (0, 1):
                    held[c * 4 + y, :, at : at + width] = stacks[j][x_far, 1 - c]

        at += width
    return held[...].reshape(SLAB, at)


def hop(value, first, offset):
    pairs = []
    for x in range(4):
        for core in (0, 1):
            for y in range(4):
                to = ((x + offset) % 4, y) if (core == 0) == first else (x, (y + offset) % 4)
                pairs.append(((x * 2 + core) * 4 + y, (to[0] * 2 + core) * 4 + to[1]))
    return lax.ppermute(value, ("x", "core", "ctx"), pairs)


def spread_near(block):
    near, far, mid = [hop(block, False, o) for o in (1, 3, 2)]
    return block, near, mid, far


def stack_blocks(blocks, start, width, scalars, name, deps=()):
    at = start // width if start % width == 0 else None
    span = width if at is not None else blocks[0].shape[1]
    first = 0 if at is not None else start
    height = blocks[0].shape[0]

    def body(s_ref, *refs):
        for k, ref in enumerate(refs[:-1]):
            refs[-1][k * height : (k + 1) * height, :] = ref[:, first : first + width]

    total = sds((height * len(blocks), width), BF)
    return call(
        body,
        (1,),
        [pl.BlockSpec((height, span), lambda i, s: (0, at or 0))] * len(blocks),
        whole(total),
        total,
        scalars,
        tuple(blocks),
        name,
        deps=deps,
    )


def spread_far(stack, gate=False):
    stack = stack.reshape(4, 2, 64, -1)
    near, far = hop(stack, True, 1), hop(stack, True, -1)
    mid = hop(tie((stack,), (near, far))[0] if gate else stack, True, 2)
    return stack, near, mid, far


def collect_far(parts, near_after=(), mid_after=None):
    near, far = parts[1], parts[3]
    if near_after:
        near, far = tie((near, far), near_after)
    got = [hop(near, True, 1), hop(far, True, -1)]
    got.append(hop(tie((parts[2],), got if mid_after is None else mid_after)[0], True, 2))
    sums = []
    for j in range(4):
        total = parts[0][j].astype(F32)
        for part in got:
            total = total + part[j].astype(F32)
        sums.append(total.astype(BF))
    return sums, got


def collect_near(sums):
    got = [hop(sums[j], False, j) for j in (1, 3, 2)]
    total = sums[0].astype(F32)
    for part in got:
        total = total + part.astype(F32)
    return total.astype(BF)


def mm_in(left, right, weight, start, width, scalars, name, deps=()):
    operands, specs = weight_operands(weight, start, width)

    def body(s_ref, a_ref, b_ref, *refs):
        out_ref = refs[len(operands)]
        step = pl.program_id(0)
        part = jnp.dot(
            jnp.concatenate((a_ref[...], b_ref[...]), axis=0),
            load_slab(s_ref, refs[: len(operands)], refs[-1]),
            preferred_element_type=F32,
        )

        @pl.when(step == 0)
        def _():
            out_ref[...] = part

        @pl.when(step > 0)
        def _():
            out_ref[...] += part

    rows = left.shape[0]
    cols = pl.BlockSpec((rows, SLAB), lambda i, s: (0, i))
    return call(
        body,
        (4,),
        [cols, cols, *specs],
        pl.BlockSpec((2 * rows, width), lambda i, s: (0, 0)),
        sds((2 * rows, width), F32),
        scalars,
        (left, right, *operands),
        name,
        flops=4 * rows * D * width,
        scratch=[pltpu.VMEM((8, 64, width), BF)],
        deps=deps,
    )


def mm_back(terms, scalars, name, deps=()):
    rows = terms[0][0].shape[0]
    half = rows // 2
    operands, specs, counts, scratch = [], [], [], []
    for grad, weight, start in terms:
        ops, sp = weight_operands(weight, start, grad.shape[1])
        operands += [grad, *ops]
        specs += [whole(grad), *sp]
        counts.append(len(ops))
        scratch.append(pltpu.VMEM((8, 64, grad.shape[1]), BF))

    def body(s_ref, *refs):
        own_ref, other_ref = refs[len(operands) : len(operands) + 2]
        at, out = 0, 0.0
        for k, count in enumerate(counts):
            slab = load_slab(s_ref, refs[at + 1 : at + 1 + count], refs[len(operands) + 2 + k])
            out += lax.dot_general(
                refs[at][...], slab, (((1,), (1,)), ((), ())), preferred_element_type=F32
            )
            at += count + 1
        own_ref[...] = out[:half]
        other_ref[...] = out[half:].astype(BF)

    cols = pl.BlockSpec((half, SLAB), lambda i, s: (0, i))
    return call(
        body,
        (4,),
        specs,
        (cols, cols),
        (sds((half, D), F32), sds((half, D), BF)),
        scalars,
        tuple(operands),
        name,
        flops=sum(2 * rows * D * grad.shape[1] for grad, _, _ in terms),
        scratch=scratch,
        deps=deps,
    )


def mm_weight(pairs, scalars, name, apart=False, deps=()):
    widths = [grad.shape[1] for _, grad in pairs]
    rows = pairs[0][0][0].shape[0]
    count = 3 * len(pairs)
    total = sum(widths)

    def body(s_ref, *refs):
        core = s_ref[0]
        outs, held = refs[count:-1], refs[-1]
        at = 0
        for k, width in enumerate(widths):
            a_ref, b_ref, g_ref = refs[3 * k : 3 * k + 3]
            out = lax.dot_general(
                jnp.concatenate((a_ref[...], b_ref[...]), axis=0),
                g_ref[...],
                (((0,), (0,)), ((), ())),
                preferred_element_type=F32,
            ).astype(BF)
            held[:, :, at : at + width] = out.reshape(8, 64, width)
            at += width
        if not apart:
            for c in (0, 1):
                for y in range(4):
                    outs[0][0, y, jnp.bitwise_xor(c, core)] = held[c * 4 + y]
            return
        x_far = lax.rem(pl.program_id(0) + 4 - s_ref[2], 4)
        for k in range(4):

            @pl.when((core == 0) & (x_far == k))
            def _(k=k):
                for j in range(4):
                    y = lax.rem(s_ref[3] + j, 4)
                    for rel in (0, 1):
                        outs[k][j, rel] = held[rel * 4 + y]

        @pl.when(core == 1)
        def _():
            for k in range(4):
                y = lax.rem(s_ref[3] + k, 4)
                for rel in (0, 1):
                    outs[k][x_far, rel] = held[(1 - rel) * 4 + y]

    cols = pl.BlockSpec((rows, SLAB), lambda i, s: (0, i))
    specs, operands = [], []
    for (a, b), grad in pairs:
        specs += [cols, cols, whole(grad)]
        operands += [a, b, grad]
    if apart:
        shapes = (sds((4, 2, 64, total), BF),) * 4
        out_specs = tuple(whole(s) for s in shapes)
    else:
        shapes = sds((4, 4, 2, 64, total), BF)
        out_specs = pl.BlockSpec((1, 4, 2, 64, total), lambda i, s: (i, 0, 0, 0, 0))
    return call(
        body,
        (4,),
        specs,
        out_specs,
        shapes,
        scalars,
        tuple(operands),
        name,
        flops=4 * rows * D * total,
        scratch=[pltpu.VMEM((8, 64, total), BF)],
        deps=deps,
    )


def split_heads(weights, scalars, name, deps=()):
    widths = [w.shape[1] // 2 for w in weights]

    def body(s_ref, *refs):
        mine_ref, theirs_ref = refs[-2:]
        core = s_ref[0]
        for out_ref, head in ((mine_ref, core), (theirs_ref, 1 - core)):
            at = 0
            for ref, width in zip(refs, widths):
                out_ref[:, at : at + width] = ref[:, pl.ds(pl.multiple_of(head * width, width), width)]
                at += width

    total = sum(widths)
    spec = pl.BlockSpec((64, total), lambda i, s: (0, 0))
    return call(
        body,
        (1,),
        [whole(w) for w in weights],
        (spec, spec),
        (sds((64, total), BF),) * 2,
        scalars,
        tuple(weights),
        name,
        deps=deps,
    )


def join_heads(mine, theirs, widths, scalars, name):
    def body(s_ref, mine_ref, theirs_ref, *outs):
        core = s_ref[0]
        for in_ref, head in ((mine_ref, core), (theirs_ref, 1 - core)):
            at = 0
            for ref, width in zip(outs, widths):
                span = pl.ds(pl.multiple_of(head * width, width), width)
                ref[:, span] = in_ref[:, at : at + width].astype(F32)
                at += width

    shapes = tuple(sds((64, 2 * w), F32) for w in widths)
    return call(
        body,
        (1,),
        [whole(mine), whole(theirs)],
        tuple(whole(s) for s in shapes),
        shapes,
        scalars,
        (mine, theirs),
        name,
    )


def scale_of(values):
    return lax.rsqrt(jnp.mean(values * values, axis=-1, keepdims=True) + 1e-06)


def turned_spec(rows):
    return pl.BlockSpec((rows, D), lambda i, s: (lax.rem(i + s[1], 4), 0))


def plain_spec(rows):
    return pl.BlockSpec((rows, D), lambda i, s: (i, 0))


def enter_rows(tokens, cotangent, gain, scalars, deps=()):
    rows = tokens.shape[0]
    block = rows // 4

    def body(s_ref, t_ref, c_ref, g_ref, t_out, c_out, n_out, l_out):
        values = t_ref[...]
        t_out[...] = values
        n_out[...] = (values * scale_of(values) * g_ref[...]).astype(BF)
        c_out[...] = c_ref[...]
        l_out[...] = c_ref[...].astype(BF)

    turn, plain = turned_spec(block), plain_spec(block)
    full = (rows, D)
    return call(
        body,
        (4,),
        [turn, turn, whole(gain)],
        (plain,) * 4,
        (sds(full, F32), sds(full, F32), sds(full, BF), sds(full, BF)),
        scalars,
        (tokens, cotangent, gain),
        "enter_rows",
        deps=deps,
    )


def each_part(refs, work):
    step = pl.program_id(0)
    for k, ref in enumerate(refs):

        @pl.when(step == k)
        def _(ref=ref):
            work(ref[...].astype(F32))


def second_norm(tokens, parts, gain, scalars, deps=()):
    rows = tokens.shape[0]
    block = rows // 4

    def body(s_ref, t_ref, g_ref, *refs):
        h_out, n_out = refs[4:]

        def work(part):
            values = t_ref[...] + part
            h_out[...] = values
            n_out[...] = (values * scale_of(values) * g_ref[...]).astype(BF)

        each_part(refs[:4], work)

    plain = plain_spec(block)
    return call(
        body,
        (4,),
        [plain, whole(gain)] + [whole(p) for p in parts],
        (plain, plain),
        (sds((rows, D), F32), sds((rows, D), BF)),
        scalars,
        (tokens, gain, *parts),
        "second_norm",
        deps=deps,
    )


def turned_total(own, came, scalars, name, deps=()):
    rows = own.shape[0]
    block = rows // 4

    def body(s_ref, own_ref, came_ref, out_ref):
        out_ref[...] = (own_ref[...] + came_ref[...].astype(F32)).astype(BF)

    plain = plain_spec(block)
    return call(
        body,
        (4,),
        [plain, plain],
        turned_spec(block),
        sds((rows, D), BF),
        scalars,
        (own, came),
        name,
        deps=deps,
    )


def first_gain(own, came, tokens, scalars, deps=()):
    rows = own.shape[0]
    block = rows // 4

    def body(s_ref, own_ref, came_ref, t_ref, *refs):
        total = own_ref[...] + came_ref[...].astype(F32)
        values = t_ref[...]
        part = jnp.sum(total * (values * scale_of(values)), axis=0, keepdims=True)
        step = pl.program_id(0)
        for k in range(4):

            @pl.when(step == k)
            def _(k=k):
                refs[k][...] = total.astype(BF)

        @pl.when(step == 0)
        def _():
            refs[4][...] = part

        @pl.when(step > 0)
        def _():
            refs[4][...] += part

    plain = plain_spec(block)
    shapes = (sds((block, D), BF),) * 4 + (sds((1, D), F32),)
    out = call(
        body,
        (4,),
        [plain] * 3,
        tuple(whole(s) for s in shapes),
        shapes,
        scalars,
        (own, came, tokens),
        "first_gain",
        deps=deps,
    )
    return out[:4], out[4]


def leave_rows(hidden, total, scalars):
    rows = hidden.shape[0]
    block = rows // 4

    def body(s_ref, h_ref, t_ref, out_ref):
        out_ref[...] = h_ref[...] + t_ref[...].astype(F32)

    turn = turned_spec(block)
    return call(
        body,
        (4,),
        [plain_spec(block), turn],
        turn,
        sds((rows, D), F32),
        scalars,
        (hidden, total),
        "leave_rows",
    )


def gain_part(values, grad, name):
    block = grad.shape[0]

    def body(v_ref, p_ref, out_ref):
        values = v_ref[...]
        out_ref[...] = jnp.sum(
            p_ref[...].astype(F32) * (values * scale_of(values)), axis=0, keepdims=True
        )

    return pl.pallas_call(
        body,
        out_shape=sds((1, D), F32),
        grid=(1,),
        in_specs=[pl.BlockSpec((block, D), lambda i: (0, 0))] * 2,
        out_specs=pl.BlockSpec((1, D), lambda i: (0, 0)),
        name=name,
    )(values, grad)


def norm_back(values, upstream, parts, gain, last, scalars, name, deps=()):
    rows = values.shape[0]
    block = rows // 4

    def body(s_ref, v_ref, u_ref, g_ref, *refs):
        outs = refs[4:]

        def work(part):
            values = v_ref[...]
            factor = scale_of(values)
            unit = values * factor
            scaled = part * g_ref[...]
            out = u_ref[...] + factor * (
                scaled - unit * jnp.mean(scaled * unit, axis=-1, keepdims=True)
            )
            outs[0][...] = out
            if not last:
                outs[1][...] = out.astype(BF)

        each_part(refs[:4], work)

    plain = plain_spec(block)
    if last:
        specs, shapes = turned_spec(block), sds((rows, D), F32)
    else:
        specs, shapes = (plain, plain), (sds((rows, D), F32), sds((rows, D), BF))
    return call(
        body,
        (4,),
        [plain, plain, whole(gain)] + [whole(p) for p in parts],
        specs,
        shapes,
        scalars,
        (values, upstream, gain, *parts),
        name,
        deps=deps,
    )


def tp_total(blocks):
    got = [shift(blocks[o], "tp", o) for o in (1, 3, 2)]
    mine = blocks[0].astype(F32)
    for part in got:
        mine = mine + part.astype(F32)
    mine = mine.astype(BF)
    near, far, mid = [shift(mine, "tp", -o) for o in (1, 3, 2)]
    return (mine, near, mid, far)


def heads_total(own, other):
    came = swap(other)
    block = own.shape[0] // 4
    blocks = [
        (own[o * block : (o + 1) * block] + came[o * block : (o + 1) * block].astype(F32)).astype(BF)
        for o in range(4)
    ]
    return tp_total(blocks), blocks


def gate_norm(gate_pre, retained):
    centred = retained - jnp.mean(retained, axis=-1, keepdims=True)
    normed = centred * lax.rsqrt(jnp.mean(centred * centred, axis=-1, keepdims=True) + 1.0 * DK)
    return gate_pre * jax.nn.sigmoid(gate_pre) * normed


def gelu_gate(hidden, linear):
    return jax.nn.gelu(hidden, approximate=True) * linear


def rotate(values, cosine, sine):
    half = DK // 2
    first = values[:, :half]
    second = values[:, half:]
    return jnp.concatenate((first * cosine - second * sine, first * sine + second * cosine), axis=1)


def ein(spec, left, right):
    return jnp.einsum(spec, left, right, preferred_element_type=F32)


def per_device(
    tokens,
    cotangent,
    gain_first,
    gain_second,
    w_query,
    w_key,
    w_value,
    w_gate,
    w_output,
    w_hidden,
    w_linear,
    w_down,
    decay_scale,
    first_length,
):
    rows = tokens.shape[0]
    core = lax.axis_index("core")
    place = lax.axis_index("ctx")
    plane = lax.axis_index("tp")
    scalars = jnp.stack((core, plane, lax.axis_index("x"), place)).astype(jnp.int32)

    w_output = w_output.T
    w_down = w_down.T
    mine, theirs = split_heads((w_key, w_value, w_gate, w_query), scalars, "split_attn")
    came = swap(theirs)
    block = stack_blocks((mine, came), 0, 1536, scalars, "stack_attn")
    attn = lax.all_gather(block, XY, axis=0, tiled=True).reshape(4, 4, 2, 64, -1)
    mine, theirs = split_heads(
        (w_output, w_down, w_hidden, w_linear), scalars, "split_rest", deps=(came,)
    )
    block = stack_blocks((mine, swap(theirs)), 0, 2048, scalars, "stack_rest", deps=(block,))
    blocks = spread_near(block)
    gain_first = gain_first.reshape(1, D)
    gain_second = gain_second.reshape(1, D)
    tokens, cotangent, normed_first, cot_low = enter_rows(
        tokens, cotangent, gain_first, scalars, deps=(block,)
    )
    x_first = (normed_first, swap(normed_first))
    g_out = (cot_low, swap(cot_low))

    rate = lax.dynamic_index_in_dim(decay_scale, core, 0, False) / 1024.0
    local = (jnp.arange(rows, dtype=jnp.int32) + plane * (rows // 4)) % rows
    index = place * rows + local
    lengths = jnp.concatenate((first_length, swap(first_length)))
    document = (index[None, :] >= lengths[:, None]).astype(jnp.int32)
    carried = (document == 0).astype(F32)
    steps = local.astype(F32)
    offsets = local[:, None] - local[None, :]
    linked = (offsets >= 0)[None] & (document[:, :, None] == document[:, None, :])
    mask = jnp.where(
        linked, jnp.exp(-rate * jnp.maximum(offsets, 0).astype(F32))[None], 0.0
    )
    enter = (carried * jnp.exp(-rate * (steps + 1.0))[None])[:, :, None]
    leave = jnp.exp(-rate * (rows - 1.0 - steps))[None, :, None]
    fade = jnp.exp(-rate * rows)
    half = DK // 2
    frequency = 10000.0 ** (-(jnp.arange(half).astype(F32) / half))
    angles = index.astype(F32)[:, None] * frequency[None, :]
    cosine = jnp.tile(jnp.cos(angles), (2, 1))
    sine = jnp.tile(jnp.sin(angles), (2, 1))

    def carry(came):
        near, mid, far = [part.astype(F32) for part in came]
        return near + fade * (mid + fade * far)

    def spread_state(low, way):
        return [shift_open(low, "ctx", way * o) for o in (1, 2, 3)]

    tables = (x_first[1], g_out[1], mask, enter, leave, cosine, sine)
    out_down = stack_blocks(blocks, 0, 1024, scalars, "stack_out", deps=tables)
    w_out = spread_far(out_down)
    mlp_stack = stack_blocks(blocks, 1024, 1024, scalars, "stack_mlp", deps=(out_down,))
    projected = mm_in(
        *x_first, attn, 0, 768, scalars, "project_kv", deps=(*w_out[1:], mlp_stack)
    )
    key = rotate(projected[:, :DK], cosine, sine).astype(BF).reshape(2, rows, DK)
    value = projected[:, DK:].astype(BF).reshape(2, rows, DV)
    key_out = (key.astype(F32) * leave).astype(BF)
    state_out = ein("gjd,gje->gde", key_out, value).astype(BF)
    came = spread_state(state_out, 1)
    projected = mm_in(*x_first, attn, 768, 768, scalars, "project_gq", deps=(state_out,))
    state_in = carry(came).astype(BF)
    gate_pre = projected[:, :DV]
    query = rotate(projected[:, DV:], cosine, sine).astype(BF).reshape(2, rows, DK)
    weighted = (ein("gid,gjd->gij", query, key) * mask).astype(BF)
    inner = ein("gij,gje->gie", weighted, value)
    retained = (inner + ein("gid,gde->gie", query, state_in) * enter).reshape(2 * rows, DV)
    mixed_full, gate_back = jax.vjp(gate_norm, gate_pre, retained)
    mixed = mixed_full.astype(BF)
    own, other = mm_back([(mixed, w_out, 0)], scalars, "project_out")
    mlp = spread_far(tie((mlp_stack,), (other,))[0], True)
    parts, _ = heads_total(own, other)
    grad_activated = mm_in(*g_out, w_out, DV, DV, scalars, "back_down", deps=(other,))
    hidden_state, normed_second = second_norm(tokens, parts, gain_second, scalars, deps=(grad_activated,))
    x_second = (normed_second, swap(normed_second))
    paired = mm_in(*x_second, mlp, 0, 2 * DV, scalars, "project_mlp")
    activated_full, gelu_back = jax.vjp(gelu_gate, paired[:, :DV], paired[:, DV:])
    activated = activated_full.astype(BF)
    grad_pair = jnp.concatenate(gelu_back(grad_activated), axis=1).astype(BF)
    own, other = mm_back([(grad_pair, mlp, 0)], scalars, "back_mlp")
    parts, totals = heads_total(own, other)
    d_mlp = mm_weight(
        ((x_second, grad_pair), (g_out, activated)), scalars, "weight_mlp", True, deps=(totals[1],)
    )
    down = mm_back([(activated, w_out, DV)], scalars, "project_down", deps=(parts[0],))
    gain_second_part = gain_part(hidden_state, parts[0], "gain_second")
    down_total = turned_total(
        down[0], swap(down[1]), scalars, "down_total", deps=(parts[1],)
    )
    mlp_sums, mlp_got = collect_far(d_mlp)
    grad_state, grad_state_low = norm_back(
        hidden_state,
        cotangent,
        parts,
        gain_second,
        False,
        scalars,
        "second_back",
        deps=(down_total, gain_second_part, *mlp_got[:2]),
    )
    g_state = (grad_state_low, swap(grad_state_low))
    grad_mixed = mm_in(*g_state, w_out, 0, DV, scalars, "back_out")
    grad_gate, grad_retained = gate_back(grad_mixed)
    grad_low = grad_retained.reshape(2, rows, DV).astype(BF)
    query_in = (query.astype(F32) * enter).astype(BF)
    back_out = ein("gid,gie->gde", query_in, grad_low).astype(BF)
    came = spread_state(back_out, -1)
    grad_scores = (ein("gie,gje->gij", grad_low, value) * mask).astype(BF)
    grad_query = ein("gij,gjd->gid", grad_scores, key) + enter * ein("gie,gde->gid", grad_low, state_in)
    grad_key = ein("gij,gid->gjd", grad_scores, query)
    grad_value = ein("gij,gie->gje", weighted, grad_low)
    grad_gq = jnp.concatenate(
        (grad_gate, rotate(grad_query.reshape(2 * rows, DK), cosine, -sine)), axis=1
    ).astype(BF)
    d_gqo = mm_weight(
        ((x_first, grad_gq), (g_state, mixed)),
        scalars,
        "weight_gqo",
        True,
        deps=(back_out, mlp_got[2]),
    )
    mlp_block = collect_near(tie(mlp_sums, (back_out,)))
    came[0] = tie((came[0],), (d_gqo[0], grad_key, grad_value))[0]
    state_back = carry(came).astype(BF)
    grad_key += leave * ein("gje,gde->gjd", value, state_back)
    grad_value += ein("gjd,gde->gje", key_out, state_back)
    grad_kv = jnp.concatenate(
        (rotate(grad_key.reshape(2 * rows, DK), cosine, -sine), grad_value.reshape(2 * rows, DV)),
        axis=1,
    ).astype(BF)
    gqo_sums, gqo_got = collect_far(d_gqo, (state_back, mlp_block))
    own, other = mm_back([(grad_kv, attn, 0), (grad_gq, attn, 768)], scalars, "back_attn")
    d_kv = mm_weight(((x_first, grad_kv),), scalars, "weight_kv", True, deps=(other,))
    chip, gain_first_part = first_gain(own, swap(other), tokens, scalars, deps=(d_kv[0],))
    parts = tp_total(chip)
    kv_sums, kv_got = collect_far(d_kv, gqo_got[2:])
    gqo_block = collect_near(gqo_sums)
    kv_block = collect_near(kv_sums)
    gains = jnp.concatenate((gain_first_part, gain_second_part))
    (gains,) = tie((gains,), kv_got[:2])
    for axis, swapped in (
        ("core", (1, 0)),
        ("tp", (1, 0, 3, 2)),
        ("tp", (3, 2, 1, 0)),
        ("ctx", (1, 0, 3, 2)),
        ("ctx", (3, 2, 1, 0)),
        ("x", (1, 0, 3, 2)),
        ("x", (3, 2, 1, 0)),
    ):
        gains = gains + lax.ppermute(gains, axis, list(enumerate(swapped)))
    spot = (lax.axis_index("x") * 2 + core) * 4 + place
    gains = lax.dynamic_slice_in_dim(gains, spot * 64, 64, 1)
    input_grad = norm_back(tokens, grad_state, parts, gain_first, True, scalars, "first_back")
    layer_total = lax.psum(down_total, "tp")
    layer_out = leave_rows(hidden_state, layer_total, scalars)
    d_hidden, d_linear, d_down = join_heads(
        mlp_block[0], swap(mlp_block[1]), (DV, DV, DV), scalars, "join_mlp"
    )
    d_gate, d_query, d_output = join_heads(
        gqo_block[0], swap(gqo_block[1]), (DV, DK, DV), scalars, "join_gqo"
    )
    d_key, d_value = join_heads(
        kv_block[0], swap(kv_block[1]), (DK, DV), scalars, "join_kv"
    )
    return (
        layer_out,
        input_grad,
        gains[0],
        gains[1],
        d_query,
        d_key,
        d_value,
        d_gate,
        d_output.T,
        d_hidden,
        d_linear,
        d_down.T,
    )


def solution(mesh):
    fine = Mesh(np.asarray(mesh.devices).reshape(4, 2, 4, 4), ("x", "core", "ctx", "tp"))
    split = ("x", "core", "ctx")
    row = P(split, None)
    win = P(split, "tp")
    wout = P("tp", split)
    in_specs = (row, row, P(), P(), win, win, win, win, wout, win, win, wout, P("tp"), P(("x", "core")))
    out_specs = (row, row, P(split), P(split), win, win, win, win, wout, win, win, wout)
    return jax.shard_map(
        per_device, mesh=fine, in_specs=in_specs, out_specs=out_specs, check_vma=False
    )
```

```python
import math

import jax
import jax.numpy as jnp
import numpy as np
from jax import lax
from jax.experimental import pallas as pl
from jax.experimental.pallas import tpu as pltpu
from jax.sharding import Mesh, PartitionSpec as P

D = 2048
DK = 256
DV = 512
SLAB = 512
BF = jnp.bfloat16
F32 = jnp.float32
XY = ("x", "ctx")
MIB = 1 << 20


def shift(value, axis, offset):
    n = lax.axis_size(axis)
    return lax.ppermute(value, axis, [(i, (i + offset) % n) for i in range(n)])


def shift_open(value, axis, offset):
    n = lax.axis_size(axis)
    return lax.ppermute(
        value, axis, [(i, i + offset) for i in range(n) if 0 <= i + offset < n]
    )


def swap(value):
    return lax.ppermute(value, "core", [(0, 1), (1, 0)])


def after(value, *earlier):
    return lax.optimization_barrier((value, *earlier))[0]


def call(body, grid, ins, outs, shapes, scalars, operands, name, flops=0, scratch=(), deps=()):
    nbytes = sum(a.size * a.dtype.itemsize for a in jax.tree.leaves((operands, shapes)))
    count = len(operands)

    def kernel(s_ref, *refs):
        body(s_ref, *refs[:count], *refs[count + len(deps) :])

    ins = [*ins, *[pl.BlockSpec(memory_space=pl.ANY)] * len(deps)]
    return pl.pallas_call(
        kernel,
        out_shape=shapes,
        grid_spec=pltpu.PrefetchScalarGridSpec(
            num_scalar_prefetch=1, grid=grid, in_specs=ins, out_specs=outs, scratch_shapes=scratch
        ),
        compiler_params=pltpu.CompilerParams(
            vmem_limit_bytes=48 * MIB, dimension_semantics=("arbitrary",) * len(grid)
        ),
        cost_estimate=pl.CostEstimate(flops=flops, bytes_accessed=nbytes, transcendentals=0),
        name=name,
    )(scalars, *operands, *deps)


def tie(values, deps):
    count = len(values)
    anywhere = pl.BlockSpec(memory_space=pl.ANY)
    return pl.pallas_call(
        lambda *refs: None,
        out_shape=tuple(sds(v.shape, v.dtype) for v in values),
        in_specs=[anywhere] * (count + len(deps)),
        out_specs=(anywhere,) * count,
        input_output_aliases={i: i for i in range(count)},
        name="tie",
    )(*values, *deps)


def whole(array):
    return pl.BlockSpec(array.shape, lambda *_: (0,) * array.ndim)


def sds(shape, dtype):
    return jax.ShapeDtypeStruct(shape, dtype)


def weight_operands(weight, start, width):
    if not isinstance(weight, tuple):
        spec = pl.BlockSpec((1, 4, 2, 64, width), lambda i, s: (i, 0, 0, 0, start // width))
        return [weight], [spec]
    piece = math.gcd(start, width) if start else width
    operands, specs = [], []
    for at in range(start, start + width, piece):
        for stack in weight:
            operands.append(stack)
            specs.append(pl.BlockSpec((4, 2, 64, piece), lambda i, s, at=at: (0, 0, 0, at // piece)))
    return operands, specs


def load_slab(s_ref, refs, held):
    core = s_ref[0]
    if len(refs) == 1:
        return jnp.concatenate(
            [refs[0][0, y, jnp.bitwise_xor(c, core)] for c in (0, 1) for y in range(4)], axis=0
        )
    x_far = lax.rem(s_ref[2] + 4 - pl.program_id(0), 4)
    at = 0
    for first in range(0, len(refs), 4):
        stacks = refs[first : first + 4]
        width = stacks[0].shape[-1]
        for j in range(4):

            @pl.when((core == 0) & (x_far == j))
            def _(j=j, at=at, width=width, stacks=stacks):
                for i in range(4):
                    y = lax.rem(s_ref[3] + 4 - i, 4)
                    for c in (0, 1):
                        held[c * 4 + y, :, at : at + width] = stacks[j][i, c]

        @pl.when(core == 1)
        def _(at=at, width=width, stacks=stacks):
            for j in range(4):
                y = lax.rem(s_ref[3] + 4 - j, 4)
                for c in (0, 1):
                    held[c * 4 + y, :, at : at + width] = stacks[j][x_far, 1 - c]

        at += width
    return held[...].reshape(SLAB, at)


def hop(value, first, offset):
    pairs = []
    for x in range(4):
        for core in (0, 1):
            for y in range(4):
                to = ((x + offset) % 4, y) if (core == 0) == first else (x, (y + offset) % 4)
                pairs.append(((x * 2 + core) * 4 + y, (to[0] * 2 + core) * 4 + to[1]))
    return lax.ppermute(value, ("x", "core", "ctx"), pairs)


def spread_near(block):
    near, far, mid = [hop(block, False, o) for o in (1, 3, 2)]
    return block, near, mid, far


def stack_blocks(blocks, start, width, scalars, name, deps=()):
    at = start // width if start % width == 0 else None
    span = width if at is not None else blocks[0].shape[1]
    first = 0 if at is not None else start
    height = blocks[0].shape[0]

    def body(s_ref, *refs):
        for k, ref in enumerate(refs[:-1]):
            refs[-1][k * height : (k + 1) * height, :] = ref[:, first : first + width]

    total = sds((height * len(blocks), width), BF)
    return call(
        body,
        (1,),
        [pl.BlockSpec((height, span), lambda i, s: (0, at or 0))] * len(blocks),
        whole(total),
        total,
        scalars,
        tuple(blocks),
        name,
        deps=deps,
    )


def spread_far(stack, gate=False):
    stack = stack.reshape(4, 2, 64, -1)
    near, far = hop(stack, True, 1), hop(stack, True, -1)
    mid = hop(tie((stack,), (near, far))[0] if gate else stack, True, 2)
    return stack, near, mid, far


def collect_far(parts, near_after=(), mid_after=None):
    near, far = parts[1], parts[3]
    if near_after:
        near, far = tie((near, far), near_after)
    got = [hop(near, True, 1), hop(far, True, -1)]
    got.append(hop(tie((parts[2],), got if mid_after is None else mid_after)[0], True, 2))
    sums = []
    for j in range(4):
        total = parts[0][j].astype(F32)
        for part in got:
            total = total + part[j].astype(F32)
        sums.append(total.astype(BF))
    return sums, got


def collect_near(sums):
    got = [hop(sums[j], False, j) for j in (1, 3, 2)]
    total = sums[0].astype(F32)
    for part in got:
        total = total + part.astype(F32)
    return total.astype(BF)


def mm_in(left, right, columns, scalars, name, deps=()):
    operands, specs, counts = [], [], []
    for weight, start, width in columns:
        ops, sp = weight_operands(weight, start, width)
        operands += ops
        specs += sp
        counts.append(len(ops))
    total = sum(width for _, _, width in columns)

    def body(s_ref, a_ref, b_ref, *refs):
        out_ref = refs[len(operands)]
        step = pl.program_id(0)
        rows = jnp.concatenate((a_ref[...], b_ref[...]), axis=0)
        at, first = 0, 0
        for k, count in enumerate(counts):
            width = columns[k][2]
            slab = load_slab(s_ref, refs[first : first + count], refs[len(operands) + 1 + k])
            part = jnp.dot(rows, slab, preferred_element_type=F32)
            span = slice(at, at + width)

            @pl.when(step == 0)
            def _(part=part, span=span):
                out_ref[:, span] = part

            @pl.when(step > 0)
            def _(part=part, span=span):
                out_ref[:, span] += part

            at += width
            first += count

    rows = left.shape[0]
    cols = pl.BlockSpec((rows, SLAB), lambda i, s: (0, i))
    return call(
        body,
        (4,),
        [cols, cols, *specs],
        pl.BlockSpec((2 * rows, total), lambda i, s: (0, 0)),
        sds((2 * rows, total), F32),
        scalars,
        (left, right, *operands),
        name,
        flops=4 * rows * D * total,
        scratch=[pltpu.VMEM((8, 64, width), BF) for _, _, width in columns],
        deps=deps,
    )


def mm_back(terms, scalars, name, deps=()):
    rows = terms[0][0].shape[0]
    half = rows // 2
    operands, specs, counts, scratch = [], [], [], []
    for grad, weight, start in terms:
        ops, sp = weight_operands(weight, start, grad.shape[1])
        operands += [grad, *ops]
        specs += [whole(grad), *sp]
        counts.append(len(ops))
        scratch.append(pltpu.VMEM((8, 64, grad.shape[1]), BF))

    def body(s_ref, *refs):
        own_ref, other_ref = refs[len(operands) : len(operands) + 2]
        at, out = 0, 0.0
        for k, count in enumerate(counts):
            slab = load_slab(s_ref, refs[at + 1 : at + 1 + count], refs[len(operands) + 2 + k])
            out += lax.dot_general(
                refs[at][...], slab, (((1,), (1,)), ((), ())), preferred_element_type=F32
            )
            at += count + 1
        own_ref[...] = out[:half]
        other_ref[...] = out[half:].astype(BF)

    cols = pl.BlockSpec((half, SLAB), lambda i, s: (0, i))
    return call(
        body,
        (4,),
        specs,
        (cols, cols),
        (sds((half, D), F32), sds((half, D), BF)),
        scalars,
        tuple(operands),
        name,
        flops=sum(2 * rows * D * grad.shape[1] for grad, _, _ in terms),
        scratch=scratch,
        deps=deps,
    )


def mm_weight(pairs, scalars, name, apart=False, deps=()):
    widths = [grad.shape[1] for _, grad in pairs]
    rows = pairs[0][0][0].shape[0]
    count = 3 * len(pairs)
    total = sum(widths)

    def body(s_ref, *refs):
        core = s_ref[0]
        outs, held = refs[count:-1], refs[-1]
        at = 0
        for k, width in enumerate(widths):
            a_ref, b_ref, g_ref = refs[3 * k : 3 * k + 3]
            out = lax.dot_general(
                jnp.concatenate((a_ref[...], b_ref[...]), axis=0),
                g_ref[...],
                (((0,), (0,)), ((), ())),
                preferred_element_type=F32,
            ).astype(BF)
            held[:, :, at : at + width] = out.reshape(8, 64, width)
            at += width
        if not apart:
            for c in (0, 1):
                for y in range(4):
                    outs[0][0, y, jnp.bitwise_xor(c, core)] = held[c * 4 + y]
            outs[1][...] = jnp.zeros_like(outs[1])
            return
        x_far = lax.rem(pl.program_id(0) + 4 - s_ref[2], 4)
        for k in range(4):

            @pl.when((core == 0) & (x_far == k))
            def _(k=k):
                for j in range(4):
                    y = lax.rem(s_ref[3] + j, 4)
                    for rel in (0, 1):
                        outs[k][j, rel] = held[rel * 4 + y]

        @pl.when(core == 1)
        def _():
            for k in range(4):
                y = lax.rem(s_ref[3] + k, 4)
                for rel in (0, 1):
                    outs[k][x_far, rel] = held[(1 - rel) * 4 + y]

    cols = pl.BlockSpec((rows, SLAB), lambda i, s: (0, i))
    specs, operands = [], []
    for (a, b), grad in pairs:
        specs += [cols, cols, whole(grad)]
        operands += [a, b, grad]
    if apart:
        shapes = (sds((4, 2, 64, total), BF),) * 4
        out_specs = tuple(whole(s) for s in shapes)
    else:
        shapes = (sds((4, 4, 2, 64, total), BF), sds((8, 128), F32))
        out_specs = (
            pl.BlockSpec((1, 4, 2, 64, total), lambda i, s: (i, 0, 0, 0, 0)),
            pl.BlockSpec((8, 128), lambda i, s: (0, 0)),
        )
    return call(
        body,
        (4,),
        specs,
        out_specs,
        shapes,
        scalars,
        tuple(operands),
        name,
        flops=4 * rows * D * total,
        scratch=[pltpu.VMEM((8, 64, total), BF)],
        deps=deps,
    )


def split_heads(weights, scalars, name, deps=()):
    widths = [w.shape[1] // 2 for w in weights]

    def body(s_ref, *refs):
        mine_ref, theirs_ref = refs[-2:]
        core = s_ref[0]
        for out_ref, head in ((mine_ref, core), (theirs_ref, 1 - core)):
            at = 0
            for ref, width in zip(refs, widths):
                out_ref[:, at : at + width] = ref[:, pl.ds(pl.multiple_of(head * width, width), width)]
                at += width

    total = sum(widths)
    spec = pl.BlockSpec((64, total), lambda i, s: (0, 0))
    return call(
        body,
        (1,),
        [whole(w) for w in weights],
        (spec, spec),
        (sds((64, total), BF),) * 2,
        scalars,
        tuple(weights),
        name,
        deps=deps,
    )


def join_heads(mine, theirs, widths, scalars, name):
    def body(s_ref, mine_ref, theirs_ref, *outs):
        core = s_ref[0]
        for in_ref, head in ((mine_ref, core), (theirs_ref, 1 - core)):
            at = 0
            for ref, width in zip(outs, widths):
                span = pl.ds(pl.multiple_of(head * width, width), width)
                ref[:, span] = in_ref[:, at : at + width].astype(F32)
                at += width

    shapes = tuple(sds((64, 2 * w), F32) for w in widths)
    return call(
        body,
        (1,),
        [whole(mine), whole(theirs)],
        tuple(whole(s) for s in shapes),
        shapes,
        scalars,
        (mine, theirs),
        name,
    )


def scale_of(values):
    return lax.rsqrt(jnp.mean(values * values, axis=-1, keepdims=True) + 1e-06)


def turned_spec(rows):
    return pl.BlockSpec((rows, D), lambda i, s: (lax.rem(i + s[1], 4), 0))


def plain_spec(rows):
    return pl.BlockSpec((rows, D), lambda i, s: (i, 0))


def enter_rows(tokens, cotangent, gain, scalars, deps=()):
    rows = tokens.shape[0]
    block = rows // 4

    def body(s_ref, t_ref, c_ref, g_ref, t_out, c_out, n_out, l_out):
        values = t_ref[...]
        t_out[...] = values
        n_out[...] = (values * scale_of(values) * g_ref[...]).astype(BF)
        c_out[...] = c_ref[...]
        l_out[...] = c_ref[...].astype(BF)

    turn, plain = turned_spec(block), plain_spec(block)
    full = (rows, D)
    return call(
        body,
        (4,),
        [turn, turn, whole(gain)],
        (plain,) * 4,
        (sds(full, F32), sds(full, F32), sds(full, BF), sds(full, BF)),
        scalars,
        (tokens, cotangent, gain),
        "enter_rows",
        deps=deps,
    )


def each_part(refs, work):
    step = pl.program_id(0)
    for k, ref in enumerate(refs):

        @pl.when(step == k)
        def _(ref=ref):
            work(ref[...].astype(F32))


def second_norm(tokens, parts, gain, scalars, deps=()):
    rows = tokens.shape[0]
    block = rows // 4

    def body(s_ref, t_ref, g_ref, *refs):
        h_out, n_out = refs[4:]

        def work(part):
            values = t_ref[...] + part
            h_out[...] = values
            n_out[...] = (values * scale_of(values) * g_ref[...]).astype(BF)

        each_part(refs[:4], work)

    plain = plain_spec(block)
    return call(
        body,
        (4,),
        [plain, whole(gain)] + [whole(p) for p in parts],
        (plain, plain),
        (sds((rows, D), F32), sds((rows, D), BF)),
        scalars,
        (tokens, gain, *parts),
        "second_norm",
        deps=deps,
    )


def first_gain(own, came, tokens, down_own, down_came, scalars, deps=()):
    rows = own.shape[0]
    block = rows // 4

    def body(s_ref, own_ref, came_ref, t_ref, d_ref, e_ref, *refs):
        total = own_ref[...] + came_ref[...].astype(F32)
        down = d_ref[...] + e_ref[...].astype(F32)
        values = t_ref[...]
        part = jnp.sum(total * (values * scale_of(values)), axis=0, keepdims=True)
        step = pl.program_id(0)
        for k in range(4):

            @pl.when(step == k)
            def _(k=k):
                refs[k][:block] = total.astype(BF)
                refs[k][block:] = down.astype(BF)

        @pl.when(step == 0)
        def _():
            refs[4][...] = part

        @pl.when(step > 0)
        def _():
            refs[4][...] += part

    plain = plain_spec(block)
    shapes = (sds((2 * block, D), BF),) * 4 + (sds((1, D), F32),)
    out = call(
        body,
        (4,),
        [plain] * 5,
        tuple(whole(s) for s in shapes),
        shapes,
        scalars,
        (own, came, tokens, down_own, down_came),
        "first_gain",
        deps=deps,
    )
    return out[:4], out[4]


def leave_rows(hidden, tokens, grad_state, parts, gain, scalars):
    rows = hidden.shape[0]
    block = rows // 4

    def body(s_ref, h_ref, t_ref, u_ref, g_ref, *refs):
        def work(part):
            refs[4][...] = h_ref[...] + part[block:]
            refs[5][...] = u_ref[...] + norm_grad(t_ref[...], part[:block], g_ref[...])

        each_part(refs[:4], work)

    plain, turn = plain_spec(block), turned_spec(block)
    return call(
        body,
        (4,),
        [plain] * 3 + [whole(gain)] + [whole(p) for p in parts],
        (turn, turn),
        (sds((rows, D), F32),) * 2,
        scalars,
        (hidden, tokens, grad_state, gain, *parts),
        "leave_rows",
    )


def gain_part(values, grad, name):
    block = grad.shape[0]

    def body(v_ref, p_ref, out_ref):
        values = v_ref[...]
        out_ref[...] = jnp.sum(
            p_ref[...].astype(F32) * (values * scale_of(values)), axis=0, keepdims=True
        )

    return pl.pallas_call(
        body,
        out_shape=sds((1, D), F32),
        grid=(1,),
        in_specs=[pl.BlockSpec((block, D), lambda i: (0, 0))] * 2,
        out_specs=pl.BlockSpec((1, D), lambda i: (0, 0)),
        name=name,
    )(values, grad)


def norm_grad(values, grad, gain):
    factor = scale_of(values)
    unit = values * factor
    scaled = grad * gain
    return factor * (scaled - unit * jnp.mean(scaled * unit, axis=-1, keepdims=True))


def norm_back(values, upstream, parts, gain, scalars, name, deps=()):
    rows = values.shape[0]
    block = rows // 4

    def body(s_ref, v_ref, u_ref, g_ref, *refs):
        def work(part):
            out = u_ref[...] + norm_grad(v_ref[...], part, g_ref[...])
            refs[4][...] = out
            refs[5][...] = out.astype(BF)

        each_part(refs[:4], work)

    plain = plain_spec(block)
    return call(
        body,
        (4,),
        [plain, plain, whole(gain)] + [whole(p) for p in parts],
        (plain, plain),
        (sds((rows, D), F32), sds((rows, D), BF)),
        scalars,
        (values, upstream, gain, *parts),
        name,
        deps=deps,
    )


def tp_total(blocks):
    got = [shift(blocks[o], "tp", o) for o in (1, 3, 2)]
    mine = blocks[0].astype(F32)
    for part in got:
        mine = mine + part.astype(F32)
    mine = mine.astype(BF)
    near, far, mid = [shift(mine, "tp", -o) for o in (1, 3, 2)]
    return (mine, near, mid, far)


def heads_total(own, other):
    came = swap(other)
    block = own.shape[0] // 4
    blocks = [
        (own[o * block : (o + 1) * block] + came[o * block : (o + 1) * block].astype(F32)).astype(BF)
        for o in range(4)
    ]
    return tp_total(blocks), blocks


def gate_norm(gate_pre, retained):
    centred = retained - jnp.mean(retained, axis=-1, keepdims=True)
    normed = centred * lax.rsqrt(jnp.mean(centred * centred, axis=-1, keepdims=True) + 1.0 * DK)
    return gate_pre * jax.nn.sigmoid(gate_pre) * normed


def gelu_gate(hidden, linear):
    return jax.nn.gelu(hidden, approximate=True) * linear


def rotate(values, cosine, sine):
    half = DK // 2
    first = values[:, :half]
    second = values[:, half:]
    return jnp.concatenate((first * cosine - second * sine, first * sine + second * cosine), axis=1)


def ein(spec, left, right):
    return jnp.einsum(spec, left, right, preferred_element_type=F32)


def per_device(
    tokens,
    cotangent,
    gain_first,
    gain_second,
    w_query,
    w_key,
    w_value,
    w_gate,
    w_output,
    w_hidden,
    w_linear,
    w_down,
    decay_scale,
    first_length,
):
    rows = tokens.shape[0]
    core = lax.axis_index("core")
    place = lax.axis_index("ctx")
    plane = lax.axis_index("tp")
    scalars = jnp.stack((core, plane, lax.axis_index("x"), place)).astype(jnp.int32)

    w_output = w_output.T
    w_down = w_down.T
    mine, theirs = split_heads((w_key, w_value, w_gate, w_output, w_query), scalars, "split_attn")
    came = swap(theirs)
    block = stack_blocks((mine, came), 0, 768, scalars, "stack_first")
    w_kv = stack_blocks(spread_near(block), 0, 768, scalars, "stack_kv")
    gathered = stack_blocks((mine, came), 768, 1280, scalars, "stack_goq", deps=(block,))
    w_goq = lax.all_gather(gathered, XY, axis=0, tiled=True).reshape(4, 4, 2, 64, -1)
    mine, theirs = split_heads(
        (w_hidden, w_linear, w_down), scalars, "split_mlp", deps=(gathered,)
    )
    came_mlp = swap(theirs)
    gain_first = gain_first.reshape(1, D)
    gain_second = gain_second.reshape(1, D)
    tokens, cotangent, normed_first, cot_low = enter_rows(
        tokens, cotangent, gain_first, scalars, deps=(w_kv,)
    )
    x_first = (normed_first, swap(normed_first))
    g_out = (cot_low, swap(cot_low))
    w_kv = spread_far(w_kv)

    rate = lax.dynamic_index_in_dim(decay_scale, core, 0, False) / 1024.0
    local = (jnp.arange(rows, dtype=jnp.int32) + plane * (rows // 4)) % rows
    index = place * rows + local
    lengths = jnp.concatenate((first_length, swap(first_length)))
    document = (index[None, :] >= lengths[:, None]).astype(jnp.int32)
    carried = (document == 0).astype(F32)
    steps = local.astype(F32)
    offsets = local[:, None] - local[None, :]
    linked = (offsets >= 0)[None] & (document[:, :, None] == document[:, None, :])
    mask = jnp.where(
        linked, jnp.exp(-rate * jnp.maximum(offsets, 0).astype(F32))[None], 0.0
    )
    enter = (carried * jnp.exp(-rate * (steps + 1.0))[None])[:, :, None]
    leave = jnp.exp(-rate * (rows - 1.0 - steps))[None, :, None]
    fade = jnp.exp(-rate * rows)
    half = DK // 2
    frequency = 10000.0 ** (-(jnp.arange(half).astype(F32) / half))
    angles = index.astype(F32)[:, None] * frequency[None, :]
    cosine = jnp.tile(jnp.cos(angles), (2, 1))
    sine = jnp.tile(jnp.sin(angles), (2, 1))

    def carry(came):
        near, mid, far = [part.astype(F32) for part in came]
        return near + fade * (mid + fade * far)

    def spread_state(low, way):
        return [shift_open(low, "ctx", way * o) for o in (1, 2, 3)]

    projected = mm_in(*x_first, [(w_kv, 0, 768)], scalars, "project_kv")
    key = rotate(projected[:, :DK], cosine, sine).astype(BF).reshape(2, rows, DK)
    value = projected[:, DK:].astype(BF).reshape(2, rows, DV)
    key_out = (key.astype(F32) * leave).astype(BF)
    state_out = ein("gjd,gje->gde", key_out, value).astype(BF)
    came = spread_state(state_out, 1)
    w_mlp = lax.all_gather(
        stack_blocks((mine, came_mlp), 0, 1536, scalars, "stack_mlp", deps=came[:2]),
        XY,
        axis=0,
        tiled=True,
    ).reshape(4, 4, 2, 64, -1)
    projected = mm_in(
        *x_first, [(w_goq, 0, DV), (w_goq, 1024, DK)], scalars, "project_gq", deps=(state_out,)
    )
    state_in = carry(came).astype(BF)
    gate_pre = projected[:, :DV]
    query = rotate(projected[:, DV:], cosine, sine).astype(BF).reshape(2, rows, DK)
    weighted = (ein("gid,gjd->gij", query, key) * mask).astype(BF)
    inner = ein("gij,gje->gie", weighted, value)
    retained = (inner + ein("gid,gde->gie", query, state_in) * enter).reshape(2 * rows, DV)
    mixed_full, gate_back = jax.vjp(gate_norm, gate_pre, retained)
    mixed = mixed_full.astype(BF)
    own, other = mm_back([(mixed, w_goq, DV)], scalars, "project_out")
    parts, _ = heads_total(own, other)
    grad_activated = mm_in(
        *g_out, [(w_mlp, 2 * DV, DV)], scalars, "back_down", deps=(other,)
    )
    hidden_state, normed_second = second_norm(tokens, parts, gain_second, scalars, deps=(grad_activated,))
    x_second = (normed_second, swap(normed_second))
    paired = mm_in(*x_second, [(w_mlp, 0, 2 * DV)], scalars, "project_mlp")
    activated_full, gelu_back = jax.vjp(gelu_gate, paired[:, :DV], paired[:, DV:])
    activated = activated_full.astype(BF)
    grad_pair = jnp.concatenate(gelu_back(grad_activated), axis=1).astype(BF)
    own, other = mm_back([(grad_pair, w_mlp, 0)], scalars, "back_mlp")
    parts, totals = heads_total(own, other)
    down = mm_back([(activated, w_mlp, 2 * DV)], scalars, "project_down", deps=(totals[1],))
    down = (down[0], swap(down[1]))
    gain_second_part = gain_part(hidden_state, parts[0], "gain_second")
    grad_state, grad_state_low = norm_back(
        hidden_state,
        cotangent,
        parts,
        gain_second,
        scalars,
        "second_back",
        deps=(down[1], gain_second_part),
    )
    g_state = (grad_state_low, swap(grad_state_low))
    grad_mixed = mm_in(*g_state, [(w_goq, DV, DV)], scalars, "back_out")
    grad_gate, grad_retained = gate_back(grad_mixed)
    grad_low = grad_retained.reshape(2, rows, DV).astype(BF)
    query_in = (query.astype(F32) * enter).astype(BF)
    back_out = ein("gid,gie->gde", query_in, grad_low).astype(BF)
    came = spread_state(back_out, -1)
    grad_scores = (ein("gie,gje->gij", grad_low, value) * mask).astype(BF)
    grad_query = ein("gij,gjd->gid", grad_scores, key) + enter * ein("gie,gde->gid", grad_low, state_in)
    grad_key = ein("gij,gid->gjd", grad_scores, query)
    grad_value = ein("gij,gie->gje", weighted, grad_low)
    grad_gate = grad_gate.astype(BF)
    grad_query = rotate(grad_query.reshape(2 * rows, DK), cosine, -sine).astype(BF)
    d_rest, d_rest_mark = mm_weight(
        ((x_second, grad_pair), (g_out, activated), (g_state, mixed), (x_first, grad_gate)),
        scalars,
        "weight_rest",
        deps=(back_out,),
    )
    rest_block = lax.psum_scatter(
        d_rest.reshape(2048, -1), XY, scatter_dimension=0, tiled=True
    ).reshape(2, 64, -1)
    came[0] = tie((came[0],), (d_rest_mark, grad_key, grad_value, grad_query))[0]
    state_back = carry(came).astype(BF)
    grad_key += leave * ein("gje,gde->gjd", value, state_back)
    grad_value += ein("gjd,gde->gje", key_out, state_back)
    grad_kv = jnp.concatenate(
        (rotate(grad_key.reshape(2 * rows, DK), cosine, -sine), grad_value.reshape(2 * rows, DV)),
        axis=1,
    ).astype(BF)
    own, other = mm_back(
        [(grad_kv, w_kv, 0), (grad_gate, w_goq, 0), (grad_query, w_goq, 1024)],
        scalars,
        "back_attn",
    )
    d_qkv = mm_weight(
        ((x_first, grad_query), (x_first, grad_kv)), scalars, "weight_qkv", True, deps=(other,)
    )
    blocks, gain_first_part = first_gain(own, swap(other), tokens, *down, scalars, deps=(d_qkv[0],))
    parts = tp_total(blocks)
    qkv_sums, qkv_got = collect_far(d_qkv)
    qkv_block = collect_near(qkv_sums)
    gains = jnp.concatenate((gain_first_part, gain_second_part))
    (gains,) = tie((gains,), qkv_got[:1])
    for axis, swapped in (
        ("core", (1, 0)),
        ("tp", (1, 0, 3, 2)),
        ("tp", (3, 2, 1, 0)),
        ("ctx", (1, 0, 3, 2)),
        ("ctx", (3, 2, 1, 0)),
        ("x", (1, 0, 3, 2)),
        ("x", (3, 2, 1, 0)),
    ):
        gains = gains + lax.ppermute(gains, axis, list(enumerate(swapped)))
    spot = (lax.axis_index("x") * 2 + core) * 4 + place
    gains = lax.dynamic_slice_in_dim(gains, spot * 64, 64, 1)
    layer_out, input_grad = leave_rows(hidden_state, tokens, grad_state, parts, gain_first, scalars)
    d_hidden, d_linear, d_down, d_output, d_gate = join_heads(
        rest_block[0], swap(rest_block[1]), (DV,) * 5, scalars, "join_rest"
    )
    d_query, d_key, d_value = join_heads(
        qkv_block[0], swap(qkv_block[1]), (DK, DK, DV), scalars, "join_qkv"
    )
    return (
        layer_out,
        input_grad,
        gains[0],
        gains[1],
        d_query,
        d_key,
        d_value,
        d_gate,
        d_output.T,
        d_hidden,
        d_linear,
        d_down.T,
    )


def solution(mesh):
    fine = Mesh(np.asarray(mesh.devices).reshape(4, 2, 4, 4), ("x", "core", "ctx", "tp"))
    split = ("x", "core", "ctx")
    row = P(split, None)
    win = P(split, "tp")
    wout = P("tp", split)
    in_specs = (row, row, P(), P(), win, win, win, win, wout, win, win, wout, P("tp"), P(("x", "core")))
    out_specs = (row, row, P(split), P(split), win, win, win, win, wout, win, win, wout)
    return jax.shard_map(
        per_device, mesh=fine, in_specs=in_specs, out_specs=out_specs, check_vma=False
    )
```

```python
import math

import jax
import jax.numpy as jnp
import numpy as np
from jax import lax
from jax.experimental import pallas as pl
from jax.experimental.pallas import tpu as pltpu
from jax.sharding import Mesh, PartitionSpec as P

D = 2048
DK = 256
DV = 512
SLAB = 512
BF = jnp.bfloat16
F32 = jnp.float32
XY = ("x", "ctx")
MIB = 1 << 20


def shift(value, axis, offset):
    n = lax.axis_size(axis)
    return lax.ppermute(value, axis, [(i, (i + offset) % n) for i in range(n)])


def shift_open(value, axis, offset):
    n = lax.axis_size(axis)
    return lax.ppermute(
        value, axis, [(i, i + offset) for i in range(n) if 0 <= i + offset < n]
    )


def swap(value):
    return lax.ppermute(value, "core", [(0, 1), (1, 0)])


def after(value, *earlier):
    return lax.optimization_barrier((value, *earlier))[0]


def call(body, grid, ins, outs, shapes, scalars, operands, name, flops=0, scratch=(), deps=()):
    nbytes = sum(a.size * a.dtype.itemsize for a in jax.tree.leaves((operands, shapes)))
    count = len(operands)

    def kernel(s_ref, *refs):
        body(s_ref, *refs[:count], *refs[count + len(deps) :])

    ins = [*ins, *[pl.BlockSpec(memory_space=pl.ANY)] * len(deps)]
    return pl.pallas_call(
        kernel,
        out_shape=shapes,
        grid_spec=pltpu.PrefetchScalarGridSpec(
            num_scalar_prefetch=1, grid=grid, in_specs=ins, out_specs=outs, scratch_shapes=scratch
        ),
        compiler_params=pltpu.CompilerParams(
            vmem_limit_bytes=60 * MIB, dimension_semantics=("arbitrary",) * len(grid)
        ),
        cost_estimate=pl.CostEstimate(flops=flops, bytes_accessed=nbytes, transcendentals=0),
        name=name,
    )(scalars, *operands, *deps)


def tie(values, deps):
    count = len(values)
    anywhere = pl.BlockSpec(memory_space=pl.ANY)
    return pl.pallas_call(
        lambda *refs: None,
        out_shape=tuple(sds(v.shape, v.dtype) for v in values),
        in_specs=[anywhere] * (count + len(deps)),
        out_specs=(anywhere,) * count,
        input_output_aliases={i: i for i in range(count)},
        name="tie",
    )(*values, *deps)


def whole(array):
    return pl.BlockSpec(array.shape, lambda *_: (0,) * array.ndim)


def sds(shape, dtype):
    return jax.ShapeDtypeStruct(shape, dtype)


def weight_operands(weight, start, width):
    if not isinstance(weight, tuple):
        spec = pl.BlockSpec((1, 4, 2, 64, width), lambda i, s: (i, 0, 0, 0, start // width))
        return [weight], [spec]
    piece = math.gcd(start, width) if start else width
    operands, specs = [], []
    for at in range(start, start + width, piece):
        for stack in weight:
            operands.append(stack)
            specs.append(pl.BlockSpec((4, 2, 64, piece), lambda i, s, at=at: (0, 0, 0, at // piece)))
    return operands, specs


def load_slab(s_ref, refs, held):
    core = s_ref[0]
    if len(refs) == 1:
        return jnp.concatenate(
            [refs[0][0, y, jnp.bitwise_xor(c, core)] for c in (0, 1) for y in range(4)], axis=0
        )
    x_far = lax.rem(s_ref[2] + 4 - pl.program_id(0), 4)
    at = 0
    for first in range(0, len(refs), 4):
        stacks = refs[first : first + 4]
        width = stacks[0].shape[-1]
        for j in range(4):

            @pl.when((core == 0) & (x_far == j))
            def _(j=j, at=at, width=width, stacks=stacks):
                for i in range(4):
                    y = lax.rem(s_ref[3] + 4 - i, 4)
                    for c in (0, 1):
                        held[c * 4 + y, :, at : at + width] = stacks[j][i, c]

        @pl.when(core == 1)
        def _(at=at, width=width, stacks=stacks):
            for j in range(4):
                y = lax.rem(s_ref[3] + 4 - j, 4)
                for c in (0, 1):
                    held[c * 4 + y, :, at : at + width] = stacks[j][x_far, 1 - c]

        at += width
    return held[...].reshape(SLAB, at)


def hop(value, first, offset):
    pairs = []
    for x in range(4):
        for core in (0, 1):
            for y in range(4):
                to = ((x + offset) % 4, y) if (core == 0) == first else (x, (y + offset) % 4)
                pairs.append(((x * 2 + core) * 4 + y, (to[0] * 2 + core) * 4 + to[1]))
    return lax.ppermute(value, ("x", "core", "ctx"), pairs)


def spread_near(block):
    near, far, mid = [hop(block, False, o) for o in (1, 3, 2)]
    return block, near, mid, far


def stack_blocks(blocks, start, width, scalars, name, deps=()):
    at = start // width if start % width == 0 else None
    span = width if at is not None else blocks[0].shape[1]
    first = 0 if at is not None else start
    height = blocks[0].shape[0]

    def body(s_ref, *refs):
        for k, ref in enumerate(refs[:-1]):
            refs[-1][k * height : (k + 1) * height, :] = ref[:, first : first + width]

    total = sds((height * len(blocks), width), BF)
    return call(
        body,
        (1,),
        [pl.BlockSpec((height, span), lambda i, s: (0, at or 0))] * len(blocks),
        whole(total),
        total,
        scalars,
        tuple(blocks),
        name,
        deps=deps,
    )


def spread_far(stack, gate=False):
    stack = stack.reshape(4, 2, 64, -1)
    near, far = hop(stack, True, 1), hop(stack, True, -1)
    mid = hop(tie((stack,), (near, far))[0] if gate else stack, True, 2)
    return stack, near, mid, far


def collect_far(parts, near_after=(), mid_after=None):
    near, far = parts[1], parts[3]
    if near_after:
        near, far = tie((near, far), near_after)
    got = [hop(near, True, 1), hop(far, True, -1)]
    got.append(hop(tie((parts[2],), got if mid_after is None else mid_after)[0], True, 2))
    sums = []
    for j in range(4):
        total = parts[0][j].astype(F32)
        for part in got:
            total = total + part[j].astype(F32)
        sums.append(total.astype(BF))
    return sums, got


def collect_near(sums):
    got = [hop(sums[j], False, j) for j in (1, 3, 2)]
    total = sums[0].astype(F32)
    for part in got:
        total = total + part.astype(F32)
    return total.astype(BF)


def mm_in(left, right, columns, scalars, name, deps=()):
    operands, specs, counts = [], [], []
    for weight, start, width in columns:
        ops, sp = weight_operands(weight, start, width)
        operands += ops
        specs += sp
        counts.append(len(ops))
    total = sum(width for _, _, width in columns)

    def body(s_ref, a_ref, b_ref, *refs):
        out_ref = refs[len(operands)]
        step = pl.program_id(0)
        rows = jnp.concatenate((a_ref[...], b_ref[...]), axis=0)
        at, first = 0, 0
        for k, count in enumerate(counts):
            width = columns[k][2]
            slab = load_slab(s_ref, refs[first : first + count], refs[len(operands) + 1 + k])
            part = jnp.dot(rows, slab, preferred_element_type=F32)
            span = slice(at, at + width)

            @pl.when(step == 0)
            def _(part=part, span=span):
                out_ref[:, span] = part

            @pl.when(step > 0)
            def _(part=part, span=span):
                out_ref[:, span] += part

            at += width
            first += count

    rows = left.shape[0]
    cols = pl.BlockSpec((rows, SLAB), lambda i, s: (0, i))
    return call(
        body,
        (4,),
        [cols, cols, *specs],
        pl.BlockSpec((2 * rows, total), lambda i, s: (0, 0)),
        sds((2 * rows, total), F32),
        scalars,
        (left, right, *operands),
        name,
        flops=4 * rows * D * total,
        scratch=[pltpu.VMEM((8, 64, width), BF) for _, _, width in columns],
        deps=deps,
    )


def mm_back(terms, scalars, name, deps=()):
    rows = terms[0][0].shape[0]
    half = rows // 2
    operands, specs, counts, scratch = [], [], [], []
    for grad, weight, start in terms:
        ops, sp = weight_operands(weight, start, grad.shape[1])
        operands += [grad, *ops]
        specs += [whole(grad), *sp]
        counts.append(len(ops))
        scratch.append(pltpu.VMEM((8, 64, grad.shape[1]), BF))

    def body(s_ref, *refs):
        own_ref, other_ref = refs[len(operands) : len(operands) + 2]
        at, out = 0, 0.0
        for k, count in enumerate(counts):
            slab = load_slab(s_ref, refs[at + 1 : at + 1 + count], refs[len(operands) + 2 + k])
            out += lax.dot_general(
                refs[at][...], slab, (((1,), (1,)), ((), ())), preferred_element_type=F32
            )
            at += count + 1
        own_ref[...] = out[:half]
        other_ref[...] = out[half:].astype(BF)

    cols = pl.BlockSpec((half, SLAB), lambda i, s: (0, i))
    return call(
        body,
        (4,),
        specs,
        (cols, cols),
        (sds((half, D), F32), sds((half, D), BF)),
        scalars,
        tuple(operands),
        name,
        flops=sum(2 * rows * D * grad.shape[1] for grad, _, _ in terms),
        scratch=scratch,
        deps=deps,
    )


def mm_weight(pairs, scalars, name, apart=False, deps=()):
    widths = [grad.shape[1] for _, grad in pairs]
    rows = pairs[0][0][0].shape[0]
    count = 3 * len(pairs)
    total = sum(widths)

    def body(s_ref, *refs):
        core = s_ref[0]
        outs, held = refs[count:-1], refs[-1]
        at = 0
        for k, width in enumerate(widths):
            a_ref, b_ref, g_ref = refs[3 * k : 3 * k + 3]
            out = lax.dot_general(
                jnp.concatenate((a_ref[...], b_ref[...]), axis=0),
                g_ref[...],
                (((0,), (0,)), ((), ())),
                preferred_element_type=F32,
            ).astype(BF)
            held[:, :, at : at + width] = out.reshape(8, 64, width)
            at += width
        if not apart:
            for c in (0, 1):
                for y in range(4):
                    outs[0][0, y, jnp.bitwise_xor(c, core)] = held[c * 4 + y]
            outs[1][...] = jnp.zeros_like(outs[1])
            return
        x_far = lax.rem(pl.program_id(0) + 4 - s_ref[2], 4)
        for k in range(4):

            @pl.when((core == 0) & (x_far == k))
            def _(k=k):
                for j in range(4):
                    y = lax.rem(s_ref[3] + j, 4)
                    for rel in (0, 1):
                        outs[k][j, rel] = held[rel * 4 + y]

        @pl.when(core == 1)
        def _():
            for k in range(4):
                y = lax.rem(s_ref[3] + k, 4)
                for rel in (0, 1):
                    outs[k][x_far, rel] = held[(1 - rel) * 4 + y]

    cols = pl.BlockSpec((rows, SLAB), lambda i, s: (0, i))
    specs, operands = [], []
    for (a, b), grad in pairs:
        specs += [cols, cols, whole(grad)]
        operands += [a, b, grad]
    if apart:
        shapes = (sds((4, 2, 64, total), BF),) * 4
        out_specs = tuple(whole(s) for s in shapes)
    else:
        shapes = (sds((4, 4, 2, 64, total), BF), sds((8, 128), F32))
        out_specs = (
            pl.BlockSpec((1, 4, 2, 64, total), lambda i, s: (i, 0, 0, 0, 0)),
            pl.BlockSpec((8, 128), lambda i, s: (0, 0)),
        )
    return call(
        body,
        (4,),
        specs,
        out_specs,
        shapes,
        scalars,
        tuple(operands),
        name,
        flops=4 * rows * D * total,
        scratch=[pltpu.VMEM((8, 64, total), BF)],
        deps=deps,
    )


def split_heads(weights, scalars, name, deps=()):
    widths = [w.shape[1] // 2 for w in weights]

    def body(s_ref, *refs):
        mine_ref, theirs_ref = refs[-2:]
        core = s_ref[0]
        for out_ref, head in ((mine_ref, core), (theirs_ref, 1 - core)):
            at = 0
            for ref, width in zip(refs, widths):
                out_ref[:, at : at + width] = ref[:, pl.ds(pl.multiple_of(head * width, width), width)]
                at += width

    total = sum(widths)
    spec = pl.BlockSpec((64, total), lambda i, s: (0, 0))
    return call(
        body,
        (1,),
        [whole(w) for w in weights],
        (spec, spec),
        (sds((64, total), BF),) * 2,
        scalars,
        tuple(weights),
        name,
        deps=deps,
    )


def join_heads(mine, theirs, widths, scalars, name):
    def body(s_ref, mine_ref, theirs_ref, *outs):
        core = s_ref[0]
        for in_ref, head in ((mine_ref, core), (theirs_ref, 1 - core)):
            at = 0
            for ref, width in zip(outs, widths):
                span = pl.ds(pl.multiple_of(head * width, width), width)
                ref[:, span] = in_ref[:, at : at + width].astype(F32)
                at += width

    shapes = tuple(sds((64, 2 * w), F32) for w in widths)
    return call(
        body,
        (1,),
        [whole(mine), whole(theirs)],
        tuple(whole(s) for s in shapes),
        shapes,
        scalars,
        (mine, theirs),
        name,
    )


def scale_of(values):
    return lax.rsqrt(jnp.mean(values * values, axis=-1, keepdims=True) + 1e-06)


def turned_spec(rows):
    return pl.BlockSpec((rows, D), lambda i, s: (lax.rem(i + s[1], 4), 0))


def plain_spec(rows):
    return pl.BlockSpec((rows, D), lambda i, s: (i, 0))


def enter_rows(tokens, cotangent, gain, scalars, deps=()):
    rows = tokens.shape[0]
    block = rows // 4

    def body(s_ref, t_ref, c_ref, g_ref, t_out, c_out, n_out, l_out):
        values = t_ref[...]
        t_out[...] = values
        n_out[...] = (values * scale_of(values) * g_ref[...]).astype(BF)
        c_out[...] = c_ref[...]
        l_out[...] = c_ref[...].astype(BF)

    turn, plain = turned_spec(block), plain_spec(block)
    full = (rows, D)
    return call(
        body,
        (4,),
        [turn, turn, whole(gain)],
        (plain,) * 4,
        (sds(full, F32), sds(full, F32), sds(full, BF), sds(full, BF)),
        scalars,
        (tokens, cotangent, gain),
        "enter_rows",
        deps=deps,
    )


def each_part(refs, work):
    step = pl.program_id(0)
    for k, ref in enumerate(refs):

        @pl.when(step == k)
        def _(ref=ref):
            work(ref[...].astype(F32))


def second_norm(tokens, parts, gain, scalars, deps=()):
    rows = tokens.shape[0]
    block = rows // 4

    def body(s_ref, t_ref, g_ref, *refs):
        h_out, n_out = refs[4:]

        def work(part):
            values = t_ref[...] + part
            h_out[...] = values
            n_out[...] = (values * scale_of(values) * g_ref[...]).astype(BF)

        each_part(refs[:4], work)

    plain = plain_spec(block)
    return call(
        body,
        (4,),
        [plain, whole(gain)] + [whole(p) for p in parts],
        (plain, plain),
        (sds((rows, D), F32), sds((rows, D), BF)),
        scalars,
        (tokens, gain, *parts),
        "second_norm",
        deps=deps,
    )


def first_gain(own, came, tokens, down_own, down_came, scalars, deps=()):
    rows = own.shape[0]
    block = rows // 4

    def body(s_ref, own_ref, came_ref, t_ref, d_ref, e_ref, *refs):
        total = own_ref[...] + came_ref[...].astype(F32)
        down = d_ref[...] + e_ref[...].astype(F32)
        values = t_ref[...]
        part = jnp.sum(total * (values * scale_of(values)), axis=0, keepdims=True)
        step = pl.program_id(0)
        for k in range(4):

            @pl.when(step == k)
            def _(k=k):
                refs[k][:block] = total.astype(BF)
                refs[k][block:] = down.astype(BF)

        @pl.when(step == 0)
        def _():
            refs[4][...] = part

        @pl.when(step > 0)
        def _():
            refs[4][...] += part

    plain = plain_spec(block)
    shapes = (sds((2 * block, D), BF),) * 4 + (sds((1, D), F32),)
    out = call(
        body,
        (4,),
        [plain] * 5,
        tuple(whole(s) for s in shapes),
        shapes,
        scalars,
        (own, came, tokens, down_own, down_came),
        "first_gain",
        deps=deps,
    )
    return out[:4], out[4]


def leave_rows(hidden, tokens, grad_state, parts, gain, scalars):
    rows = hidden.shape[0]
    block = rows // 4

    def body(s_ref, h_ref, t_ref, u_ref, g_ref, *refs):
        def work(part):
            refs[4][...] = h_ref[...] + part[block:]
            refs[5][...] = u_ref[...] + norm_grad(t_ref[...], part[:block], g_ref[...])

        each_part(refs[:4], work)

    plain, turn = plain_spec(block), turned_spec(block)
    return call(
        body,
        (4,),
        [plain] * 3 + [whole(gain)] + [whole(p) for p in parts],
        (turn, turn),
        (sds((rows, D), F32),) * 2,
        scalars,
        (hidden, tokens, grad_state, gain, *parts),
        "leave_rows",
    )


def gain_part(values, grad, name):
    block = grad.shape[0]

    def body(v_ref, p_ref, out_ref):
        values = v_ref[...]
        out_ref[...] = jnp.sum(
            p_ref[...].astype(F32) * (values * scale_of(values)), axis=0, keepdims=True
        )

    return pl.pallas_call(
        body,
        out_shape=sds((1, D), F32),
        grid=(1,),
        in_specs=[pl.BlockSpec((block, D), lambda i: (0, 0))] * 2,
        out_specs=pl.BlockSpec((1, D), lambda i: (0, 0)),
        name=name,
    )(values, grad)


def norm_grad(values, grad, gain):
    factor = scale_of(values)
    unit = values * factor
    scaled = grad * gain
    return factor * (scaled - unit * jnp.mean(scaled * unit, axis=-1, keepdims=True))


def norm_back(values, upstream, parts, gain, scalars, name, deps=()):
    rows = values.shape[0]
    block = rows // 4

    def body(s_ref, v_ref, u_ref, g_ref, *refs):
        def work(part):
            out = u_ref[...] + norm_grad(v_ref[...], part, g_ref[...])
            refs[4][...] = out
            refs[5][...] = out.astype(BF)

        each_part(refs[:4], work)

    plain = plain_spec(block)
    return call(
        body,
        (4,),
        [plain, plain, whole(gain)] + [whole(p) for p in parts],
        (plain, plain),
        (sds((rows, D), F32), sds((rows, D), BF)),
        scalars,
        (values, upstream, gain, *parts),
        name,
        deps=deps,
    )


def tp_total(blocks):
    got = [shift(blocks[o], "tp", o) for o in (1, 3, 2)]
    mine = blocks[0].astype(F32)
    for part in got:
        mine = mine + part.astype(F32)
    mine = mine.astype(BF)
    near, far, mid = [shift(mine, "tp", -o) for o in (1, 3, 2)]
    return (mine, near, mid, far)


def heads_total(own, other):
    came = swap(other)
    block = own.shape[0] // 4
    blocks = [
        (own[o * block : (o + 1) * block] + came[o * block : (o + 1) * block].astype(F32)).astype(BF)
        for o in range(4)
    ]
    return tp_total(blocks), blocks


def gate_norm(gate_pre, retained):
    centred = retained - jnp.mean(retained, axis=-1, keepdims=True)
    normed = centred * lax.rsqrt(jnp.mean(centred * centred, axis=-1, keepdims=True) + 1.0 * DK)
    return gate_pre * jax.nn.sigmoid(gate_pre) * normed


def gelu_gate(hidden, linear):
    return jax.nn.gelu(hidden, approximate=True) * linear


def rotate(values, cosine, sine):
    half = DK // 2
    first = values[:, :half]
    second = values[:, half:]
    return jnp.concatenate((first * cosine - second * sine, first * sine + second * cosine), axis=1)


def ein(spec, left, right):
    return jnp.einsum(spec, left, right, preferred_element_type=F32)


def per_device(
    tokens,
    cotangent,
    gain_first,
    gain_second,
    w_query,
    w_key,
    w_value,
    w_gate,
    w_output,
    w_hidden,
    w_linear,
    w_down,
    decay_scale,
    first_length,
):
    rows = tokens.shape[0]
    core = lax.axis_index("core")
    place = lax.axis_index("ctx")
    plane = lax.axis_index("tp")
    scalars = jnp.stack((core, plane, lax.axis_index("x"), place)).astype(jnp.int32)

    w_output = w_output.T
    w_down = w_down.T
    mine, theirs = split_heads((w_key, w_value, w_gate, w_output, w_query), scalars, "split_attn")
    came = swap(theirs)
    block = stack_blocks((mine, came), 0, 768, scalars, "stack_first")
    w_kv = stack_blocks(spread_near(block), 0, 768, scalars, "stack_kv")
    gathered = stack_blocks((mine, came), 768, 1280, scalars, "stack_goq", deps=(block,))
    w_goq = lax.all_gather(gathered, XY, axis=0, tiled=True).reshape(4, 4, 2, 64, -1)
    mine, theirs = split_heads(
        (w_hidden, w_linear, w_down), scalars, "split_mlp", deps=(gathered,)
    )
    came_mlp = swap(theirs)
    gain_first = gain_first.reshape(1, D)
    gain_second = gain_second.reshape(1, D)
    w_kv = spread_far(w_kv)
    tokens, cotangent, normed_first, cot_low = enter_rows(
        tokens, cotangent, gain_first, scalars, deps=(w_kv[1],)
    )
    x_first = (normed_first, swap(normed_first))
    g_out = (cot_low, swap(cot_low))

    rate = lax.dynamic_index_in_dim(decay_scale, core, 0, False) / 1024.0
    local = (jnp.arange(rows, dtype=jnp.int32) + plane * (rows // 4)) % rows
    index = place * rows + local
    lengths = jnp.concatenate((first_length, swap(first_length)))
    document = (index[None, :] >= lengths[:, None]).astype(jnp.int32)
    carried = (document == 0).astype(F32)
    steps = local.astype(F32)
    offsets = local[:, None] - local[None, :]
    linked = (offsets >= 0)[None] & (document[:, :, None] == document[:, None, :])
    mask = jnp.where(
        linked, jnp.exp(-rate * jnp.maximum(offsets, 0).astype(F32))[None], 0.0
    )
    enter = (carried * jnp.exp(-rate * (steps + 1.0))[None])[:, :, None]
    leave = jnp.exp(-rate * (rows - 1.0 - steps))[None, :, None]
    fade = jnp.exp(-rate * rows)
    half = DK // 2
    frequency = 10000.0 ** (-(jnp.arange(half).astype(F32) / half))
    angles = index.astype(F32)[:, None] * frequency[None, :]
    cosine = jnp.tile(jnp.cos(angles), (2, 1))
    sine = jnp.tile(jnp.sin(angles), (2, 1))

    def carry(came):
        near, mid, far = [part.astype(F32) for part in came]
        return near + fade * (mid + fade * far)

    def spread_state(low, way):
        return [shift_open(low, "ctx", way * o) for o in (1, 2, 3)]

    projected = mm_in(*x_first, [(w_kv, 0, 768)], scalars, "project_kv")
    key = rotate(projected[:, :DK], cosine, sine).astype(BF).reshape(2, rows, DK)
    value = projected[:, DK:].astype(BF).reshape(2, rows, DV)
    key_out = (key.astype(F32) * leave).astype(BF)
    state_out = ein("gjd,gje->gde", key_out, value).astype(BF)
    came = spread_state(state_out, 1)
    w_mlp = lax.all_gather(
        stack_blocks((mine, came_mlp), 0, 1536, scalars, "stack_mlp", deps=came),
        XY,
        axis=0,
        tiled=True,
    ).reshape(4, 4, 2, 64, -1)
    projected = mm_in(
        *x_first, [(w_goq, 0, DV), (w_goq, 1024, DK)], scalars, "project_gq", deps=(state_out,)
    )
    state_in = carry(came).astype(BF)
    gate_pre = projected[:, :DV]
    query = rotate(projected[:, DV:], cosine, sine).astype(BF).reshape(2, rows, DK)
    weighted = (ein("gid,gjd->gij", query, key) * mask).astype(BF)
    inner = ein("gij,gje->gie", weighted, value)
    retained = (inner + ein("gid,gde->gie", query, state_in) * enter).reshape(2 * rows, DV)
    mixed_full, gate_back = jax.vjp(gate_norm, gate_pre, retained)
    mixed = mixed_full.astype(BF)
    own, other = mm_back([(mixed, w_goq, DV)], scalars, "project_out")
    parts, _ = heads_total(own, other)
    grad_activated = mm_in(
        *g_out, [(w_mlp, 2 * DV, DV)], scalars, "back_down", deps=(other,)
    )
    hidden_state, normed_second = second_norm(tokens, parts, gain_second, scalars, deps=(grad_activated,))
    x_second = (normed_second, swap(normed_second))
    paired = mm_in(*x_second, [(w_mlp, 0, 2 * DV)], scalars, "project_mlp")
    activated_full, gelu_back = jax.vjp(gelu_gate, paired[:, :DV], paired[:, DV:])
    activated = activated_full.astype(BF)
    grad_pair = jnp.concatenate(gelu_back(grad_activated), axis=1).astype(BF)
    own, other = mm_back([(grad_pair, w_mlp, 0)], scalars, "back_mlp")
    parts, totals = heads_total(own, other)
    down = mm_back([(activated, w_mlp, 2 * DV)], scalars, "project_down", deps=(parts[0],))
    down = (down[0], swap(down[1]))
    d_mlp, d_mlp_mark = mm_weight(
        ((x_second, grad_pair), (g_out, activated)), scalars, "weight_mlp", deps=(totals[1],)
    )
    mlp_block = lax.psum_scatter(
        d_mlp.reshape(2048, -1), XY, scatter_dimension=0, tiled=True
    ).reshape(2, 64, -1)
    gain_second_part = gain_part(hidden_state, parts[0], "gain_second")
    grad_state, grad_state_low = norm_back(
        hidden_state,
        cotangent,
        parts,
        gain_second,
        scalars,
        "second_back",
        deps=(down[1], gain_second_part, d_mlp_mark),
    )
    g_state = (grad_state_low, swap(grad_state_low))
    grad_mixed = mm_in(*g_state, [(w_goq, DV, DV)], scalars, "back_out")
    grad_gate, grad_retained = gate_back(grad_mixed)
    grad_low = grad_retained.reshape(2, rows, DV).astype(BF)
    query_in = (query.astype(F32) * enter).astype(BF)
    back_out = ein("gid,gie->gde", query_in, grad_low).astype(BF)
    came = spread_state(back_out, -1)
    grad_scores = (ein("gie,gje->gij", grad_low, value) * mask).astype(BF)
    grad_query = ein("gij,gjd->gid", grad_scores, key) + enter * ein("gie,gde->gid", grad_low, state_in)
    grad_key = ein("gij,gid->gjd", grad_scores, query)
    grad_value = ein("gij,gie->gje", weighted, grad_low)
    grad_gate = grad_gate.astype(BF)
    grad_query = rotate(grad_query.reshape(2 * rows, DK), cosine, -sine).astype(BF)
    d_goq = mm_weight(
        ((x_first, grad_gate), (g_state, mixed), (x_first, grad_query)),
        scalars,
        "weight_goq",
        True,
        deps=(back_out,),
    )
    came[0] = tie((came[0],), (d_goq[0], grad_key, grad_value))[0]
    state_back = carry(came).astype(BF)
    grad_key += leave * ein("gje,gde->gjd", value, state_back)
    grad_value += ein("gjd,gde->gje", key_out, state_back)
    grad_kv = jnp.concatenate(
        (rotate(grad_key.reshape(2 * rows, DK), cosine, -sine), grad_value.reshape(2 * rows, DV)),
        axis=1,
    ).astype(BF)
    own, other = mm_back(
        [(grad_kv, w_kv, 0), (grad_gate, w_goq, 0), (grad_query, w_goq, 1024)],
        scalars,
        "back_attn",
    )
    d_kv = mm_weight(((x_first, grad_kv),), scalars, "weight_kv", True, deps=(other,))
    blocks, gain_first_part = first_gain(own, swap(other), tokens, *down, scalars, deps=(d_kv[0],))
    goq_sums, goq_got = collect_far(d_goq, (state_back,), blocks[1:2])
    parts = tp_total(blocks)
    kv_sums, kv_got = collect_far(d_kv, (*goq_got[:2], blocks[1]), parts[:1])
    goq_block = collect_near(goq_sums)
    kv_block = collect_near(kv_sums)
    gains = jnp.concatenate((gain_first_part, gain_second_part))
    for axis, swapped in (
        ("core", (1, 0)),
        ("tp", (1, 0, 3, 2)),
        ("tp", (3, 2, 1, 0)),
        ("ctx", (1, 0, 3, 2)),
        ("ctx", (3, 2, 1, 0)),
        ("x", (1, 0, 3, 2)),
        ("x", (3, 2, 1, 0)),
    ):
        if axis == "ctx" and swapped[0] == 1:
            (gains,) = tie((gains,), parts[1:])
        gains = gains + lax.ppermute(gains, axis, list(enumerate(swapped)))
    spot = (lax.axis_index("x") * 2 + core) * 4 + place
    gains = lax.dynamic_slice_in_dim(gains, spot * 64, 64, 1)
    layer_out, input_grad = leave_rows(hidden_state, tokens, grad_state, parts, gain_first, scalars)
    d_hidden, d_linear, d_down = join_heads(
        mlp_block[0], swap(mlp_block[1]), (DV, DV, DV), scalars, "join_mlp"
    )
    d_gate, d_output, d_query = join_heads(
        goq_block[0], swap(goq_block[1]), (DV, DV, DK), scalars, "join_goq"
    )
    d_key, d_value = join_heads(kv_block[0], swap(kv_block[1]), (DK, DV), scalars, "join_kv")
    return (
        layer_out,
        input_grad,
        gains[0],
        gains[1],
        d_query,
        d_key,
        d_value,
        d_gate,
        d_output.T,
        d_hidden,
        d_linear,
        d_down.T,
    )


def solution(mesh):
    fine = Mesh(np.asarray(mesh.devices).reshape(4, 2, 4, 4), ("x", "core", "ctx", "tp"))
    split = ("x", "core", "ctx")
    row = P(split, None)
    win = P(split, "tp")
    wout = P("tp", split)
    in_specs = (row, row, P(), P(), win, win, win, win, wout, win, win, wout, P("tp"), P(("x", "core")))
    out_specs = (row, row, P(split), P(split), win, win, win, win, wout, win, win, wout)
    return jax.shard_map(
        per_device, mesh=fine, in_specs=in_specs, out_specs=out_specs, check_vma=False
    )
```

```python
import math

import jax
import jax.numpy as jnp
import numpy as np
from jax import lax
from jax.experimental import pallas as pl
from jax.experimental.pallas import tpu as pltpu
from jax.sharding import Mesh, PartitionSpec as P

D = 2048
DK = 256
DV = 512
SLAB = 512
BF = jnp.bfloat16
F32 = jnp.float32
XY = ("x", "ctx")
MIB = 1 << 20


def shift(value, axis, offset):
    n = lax.axis_size(axis)
    return lax.ppermute(value, axis, [(i, (i + offset) % n) for i in range(n)])


def shift_open(value, axis, offset):
    n = lax.axis_size(axis)
    return lax.ppermute(
        value, axis, [(i, i + offset) for i in range(n) if 0 <= i + offset < n]
    )


def swap(value):
    return lax.ppermute(value, "core", [(0, 1), (1, 0)])


def after(value, *earlier):
    return lax.optimization_barrier((value, *earlier))[0]


def call(body, grid, ins, outs, shapes, scalars, operands, name, scratch=(), deps=()):
    count = len(operands)

    def kernel(s_ref, *refs):
        body(s_ref, *refs[:count], *refs[count + len(deps) :])

    ins = [*ins, *[pl.BlockSpec(memory_space=pl.ANY)] * len(deps)]
    return pl.pallas_call(
        kernel,
        out_shape=shapes,
        grid_spec=pltpu.PrefetchScalarGridSpec(
            num_scalar_prefetch=1, grid=grid, in_specs=ins, out_specs=outs, scratch_shapes=scratch
        ),
        compiler_params=pltpu.CompilerParams(
            vmem_limit_bytes=32 * MIB, dimension_semantics=("arbitrary",) * len(grid)
        ),
        cost_estimate=pl.CostEstimate(flops=1, bytes_accessed=1, transcendentals=0),
        name=name,
    )(scalars, *operands, *deps)


def tie(values, deps):
    count = len(values)
    anywhere = pl.BlockSpec(memory_space=pl.ANY)
    return pl.pallas_call(
        lambda *refs: None,
        out_shape=tuple(sds(v.shape, v.dtype) for v in values),
        in_specs=[anywhere] * (count + len(deps)),
        out_specs=(anywhere,) * count,
        input_output_aliases={i: i for i in range(count)},
        name="tie",
    )(*values, *deps)


def whole(array):
    return pl.BlockSpec(array.shape, lambda *_: (0,) * array.ndim)


def sds(shape, dtype):
    return jax.ShapeDtypeStruct(shape, dtype)


def weight_operands(weight, start, width):
    if not isinstance(weight, tuple):
        spec = pl.BlockSpec((1, 4, 2, 64, width), lambda i, s: (i, 0, 0, 0, start // width))
        return [weight], [spec]
    piece = math.gcd(start, width) if start else width
    operands, specs = [], []
    for at in range(start, start + width, piece):
        for stack in weight:
            operands.append(stack)
            specs.append(pl.BlockSpec((4, 2, 64, piece), lambda i, s, at=at: (0, 0, 0, at // piece)))
    return operands, specs


def load_slab(s_ref, refs, held):
    core = s_ref[0]
    if len(refs) == 1:
        return jnp.concatenate(
            [refs[0][0, y, jnp.bitwise_xor(c, core)] for c in (0, 1) for y in range(4)], axis=0
        )
    x_far = lax.rem(s_ref[2] + 4 - pl.program_id(0), 4)
    at = 0
    for first in range(0, len(refs), 4):
        stacks = refs[first : first + 4]
        width = stacks[0].shape[-1]
        for j in range(4):

            @pl.when((core == 0) & (x_far == j))
            def _(j=j, at=at, width=width, stacks=stacks):
                for i in range(4):
                    y = lax.rem(s_ref[3] + 4 - i, 4)
                    for c in (0, 1):
                        held[c * 4 + y, :, at : at + width] = stacks[j][i, c]

        @pl.when(core == 1)
        def _(at=at, width=width, stacks=stacks):
            for j in range(4):
                y = lax.rem(s_ref[3] + 4 - j, 4)
                for c in (0, 1):
                    held[c * 4 + y, :, at : at + width] = stacks[j][x_far, 1 - c]

        at += width
    return held[...].reshape(SLAB, at)


def hop(value, first, offset):
    pairs = []
    for x in range(4):
        for core in (0, 1):
            for y in range(4):
                to = ((x + offset) % 4, y) if (core == 0) == first else (x, (y + offset) % 4)
                pairs.append(((x * 2 + core) * 4 + y, (to[0] * 2 + core) * 4 + to[1]))
    return lax.ppermute(value, ("x", "core", "ctx"), pairs)


def spread_near(block):
    near, far, mid = [hop(block, False, o) for o in (1, 3, 2)]
    return block, near, mid, far


def stack_blocks(blocks, start, width, scalars, name, deps=()):
    at = start // width if start % width == 0 else None
    span = width if at is not None else blocks[0].shape[1]
    first = 0 if at is not None else start
    height = blocks[0].shape[0]

    def body(s_ref, *refs):
        for k, ref in enumerate(refs[:-1]):
            refs[-1][k * height : (k + 1) * height, :] = ref[:, first : first + width]

    total = sds((height * len(blocks), width), BF)
    return call(
        body,
        (1,),
        [pl.BlockSpec((height, span), lambda i, s: (0, at or 0))] * len(blocks),
        whole(total),
        total,
        scalars,
        tuple(blocks),
        name,
        deps=deps,
    )


def stack_attn(mine, came, scalars):
    height, total = mine.shape

    def body(s_ref, mine_ref, came_ref, first_ref, other_ref):
        for k, ref in enumerate((mine_ref, came_ref)):
            span = slice(k * height, (k + 1) * height)
            first_ref[span, :] = ref[:, :768]
            other_ref[span, :] = ref[:, 768:]

    shapes = (sds((2 * height, 768), BF), sds((2 * height, total - 768), BF))
    return call(
        body,
        (1,),
        [whole(mine), whole(came)],
        tuple(whole(s) for s in shapes),
        shapes,
        scalars,
        (mine, came),
        "stack_attn",
    )


def spread_far(stack, gate=False):
    stack = stack.reshape(4, 2, 64, -1)
    near, far = hop(stack, True, 1), hop(stack, True, -1)
    mid = hop(tie((stack,), (near, far))[0] if gate else stack, True, 2)
    return stack, near, mid, far


def collect_far(parts, near_after=(), mid_after=None):
    near, far = parts[1], parts[3]
    if near_after:
        near, far = tie((near, far), near_after)
    got = [hop(near, True, 1), hop(far, True, -1)]
    got.append(hop(tie((parts[2],), got if mid_after is None else mid_after)[0], True, 2))
    sums = []
    for j in range(4):
        total = parts[0][j].astype(F32)
        for part in got:
            total = total + part[j].astype(F32)
        sums.append(total.astype(BF))
    return sums, got


def collect_near(sums):
    got = [hop(sums[j], False, j) for j in (1, 3, 2)]
    total = sums[0].astype(F32)
    for part in got:
        total = total + part.astype(F32)
    return total.astype(BF)


def mm_in(left, right, columns, scalars, name, deps=()):
    operands, specs, counts = [], [], []
    for weight, start, width in columns:
        ops, sp = weight_operands(weight, start, width)
        operands += ops
        specs += sp
        counts.append(len(ops))
    total = sum(width for _, _, width in columns)

    def body(s_ref, a_ref, b_ref, *refs):
        out_ref = refs[len(operands)]
        step = pl.program_id(0)
        rows = jnp.concatenate((a_ref[...], b_ref[...]), axis=0)
        at, first = 0, 0
        for k, count in enumerate(counts):
            width = columns[k][2]
            slab = load_slab(s_ref, refs[first : first + count], refs[len(operands) + 1 + k])
            part = jnp.dot(rows, slab, preferred_element_type=F32)
            span = slice(at, at + width)

            @pl.when(step == 0)
            def _(part=part, span=span):
                out_ref[:, span] = part

            @pl.when(step > 0)
            def _(part=part, span=span):
                out_ref[:, span] += part

            at += width
            first += count

    rows = left.shape[0]
    cols = pl.BlockSpec((rows, SLAB), lambda i, s: (0, i))
    return call(
        body,
        (4,),
        [cols, cols, *specs],
        pl.BlockSpec((2 * rows, total), lambda i, s: (0, 0)),
        sds((2 * rows, total), F32),
        scalars,
        (left, right, *operands),
        name,
        scratch=[pltpu.VMEM((8, 64, width), BF) for _, _, width in columns],
        deps=deps,
    )


def mm_back(terms, scalars, name, deps=()):
    rows = terms[0][0].shape[0]
    half = rows // 2
    operands, specs, counts, scratch = [], [], [], []
    for grad, weight, start in terms:
        ops, sp = weight_operands(weight, start, grad.shape[1])
        operands += [grad, *ops]
        specs += [whole(grad), *sp]
        counts.append(len(ops))
        scratch.append(pltpu.VMEM((8, 64, grad.shape[1]), BF))

    def body(s_ref, *refs):
        own_ref, other_ref = refs[len(operands) : len(operands) + 2]
        at, out = 0, 0.0
        for k, count in enumerate(counts):
            slab = load_slab(s_ref, refs[at + 1 : at + 1 + count], refs[len(operands) + 2 + k])
            out += lax.dot_general(
                refs[at][...], slab, (((1,), (1,)), ((), ())), preferred_element_type=F32
            )
            at += count + 1
        own_ref[...] = out[:half]
        other_ref[...] = out[half:].astype(BF)

    cols = pl.BlockSpec((half, SLAB), lambda i, s: (0, i))
    return call(
        body,
        (4,),
        specs,
        (cols, cols),
        (sds((half, D), F32), sds((half, D), BF)),
        scalars,
        tuple(operands),
        name,
        scratch=scratch,
        deps=deps,
    )


def mm_weight(pairs, scalars, name, apart=False, deps=()):
    widths = [grad.shape[1] for _, grad in pairs]
    rows = pairs[0][0][0].shape[0]
    count = 3 * len(pairs)
    total = sum(widths)

    def body(s_ref, *refs):
        core = s_ref[0]
        outs, held = refs[count:-1], refs[-1]
        at = 0
        for k, width in enumerate(widths):
            a_ref, b_ref, g_ref = refs[3 * k : 3 * k + 3]
            out = lax.dot_general(
                jnp.concatenate((a_ref[...], b_ref[...]), axis=0),
                g_ref[...],
                (((0,), (0,)), ((), ())),
                preferred_element_type=F32,
            ).astype(BF)
            held[:, :, at : at + width] = out.reshape(8, 64, width)
            at += width
        if not apart:
            for c in (0, 1):
                for y in range(4):
                    outs[0][0, y, jnp.bitwise_xor(c, core)] = held[c * 4 + y]
            outs[1][...] = jnp.zeros_like(outs[1])
            return
        x_far = lax.rem(pl.program_id(0) + 4 - s_ref[2], 4)
        for k in range(4):

            @pl.when((core == 0) & (x_far == k))
            def _(k=k):
                for j in range(4):
                    y = lax.rem(s_ref[3] + j, 4)
                    for rel in (0, 1):
                        outs[k][j, rel] = held[rel * 4 + y]

        @pl.when(core == 1)
        def _():
            for k in range(4):
                y = lax.rem(s_ref[3] + k, 4)
                for rel in (0, 1):
                    outs[k][x_far, rel] = held[(1 - rel) * 4 + y]

    cols = pl.BlockSpec((rows, SLAB), lambda i, s: (0, i))
    specs, operands = [], []
    for (a, b), grad in pairs:
        specs += [cols, cols, whole(grad)]
        operands += [a, b, grad]
    if apart:
        shapes = (sds((4, 2, 64, total), BF),) * 4
        out_specs = tuple(whole(s) for s in shapes)
    else:
        shapes = (sds((4, 4, 2, 64, total), BF), sds((8, 128), F32))
        out_specs = (
            pl.BlockSpec((1, 4, 2, 64, total), lambda i, s: (i, 0, 0, 0, 0)),
            pl.BlockSpec((8, 128), lambda i, s: (0, 0)),
        )
    return call(
        body,
        (4,),
        specs,
        out_specs,
        shapes,
        scalars,
        tuple(operands),
        name,
        scratch=[pltpu.VMEM((8, 64, total), BF)],
        deps=deps,
    )


def split_heads(weights, scalars, name, deps=()):
    widths = [w.shape[1] // 2 for w in weights]

    def body(s_ref, *refs):
        mine_ref, theirs_ref = refs[-2:]
        core = s_ref[0]
        for out_ref, head in ((mine_ref, core), (theirs_ref, 1 - core)):
            at = 0
            for ref, width in zip(refs, widths):
                out_ref[:, at : at + width] = ref[:, pl.ds(pl.multiple_of(head * width, width), width)]
                at += width

    total = sum(widths)
    spec = pl.BlockSpec((64, total), lambda i, s: (0, 0))
    return call(
        body,
        (1,),
        [whole(w) for w in weights],
        (spec, spec),
        (sds((64, total), BF),) * 2,
        scalars,
        tuple(weights),
        name,
        deps=deps,
    )


def join_heads(mine, theirs, widths, scalars, name):
    def body(s_ref, mine_ref, theirs_ref, *outs):
        core = s_ref[0]
        for in_ref, head in ((mine_ref, core), (theirs_ref, 1 - core)):
            at = 0
            for ref, width in zip(outs, widths):
                span = pl.ds(pl.multiple_of(head * width, width), width)
                ref[:, span] = in_ref[:, at : at + width].astype(F32)
                at += width

    shapes = tuple(sds((64, 2 * w), F32) for w in widths)
    return call(
        body,
        (1,),
        [whole(mine), whole(theirs)],
        tuple(whole(s) for s in shapes),
        shapes,
        scalars,
        (mine, theirs),
        name,
    )


def scale_of(values):
    return lax.rsqrt(jnp.mean(values * values, axis=-1, keepdims=True) + 1e-06)


def turned_spec(rows):
    return pl.BlockSpec((rows, D), lambda i, s: (lax.rem(i + s[1], 4), 0))


def plain_spec(rows):
    return pl.BlockSpec((rows, D), lambda i, s: (i, 0))


def enter_rows(tokens, gain, scalars, deps=()):
    rows = tokens.shape[0]
    block = rows // 4

    def body(s_ref, t_ref, g_ref, n_out):
        values = t_ref[...]
        n_out[...] = (values * scale_of(values) * g_ref[...]).astype(BF)

    return call(
        body,
        (4,),
        [turned_spec(block), whole(gain)],
        plain_spec(block),
        sds((rows, D), BF),
        scalars,
        (tokens, gain),
        "enter_rows",
        deps=deps,
    )


def low_rows(cotangent, scalars, deps=()):
    rows = cotangent.shape[0]
    block = rows // 4

    def body(s_ref, c_ref, l_out):
        l_out[...] = c_ref[...].astype(BF)

    return call(
        body,
        (4,),
        [turned_spec(block)],
        plain_spec(block),
        sds((rows, D), BF),
        scalars,
        (cotangent,),
        "low_rows",
        deps=deps,
    )


def each_part(refs, work):
    step = pl.program_id(0)
    for k, ref in enumerate(refs):

        @pl.when(step == k)
        def _(ref=ref):
            work(ref[...].astype(F32))


def second_norm(tokens, parts, gain, scalars, deps=()):
    rows = tokens.shape[0]
    block = rows // 4

    def body(s_ref, t_ref, g_ref, *refs):
        h_out, n_out = refs[4:]

        def work(part):
            values = t_ref[...] + part
            h_out[...] = values
            n_out[...] = (values * scale_of(values) * g_ref[...]).astype(BF)

        each_part(refs[:4], work)

    plain = plain_spec(block)
    return call(
        body,
        (4,),
        [turned_spec(block), whole(gain)] + [whole(p) for p in parts],
        (plain, plain),
        (sds((rows, D), F32), sds((rows, D), BF)),
        scalars,
        (tokens, gain, *parts),
        "second_norm",
        deps=deps,
    )


def first_gain(own, came, tokens, down_own, down_came, scalars, deps=()):
    rows = own.shape[0]
    block = rows // 4

    def body(s_ref, own_ref, came_ref, t_ref, d_ref, e_ref, *refs):
        total = own_ref[...] + came_ref[...].astype(F32)
        down = d_ref[...] + e_ref[...].astype(F32)
        values = t_ref[...]
        part = jnp.sum(total * (values * scale_of(values)), axis=0, keepdims=True)
        step = pl.program_id(0)
        for k in range(4):

            @pl.when(step == k)
            def _(k=k):
                refs[k][:block] = total.astype(BF)
                refs[k][block:] = down.astype(BF)

        @pl.when(step == 0)
        def _():
            refs[4][...] = part

        @pl.when(step > 0)
        def _():
            refs[4][...] += part

    plain = plain_spec(block)
    shapes = (sds((2 * block, D), BF),) * 4 + (sds((1, D), F32),)
    out = call(
        body,
        (4,),
        [plain, plain, turned_spec(block), plain, plain],
        tuple(whole(s) for s in shapes),
        shapes,
        scalars,
        (own, came, tokens, down_own, down_came),
        "first_gain",
        deps=deps,
    )
    return out[:4], out[4]


def leave_rows(hidden, tokens, grad_state, parts, gain, scalars):
    rows = hidden.shape[0]
    block = rows // 4

    def body(s_ref, h_ref, t_ref, u_ref, g_ref, *refs):
        def work(part):
            refs[4][...] = h_ref[...] + part[block:]
            refs[5][...] = u_ref[...] + norm_grad(t_ref[...], part[:block], g_ref[...])

        each_part(refs[:4], work)

    plain, turn = plain_spec(block), turned_spec(block)
    return call(
        body,
        (4,),
        [plain, turn, plain, whole(gain)] + [whole(p) for p in parts],
        (turn, turn),
        (sds((rows, D), F32),) * 2,
        scalars,
        (hidden, tokens, grad_state, gain, *parts),
        "leave_rows",
    )


def gain_part(values, grad, name):
    block = grad.shape[0]

    def body(v_ref, p_ref, out_ref):
        values = v_ref[...]
        out_ref[...] = jnp.sum(
            p_ref[...].astype(F32) * (values * scale_of(values)), axis=0, keepdims=True
        )

    return pl.pallas_call(
        body,
        out_shape=sds((1, D), F32),
        grid=(1,),
        in_specs=[pl.BlockSpec((block, D), lambda i: (0, 0))] * 2,
        out_specs=pl.BlockSpec((1, D), lambda i: (0, 0)),
        name=name,
    )(values, grad)


def norm_grad(values, grad, gain):
    factor = scale_of(values)
    unit = values * factor
    scaled = grad * gain
    return factor * (scaled - unit * jnp.mean(scaled * unit, axis=-1, keepdims=True))


def norm_back(values, upstream, parts, gain, scalars, name, deps=()):
    rows = values.shape[0]
    block = rows // 4

    def body(s_ref, v_ref, u_ref, g_ref, *refs):
        def work(part):
            out = u_ref[...] + norm_grad(v_ref[...], part, g_ref[...])
            refs[4][...] = out
            refs[5][...] = out.astype(BF)

        each_part(refs[:4], work)

    plain = plain_spec(block)
    return call(
        body,
        (4,),
        [plain, turned_spec(block), whole(gain)] + [whole(p) for p in parts],
        (plain, plain),
        (sds((rows, D), F32), sds((rows, D), BF)),
        scalars,
        (values, upstream, gain, *parts),
        name,
        deps=deps,
    )


def tp_total(blocks, deps=()):
    got = [shift(blocks[o], "tp", o) for o in (1, 3, 2)]
    mine = blocks[0].astype(F32)
    for part in got:
        mine = mine + part.astype(F32)
    mine = mine.astype(BF)
    if deps:
        (mine,) = tie((mine,), deps)
    near, far, mid = [shift(mine, "tp", -o) for o in (1, 3, 2)]
    return (mine, near, mid, far)


def heads_total(own, other):
    came = swap(other)
    block = own.shape[0] // 4
    blocks = [
        (own[o * block : (o + 1) * block] + came[o * block : (o + 1) * block].astype(F32)).astype(BF)
        for o in range(4)
    ]
    return tp_total(blocks), blocks


def gate_norm(gate_pre, retained):
    centred = retained - jnp.mean(retained, axis=-1, keepdims=True)
    normed = centred * lax.rsqrt(jnp.mean(centred * centred, axis=-1, keepdims=True) + 1.0 * DK)
    return gate_pre * jax.nn.sigmoid(gate_pre) * normed


def gelu_gate(hidden, linear):
    return jax.nn.gelu(hidden, approximate=True) * linear


def rotate(values, cosine, sine):
    half = DK // 2
    first = values[:, :half]
    second = values[:, half:]
    return jnp.concatenate((first * cosine - second * sine, first * sine + second * cosine), axis=1)


def ein(spec, left, right):
    return jnp.einsum(spec, left, right, preferred_element_type=F32)


def per_device(
    tokens,
    cotangent,
    gain_first,
    gain_second,
    w_query,
    w_key,
    w_value,
    w_gate,
    w_output,
    w_hidden,
    w_linear,
    w_down,
    decay_scale,
    first_length,
):
    rows = tokens.shape[0]
    core = lax.axis_index("core")
    place = lax.axis_index("ctx")
    plane = lax.axis_index("tp")
    scalars = jnp.stack((core, plane, lax.axis_index("x"), place)).astype(jnp.int32)

    w_output = w_output.T
    w_down = w_down.T
    mine, theirs = split_heads((w_key, w_value, w_gate, w_output, w_query), scalars, "split_attn")
    came = swap(theirs)
    block, gathered = stack_attn(mine, came, scalars)
    lengths = jnp.concatenate((first_length, swap(first_length)))
    normed_first = enter_rows(tokens, gain_first.reshape(1, D), scalars, deps=(block,))
    w_kv = stack_blocks(
        spread_near(block), 0, 768, scalars, "stack_kv", deps=(normed_first, lengths)
    )
    w_goq = lax.all_gather(gathered, XY, axis=0, tiled=True).reshape(4, 4, 2, 64, -1)
    mine, theirs = split_heads(
        (w_hidden, w_linear, w_down), scalars, "split_mlp", deps=(gathered,)
    )
    came_mlp = swap(theirs)
    gain_first = gain_first.reshape(1, D)
    gain_second = gain_second.reshape(1, D)
    x_first = (normed_first, swap(normed_first))
    cot_low = low_rows(cotangent, scalars, deps=(x_first[1],))
    g_out = (cot_low, swap(cot_low))
    w_kv = spread_far(w_kv)

    rate = lax.dynamic_index_in_dim(decay_scale, core, 0, False) / 1024.0
    local = (jnp.arange(rows, dtype=jnp.int32) + plane * (rows // 4)) % rows
    index = place * rows + local
    document = (index[None, :] >= lengths[:, None]).astype(jnp.int32)
    carried = (document == 0).astype(F32)
    steps = local.astype(F32)
    offsets = local[:, None] - local[None, :]
    linked = (offsets >= 0)[None] & (document[:, :, None] == document[:, None, :])
    mask = jnp.where(
        linked, jnp.exp(-rate * jnp.maximum(offsets, 0).astype(F32))[None], 0.0
    )
    enter = (carried * jnp.exp(-rate * (steps + 1.0))[None])[:, :, None]
    leave = jnp.exp(-rate * (rows - 1.0 - steps))[None, :, None]
    fade = jnp.exp(-rate * rows)
    half = DK // 2
    frequency = 10000.0 ** (-(jnp.arange(half).astype(F32) / half))
    angles = index.astype(F32)[:, None] * frequency[None, :]
    cosine = jnp.tile(jnp.cos(angles), (2, 1))
    sine = jnp.tile(jnp.sin(angles), (2, 1))

    def carry(came):
        near, mid, far = [part.astype(F32) for part in came]
        return near + fade * (mid + fade * far)

    def spread_state(low, way):
        return [shift_open(low, "ctx", way * o) for o in (1, 2, 3)]

    projected = mm_in(*x_first, [(w_kv, 0, 768)], scalars, "project_kv")
    key = rotate(projected[:, :DK], cosine, sine).astype(BF).reshape(2, rows, DK)
    value = projected[:, DK:].astype(BF).reshape(2, rows, DV)
    key_out = (key.astype(F32) * leave).astype(BF)
    state_out = ein("gjd,gje->gde", key_out, value).astype(BF)
    came = spread_state(state_out, 1)
    w_mlp = lax.all_gather(
        stack_blocks((mine, came_mlp), 0, 1536, scalars, "stack_mlp", deps=came),
        XY,
        axis=0,
        tiled=True,
    ).reshape(4, 4, 2, 64, -1)
    projected = mm_in(
        *x_first, [(w_goq, 0, DV), (w_goq, 1024, DK)], scalars, "project_gq", deps=(state_out, mask, enter)
    )
    state_in = carry(came).astype(BF)
    gate_pre = projected[:, :DV]
    query = rotate(projected[:, DV:], cosine, sine).astype(BF).reshape(2, rows, DK)
    weighted = (ein("gid,gjd->gij", query, key) * mask).astype(BF)
    inner = ein("gij,gje->gie", weighted, value)
    retained = (inner + ein("gid,gde->gie", query, state_in) * enter).reshape(2 * rows, DV)
    mixed_full, gate_back = jax.vjp(gate_norm, gate_pre, retained)
    mixed = mixed_full.astype(BF)
    own, other = mm_back([(mixed, w_goq, DV)], scalars, "project_out")
    parts, _ = heads_total(own, other)
    grad_activated = mm_in(
        *g_out, [(w_mlp, 2 * DV, DV)], scalars, "back_down", deps=(other,)
    )
    hidden_state, normed_second = second_norm(tokens, parts, gain_second, scalars, deps=(grad_activated,))
    x_second = (normed_second, swap(normed_second))
    paired = mm_in(*x_second, [(w_mlp, 0, 2 * DV)], scalars, "project_mlp")
    activated_full, gelu_back = jax.vjp(gelu_gate, paired[:, :DV], paired[:, DV:])
    activated = activated_full.astype(BF)
    grad_pair = jnp.concatenate(gelu_back(grad_activated), axis=1).astype(BF)
    own, other = mm_back([(grad_pair, w_mlp, 0)], scalars, "back_mlp")
    parts, totals = heads_total(own, other)
    down = mm_back([(activated, w_mlp, 2 * DV)], scalars, "project_down", deps=(parts[0],))
    d_mlp, d_mlp_mark = mm_weight(
        ((x_second, grad_pair), (g_out, activated)), scalars, "weight_mlp", deps=(totals[1],)
    )
    mlp_block = lax.psum_scatter(
        d_mlp.reshape(2048, -1), XY, scatter_dimension=0, tiled=True
    ).reshape(2, 64, -1)
    gain_second_part = gain_part(hidden_state, parts[0], "gain_second")
    grad_state, grad_state_low = norm_back(
        hidden_state,
        cotangent,
        parts,
        gain_second,
        scalars,
        "second_back",
        deps=(down[1], gain_second_part, d_mlp_mark),
    )
    g_state = (grad_state_low, swap(grad_state_low))
    grad_mixed = mm_in(*g_state, [(w_goq, DV, DV)], scalars, "back_out")
    grad_gate, grad_retained = gate_back(grad_mixed)
    grad_low = grad_retained.reshape(2, rows, DV).astype(BF)
    query_in = (query.astype(F32) * enter).astype(BF)
    back_out = ein("gid,gie->gde", query_in, grad_low).astype(BF)
    came = spread_state(back_out, -1)
    grad_scores = (ein("gie,gje->gij", grad_low, value) * mask).astype(BF)
    grad_query = ein("gij,gjd->gid", grad_scores, key) + enter * ein("gie,gde->gid", grad_low, state_in)
    grad_key = ein("gij,gid->gjd", grad_scores, query)
    grad_value = ein("gij,gie->gje", weighted, grad_low)
    grad_gate = grad_gate.astype(BF)
    grad_query = rotate(grad_query.reshape(2 * rows, DK), cosine, -sine).astype(BF)
    d_goq = mm_weight(
        ((x_first, grad_gate), (g_state, mixed), (x_first, grad_query)),
        scalars,
        "weight_goq",
        True,
        deps=(back_out,),
    )
    came[0] = tie((came[0],), (d_goq[0], grad_key, grad_value))[0]
    state_back = carry(came).astype(BF)
    grad_key += leave * ein("gje,gde->gjd", value, state_back)
    grad_value += ein("gjd,gde->gje", key_out, state_back)
    grad_kv = jnp.concatenate(
        (rotate(grad_key.reshape(2 * rows, DK), cosine, -sine), grad_value.reshape(2 * rows, DV)),
        axis=1,
    ).astype(BF)
    own, other = mm_back(
        [(grad_kv, w_kv, 0), (grad_gate, w_goq, 0), (grad_query, w_goq, 1024)],
        scalars,
        "back_attn",
    )
    d_kv = mm_weight(((x_first, grad_kv),), scalars, "weight_kv", True, deps=(other,))
    goq_sums, goq_got = collect_far(d_goq, (state_back,))
    down = (down[0], swap(tie((down[1],), (state_back,))[0]))
    blocks, gain_first_part = first_gain(
        own, swap(other), tokens, *down, scalars, deps=(d_kv[0], *goq_got[:2])
    )
    parts = tp_total(blocks, goq_got[2:])
    kv_sums, kv_got = collect_far(d_kv, (*goq_got[:2], blocks[1]), parts[:1])
    goq_block = collect_near(goq_sums)
    kv_block = collect_near(kv_sums)
    gains = jnp.concatenate((gain_first_part, gain_second_part))
    for axis, swapped in (
        ("core", (1, 0)),
        ("tp", (1, 0, 3, 2)),
        ("tp", (3, 2, 1, 0)),
        ("ctx", (1, 0, 3, 2)),
        ("ctx", (3, 2, 1, 0)),
        ("x", (1, 0, 3, 2)),
        ("x", (3, 2, 1, 0)),
    ):
        if axis == "ctx" and swapped[0] == 1:
            (gains,) = tie((gains,), (*parts[1:], *kv_got[:2]))
        gains = gains + lax.ppermute(gains, axis, list(enumerate(swapped)))
    spot = (lax.axis_index("x") * 2 + core) * 4 + place
    gains = lax.dynamic_slice_in_dim(gains, spot * 64, 64, 1)
    layer_out, input_grad = leave_rows(hidden_state, tokens, grad_state, parts, gain_first, scalars)
    d_hidden, d_linear, d_down = join_heads(
        mlp_block[0], swap(mlp_block[1]), (DV, DV, DV), scalars, "join_mlp"
    )
    d_gate, d_output, d_query = join_heads(
        goq_block[0], swap(goq_block[1]), (DV, DV, DK), scalars, "join_goq"
    )
    d_key, d_value = join_heads(kv_block[0], swap(kv_block[1]), (DK, DV), scalars, "join_kv")
    return (
        layer_out,
        input_grad,
        gains[0],
        gains[1],
        d_query,
        d_key,
        d_value,
        d_gate,
        d_output.T,
        d_hidden,
        d_linear,
        d_down.T,
    )


def solution(mesh):
    fine = Mesh(np.asarray(mesh.devices).reshape(4, 2, 4, 4), ("x", "core", "ctx", "tp"))
    split = ("x", "core", "ctx")
    row = P(split, None)
    win = P(split, "tp")
    wout = P("tp", split)
    in_specs = (row, row, P(), P(), win, win, win, win, wout, win, win, wout, P("tp"), P(("x", "core")))
    out_specs = (row, row, P(split), P(split), win, win, win, win, wout, win, win, wout)
    return jax.shard_map(
        per_device, mesh=fine, in_specs=in_specs, out_specs=out_specs, check_vma=False
    )
```

```python
import math

import jax
import jax.numpy as jnp
import numpy as np
from jax import lax
from jax.experimental import pallas as pl
from jax.experimental.pallas import tpu as pltpu
from jax.sharding import Mesh, PartitionSpec as P

D = 2048
DK = 256
DV = 512
SLAB = 512
BF = jnp.bfloat16
F32 = jnp.float32
XY = ("x", "ctx")
MIB = 1 << 20


def shift(value, axis, offset):
    n = lax.axis_size(axis)
    return lax.ppermute(value, axis, [(i, (i + offset) % n) for i in range(n)])


def shift_open(value, axis, offset):
    n = lax.axis_size(axis)
    return lax.ppermute(
        value, axis, [(i, i + offset) for i in range(n) if 0 <= i + offset < n]
    )


def swap(value):
    return lax.ppermute(value, "core", [(0, 1), (1, 0)])


def after(value, *earlier):
    return lax.optimization_barrier((value, *earlier))[0]


def call(
    body, grid, ins, outs, shapes, scalars, operands, name, scratch=(), deps=(), stream=False
):
    count = len(operands)

    def kernel(s_ref, *refs):
        body(s_ref, *refs[:count], *refs[count + len(deps) :])

    ins = [*ins, *[pl.BlockSpec(memory_space=pl.ANY)] * len(deps)]
    return pl.pallas_call(
        kernel,
        out_shape=shapes,
        grid_spec=pltpu.PrefetchScalarGridSpec(
            num_scalar_prefetch=1, grid=grid, in_specs=ins, out_specs=outs, scratch_shapes=scratch
        ),
        compiler_params=pltpu.CompilerParams(
            vmem_limit_bytes=(60 if stream else 32) * MIB, dimension_semantics=("arbitrary",) * len(grid)
        ),
        cost_estimate=pl.CostEstimate(flops=1, bytes_accessed=1, transcendentals=0),
        name=name,
    )(scalars, *operands, *deps)


def tie(values, deps):
    count = len(values)
    anywhere = pl.BlockSpec(memory_space=pl.ANY)
    return pl.pallas_call(
        lambda *refs: None,
        out_shape=tuple(sds(v.shape, v.dtype) for v in values),
        in_specs=[anywhere] * (count + len(deps)),
        out_specs=(anywhere,) * count,
        input_output_aliases={i: i for i in range(count)},
        name="tie",
    )(*values, *deps)


def whole(array):
    return pl.BlockSpec(array.shape, lambda *_: (0,) * array.ndim)


def sds(shape, dtype):
    return jax.ShapeDtypeStruct(shape, dtype)


def weight_operands(weight, start, width):
    if not isinstance(weight, tuple):
        spec = pl.BlockSpec((1, 4, 2, 64, width), lambda i, s: (i, 0, 0, 0, start // width))
        return [weight], [spec]
    piece = math.gcd(start, width) if start else width
    operands, specs = [], []
    for at in range(start, start + width, piece):
        for stack in weight:
            operands.append(stack)
            specs.append(pl.BlockSpec((4, 2, 64, piece), lambda i, s, at=at: (0, 0, 0, at // piece)))
    return operands, specs


def load_slab(s_ref, refs, held):
    core = s_ref[0]
    if len(refs) == 1:
        return jnp.concatenate(
            [refs[0][0, y, jnp.bitwise_xor(c, core)] for c in (0, 1) for y in range(4)], axis=0
        )
    x_far = lax.rem(s_ref[2] + 4 - pl.program_id(0), 4)
    at = 0
    for first in range(0, len(refs), 4):
        stacks = refs[first : first + 4]
        width = stacks[0].shape[-1]
        for j in range(4):

            @pl.when((core == 0) & (x_far == j))
            def _(j=j, at=at, width=width, stacks=stacks):
                for i in range(4):
                    y = lax.rem(s_ref[3] + 4 - i, 4)
                    for c in (0, 1):
                        held[c * 4 + y, :, at : at + width] = stacks[j][i, c]

        @pl.when(core == 1)
        def _(at=at, width=width, stacks=stacks):
            for j in range(4):
                y = lax.rem(s_ref[3] + 4 - j, 4)
                for c in (0, 1):
                    held[c * 4 + y, :, at : at + width] = stacks[j][x_far, 1 - c]

        at += width
    return held[...].reshape(SLAB, at)


def hop(value, first, offset):
    pairs = []
    for x in range(4):
        for core in (0, 1):
            for y in range(4):
                to = ((x + offset) % 4, y) if (core == 0) == first else (x, (y + offset) % 4)
                pairs.append(((x * 2 + core) * 4 + y, (to[0] * 2 + core) * 4 + to[1]))
    return lax.ppermute(value, ("x", "core", "ctx"), pairs)


def spread_near(block):
    near, far, mid = [hop(block, False, o) for o in (1, 3, 2)]
    return block, near, mid, far


def stack_blocks(blocks, start, width, scalars, name, deps=()):
    at = start // width if start % width == 0 else None
    span = width if at is not None else blocks[0].shape[1]
    first = 0 if at is not None else start
    height = blocks[0].shape[0]

    def body(s_ref, *refs):
        for k, ref in enumerate(refs[:-1]):
            refs[-1][k * height : (k + 1) * height, :] = ref[:, first : first + width]

    total = sds((height * len(blocks), width), BF)
    return call(
        body,
        (1,),
        [pl.BlockSpec((height, span), lambda i, s: (0, at or 0))] * len(blocks),
        whole(total),
        total,
        scalars,
        tuple(blocks),
        name,
        deps=deps,
    )


def stack_attn(mine, came, scalars):
    height, total = mine.shape

    def body(s_ref, mine_ref, came_ref, first_ref, other_ref):
        for k, ref in enumerate((mine_ref, came_ref)):
            span = slice(k * height, (k + 1) * height)
            first_ref[span, :] = ref[:, :768]
            other_ref[span, :] = ref[:, 768:]

    shapes = (sds((2 * height, 768), BF), sds((2 * height, total - 768), BF))
    return call(
        body,
        (1,),
        [whole(mine), whole(came)],
        tuple(whole(s) for s in shapes),
        shapes,
        scalars,
        (mine, came),
        "stack_attn",
    )


def spread_far(stack, gate=False):
    stack = stack.reshape(4, 2, 64, -1)
    near, far = hop(stack, True, 1), hop(stack, True, -1)
    mid = hop(tie((stack,), (near, far))[0] if gate else stack, True, 2)
    return stack, near, mid, far


def collect_far(parts, near_after=(), mid_after=None):
    near, far = parts[1], parts[3]
    if near_after:
        near, far = tie((near, far), near_after)
    got = [hop(near, True, 1), hop(far, True, -1)]
    got.append(hop(tie((parts[2],), got if mid_after is None else mid_after)[0], True, 2))
    sums = []
    for j in range(4):
        total = parts[0][j].astype(F32)
        for part in got:
            total = total + part[j].astype(F32)
        sums.append(total.astype(BF))
    return sums, got


def collect_near(sums):
    got = [hop(sums[j], False, j) for j in (1, 3, 2)]
    total = sums[0].astype(F32)
    for part in got:
        total = total + part.astype(F32)
    return total.astype(BF)


def mm_in(left, right, columns, scalars, name, deps=()):
    operands, specs, counts = [], [], []
    for weight, start, width in columns:
        ops, sp = weight_operands(weight, start, width)
        operands += ops
        specs += sp
        counts.append(len(ops))
    total = sum(width for _, _, width in columns)

    def body(s_ref, a_ref, b_ref, *refs):
        out_ref = refs[len(operands)]
        step = pl.program_id(0)
        rows = jnp.concatenate((a_ref[...], b_ref[...]), axis=0)
        at, first = 0, 0
        for k, count in enumerate(counts):
            width = columns[k][2]
            slab = load_slab(s_ref, refs[first : first + count], refs[len(operands) + 1 + k])
            part = jnp.dot(rows, slab, preferred_element_type=F32)
            span = slice(at, at + width)

            @pl.when(step == 0)
            def _(part=part, span=span):
                out_ref[:, span] = part

            @pl.when(step > 0)
            def _(part=part, span=span):
                out_ref[:, span] += part

            at += width
            first += count

    rows = left.shape[0]
    cols = pl.BlockSpec((rows, SLAB), lambda i, s: (0, i))
    return call(
        body,
        (4,),
        [cols, cols, *specs],
        pl.BlockSpec((2 * rows, total), lambda i, s: (0, 0)),
        sds((2 * rows, total), F32),
        scalars,
        (left, right, *operands),
        name,
        scratch=[pltpu.VMEM((8, 64, width), BF) for _, _, width in columns],
        deps=deps,
    )


def mm_back(terms, scalars, name, deps=()):
    rows = terms[0][0].shape[0]
    half = rows // 2
    operands, specs, counts, scratch = [], [], [], []
    for grad, weight, start in terms:
        ops, sp = weight_operands(weight, start, grad.shape[1])
        operands += [grad, *ops]
        specs += [whole(grad), *sp]
        counts.append(len(ops))
        scratch.append(pltpu.VMEM((8, 64, grad.shape[1]), BF))

    def body(s_ref, *refs):
        own_ref, other_ref = refs[len(operands) : len(operands) + 2]
        at, out = 0, 0.0
        for k, count in enumerate(counts):
            slab = load_slab(s_ref, refs[at + 1 : at + 1 + count], refs[len(operands) + 2 + k])
            out += lax.dot_general(
                refs[at][...], slab, (((1,), (1,)), ((), ())), preferred_element_type=F32
            )
            at += count + 1
        own_ref[...] = out[:half]
        other_ref[...] = out[half:].astype(BF)

    cols = pl.BlockSpec((half, SLAB), lambda i, s: (0, i))
    return call(
        body,
        (4,),
        specs,
        (cols, cols),
        (sds((half, D), F32), sds((half, D), BF)),
        scalars,
        tuple(operands),
        name,
        scratch=scratch,
        deps=deps,
    )


def mm_weight(pairs, scalars, name, apart=False, deps=()):
    widths = [grad.shape[1] for _, grad in pairs]
    rows = pairs[0][0][0].shape[0]
    count = 3 * len(pairs)
    total = sum(widths)

    def body(s_ref, *refs):
        core = s_ref[0]
        outs, held = refs[count:-1], refs[-1]
        at = 0
        for k, width in enumerate(widths):
            a_ref, b_ref, g_ref = refs[3 * k : 3 * k + 3]
            out = lax.dot_general(
                jnp.concatenate((a_ref[...], b_ref[...]), axis=0),
                g_ref[...],
                (((0,), (0,)), ((), ())),
                preferred_element_type=F32,
            ).astype(BF)
            held[:, :, at : at + width] = out.reshape(8, 64, width)
            at += width
        if not apart:
            for c in (0, 1):
                for y in range(4):
                    outs[0][0, y, jnp.bitwise_xor(c, core)] = held[c * 4 + y]
            outs[1][...] = jnp.zeros_like(outs[1])
            return
        x_far = lax.rem(pl.program_id(0) + 4 - s_ref[2], 4)
        for k in range(4):

            @pl.when((core == 0) & (x_far == k))
            def _(k=k):
                for j in range(4):
                    y = lax.rem(s_ref[3] + j, 4)
                    for rel in (0, 1):
                        outs[k][j, rel] = held[rel * 4 + y]

        @pl.when(core == 1)
        def _():
            for k in range(4):
                y = lax.rem(s_ref[3] + k, 4)
                for rel in (0, 1):
                    outs[k][x_far, rel] = held[(1 - rel) * 4 + y]

    cols = pl.BlockSpec((rows, SLAB), lambda i, s: (0, i))
    specs, operands = [], []
    for (a, b), grad in pairs:
        specs += [cols, cols, whole(grad)]
        operands += [a, b, grad]
    if apart:
        shapes = (sds((4, 2, 64, total), BF),) * 4
        out_specs = tuple(whole(s) for s in shapes)
    else:
        shapes = (sds((4, 4, 2, 64, total), BF), sds((8, 128), F32))
        out_specs = (
            pl.BlockSpec((1, 4, 2, 64, total), lambda i, s: (i, 0, 0, 0, 0)),
            pl.BlockSpec((8, 128), lambda i, s: (0, 0)),
        )
    return call(
        body,
        (4,),
        specs,
        out_specs,
        shapes,
        scalars,
        tuple(operands),
        name,
        scratch=[pltpu.VMEM((8, 64, total), BF)],
        deps=deps,
    )


def split_heads(weights, scalars, name, deps=()):
    widths = [w.shape[1] // 2 for w in weights]

    def body(s_ref, *refs):
        mine_ref, theirs_ref = refs[-2:]
        core = s_ref[0]
        for out_ref, head in ((mine_ref, core), (theirs_ref, 1 - core)):
            at = 0
            for ref, width in zip(refs, widths):
                out_ref[:, at : at + width] = ref[:, pl.ds(pl.multiple_of(head * width, width), width)]
                at += width

    total = sum(widths)
    spec = pl.BlockSpec((64, total), lambda i, s: (0, 0))
    return call(
        body,
        (1,),
        [whole(w) for w in weights],
        (spec, spec),
        (sds((64, total), BF),) * 2,
        scalars,
        tuple(weights),
        name,
        deps=deps,
    )


def join_heads(mine, theirs, widths, scalars, name):
    def body(s_ref, mine_ref, theirs_ref, *outs):
        core = s_ref[0]
        for in_ref, head in ((mine_ref, core), (theirs_ref, 1 - core)):
            at = 0
            for ref, width in zip(outs, widths):
                span = pl.ds(pl.multiple_of(head * width, width), width)
                ref[:, span] = in_ref[:, at : at + width].astype(F32)
                at += width

    shapes = tuple(sds((64, 2 * w), F32) for w in widths)
    return call(
        body,
        (1,),
        [whole(mine), whole(theirs)],
        tuple(whole(s) for s in shapes),
        shapes,
        scalars,
        (mine, theirs),
        name,
    )


def scale_of(values):
    return lax.rsqrt(jnp.mean(values * values, axis=-1, keepdims=True) + 1e-06)


def turned_spec(rows):
    return pl.BlockSpec((rows, D), lambda i, s: (lax.rem(i + s[1], 4), 0))


def plain_spec(rows):
    return pl.BlockSpec((rows, D), lambda i, s: (i, 0))


def enter_rows(tokens, gain, scalars, deps=()):
    rows = tokens.shape[0]
    block = rows // 4

    def body(s_ref, t_ref, g_ref, n_out):
        values = t_ref[...]
        n_out[...] = (values * scale_of(values) * g_ref[...]).astype(BF)

    return call(
        body,
        (4,),
        [turned_spec(block), whole(gain)],
        plain_spec(block),
        sds((rows, D), BF),
        scalars,
        (tokens, gain),
        "enter_rows",
        deps=deps,
    )


def low_rows(cotangent, scalars, deps=()):
    rows = cotangent.shape[0]
    block = rows // 4

    def body(s_ref, c_ref, l_out):
        l_out[...] = c_ref[...].astype(BF)

    return call(
        body,
        (4,),
        [turned_spec(block)],
        plain_spec(block),
        sds((rows, D), BF),
        scalars,
        (cotangent,),
        "low_rows",
        deps=deps,
    )


def each_part(refs, work):
    step = pl.program_id(0)
    for k, ref in enumerate(refs):

        @pl.when(step == k)
        def _(ref=ref):
            work(ref[...].astype(F32))


def second_norm(tokens, parts, gain, scalars, deps=()):
    rows = tokens.shape[0]
    block = rows // 4

    def body(s_ref, t_ref, g_ref, *refs):
        h_out, n_out = refs[4:]

        def work(part):
            values = t_ref[...] + part
            h_out[...] = values
            n_out[...] = (values * scale_of(values) * g_ref[...]).astype(BF)

        each_part(refs[:4], work)

    plain = plain_spec(block)
    return call(
        body,
        (4,),
        [turned_spec(block), whole(gain)] + [whole(p) for p in parts],
        (plain, plain),
        (sds((rows, D), F32), sds((rows, D), BF)),
        scalars,
        (tokens, gain, *parts),
        "second_norm",
        deps=deps,
        stream=True,
    )


def first_gain(own, came, tokens, scalars, deps=()):
    rows = own.shape[0]
    block = rows // 4

    def body(s_ref, own_ref, came_ref, t_ref, *refs):
        total = own_ref[...] + came_ref[...].astype(F32)
        values = t_ref[...]
        part = jnp.sum(total * (values * scale_of(values)), axis=0, keepdims=True)
        step = pl.program_id(0)
        for k in range(4):

            @pl.when(step == k)
            def _(k=k):
                refs[k][...] = total.astype(BF)

        @pl.when(step == 0)
        def _():
            refs[4][...] = part

        @pl.when(step > 0)
        def _():
            refs[4][...] += part

    plain = plain_spec(block)
    shapes = (sds((block, D), BF),) * 4 + (sds((1, D), F32),)
    out = call(
        body,
        (4,),
        [plain, plain, turned_spec(block)],
        tuple(whole(s) for s in shapes),
        shapes,
        scalars,
        (own, came, tokens),
        "first_gain",
        deps=deps,
        stream=True,
    )
    return out[:4], out[4]


def leave_layer(hidden, parts, scalars):
    rows = hidden.shape[0]
    block = rows // 4

    def body(s_ref, h_ref, *refs):
        def work(part):
            refs[4][...] = h_ref[...] + part

        each_part(refs[:4], work)

    return call(
        body,
        (4,),
        [plain_spec(block)] + [whole(p) for p in parts],
        turned_spec(block),
        sds((rows, D), F32),
        scalars,
        (hidden, *parts),
        "leave_layer",
        stream=True,
    )


def leave_grad(tokens, grad_state, parts, gain, scalars):
    rows = tokens.shape[0]
    block = rows // 4

    def body(s_ref, t_ref, u_ref, g_ref, *refs):
        def work(part):
            refs[4][...] = u_ref[...] + norm_grad(t_ref[...], part, g_ref[...])

        each_part(refs[:4], work)

    turn = turned_spec(block)
    return call(
        body,
        (4,),
        [turn, plain_spec(block), whole(gain)] + [whole(p) for p in parts],
        turn,
        sds((rows, D), F32),
        scalars,
        (tokens, grad_state, gain, *parts),
        "leave_grad",
        stream=True,
    )


def gain_part(values, grad, name):
    block = grad.shape[0]

    def body(v_ref, p_ref, out_ref):
        values = v_ref[...]
        out_ref[...] = jnp.sum(
            p_ref[...].astype(F32) * (values * scale_of(values)), axis=0, keepdims=True
        )

    return pl.pallas_call(
        body,
        out_shape=sds((1, D), F32),
        grid=(1,),
        in_specs=[pl.BlockSpec((block, D), lambda i: (0, 0))] * 2,
        out_specs=pl.BlockSpec((1, D), lambda i: (0, 0)),
        name=name,
    )(values, grad)


def norm_grad(values, grad, gain):
    factor = scale_of(values)
    unit = values * factor
    scaled = grad * gain
    return factor * (scaled - unit * jnp.mean(scaled * unit, axis=-1, keepdims=True))


def norm_back(values, upstream, parts, gain, scalars, name, deps=()):
    rows = values.shape[0]
    block = rows // 4

    def body(s_ref, v_ref, u_ref, g_ref, *refs):
        def work(part):
            out = u_ref[...] + norm_grad(v_ref[...], part, g_ref[...])
            refs[4][...] = out
            refs[5][...] = out.astype(BF)

        each_part(refs[:4], work)

    plain = plain_spec(block)
    return call(
        body,
        (4,),
        [plain, turned_spec(block), whole(gain)] + [whole(p) for p in parts],
        (plain, plain),
        (sds((rows, D), F32), sds((rows, D), BF)),
        scalars,
        (values, upstream, gain, *parts),
        name,
        deps=deps,
        stream=True,
    )


def tp_first(blocks):
    got = [shift(blocks[o], "tp", o) for o in (1, 3, 2)]
    mine = blocks[0].astype(F32)
    for part in got:
        mine = mine + part.astype(F32)
    return mine.astype(BF), got


def tp_second(mine):
    near, far, mid = [shift(mine, "tp", -o) for o in (1, 3, 2)]
    return mine, near, mid, far


def chip_blocks(own, came):
    block = own.shape[0] // 4
    return [
        (own[o * block : (o + 1) * block] + came[o * block : (o + 1) * block].astype(F32)).astype(BF)
        for o in range(4)
    ]


def gate_norm(gate_pre, retained):
    centred = retained - jnp.mean(retained, axis=-1, keepdims=True)
    normed = centred * lax.rsqrt(jnp.mean(centred * centred, axis=-1, keepdims=True) + 1.0 * DK)
    return gate_pre * jax.nn.sigmoid(gate_pre) * normed


def gelu_gate(hidden, linear):
    return jax.nn.gelu(hidden, approximate=True) * linear


def rotate(values, cosine, sine):
    half = DK // 2
    first = values[:, :half]
    second = values[:, half:]
    return jnp.concatenate((first * cosine - second * sine, first * sine + second * cosine), axis=1)


def ein(spec, left, right):
    return jnp.einsum(spec, left, right, preferred_element_type=F32)


def per_device(
    tokens,
    cotangent,
    gain_first,
    gain_second,
    w_query,
    w_key,
    w_value,
    w_gate,
    w_output,
    w_hidden,
    w_linear,
    w_down,
    decay_scale,
    first_length,
):
    rows = tokens.shape[0]
    core = lax.axis_index("core")
    place = lax.axis_index("ctx")
    plane = lax.axis_index("tp")
    scalars = jnp.stack((core, plane, lax.axis_index("x"), place)).astype(jnp.int32)

    w_output = w_output.T
    w_down = w_down.T
    mine, theirs = split_heads((w_key, w_value, w_gate, w_output, w_query), scalars, "split_attn")
    came = swap(theirs)
    block, gathered = stack_attn(mine, came, scalars)
    lengths = jnp.concatenate((first_length, swap(first_length)))
    normed_first = enter_rows(tokens, gain_first.reshape(1, D), scalars, deps=(block,))
    w_kv = stack_blocks(
        spread_near(block), 0, 768, scalars, "stack_kv", deps=(normed_first, lengths)
    )
    w_goq = lax.all_gather(gathered, XY, axis=0, tiled=True).reshape(4, 4, 2, 64, -1)
    mine, theirs = split_heads(
        (w_hidden, w_linear, w_down), scalars, "split_mlp", deps=(gathered,)
    )
    came_mlp = swap(theirs)
    gain_first = gain_first.reshape(1, D)
    gain_second = gain_second.reshape(1, D)
    x_first = (normed_first, swap(normed_first))
    cot_low = low_rows(cotangent, scalars, deps=(x_first[1],))
    g_out = (cot_low, swap(cot_low))
    w_kv = spread_far(w_kv)

    rate = lax.dynamic_index_in_dim(decay_scale, core, 0, False) / 1024.0
    local = (jnp.arange(rows, dtype=jnp.int32) + plane * (rows // 4)) % rows
    index = place * rows + local
    document = (index[None, :] >= lengths[:, None]).astype(jnp.int32)
    carried = (document == 0).astype(F32)
    steps = local.astype(F32)
    offsets = local[:, None] - local[None, :]
    linked = (offsets >= 0)[None] & (document[:, :, None] == document[:, None, :])
    mask = jnp.where(
        linked, jnp.exp(-rate * jnp.maximum(offsets, 0).astype(F32))[None], 0.0
    )
    enter = (carried * jnp.exp(-rate * (steps + 1.0))[None])[:, :, None]
    leave = jnp.exp(-rate * (rows - 1.0 - steps))[None, :, None]
    fade = jnp.exp(-rate * rows)
    half = DK // 2
    frequency = 10000.0 ** (-(jnp.arange(half).astype(F32) / half))
    angles = index.astype(F32)[:, None] * frequency[None, :]
    cosine = jnp.tile(jnp.cos(angles), (2, 1))
    sine = jnp.tile(jnp.sin(angles), (2, 1))

    def carry(came):
        near, mid, far = [part.astype(F32) for part in came]
        return near + fade * (mid + fade * far)

    def spread_state(low, way):
        return [shift_open(low, "ctx", way * o) for o in (1, 2, 3)]

    projected = mm_in(*x_first, [(w_kv, 0, 768)], scalars, "project_kv")
    key = rotate(projected[:, :DK], cosine, sine).astype(BF).reshape(2, rows, DK)
    value = projected[:, DK:].astype(BF).reshape(2, rows, DV)
    key_out = (key.astype(F32) * leave).astype(BF)
    state_out = ein("gjd,gje->gde", key_out, value).astype(BF)
    came = spread_state(state_out, 1)
    w_mlp = lax.all_gather(
        stack_blocks((mine, came_mlp), 0, 1536, scalars, "stack_mlp", deps=came),
        XY,
        axis=0,
        tiled=True,
    ).reshape(4, 4, 2, 64, -1)
    projected = mm_in(
        *x_first, [(w_goq, 0, DV), (w_goq, 1024, DK)], scalars, "project_gq", deps=(state_out, mask, enter)
    )
    state_in = carry(came).astype(BF)
    gate_pre = projected[:, :DV]
    query = rotate(projected[:, DV:], cosine, sine).astype(BF).reshape(2, rows, DK)
    weighted = (ein("gid,gjd->gij", query, key) * mask).astype(BF)
    inner = ein("gij,gje->gie", weighted, value)
    retained = (inner + ein("gid,gde->gie", query, state_in) * enter).reshape(2 * rows, DV)
    mixed_full, gate_back = jax.vjp(gate_norm, gate_pre, retained)
    mixed = mixed_full.astype(BF)
    own, other = mm_back([(mixed, w_goq, DV)], scalars, "project_out")
    mine_sum, _ = tp_first(chip_blocks(own, swap(other)))
    parts = tp_second(mine_sum)
    grad_activated = mm_in(
        *g_out, [(w_mlp, 2 * DV, DV)], scalars, "back_down", deps=(other,)
    )
    hidden_state, normed_second = second_norm(tokens, parts, gain_second, scalars, deps=(grad_activated,))
    x_second = (normed_second, swap(normed_second))
    paired = mm_in(*x_second, [(w_mlp, 0, 2 * DV)], scalars, "project_mlp")
    activated_full, gelu_back = jax.vjp(gelu_gate, paired[:, :DV], paired[:, DV:])
    activated = activated_full.astype(BF)
    grad_pair = jnp.concatenate(gelu_back(grad_activated), axis=1).astype(BF)
    own, other = mm_back([(grad_pair, w_mlp, 0)], scalars, "back_mlp")
    mine_sum, _ = tp_first(chip_blocks(own, swap(other)))
    parts = tp_second(mine_sum)
    d_mlp, d_mlp_mark = mm_weight(
        ((x_second, grad_pair), (g_out, activated)), scalars, "weight_mlp", deps=(mine_sum,)
    )
    (d_mlp,) = tie((d_mlp,), parts[1:])
    mlp_block = lax.psum_scatter(
        d_mlp.reshape(2048, -1), XY, scatter_dimension=0, tiled=True
    ).reshape(2, 64, -1)
    down = mm_back([(activated, w_mlp, 2 * DV)], scalars, "project_down", deps=(mine_sum,))
    gain_second_part = gain_part(hidden_state, mine_sum, "gain_second")
    grad_state, grad_state_low = norm_back(
        hidden_state,
        cotangent,
        parts,
        gain_second,
        scalars,
        "second_back",
        deps=(down[1], gain_second_part, d_mlp_mark),
    )
    g_state = (grad_state_low, swap(grad_state_low))
    grad_mixed = mm_in(*g_state, [(w_goq, DV, DV)], scalars, "back_out")
    grad_gate, grad_retained = gate_back(grad_mixed)
    grad_low = grad_retained.reshape(2, rows, DV).astype(BF)
    query_in = (query.astype(F32) * enter).astype(BF)
    back_out = ein("gid,gie->gde", query_in, grad_low).astype(BF)
    came = spread_state(back_out, -1)
    grad_scores = (ein("gie,gje->gij", grad_low, value) * mask).astype(BF)
    grad_query = ein("gij,gjd->gid", grad_scores, key) + enter * ein("gie,gde->gid", grad_low, state_in)
    grad_key = ein("gij,gid->gjd", grad_scores, query)
    grad_value = ein("gij,gie->gje", weighted, grad_low)
    grad_gate = grad_gate.astype(BF)
    grad_query = rotate(grad_query.reshape(2 * rows, DK), cosine, -sine).astype(BF)
    layer_blocks = chip_blocks(down[0], swap(tie((down[1],), (grad_low,))[0]))
    layer_sum, _ = tp_first(tie(layer_blocks, (came[0],)))
    layer_parts = tp_second(layer_sum)
    d_goq, d_goq_mark = mm_weight(
        ((x_first, grad_gate), (g_state, mixed), (x_first, grad_query)),
        scalars,
        "weight_goq",
        deps=(back_out, mlp_block),
    )
    goq_block = lax.psum_scatter(
        d_goq.reshape(2048, -1), XY, scatter_dimension=0, tiled=True
    ).reshape(2, 64, -1)
    came[0] = tie((came[0],), (d_goq_mark, layer_sum, grad_key, grad_value))[0]
    state_back = carry(came).astype(BF)
    grad_key += leave * ein("gje,gde->gjd", value, state_back)
    grad_value += ein("gjd,gde->gje", key_out, state_back)
    grad_kv = jnp.concatenate(
        (rotate(grad_key.reshape(2 * rows, DK), cosine, -sine), grad_value.reshape(2 * rows, DV)),
        axis=1,
    ).astype(BF)
    own, other = mm_back(
        [(grad_kv, w_kv, 0), (grad_gate, w_goq, 0), (grad_query, w_goq, 1024)],
        scalars,
        "back_attn",
        deps=layer_parts[1:],
    )
    d_kv = mm_weight(((x_first, grad_kv),), scalars, "weight_kv", True, deps=(other,))
    blocks, gain_first_part = first_gain(
        own, swap(other), tokens, scalars, deps=(d_kv[0],)
    )
    mine_sum, got = tp_first(blocks)
    kv_sums, kv_got = collect_far(d_kv, (), got[:1])
    parts = tp_second(tie((mine_sum,), kv_got[:2])[0])
    kv_block = collect_near(kv_sums)
    gains = jnp.concatenate((gain_first_part, gain_second_part))
    for axis, swapped in (
        ("core", (1, 0)),
        ("tp", (1, 0, 3, 2)),
        ("tp", (3, 2, 1, 0)),
        ("ctx", (1, 0, 3, 2)),
        ("ctx", (3, 2, 1, 0)),
        ("x", (1, 0, 3, 2)),
        ("x", (3, 2, 1, 0)),
    ):
        if axis == "ctx" and swapped[0] == 1:
            (gains,) = tie((gains,), (*parts[1:], goq_block))
        gains = gains + lax.ppermute(gains, axis, list(enumerate(swapped)))
    spot = (lax.axis_index("x") * 2 + core) * 4 + place
    gains = lax.dynamic_slice_in_dim(gains, spot * 64, 64, 1)
    layer_out = leave_layer(hidden_state, layer_parts, scalars)
    input_grad = leave_grad(tokens, grad_state, parts, gain_first, scalars)
    d_hidden, d_linear, d_down = join_heads(
        mlp_block[0], swap(mlp_block[1]), (DV, DV, DV), scalars, "join_mlp"
    )
    d_gate, d_output, d_query = join_heads(
        goq_block[0], swap(goq_block[1]), (DV, DV, DK), scalars, "join_goq"
    )
    d_key, d_value = join_heads(kv_block[0], swap(kv_block[1]), (DK, DV), scalars, "join_kv")
    return (
        layer_out,
        input_grad,
        gains[0],
        gains[1],
        d_query,
        d_key,
        d_value,
        d_gate,
        d_output.T,
        d_hidden,
        d_linear,
        d_down.T,
    )


def solution(mesh):
    fine = Mesh(np.asarray(mesh.devices).reshape(4, 2, 4, 4), ("x", "core", "ctx", "tp"))
    split = ("x", "core", "ctx")
    row = P(split, None)
    win = P(split, "tp")
    wout = P("tp", split)
    in_specs = (row, row, P(), P(), win, win, win, win, wout, win, win, wout, P("tp"), P(("x", "core")))
    out_specs = (row, row, P(split), P(split), win, win, win, win, wout, win, win, wout)
    return jax.shard_map(
        per_device, mesh=fine, in_specs=in_specs, out_specs=out_specs, check_vma=False
    )
```

```python
import math

import jax
import jax.numpy as jnp
import numpy as np
from jax import lax
from jax.experimental import pallas as pl
from jax.experimental.pallas import tpu as pltpu
from jax.sharding import Mesh, PartitionSpec as P

D = 2048
DK = 256
DV = 512
SLAB = 512
BF = jnp.bfloat16
F32 = jnp.float32
XY = ("x", "ctx")
MIB = 1 << 20


def shift(value, axis, offset):
    n = lax.axis_size(axis)
    return lax.ppermute(value, axis, [(i, (i + offset) % n) for i in range(n)])


def shift_open(value, axis, offset):
    n = lax.axis_size(axis)
    return lax.ppermute(
        value, axis, [(i, i + offset) for i in range(n) if 0 <= i + offset < n]
    )


def swap(value):
    return lax.ppermute(value, "core", [(0, 1), (1, 0)])


def after(value, *earlier):
    return lax.optimization_barrier((value, *earlier))[0]


def call(
    body,
    grid,
    ins,
    outs,
    shapes,
    scalars,
    operands,
    name,
    scratch=(),
    deps=(),
    stream=False,
    aliases=None,
):
    count = len(operands)

    def kernel(s_ref, *refs):
        body(s_ref, *refs[:count], *refs[count + len(deps) :])

    ins = [*ins, *[pl.BlockSpec(memory_space=pl.ANY)] * len(deps)]
    return pl.pallas_call(
        kernel,
        out_shape=shapes,
        grid_spec=pltpu.PrefetchScalarGridSpec(
            num_scalar_prefetch=1, grid=grid, in_specs=ins, out_specs=outs, scratch_shapes=scratch
        ),
        compiler_params=pltpu.CompilerParams(
            vmem_limit_bytes=(60 if stream else 32) * MIB, dimension_semantics=("arbitrary",) * len(grid)
        ),
        cost_estimate=pl.CostEstimate(flops=1, bytes_accessed=1, transcendentals=0),
        input_output_aliases=aliases or {},
        name=name,
    )(scalars, *operands, *deps)


def tie(values, deps):
    count = len(values)
    anywhere = pl.BlockSpec(memory_space=pl.ANY)
    return pl.pallas_call(
        lambda *refs: None,
        out_shape=tuple(sds(v.shape, v.dtype) for v in values),
        in_specs=[anywhere] * (count + len(deps)),
        out_specs=(anywhere,) * count,
        input_output_aliases={i: i for i in range(count)},
        name="tie",
    )(*values, *deps)


def whole(array):
    return pl.BlockSpec(array.shape, lambda *_: (0,) * array.ndim)


def sds(shape, dtype):
    return jax.ShapeDtypeStruct(shape, dtype)


def weight_operands(weight, start, width):
    if not isinstance(weight, tuple):
        spec = pl.BlockSpec((1, 4, 2, 64, width), lambda i, s: (i, 0, 0, 0, start // width))
        return [weight], [spec]
    piece = math.gcd(start, width) if start else width
    operands, specs = [], []
    for at in range(start, start + width, piece):
        for stack in weight:
            operands.append(stack)
            specs.append(pl.BlockSpec((4, 2, 64, piece), lambda i, s, at=at: (0, 0, 0, at // piece)))
    return operands, specs


def load_slab(s_ref, refs, held):
    core = s_ref[0]
    if len(refs) == 1:
        return jnp.concatenate(
            [refs[0][0, y, jnp.bitwise_xor(c, core)] for c in (0, 1) for y in range(4)], axis=0
        )
    x_far = lax.rem(s_ref[2] + 4 - pl.program_id(0), 4)
    at = 0
    for first in range(0, len(refs), 4):
        stacks = refs[first : first + 4]
        width = stacks[0].shape[-1]
        for j in range(4):

            @pl.when((core == 0) & (x_far == j))
            def _(j=j, at=at, width=width, stacks=stacks):
                for i in range(4):
                    y = lax.rem(s_ref[3] + 4 - i, 4)
                    for c in (0, 1):
                        held[c * 4 + y, :, at : at + width] = stacks[j][i, c]

        @pl.when(core == 1)
        def _(at=at, width=width, stacks=stacks):
            for j in range(4):
                y = lax.rem(s_ref[3] + 4 - j, 4)
                for c in (0, 1):
                    held[c * 4 + y, :, at : at + width] = stacks[j][x_far, 1 - c]

        at += width
    return held[...].reshape(SLAB, at)


def hop(value, first, offset):
    pairs = []
    for x in range(4):
        for core in (0, 1):
            for y in range(4):
                to = ((x + offset) % 4, y) if (core == 0) == first else (x, (y + offset) % 4)
                pairs.append(((x * 2 + core) * 4 + y, (to[0] * 2 + core) * 4 + to[1]))
    return lax.ppermute(value, ("x", "core", "ctx"), pairs)


def spread_near(block):
    near, far, mid = [hop(block, False, o) for o in (1, 3, 2)]
    return block, near, mid, far


def stack_blocks(blocks, start, width, scalars, name, deps=()):
    at = start // width if start % width == 0 else None
    span = width if at is not None else blocks[0].shape[1]
    first = 0 if at is not None else start
    height = blocks[0].shape[0]

    def body(s_ref, *refs):
        for k, ref in enumerate(refs[:-1]):
            refs[-1][k * height : (k + 1) * height, :] = ref[:, first : first + width]

    total = sds((height * len(blocks), width), BF)
    return call(
        body,
        (1,),
        [pl.BlockSpec((height, span), lambda i, s: (0, at or 0))] * len(blocks),
        whole(total),
        total,
        scalars,
        tuple(blocks),
        name,
        deps=deps,
    )


def stack_attn(mine, came, scalars):
    height, total = mine.shape

    def body(s_ref, mine_ref, came_ref, first_ref, other_ref):
        for k, ref in enumerate((mine_ref, came_ref)):
            span = slice(k * height, (k + 1) * height)
            first_ref[span, :] = ref[:, :768]
            other_ref[span, :] = ref[:, 768:]

    shapes = (sds((2 * height, 768), BF), sds((2 * height, total - 768), BF))
    return call(
        body,
        (1,),
        [whole(mine), whole(came)],
        tuple(whole(s) for s in shapes),
        shapes,
        scalars,
        (mine, came),
        "stack_attn",
        stream=True,
    )


def spread_far(stack, gate=False):
    stack = stack.reshape(4, 2, 64, -1)
    near, far = hop(stack, True, 1), hop(stack, True, -1)
    mid = hop(tie((stack,), (near, far))[0] if gate else stack, True, 2)
    return stack, near, mid, far


def mm_in(left, right, columns, scalars, name, deps=()):
    operands, specs, counts = [], [], []
    for weight, start, width in columns:
        ops, sp = weight_operands(weight, start, width)
        operands += ops
        specs += sp
        counts.append(len(ops))
    total = sum(width for _, _, width in columns)

    def body(s_ref, a_ref, b_ref, *refs):
        out_ref = refs[len(operands)]
        step = pl.program_id(0)
        rows = jnp.concatenate((a_ref[...], b_ref[...]), axis=0)
        at, first = 0, 0
        for k, count in enumerate(counts):
            width = columns[k][2]
            slab = load_slab(s_ref, refs[first : first + count], refs[len(operands) + 1 + k])
            part = jnp.dot(rows, slab, preferred_element_type=F32)
            span = slice(at, at + width)

            @pl.when(step == 0)
            def _(part=part, span=span):
                out_ref[:, span] = part

            @pl.when(step > 0)
            def _(part=part, span=span):
                out_ref[:, span] += part

            at += width
            first += count

    rows = left.shape[0]
    cols = pl.BlockSpec((rows, SLAB), lambda i, s: (0, i))
    return call(
        body,
        (4,),
        [cols, cols, *specs],
        pl.BlockSpec((2 * rows, total), lambda i, s: (0, 0)),
        sds((2 * rows, total), F32),
        scalars,
        (left, right, *operands),
        name,
        scratch=[pltpu.VMEM((8, 64, width), BF) for _, _, width in columns],
        deps=deps,
    )


def mm_back(terms, scalars, name, deps=()):
    rows = terms[0][0].shape[0]
    half = rows // 2
    operands, specs, counts, scratch = [], [], [], []
    for grad, weight, start in terms:
        ops, sp = weight_operands(weight, start, grad.shape[1])
        operands += [grad, *ops]
        specs += [whole(grad), *sp]
        counts.append(len(ops))
        scratch.append(pltpu.VMEM((8, 64, grad.shape[1]), BF))

    def body(s_ref, *refs):
        own_ref, other_ref = refs[len(operands) : len(operands) + 2]
        at, out = 0, 0.0
        for k, count in enumerate(counts):
            slab = load_slab(s_ref, refs[at + 1 : at + 1 + count], refs[len(operands) + 2 + k])
            out += lax.dot_general(
                refs[at][...], slab, (((1,), (1,)), ((), ())), preferred_element_type=F32
            )
            at += count + 1
        own_ref[...] = out[:half]
        other_ref[...] = out[half:].astype(BF)

    cols = pl.BlockSpec((half, SLAB), lambda i, s: (0, i))
    return call(
        body,
        (4,),
        specs,
        (cols, cols),
        (sds((half, D), F32), sds((half, D), BF)),
        scalars,
        tuple(operands),
        name,
        scratch=scratch,
        deps=deps,
    )


def mm_weight(into, pair, grad, start, scalars, name, deps=()):
    rows, width = pair[0].shape[0], grad.shape[1]
    span = math.gcd(start, width) if start else width
    total = 3584
    operands = (*pair, grad) if into is None else (*pair, grad, into)

    def body(s_ref, a_ref, b_ref, g_ref, *refs):
        out_ref, mark_ref = refs[-2:]
        out = lax.dot_general(
            jnp.concatenate((a_ref[...], b_ref[...]), axis=0),
            g_ref[...],
            (((0,), (0,)), ((), ())),
            preferred_element_type=F32,
        ).astype(BF)
        for c in (0, 1):
            for y in range(4):
                first = (c * 4 + y) * 64
                out_ref[0, y, jnp.bitwise_xor(c, s_ref[0])] = out[first : first + 64]
        mark_ref[...] = jnp.zeros_like(mark_ref)

    cols = pl.BlockSpec((rows, SLAB), lambda i, j, s: (0, i))
    specs = [cols, cols, pl.BlockSpec((2 * rows, span), lambda i, j, s: (0, j))]
    if into is not None:
        specs.append(pl.BlockSpec(memory_space=pl.ANY))
    return call(
        body,
        (4, width // span),
        specs,
        (
            pl.BlockSpec((1, 4, 2, 64, span), lambda i, j, s: (i, 0, 0, 0, start // span + j)),
            pl.BlockSpec((8, 128), lambda i, j, s: (0, 0)),
        ),
        (sds((4, 4, 2, 64, total), BF), sds((8, 128), F32)),
        scalars,
        operands,
        name,
        deps=deps,
        aliases=None if into is None else {4: 0},
    )


def split_heads(weights, scalars, name, deps=()):
    widths = [w.shape[1] // 2 for w in weights]

    def body(s_ref, *refs):
        mine_ref, theirs_ref = refs[-2:]
        core = s_ref[0]
        for out_ref, head in ((mine_ref, core), (theirs_ref, 1 - core)):
            at = 0
            for ref, width in zip(refs, widths):
                out_ref[:, at : at + width] = ref[:, pl.ds(pl.multiple_of(head * width, width), width)]
                at += width

    total = sum(widths)
    spec = pl.BlockSpec((64, total), lambda i, s: (0, 0))
    return call(
        body,
        (1,),
        [whole(w) for w in weights],
        (spec, spec),
        (sds((64, total), BF),) * 2,
        scalars,
        tuple(weights),
        name,
        deps=deps,
        stream=True,
    )


def join_heads(mine, theirs, widths, scalars, name):
    def body(s_ref, mine_ref, theirs_ref, *outs):
        core = s_ref[0]
        for in_ref, head in ((mine_ref, core), (theirs_ref, 1 - core)):
            at = 0
            for ref, width in zip(outs, widths):
                span = pl.ds(pl.multiple_of(head * width, width), width)
                ref[:, span] = in_ref[:, at : at + width].astype(F32)
                at += width

    shapes = tuple(sds((64, 2 * w), F32) for w in widths)
    return call(
        body,
        (1,),
        [whole(mine), whole(theirs)],
        tuple(whole(s) for s in shapes),
        shapes,
        scalars,
        (mine, theirs),
        name,
    )


def scale_of(values):
    return lax.rsqrt(jnp.mean(values * values, axis=-1, keepdims=True) + 1e-06)


def turned_spec(rows):
    return pl.BlockSpec((rows, D), lambda i, s: (lax.rem(i + s[1], 4), 0))


def plain_spec(rows):
    return pl.BlockSpec((rows, D), lambda i, s: (i, 0))


def enter_rows(tokens, gain, scalars, deps=()):
    rows = tokens.shape[0]
    block = rows // 4

    def body(s_ref, t_ref, g_ref, n_out):
        values = t_ref[...]
        n_out[...] = (values * scale_of(values) * g_ref[...]).astype(BF)

    return call(
        body,
        (4,),
        [turned_spec(block), whole(gain)],
        plain_spec(block),
        sds((rows, D), BF),
        scalars,
        (tokens, gain),
        "enter_rows",
        deps=deps,
    )


def low_rows(cotangent, scalars, deps=()):
    rows = cotangent.shape[0]
    block = rows // 4

    def body(s_ref, c_ref, l_out):
        l_out[...] = c_ref[...].astype(BF)

    return call(
        body,
        (4,),
        [turned_spec(block)],
        plain_spec(block),
        sds((rows, D), BF),
        scalars,
        (cotangent,),
        "low_rows",
        deps=deps,
    )


def each_part(refs, work):
    step = pl.program_id(0)
    for k, ref in enumerate(refs):

        @pl.when(step == k)
        def _(ref=ref):
            work(ref[...].astype(F32))


def second_norm(tokens, parts, gain, scalars, deps=()):
    rows = tokens.shape[0]
    block = rows // 4

    def body(s_ref, t_ref, g_ref, *refs):
        h_out, n_out = refs[4:]

        def work(part):
            values = t_ref[...] + part
            h_out[...] = values
            n_out[...] = (values * scale_of(values) * g_ref[...]).astype(BF)

        each_part(refs[:4], work)

    plain = plain_spec(block)
    return call(
        body,
        (4,),
        [turned_spec(block), whole(gain)] + [whole(p) for p in parts],
        (plain, plain),
        (sds((rows, D), F32), sds((rows, D), BF)),
        scalars,
        (tokens, gain, *parts),
        "second_norm",
        deps=deps,
        stream=True,
    )


def first_gain(own, came, tokens, down_own, down_came, scalars, deps=()):
    rows = own.shape[0]
    block = rows // 4

    def body(s_ref, own_ref, came_ref, t_ref, d_ref, e_ref, *refs):
        total = own_ref[...] + came_ref[...].astype(F32)
        down = d_ref[...] + e_ref[...].astype(F32)
        values = t_ref[...]
        part = jnp.sum(total * (values * scale_of(values)), axis=0, keepdims=True)
        step = pl.program_id(0)
        for k in range(4):

            @pl.when(step == k)
            def _(k=k):
                refs[k][:block] = total.astype(BF)
                refs[k][block:] = down.astype(BF)

        @pl.when(step == 0)
        def _():
            refs[4][...] = part

        @pl.when(step > 0)
        def _():
            refs[4][...] += part

    plain = plain_spec(block)
    shapes = (sds((2 * block, D), BF),) * 4 + (sds((1, D), F32),)
    out = call(
        body,
        (4,),
        [plain, plain, turned_spec(block), plain, plain],
        tuple(whole(s) for s in shapes),
        shapes,
        scalars,
        (own, came, tokens, down_own, down_came),
        "first_gain",
        deps=deps,
        stream=True,
    )
    return out[:4], out[4]


def leave_rows(hidden, tokens, grad_state, parts, gain, scalars):
    rows = hidden.shape[0]
    block = rows // 4

    def body(s_ref, h_ref, t_ref, u_ref, g_ref, *refs):
        def work(part):
            refs[4][...] = h_ref[...] + part[block:]
            refs[5][...] = u_ref[...] + norm_grad(t_ref[...], part[:block], g_ref[...])

        each_part(refs[:4], work)

    plain, turn = plain_spec(block), turned_spec(block)
    return call(
        body,
        (4,),
        [plain, turn, plain, whole(gain)] + [whole(p) for p in parts],
        (turn, turn),
        (sds((rows, D), F32),) * 2,
        scalars,
        (hidden, tokens, grad_state, gain, *parts),
        "leave_rows",
        stream=True,
    )


def gain_part(values, grad, name):
    block = grad.shape[0]

    def body(v_ref, p_ref, out_ref):
        values = v_ref[...]
        out_ref[...] = jnp.sum(
            p_ref[...].astype(F32) * (values * scale_of(values)), axis=0, keepdims=True
        )

    return pl.pallas_call(
        body,
        out_shape=sds((1, D), F32),
        grid=(1,),
        in_specs=[pl.BlockSpec((block, D), lambda i: (0, 0))] * 2,
        out_specs=pl.BlockSpec((1, D), lambda i: (0, 0)),
        name=name,
    )(values, grad)


def norm_grad(values, grad, gain):
    factor = scale_of(values)
    unit = values * factor
    scaled = grad * gain
    return factor * (scaled - unit * jnp.mean(scaled * unit, axis=-1, keepdims=True))


def norm_back(values, upstream, parts, gain, scalars, name, deps=()):
    rows = values.shape[0]
    block = rows // 4

    def body(s_ref, v_ref, u_ref, g_ref, *refs):
        def work(part):
            out = u_ref[...] + norm_grad(v_ref[...], part, g_ref[...])
            refs[4][...] = out
            refs[5][...] = out.astype(BF)

        each_part(refs[:4], work)

    plain = plain_spec(block)
    return call(
        body,
        (4,),
        [plain, turned_spec(block), whole(gain)] + [whole(p) for p in parts],
        (plain, plain),
        (sds((rows, D), F32), sds((rows, D), BF)),
        scalars,
        (values, upstream, gain, *parts),
        name,
        deps=deps,
        stream=True,
    )


def tp_total(blocks, deps=()):
    got = [shift(blocks[o], "tp", o) for o in (1, 3, 2)]
    mine = blocks[0].astype(F32)
    for part in got:
        mine = mine + part.astype(F32)
    mine = mine.astype(BF)
    if deps:
        (mine,) = tie((mine,), deps)
    near, far, mid = [shift(mine, "tp", -o) for o in (1, 3, 2)]
    return (mine, near, mid, far)


def heads_total(own, other):
    came = swap(other)
    block = own.shape[0] // 4
    blocks = [
        (own[o * block : (o + 1) * block] + came[o * block : (o + 1) * block].astype(F32)).astype(BF)
        for o in range(4)
    ]
    return tp_total(blocks), blocks


def gate_norm(gate_pre, retained):
    centred = retained - jnp.mean(retained, axis=-1, keepdims=True)
    normed = centred * lax.rsqrt(jnp.mean(centred * centred, axis=-1, keepdims=True) + 1.0 * DK)
    return gate_pre * jax.nn.sigmoid(gate_pre) * normed


def gelu_gate(hidden, linear):
    return jax.nn.gelu(hidden, approximate=True) * linear


def rotate(values, cosine, sine):
    half = DK // 2
    first = values[:, :half]
    second = values[:, half:]
    return jnp.concatenate((first * cosine - second * sine, first * sine + second * cosine), axis=1)


def ein(spec, left, right):
    return jnp.einsum(spec, left, right, preferred_element_type=F32)


def per_device(
    tokens,
    cotangent,
    gain_first,
    gain_second,
    w_query,
    w_key,
    w_value,
    w_gate,
    w_output,
    w_hidden,
    w_linear,
    w_down,
    decay_scale,
    first_length,
):
    rows = tokens.shape[0]
    core = lax.axis_index("core")
    place = lax.axis_index("ctx")
    plane = lax.axis_index("tp")
    scalars = jnp.stack((core, plane, lax.axis_index("x"), place)).astype(jnp.int32)

    w_output = w_output.T
    w_down = w_down.T
    mine, theirs = split_heads((w_value, w_key, w_gate, w_output, w_query), scalars, "split_attn")
    came = swap(theirs)
    block, gathered = stack_attn(mine, came, scalars)
    lengths = jnp.concatenate((first_length, swap(first_length)))
    normed_first = enter_rows(tokens, gain_first.reshape(1, D), scalars, deps=(block,))
    w_kv = stack_blocks(
        spread_near(block), 0, 768, scalars, "stack_kv", deps=(normed_first, lengths)
    )
    w_goq = lax.all_gather(gathered, XY, axis=0, tiled=True).reshape(4, 4, 2, 64, -1)
    mine, theirs = split_heads(
        (w_hidden, w_linear, w_down), scalars, "split_mlp", deps=(gathered,)
    )
    came_mlp = swap(theirs)
    gain_first = gain_first.reshape(1, D)
    gain_second = gain_second.reshape(1, D)
    x_first = (normed_first, swap(normed_first))
    cot_low = low_rows(cotangent, scalars, deps=(x_first[1],))
    g_out = (cot_low, swap(cot_low))
    w_kv = spread_far(w_kv)

    rate = lax.dynamic_index_in_dim(decay_scale, core, 0, False) / 1024.0
    local = (jnp.arange(rows, dtype=jnp.int32) + plane * (rows // 4)) % rows
    index = place * rows + local
    document = (index[None, :] >= lengths[:, None]).astype(jnp.int32)
    carried = (document == 0).astype(F32)
    steps = local.astype(F32)
    offsets = local[:, None] - local[None, :]
    linked = (offsets >= 0)[None] & (document[:, :, None] == document[:, None, :])
    mask = jnp.where(
        linked, jnp.exp(-rate * jnp.maximum(offsets, 0).astype(F32))[None], 0.0
    )
    enter = (carried * jnp.exp(-rate * (steps + 1.0))[None])[:, :, None]
    leave = jnp.exp(-rate * (rows - 1.0 - steps))[None, :, None]
    fade = jnp.exp(-rate * rows)
    half = DK // 2
    frequency = 10000.0 ** (-(jnp.arange(half).astype(F32) / half))
    angles = index.astype(F32)[:, None] * frequency[None, :]
    cosine = jnp.tile(jnp.cos(angles), (2, 1))
    sine = jnp.tile(jnp.sin(angles), (2, 1))

    def carry(came):
        near, mid, far = [part.astype(F32) for part in came]
        return near + fade * (mid + fade * far)

    def spread_state(low, way):
        return [shift_open(low, "ctx", way * o) for o in (1, 2, 3)]

    projected = mm_in(*x_first, [(w_kv, 0, 768)], scalars, "project_kv")
    key = rotate(projected[:, DV:], cosine, sine).astype(BF).reshape(2, rows, DK)
    value = projected[:, :DV].astype(BF).reshape(2, rows, DV)
    key_out = (key.astype(F32) * leave).astype(BF)
    state_out = ein("gjd,gje->gde", key_out, value).astype(BF)
    came = spread_state(state_out, 1)
    w_mlp = lax.all_gather(
        stack_blocks((mine, came_mlp), 0, 1536, scalars, "stack_mlp", deps=came),
        XY,
        axis=0,
        tiled=True,
    ).reshape(4, 4, 2, 64, -1)
    projected = mm_in(
        *x_first, [(w_goq, 0, DV), (w_goq, 1024, DK)], scalars, "project_gq", deps=(state_out, mask, enter)
    )
    state_in = carry(came).astype(BF)
    gate_pre = projected[:, :DV]
    query = rotate(projected[:, DV:], cosine, sine).astype(BF).reshape(2, rows, DK)
    weighted = (ein("gid,gjd->gij", query, key) * mask).astype(BF)
    inner = ein("gij,gje->gie", weighted, value)
    retained = (inner + ein("gid,gde->gie", query, state_in) * enter).reshape(2 * rows, DV)
    mixed_full, gate_back = jax.vjp(gate_norm, gate_pre, retained)
    mixed = mixed_full.astype(BF)
    own, other = mm_back([(mixed, w_goq, DV)], scalars, "project_out")
    parts, _ = heads_total(own, other)
    grad_activated = mm_in(
        *g_out, [(w_mlp, 2 * DV, DV)], scalars, "back_down", deps=(other,)
    )
    hidden_state, normed_second = second_norm(tokens, parts, gain_second, scalars, deps=(grad_activated,))
    x_second = (normed_second, swap(normed_second))
    paired = mm_in(*x_second, [(w_mlp, 0, 2 * DV)], scalars, "project_mlp")
    activated_full, gelu_back = jax.vjp(gelu_gate, paired[:, :DV], paired[:, DV:])
    activated = activated_full.astype(BF)
    grad_pair = jnp.concatenate(gelu_back(grad_activated), axis=1).astype(BF)
    own, other = mm_back([(grad_pair, w_mlp, 0)], scalars, "back_mlp")
    parts, totals = heads_total(own, other)
    down = mm_back([(activated, w_mlp, 2 * DV)], scalars, "project_down", deps=(parts[0],))
    grads, mark = mm_weight(
        None, x_second, grad_pair, 0, scalars, "weight_mlp", deps=(parts[0],)
    )
    grads, mark = mm_weight(grads, g_out, activated, 2 * DV, scalars, "weight_down")
    gain_second_part = gain_part(hidden_state, parts[0], "gain_second")
    grad_state, grad_state_low = norm_back(
        hidden_state,
        cotangent,
        parts,
        gain_second,
        scalars,
        "second_back",
        deps=(down[1], gain_second_part, mark),
    )
    g_state = (grad_state_low, swap(grad_state_low))
    grad_mixed = mm_in(*g_state, [(w_goq, DV, DV)], scalars, "back_out")
    grad_gate, grad_retained = gate_back(grad_mixed)
    grad_low = grad_retained.reshape(2, rows, DV).astype(BF)
    query_in = (query.astype(F32) * enter).astype(BF)
    back_out = ein("gid,gie->gde", query_in, grad_low).astype(BF)
    came = spread_state(back_out, -1)
    grad_scores = (ein("gie,gje->gij", grad_low, value) * mask).astype(BF)
    grad_query = ein("gij,gjd->gid", grad_scores, key) + enter * ein("gie,gde->gid", grad_low, state_in)
    grad_key = ein("gij,gid->gjd", grad_scores, query)
    grad_value = ein("gij,gie->gje", weighted, grad_low)
    grad_gate = grad_gate.astype(BF)
    grad_query = rotate(grad_query.reshape(2 * rows, DK), cosine, -sine).astype(BF)
    grads, mark = mm_weight(
        grads, g_state, mixed, 3 * DV, scalars, "weight_output", deps=(back_out,)
    )
    grads, mark = mm_weight(grads, x_first, grad_gate, 4 * DV, scalars, "weight_gate")
    came[0] = tie((came[0],), (mark, grad_key, grad_value, grad_query))[0]
    state_back = carry(came).astype(BF)
    grad_key += leave * ein("gje,gde->gjd", value, state_back)
    grad_value += ein("gjd,gde->gje", key_out, state_back)
    grad_key = rotate(grad_key.reshape(2 * rows, DK), cosine, -sine)
    grad_vkq = jnp.concatenate(
        (grad_value.reshape(2 * rows, DV).astype(BF), grad_key.astype(BF), grad_query), axis=1
    )
    grads, mark = mm_weight(grads, x_first, grad_vkq, 5 * DV, scalars, "weight_vkq")
    block = lax.psum_scatter(
        grads.reshape(2048, -1), XY, scatter_dimension=0, tiled=True
    ).reshape(2, 64, -1)
    own, other = mm_back(
        [(grad_vkq[:, : DV + DK], w_kv, 0), (grad_gate, w_goq, 0), (grad_query, w_goq, 1024)],
        scalars,
        "back_attn",
        deps=(mark,),
    )
    down = (down[0], swap(tie((down[1],), (mark,))[0]))
    blocks, gain_first_part = first_gain(own, swap(other), tokens, *down, scalars)
    parts = tp_total(blocks)
    gains = jnp.concatenate((gain_first_part, gain_second_part))
    for axis, swapped in (
        ("core", (1, 0)),
        ("tp", (1, 0, 3, 2)),
        ("tp", (3, 2, 1, 0)),
        ("ctx", (1, 0, 3, 2)),
        ("ctx", (3, 2, 1, 0)),
        ("x", (1, 0, 3, 2)),
        ("x", (3, 2, 1, 0)),
    ):
        if axis == "ctx" and swapped[0] == 1:
            (gains,) = tie((gains,), parts[1:])
        gains = gains + lax.ppermute(gains, axis, list(enumerate(swapped)))
    spot = (lax.axis_index("x") * 2 + core) * 4 + place
    gains = lax.dynamic_slice_in_dim(gains, spot * 64, 64, 1)
    layer_out, input_grad = leave_rows(hidden_state, tokens, grad_state, parts, gain_first, scalars)
    d_hidden, d_linear, d_down, d_output, d_gate, d_value, d_key, d_query = join_heads(
        block[0], swap(block[1]), (DV,) * 6 + (DK,) * 2, scalars, "join_heads"
    )
    return (
        layer_out,
        input_grad,
        gains[0],
        gains[1],
        d_query,
        d_key,
        d_value,
        d_gate,
        d_output.T,
        d_hidden,
        d_linear,
        d_down.T,
    )


def solution(mesh):
    fine = Mesh(np.asarray(mesh.devices).reshape(4, 2, 4, 4), ("x", "core", "ctx", "tp"))
    split = ("x", "core", "ctx")
    row = P(split, None)
    win = P(split, "tp")
    wout = P("tp", split)
    in_specs = (row, row, P(), P(), win, win, win, win, wout, win, win, wout, P("tp"), P(("x", "core")))
    out_specs = (row, row, P(split), P(split), win, win, win, win, wout, win, win, wout)
    return jax.shard_map(
        per_device, mesh=fine, in_specs=in_specs, out_specs=out_specs, check_vma=False
    )
```

```python
import math

import jax
import jax.numpy as jnp
import numpy as np
from jax import lax
from jax.experimental import pallas as pl
from jax.experimental.pallas import tpu as pltpu
from jax.sharding import Mesh, PartitionSpec as P

D = 2048
DK = 256
DV = 512
SLAB = 512
BF = jnp.bfloat16
F32 = jnp.float32
XY = ("x", "ctx")
MIB = 1 << 20


def shift(value, axis, offset):
    n = lax.axis_size(axis)
    return lax.ppermute(value, axis, [(i, (i + offset) % n) for i in range(n)])


def shift_open(value, axis, offset):
    n = lax.axis_size(axis)
    return lax.ppermute(
        value, axis, [(i, i + offset) for i in range(n) if 0 <= i + offset < n]
    )


def swap(value):
    return lax.ppermute(value, "core", [(0, 1), (1, 0)])


def after(value, *earlier):
    return lax.optimization_barrier((value, *earlier))[0]


def call(
    body,
    grid,
    ins,
    outs,
    shapes,
    scalars,
    operands,
    name,
    scratch=(),
    deps=(),
    stream=False,
    aliases=None,
):
    count = len(operands)

    def kernel(s_ref, *refs):
        body(s_ref, *refs[:count], *refs[count + len(deps) :])

    ins = [*ins, *[pl.BlockSpec(memory_space=pl.ANY)] * len(deps)]
    return pl.pallas_call(
        kernel,
        out_shape=shapes,
        grid_spec=pltpu.PrefetchScalarGridSpec(
            num_scalar_prefetch=1, grid=grid, in_specs=ins, out_specs=outs, scratch_shapes=scratch
        ),
        compiler_params=pltpu.CompilerParams(
            vmem_limit_bytes=(60 if stream else 32) * MIB, dimension_semantics=("arbitrary",) * len(grid)
        ),
        cost_estimate=pl.CostEstimate(flops=1, bytes_accessed=1, transcendentals=0),
        input_output_aliases=aliases or {},
        name=name,
    )(scalars, *operands, *deps)


def tie(values, deps):
    count = len(values)
    anywhere = pl.BlockSpec(memory_space=pl.ANY)
    return pl.pallas_call(
        lambda *refs: None,
        out_shape=tuple(sds(v.shape, v.dtype) for v in values),
        in_specs=[anywhere] * (count + len(deps)),
        out_specs=(anywhere,) * count,
        input_output_aliases={i: i for i in range(count)},
        name="tie",
    )(*values, *deps)


def whole(array):
    return pl.BlockSpec(array.shape, lambda *_: (0,) * array.ndim)


def sds(shape, dtype):
    return jax.ShapeDtypeStruct(shape, dtype)


def weight_operands(weight, start, width):
    if not isinstance(weight, tuple):
        spec = pl.BlockSpec((1, 4, 2, 64, width), lambda i, s: (i, 0, 0, 0, start // width))
        return [weight], [spec]
    piece = math.gcd(start, width) if start else width
    operands, specs = [], []
    for at in range(start, start + width, piece):
        for stack in weight:
            operands.append(stack)
            specs.append(pl.BlockSpec((4, 2, 64, piece), lambda i, s, at=at: (0, 0, 0, at // piece)))
    return operands, specs


def load_slab(s_ref, refs, held):
    core = s_ref[0]
    if len(refs) == 1:
        return jnp.concatenate(
            [refs[0][0, y, jnp.bitwise_xor(c, core)] for c in (0, 1) for y in range(4)], axis=0
        )
    x_far = lax.rem(s_ref[2] + 4 - pl.program_id(0), 4)
    at = 0
    for first in range(0, len(refs), 4):
        stacks = refs[first : first + 4]
        width = stacks[0].shape[-1]
        for j in range(4):

            @pl.when((core == 0) & (x_far == j))
            def _(j=j, at=at, width=width, stacks=stacks):
                for i in range(4):
                    y = lax.rem(s_ref[3] + 4 - i, 4)
                    for c in (0, 1):
                        held[c * 4 + y, :, at : at + width] = stacks[j][i, c]

        @pl.when(core == 1)
        def _(at=at, width=width, stacks=stacks):
            for j in range(4):
                y = lax.rem(s_ref[3] + 4 - j, 4)
                for c in (0, 1):
                    held[c * 4 + y, :, at : at + width] = stacks[j][x_far, 1 - c]

        at += width
    return held[...].reshape(SLAB, at)


def hop(value, first, offset):
    pairs = []
    for x in range(4):
        for core in (0, 1):
            for y in range(4):
                to = ((x + offset) % 4, y) if (core == 0) == first else (x, (y + offset) % 4)
                pairs.append(((x * 2 + core) * 4 + y, (to[0] * 2 + core) * 4 + to[1]))
    return lax.ppermute(value, ("x", "core", "ctx"), pairs)


def spread_near(block):
    near, far, mid = [hop(block, False, o) for o in (1, 3, 2)]
    return block, near, mid, far


def stack_blocks(blocks, start, width, scalars, name, deps=()):
    at = start // width if start % width == 0 else None
    span = width if at is not None else blocks[0].shape[1]
    first = 0 if at is not None else start
    height = blocks[0].shape[0]

    def body(s_ref, *refs):
        for k, ref in enumerate(refs[:-1]):
            refs[-1][k * height : (k + 1) * height, :] = ref[:, first : first + width]

    total = sds((height * len(blocks), width), BF)
    return call(
        body,
        (1,),
        [pl.BlockSpec((height, span), lambda i, s: (0, at or 0))] * len(blocks),
        whole(total),
        total,
        scalars,
        tuple(blocks),
        name,
        deps=deps,
    )


def stack_attn(mine, came, scalars):
    height, total = mine.shape

    def body(s_ref, mine_ref, came_ref, first_ref, other_ref):
        for k, ref in enumerate((mine_ref, came_ref)):
            span = slice(k * height, (k + 1) * height)
            first_ref[span, :] = ref[:, :768]
            other_ref[span, :] = ref[:, 768:]

    shapes = (sds((2 * height, 768), BF), sds((2 * height, total - 768), BF))
    return call(
        body,
        (1,),
        [whole(mine), whole(came)],
        tuple(whole(s) for s in shapes),
        shapes,
        scalars,
        (mine, came),
        "stack_attn",
        stream=True,
    )


def spread_far(stack, gate=False):
    stack = stack.reshape(4, 2, 64, -1)
    near, far = hop(stack, True, 1), hop(stack, True, -1)
    mid = hop(tie((stack,), (near, far))[0] if gate else stack, True, 2)
    return stack, near, mid, far


def mm_in(left, right, columns, scalars, name, deps=()):
    operands, specs, counts = [], [], []
    for weight, start, width in columns:
        ops, sp = weight_operands(weight, start, width)
        operands += ops
        specs += sp
        counts.append(len(ops))
    total = sum(width for _, _, width in columns)

    def body(s_ref, a_ref, b_ref, *refs):
        out_ref = refs[len(operands)]
        step = pl.program_id(0)
        rows = jnp.concatenate((a_ref[...], b_ref[...]), axis=0)
        at, first = 0, 0
        for k, count in enumerate(counts):
            width = columns[k][2]
            slab = load_slab(s_ref, refs[first : first + count], refs[len(operands) + 1 + k])
            part = jnp.dot(rows, slab, preferred_element_type=F32)
            span = slice(at, at + width)

            @pl.when(step == 0)
            def _(part=part, span=span):
                out_ref[:, span] = part

            @pl.when(step > 0)
            def _(part=part, span=span):
                out_ref[:, span] += part

            at += width
            first += count

    rows = left.shape[0]
    cols = pl.BlockSpec((rows, SLAB), lambda i, s: (0, i))
    return call(
        body,
        (4,),
        [cols, cols, *specs],
        pl.BlockSpec((2 * rows, total), lambda i, s: (0, 0)),
        sds((2 * rows, total), F32),
        scalars,
        (left, right, *operands),
        name,
        scratch=[pltpu.VMEM((8, 64, width), BF) for _, _, width in columns],
        deps=deps,
    )


def mm_back(terms, scalars, name, deps=()):
    rows = terms[0][0].shape[0]
    half = rows // 2
    operands, specs, counts, scratch = [], [], [], []
    for grad, weight, start in terms:
        ops, sp = weight_operands(weight, start, grad.shape[1])
        operands += [grad, *ops]
        specs += [whole(grad), *sp]
        counts.append(len(ops))
        scratch.append(pltpu.VMEM((8, 64, grad.shape[1]), BF))

    def body(s_ref, *refs):
        own_ref, other_ref = refs[len(operands) : len(operands) + 2]
        at, out = 0, 0.0
        for k, count in enumerate(counts):
            slab = load_slab(s_ref, refs[at + 1 : at + 1 + count], refs[len(operands) + 2 + k])
            out += lax.dot_general(
                refs[at][...], slab, (((1,), (1,)), ((), ())), preferred_element_type=F32
            )
            at += count + 1
        own_ref[...] = out[:half]
        other_ref[...] = out[half:].astype(BF)

    cols = pl.BlockSpec((half, SLAB), lambda i, s: (0, i))
    return call(
        body,
        (4,),
        specs,
        (cols, cols),
        (sds((half, D), F32), sds((half, D), BF)),
        scalars,
        tuple(operands),
        name,
        scratch=scratch,
        deps=deps,
    )


def mm_weight(into, pair, grad, start, scalars, name, deps=()):
    rows, width = pair[0].shape[0], grad.shape[1]
    span = math.gcd(start, width) if start else width
    total = 3584
    operands = (*pair, grad) if into is None else (*pair, grad, into)

    def body(s_ref, a_ref, b_ref, g_ref, *refs):
        out_ref, mark_ref = refs[-2:]
        out = lax.dot_general(
            jnp.concatenate((a_ref[...], b_ref[...]), axis=0),
            g_ref[...],
            (((0,), (0,)), ((), ())),
            preferred_element_type=F32,
        ).astype(BF)
        for c in (0, 1):
            for y in range(4):
                first = (c * 4 + y) * 64
                out_ref[0, y, jnp.bitwise_xor(c, s_ref[0])] = out[first : first + 64]
        mark_ref[...] = jnp.zeros_like(mark_ref)

    cols = pl.BlockSpec((rows, SLAB), lambda i, j, s: (0, i))
    specs = [cols, cols, pl.BlockSpec((2 * rows, span), lambda i, j, s: (0, j))]
    if into is not None:
        specs.append(pl.BlockSpec(memory_space=pl.ANY))
    return call(
        body,
        (4, width // span),
        specs,
        (
            pl.BlockSpec((1, 4, 2, 64, span), lambda i, j, s: (i, 0, 0, 0, start // span + j)),
            pl.BlockSpec((8, 128), lambda i, j, s: (0, 0)),
        ),
        (sds((4, 4, 2, 64, total), BF), sds((8, 128), F32)),
        scalars,
        operands,
        name,
        deps=deps,
        aliases=None if into is None else {4: 0},
        stream=True,
    )


def split_heads(weights, scalars, name, deps=()):
    widths = [w.shape[1] // 2 for w in weights]

    def body(s_ref, *refs):
        mine_ref, theirs_ref = refs[-2:]
        core = s_ref[0]
        for out_ref, head in ((mine_ref, core), (theirs_ref, 1 - core)):
            at = 0
            for ref, width in zip(refs, widths):
                out_ref[:, at : at + width] = ref[:, pl.ds(pl.multiple_of(head * width, width), width)]
                at += width

    total = sum(widths)
    spec = pl.BlockSpec((64, total), lambda i, s: (0, 0))
    return call(
        body,
        (1,),
        [whole(w) for w in weights],
        (spec, spec),
        (sds((64, total), BF),) * 2,
        scalars,
        tuple(weights),
        name,
        deps=deps,
        stream=True,
    )


def join_heads(mine, theirs, widths, scalars, name):
    def body(s_ref, mine_ref, theirs_ref, *outs):
        core = s_ref[0]
        for in_ref, head in ((mine_ref, core), (theirs_ref, 1 - core)):
            at = 0
            for ref, width in zip(outs, widths):
                span = pl.ds(pl.multiple_of(head * width, width), width)
                ref[:, span] = in_ref[:, at : at + width].astype(F32)
                at += width

    shapes = tuple(sds((64, 2 * w), F32) for w in widths)
    return call(
        body,
        (1,),
        [whole(mine), whole(theirs)],
        tuple(whole(s) for s in shapes),
        shapes,
        scalars,
        (mine, theirs),
        name,
    )


def scale_of(values):
    return lax.rsqrt(jnp.mean(values * values, axis=-1, keepdims=True) + 1e-06)


def turned_spec(rows):
    return pl.BlockSpec((rows, D), lambda i, s: (lax.rem(i + s[1], 4), 0))


def plain_spec(rows):
    return pl.BlockSpec((rows, D), lambda i, s: (i, 0))


def enter_rows(tokens, gain, scalars, deps=()):
    rows = tokens.shape[0]
    block = rows // 4

    def body(s_ref, t_ref, g_ref, n_out):
        values = t_ref[...]
        n_out[...] = (values * scale_of(values) * g_ref[...]).astype(BF)

    return call(
        body,
        (4,),
        [turned_spec(block), whole(gain)],
        plain_spec(block),
        sds((rows, D), BF),
        scalars,
        (tokens, gain),
        "enter_rows",
        deps=deps,
    )


def low_rows(cotangent, scalars, deps=()):
    rows = cotangent.shape[0]
    block = rows // 4

    def body(s_ref, c_ref, l_out):
        l_out[...] = c_ref[...].astype(BF)

    return call(
        body,
        (4,),
        [turned_spec(block)],
        plain_spec(block),
        sds((rows, D), BF),
        scalars,
        (cotangent,),
        "low_rows",
        deps=deps,
    )


def each_part(refs, work):
    step = pl.program_id(0)
    for k, ref in enumerate(refs):

        @pl.when(step == k)
        def _(ref=ref):
            work(ref[...].astype(F32))


def second_norm(tokens, parts, gain, scalars, deps=()):
    rows = tokens.shape[0]
    block = rows // 4

    def body(s_ref, t_ref, g_ref, *refs):
        h_out, n_out = refs[4:]

        def work(part):
            values = t_ref[...] + part
            h_out[...] = values
            n_out[...] = (values * scale_of(values) * g_ref[...]).astype(BF)

        each_part(refs[:4], work)

    plain = plain_spec(block)
    return call(
        body,
        (4,),
        [turned_spec(block), whole(gain)] + [whole(p) for p in parts],
        (plain, plain),
        (sds((rows, D), F32), sds((rows, D), BF)),
        scalars,
        (tokens, gain, *parts),
        "second_norm",
        deps=deps,
        stream=True,
    )


def first_gain(own, came, tokens, down_own, down_came, scalars, deps=()):
    rows = own.shape[0]
    block = rows // 4

    def body(s_ref, own_ref, came_ref, t_ref, d_ref, e_ref, *refs):
        total = own_ref[...] + came_ref[...].astype(F32)
        down = d_ref[...] + e_ref[...].astype(F32)
        values = t_ref[...]
        part = jnp.sum(total * (values * scale_of(values)), axis=0, keepdims=True)
        step = pl.program_id(0)
        for k in range(4):

            @pl.when(step == k)
            def _(k=k):
                refs[k][:block] = total.astype(BF)
                refs[k][block:] = down.astype(BF)

        @pl.when(step == 0)
        def _():
            refs[4][...] = part

        @pl.when(step > 0)
        def _():
            refs[4][...] += part

    plain = plain_spec(block)
    shapes = (sds((2 * block, D), BF),) * 4 + (sds((1, D), F32),)
    out = call(
        body,
        (4,),
        [plain, plain, turned_spec(block), plain, plain],
        tuple(whole(s) for s in shapes),
        shapes,
        scalars,
        (own, came, tokens, down_own, down_came),
        "first_gain",
        deps=deps,
        stream=True,
    )
    return out[:4], out[4]


def leave_rows(hidden, tokens, grad_state, parts, gain, scalars):
    rows = hidden.shape[0]
    block = rows // 4

    def body(s_ref, h_ref, t_ref, u_ref, g_ref, *refs):
        def work(part):
            refs[4][...] = h_ref[...] + part[block:]
            refs[5][...] = u_ref[...] + norm_grad(t_ref[...], part[:block], g_ref[...])

        each_part(refs[:4], work)

    plain, turn = plain_spec(block), turned_spec(block)
    return call(
        body,
        (4,),
        [plain, turn, plain, whole(gain)] + [whole(p) for p in parts],
        (turn, turn),
        (sds((rows, D), F32),) * 2,
        scalars,
        (hidden, tokens, grad_state, gain, *parts),
        "leave_rows",
        stream=True,
    )


def gain_part(values, grad, name):
    block = grad.shape[0]

    def body(v_ref, p_ref, out_ref):
        values = v_ref[...]
        out_ref[...] = jnp.sum(
            p_ref[...].astype(F32) * (values * scale_of(values)), axis=0, keepdims=True
        )

    return pl.pallas_call(
        body,
        out_shape=sds((1, D), F32),
        grid=(1,),
        in_specs=[pl.BlockSpec((block, D), lambda i: (0, 0))] * 2,
        out_specs=pl.BlockSpec((1, D), lambda i: (0, 0)),
        name=name,
    )(values, grad)


def norm_grad(values, grad, gain):
    factor = scale_of(values)
    unit = values * factor
    scaled = grad * gain
    return factor * (scaled - unit * jnp.mean(scaled * unit, axis=-1, keepdims=True))


def norm_back(values, upstream, parts, gain, scalars, name, deps=()):
    rows = values.shape[0]
    block = rows // 4

    def body(s_ref, v_ref, u_ref, g_ref, *refs):
        def work(part):
            out = u_ref[...] + norm_grad(v_ref[...], part, g_ref[...])
            refs[4][...] = out
            refs[5][...] = out.astype(BF)

        each_part(refs[:4], work)

    plain = plain_spec(block)
    return call(
        body,
        (4,),
        [plain, turned_spec(block), whole(gain)] + [whole(p) for p in parts],
        (plain, plain),
        (sds((rows, D), F32), sds((rows, D), BF)),
        scalars,
        (values, upstream, gain, *parts),
        name,
        deps=deps,
        stream=True,
    )


def tp_total(blocks, deps=()):
    got = [shift(blocks[o], "tp", o) for o in (1, 3, 2)]
    mine = blocks[0].astype(F32)
    for part in got:
        mine = mine + part.astype(F32)
    mine = mine.astype(BF)
    if deps:
        (mine,) = tie((mine,), deps)
    near, far, mid = [shift(mine, "tp", -o) for o in (1, 3, 2)]
    return (mine, near, mid, far)


def heads_total(own, other):
    came = swap(other)
    block = own.shape[0] // 4
    blocks = [
        (own[o * block : (o + 1) * block] + came[o * block : (o + 1) * block].astype(F32)).astype(BF)
        for o in range(4)
    ]
    return tp_total(blocks), blocks


def gate_norm(gate_pre, retained):
    centred = retained - jnp.mean(retained, axis=-1, keepdims=True)
    normed = centred * lax.rsqrt(jnp.mean(centred * centred, axis=-1, keepdims=True) + 1.0 * DK)
    return gate_pre * jax.nn.sigmoid(gate_pre) * normed


def gelu_gate(hidden, linear):
    return jax.nn.gelu(hidden, approximate=True) * linear


def rotate(values, cosine, sine):
    half = DK // 2
    first = values[:, :half]
    second = values[:, half:]
    return jnp.concatenate((first * cosine - second * sine, first * sine + second * cosine), axis=1)


def ein(spec, left, right):
    return jnp.einsum(spec, left, right, preferred_element_type=F32)


def per_device(
    tokens,
    cotangent,
    gain_first,
    gain_second,
    w_query,
    w_key,
    w_value,
    w_gate,
    w_output,
    w_hidden,
    w_linear,
    w_down,
    decay_scale,
    first_length,
):
    rows = tokens.shape[0]
    core = lax.axis_index("core")
    place = lax.axis_index("ctx")
    plane = lax.axis_index("tp")
    scalars = jnp.stack((core, plane, lax.axis_index("x"), place)).astype(jnp.int32)

    w_output = w_output.T
    w_down = w_down.T
    mine, theirs = split_heads((w_value, w_key, w_gate, w_output, w_query), scalars, "split_attn")
    came = swap(theirs)
    block, gathered = stack_attn(mine, came, scalars)
    lengths = jnp.concatenate((first_length, swap(first_length)))
    normed_first = enter_rows(tokens, gain_first.reshape(1, D), scalars, deps=(block,))
    w_kv = stack_blocks(
        spread_near(block), 0, 768, scalars, "stack_kv", deps=(normed_first, lengths)
    )
    w_goq = lax.all_gather(gathered, XY, axis=0, tiled=True).reshape(4, 4, 2, 64, -1)
    mine, theirs = split_heads(
        (w_hidden, w_linear, w_down), scalars, "split_mlp", deps=(gathered,)
    )
    came_mlp = swap(theirs)
    gain_first = gain_first.reshape(1, D)
    gain_second = gain_second.reshape(1, D)
    x_first = (normed_first, swap(normed_first))
    cot_low = low_rows(cotangent, scalars, deps=(x_first[1],))
    g_out = (cot_low, swap(cot_low))
    w_kv = spread_far(w_kv)

    rate = lax.dynamic_index_in_dim(decay_scale, core, 0, False) / 1024.0
    local = (jnp.arange(rows, dtype=jnp.int32) + plane * (rows // 4)) % rows
    index = place * rows + local
    document = (index[None, :] >= lengths[:, None]).astype(jnp.int32)
    carried = (document == 0).astype(F32)
    steps = local.astype(F32)
    offsets = local[:, None] - local[None, :]
    linked = (offsets >= 0)[None] & (document[:, :, None] == document[:, None, :])
    mask = jnp.where(
        linked, jnp.exp(-rate * jnp.maximum(offsets, 0).astype(F32))[None], 0.0
    )
    enter = (carried * jnp.exp(-rate * (steps + 1.0))[None])[:, :, None]
    leave = jnp.exp(-rate * (rows - 1.0 - steps))[None, :, None]
    fade = jnp.exp(-rate * rows)
    half = DK // 2
    frequency = 10000.0 ** (-(jnp.arange(half).astype(F32) / half))
    angles = index.astype(F32)[:, None] * frequency[None, :]
    cosine = jnp.tile(jnp.cos(angles), (2, 1))
    sine = jnp.tile(jnp.sin(angles), (2, 1))

    def carry(came):
        near, mid, far = [part.astype(F32) for part in came]
        return near + fade * (mid + fade * far)

    def spread_state(low, way):
        return [shift_open(low, "ctx", way * o) for o in (1, 2, 3)]

    projected = mm_in(*x_first, [(w_kv, 0, 768)], scalars, "project_kv")
    key = rotate(projected[:, DV:], cosine, sine).astype(BF).reshape(2, rows, DK)
    value = projected[:, :DV].astype(BF).reshape(2, rows, DV)
    key_out = (key.astype(F32) * leave).astype(BF)
    state_out = ein("gjd,gje->gde", key_out, value).astype(BF)
    came = spread_state(state_out, 1)
    w_mlp = lax.all_gather(
        stack_blocks((mine, came_mlp), 0, 1536, scalars, "stack_mlp", deps=came),
        XY,
        axis=0,
        tiled=True,
    ).reshape(4, 4, 2, 64, -1)
    projected = mm_in(
        *x_first, [(w_goq, 0, DV), (w_goq, 1024, DK)], scalars, "project_gq", deps=(state_out, mask, enter)
    )
    state_in = carry(came).astype(BF)
    gate_pre = projected[:, :DV]
    query = rotate(projected[:, DV:], cosine, sine).astype(BF).reshape(2, rows, DK)
    weighted = (ein("gid,gjd->gij", query, key) * mask).astype(BF)
    inner = ein("gij,gje->gie", weighted, value)
    retained = (inner + ein("gid,gde->gie", query, state_in) * enter).reshape(2 * rows, DV)
    mixed_full, gate_back = jax.vjp(gate_norm, gate_pre, retained)
    mixed = mixed_full.astype(BF)
    own, other = mm_back([(mixed, w_goq, DV)], scalars, "project_out")
    parts, _ = heads_total(own, other)
    grad_activated = mm_in(
        *g_out, [(w_mlp, 2 * DV, DV)], scalars, "back_down", deps=(other,)
    )
    hidden_state, normed_second = second_norm(tokens, parts, gain_second, scalars, deps=(grad_activated,))
    x_second = (normed_second, swap(normed_second))
    paired = mm_in(*x_second, [(w_mlp, 0, 2 * DV)], scalars, "project_mlp")
    activated_full, gelu_back = jax.vjp(gelu_gate, paired[:, :DV], paired[:, DV:])
    activated = activated_full.astype(BF)
    grad_pair = jnp.concatenate(gelu_back(grad_activated), axis=1).astype(BF)
    own, other = mm_back([(grad_pair, w_mlp, 0)], scalars, "back_mlp")
    parts, totals = heads_total(own, other)
    down = mm_back([(activated, w_mlp, 2 * DV)], scalars, "project_down", deps=(parts[0],))
    grads, mark = mm_weight(
        None, x_second, grad_pair, 0, scalars, "weight_mlp", deps=(parts[0],)
    )
    grads, mark = mm_weight(grads, g_out, activated, 2 * DV, scalars, "weight_down")
    gain_second_part = gain_part(hidden_state, parts[0], "gain_second")
    grad_state, grad_state_low = norm_back(
        hidden_state,
        cotangent,
        parts,
        gain_second,
        scalars,
        "second_back",
        deps=(down[1], gain_second_part, mark),
    )
    g_state = (grad_state_low, swap(grad_state_low))
    grad_mixed = mm_in(*g_state, [(w_goq, DV, DV)], scalars, "back_out")
    grad_gate, grad_retained = gate_back(grad_mixed)
    grad_low = grad_retained.reshape(2, rows, DV).astype(BF)
    query_in = (query.astype(F32) * enter).astype(BF)
    back_out = ein("gid,gie->gde", query_in, grad_low).astype(BF)
    came = spread_state(back_out, -1)
    grad_scores = (ein("gie,gje->gij", grad_low, value) * mask).astype(BF)
    grad_query = ein("gij,gjd->gid", grad_scores, key) + enter * ein("gie,gde->gid", grad_low, state_in)
    grad_key = ein("gij,gid->gjd", grad_scores, query)
    grad_value = ein("gij,gie->gje", weighted, grad_low)
    grad_gate = grad_gate.astype(BF)
    grad_query = rotate(grad_query.reshape(2 * rows, DK), cosine, -sine).astype(BF)
    grads, mark = mm_weight(
        grads, g_state, mixed, 3 * DV, scalars, "weight_output", deps=(back_out,)
    )
    grads, mark = mm_weight(grads, x_first, grad_gate, 4 * DV, scalars, "weight_gate")
    came[0] = tie((came[0],), (mark, grad_key, grad_value, grad_query))[0]
    state_back = carry(came).astype(BF)
    grad_key += leave * ein("gje,gde->gjd", value, state_back)
    grad_value += ein("gjd,gde->gje", key_out, state_back)
    grad_key = rotate(grad_key.reshape(2 * rows, DK), cosine, -sine)
    grad_vkq = jnp.concatenate(
        (grad_value.reshape(2 * rows, DV).astype(BF), grad_key.astype(BF), grad_query), axis=1
    )
    grads, mark = mm_weight(grads, x_first, grad_vkq, 5 * DV, scalars, "weight_vkq")
    block = lax.psum_scatter(grads.reshape(2048, -1), XY, scatter_dimension=0, tiled=True)
    own, other = mm_back(
        [(grad_vkq[:, : DV + DK], w_kv, 0), (grad_gate, w_goq, 0), (grad_query, w_goq, 1024)],
        scalars,
        "back_attn",
        deps=(mark,),
    )
    down = (down[0], swap(tie((down[1],), (mark,))[0]))
    blocks, gain_first_part = first_gain(own, swap(other), tokens, *down, scalars)
    parts = tp_total(blocks)
    gains = jnp.concatenate((gain_first_part, gain_second_part))
    for axis, swapped in (
        ("core", (1, 0)),
        ("tp", (1, 0, 3, 2)),
        ("tp", (3, 2, 1, 0)),
        ("ctx", (1, 0, 3, 2)),
        ("ctx", (3, 2, 1, 0)),
        ("x", (1, 0, 3, 2)),
        ("x", (3, 2, 1, 0)),
    ):
        if axis == "ctx" and swapped[0] == 1:
            (gains,) = tie((gains,), parts[1:])
        gains = gains + lax.ppermute(gains, axis, list(enumerate(swapped)))
    spot = (lax.axis_index("x") * 2 + core) * 4 + place
    gains = lax.dynamic_slice_in_dim(gains, spot * 64, 64, 1)
    layer_out, input_grad = leave_rows(hidden_state, tokens, grad_state, parts, gain_first, scalars)
    block = tie((block,), (gains, input_grad))[0].reshape(2, 64, -1)
    d_hidden, d_linear, d_down, d_output, d_gate, d_value, d_key, d_query = join_heads(
        block[0], swap(block[1]), (DV,) * 6 + (DK,) * 2, scalars, "join_heads"
    )
    return (
        layer_out,
        input_grad,
        gains[0],
        gains[1],
        d_query,
        d_key,
        d_value,
        d_gate,
        d_output.T,
        d_hidden,
        d_linear,
        d_down.T,
    )


def solution(mesh):
    fine = Mesh(np.asarray(mesh.devices).reshape(4, 2, 4, 4), ("x", "core", "ctx", "tp"))
    split = ("x", "core", "ctx")
    row = P(split, None)
    win = P(split, "tp")
    wout = P("tp", split)
    in_specs = (row, row, P(), P(), win, win, win, win, wout, win, win, wout, P("tp"), P(("x", "core")))
    out_specs = (row, row, P(split), P(split), win, win, win, win, wout, win, win, wout)
    return jax.shard_map(
        per_device, mesh=fine, in_specs=in_specs, out_specs=out_specs, check_vma=False
    )
```

```python
import math

import jax
import jax.numpy as jnp
import numpy as np
from jax import lax
from jax.experimental import pallas as pl
from jax.experimental.pallas import tpu as pltpu
from jax.sharding import Mesh, PartitionSpec as P

D = 2048
DK = 256
DV = 512
SLAB = 512
BF = jnp.bfloat16
F32 = jnp.float32
XY = ("x", "ctx")
MIB = 1 << 20


def shift(value, axis, offset):
    n = lax.axis_size(axis)
    return lax.ppermute(value, axis, [(i, (i + offset) % n) for i in range(n)])


def shift_open(value, axis, offset):
    n = lax.axis_size(axis)
    return lax.ppermute(
        value, axis, [(i, i + offset) for i in range(n) if 0 <= i + offset < n]
    )


def swap(value):
    return lax.ppermute(value, "core", [(0, 1), (1, 0)])


def after(value, *earlier):
    return lax.optimization_barrier((value, *earlier))[0]


def call(
    body,
    grid,
    ins,
    outs,
    shapes,
    scalars,
    operands,
    name,
    scratch=(),
    deps=(),
    stream=False,
    aliases=None,
):
    count = len(operands)

    def kernel(s_ref, *refs):
        body(s_ref, *refs[:count], *refs[count + len(deps) :])

    ins = [*ins, *[pl.BlockSpec(memory_space=pl.ANY)] * len(deps)]
    return pl.pallas_call(
        kernel,
        out_shape=shapes,
        grid_spec=pltpu.PrefetchScalarGridSpec(
            num_scalar_prefetch=1, grid=grid, in_specs=ins, out_specs=outs, scratch_shapes=scratch
        ),
        compiler_params=pltpu.CompilerParams(
            vmem_limit_bytes=(60 if stream else 32) * MIB, dimension_semantics=("arbitrary",) * len(grid)
        ),
        cost_estimate=pl.CostEstimate(flops=1, bytes_accessed=1, transcendentals=0),
        input_output_aliases=aliases or {},
        name=name,
    )(scalars, *operands, *deps)


def tie(values, deps):
    count = len(values)
    anywhere = pl.BlockSpec(memory_space=pl.ANY)
    return pl.pallas_call(
        lambda *refs: None,
        out_shape=tuple(sds(v.shape, v.dtype) for v in values),
        in_specs=[anywhere] * (count + len(deps)),
        out_specs=(anywhere,) * count,
        input_output_aliases={i: i for i in range(count)},
        name="tie",
    )(*values, *deps)


def whole(array):
    return pl.BlockSpec(array.shape, lambda *_: (0,) * array.ndim)


def sds(shape, dtype):
    return jax.ShapeDtypeStruct(shape, dtype)


def weight_operands(weight, start, width):
    if not isinstance(weight, tuple):
        spec = pl.BlockSpec((1, 4, 2, 64, width), lambda i, s: (i, 0, 0, 0, start // width))
        return [weight], [spec]
    piece = math.gcd(start, width) if start else width
    operands, specs = [], []
    for at in range(start, start + width, piece):
        for stack in weight:
            operands.append(stack)
            specs.append(pl.BlockSpec((4, 2, 64, piece), lambda i, s, at=at: (0, 0, 0, at // piece)))
    return operands, specs


def load_slab(s_ref, refs, held):
    core = s_ref[0]
    if len(refs) == 1:
        return jnp.concatenate(
            [refs[0][0, y, jnp.bitwise_xor(c, core)] for c in (0, 1) for y in range(4)], axis=0
        )
    x_far = lax.rem(s_ref[2] + 4 - pl.program_id(0), 4)
    at = 0
    for first in range(0, len(refs), 4):
        stacks = refs[first : first + 4]
        width = stacks[0].shape[-1]
        for j in range(4):

            @pl.when((core == 0) & (x_far == j))
            def _(j=j, at=at, width=width, stacks=stacks):
                for i in range(4):
                    y = lax.rem(s_ref[3] + 4 - i, 4)
                    for c in (0, 1):
                        held[c * 4 + y, :, at : at + width] = stacks[j][i, c]

        @pl.when(core == 1)
        def _(at=at, width=width, stacks=stacks):
            for j in range(4):
                y = lax.rem(s_ref[3] + 4 - j, 4)
                for c in (0, 1):
                    held[c * 4 + y, :, at : at + width] = stacks[j][x_far, 1 - c]

        at += width
    return held[...].reshape(SLAB, at)


def hop(value, first, offset):
    pairs = []
    for x in range(4):
        for core in (0, 1):
            for y in range(4):
                to = ((x + offset) % 4, y) if (core == 0) == first else (x, (y + offset) % 4)
                pairs.append(((x * 2 + core) * 4 + y, (to[0] * 2 + core) * 4 + to[1]))
    return lax.ppermute(value, ("x", "core", "ctx"), pairs)


def spread_near(block):
    near, far, mid = [hop(block, False, o) for o in (1, 3, 2)]
    return block, near, mid, far


def stack_blocks(blocks, start, width, scalars, name, deps=()):
    at = start // width if start % width == 0 else None
    span = width if at is not None else blocks[0].shape[1]
    first = 0 if at is not None else start
    height = blocks[0].shape[0]

    def body(s_ref, *refs):
        for k, ref in enumerate(refs[:-1]):
            refs[-1][k * height : (k + 1) * height, :] = ref[:, first : first + width]

    total = sds((height * len(blocks), width), BF)
    return call(
        body,
        (1,),
        [pl.BlockSpec((height, span), lambda i, s: (0, at or 0))] * len(blocks),
        whole(total),
        total,
        scalars,
        tuple(blocks),
        name,
        deps=deps,
    )


def stack_attn(mine, came, scalars):
    height, total = mine.shape

    def body(s_ref, mine_ref, came_ref, first_ref, other_ref):
        for k, ref in enumerate((mine_ref, came_ref)):
            span = slice(k * height, (k + 1) * height)
            first_ref[span, :] = ref[:, :768]
            other_ref[span, :] = ref[:, 768:]

    shapes = (sds((2 * height, 768), BF), sds((2 * height, total - 768), BF))
    return call(
        body,
        (1,),
        [whole(mine), whole(came)],
        tuple(whole(s) for s in shapes),
        shapes,
        scalars,
        (mine, came),
        "stack_attn",
        stream=True,
    )


def spread_far(stack, gate=False):
    stack = stack.reshape(4, 2, 64, -1)
    near, far = hop(stack, True, 1), hop(stack, True, -1)
    mid = hop(tie((stack,), (near, far))[0] if gate else stack, True, 2)
    return stack, near, mid, far


def send_far(parts, near_after=(), mid_after=()):
    near, far = parts[1], parts[3]
    if near_after:
        near, far = tie((near, far), near_after)
    near, far = hop(near, True, 1), hop(far, True, -1)
    (mid,) = tie((parts[2],), (near, far, *mid_after))
    return near, far, hop(mid, True, 2)


def mm_in(left, right, columns, scalars, name, deps=()):
    operands, specs, counts = [], [], []
    for weight, start, width in columns:
        ops, sp = weight_operands(weight, start, width)
        operands += ops
        specs += sp
        counts.append(len(ops))
    total = sum(width for _, _, width in columns)

    def body(s_ref, a_ref, b_ref, *refs):
        out_ref = refs[len(operands)]
        step = pl.program_id(0)
        rows = jnp.concatenate((a_ref[...], b_ref[...]), axis=0)
        at, first = 0, 0
        for k, count in enumerate(counts):
            width = columns[k][2]
            slab = load_slab(s_ref, refs[first : first + count], refs[len(operands) + 1 + k])
            part = jnp.dot(rows, slab, preferred_element_type=F32)
            span = slice(at, at + width)

            @pl.when(step == 0)
            def _(part=part, span=span):
                out_ref[:, span] = part

            @pl.when(step > 0)
            def _(part=part, span=span):
                out_ref[:, span] += part

            at += width
            first += count

    rows = left.shape[0]
    cols = pl.BlockSpec((rows, SLAB), lambda i, s: (0, i))
    return call(
        body,
        (4,),
        [cols, cols, *specs],
        pl.BlockSpec((2 * rows, total), lambda i, s: (0, 0)),
        sds((2 * rows, total), F32),
        scalars,
        (left, right, *operands),
        name,
        scratch=[pltpu.VMEM((8, 64, width), BF) for _, _, width in columns],
        deps=deps,
    )


def mm_back(terms, scalars, name, deps=()):
    rows = terms[0][0].shape[0]
    half = rows // 2
    operands, specs, counts, scratch = [], [], [], []
    for grad, weight, start in terms:
        ops, sp = weight_operands(weight, start, grad.shape[1])
        operands += [grad, *ops]
        specs += [whole(grad), *sp]
        counts.append(len(ops))
        scratch.append(pltpu.VMEM((8, 64, grad.shape[1]), BF))

    def body(s_ref, *refs):
        own_ref, other_ref = refs[len(operands) : len(operands) + 2]
        at, out = 0, 0.0
        for k, count in enumerate(counts):
            slab = load_slab(s_ref, refs[at + 1 : at + 1 + count], refs[len(operands) + 2 + k])
            out += lax.dot_general(
                refs[at][...], slab, (((1,), (1,)), ((), ())), preferred_element_type=F32
            )
            at += count + 1
        own_ref[...] = out[:half]
        other_ref[...] = out[half:].astype(BF)

    cols = pl.BlockSpec((half, SLAB), lambda i, s: (0, i))
    return call(
        body,
        (4,),
        specs,
        (cols, cols),
        (sds((half, D), F32), sds((half, D), BF)),
        scalars,
        tuple(operands),
        name,
        scratch=scratch,
        deps=deps,
    )


def mm_weight(pairs, scalars, name, deps=()):
    widths = [grad.shape[1] for _, grad in pairs]
    rows = pairs[0][0][0].shape[0]
    count = 3 * len(pairs)
    total = sum(widths)

    def body(s_ref, *refs):
        core = s_ref[0]
        outs, held = refs[count:-1], refs[-1]
        at = 0
        for k, width in enumerate(widths):
            a_ref, b_ref, g_ref = refs[3 * k : 3 * k + 3]
            out = lax.dot_general(
                jnp.concatenate((a_ref[...], b_ref[...]), axis=0),
                g_ref[...],
                (((0,), (0,)), ((), ())),
                preferred_element_type=F32,
            ).astype(BF)
            held[:, :, at : at + width] = out.reshape(8, 64, width)
            at += width
        x_far = lax.rem(pl.program_id(0) + 4 - s_ref[2], 4)
        for k in range(4):

            @pl.when((core == 0) & (x_far == k))
            def _(k=k):
                for j in range(4):
                    y = lax.rem(s_ref[3] + j, 4)
                    for rel in (0, 1):
                        outs[k][j, rel] = held[rel * 4 + y]

        @pl.when(core == 1)
        def _():
            for k in range(4):
                y = lax.rem(s_ref[3] + k, 4)
                for rel in (0, 1):
                    outs[k][x_far, rel] = held[(1 - rel) * 4 + y]

    cols = pl.BlockSpec((rows, SLAB), lambda i, s: (0, i))
    specs, operands = [], []
    for (a, b), grad in pairs:
        specs += [cols, cols, whole(grad)]
        operands += [a, b, grad]
    shapes = (sds((4, 2, 64, total), BF),) * 4
    return call(
        body,
        (4,),
        specs,
        tuple(whole(s) for s in shapes),
        shapes,
        scalars,
        tuple(operands),
        name,
        scratch=[pltpu.VMEM((8, 64, total), BF)],
        deps=deps,
    )


def far_sums(into, parts, got, start, total, scalars, name):
    width = parts[0].shape[-1]
    span = 512

    def body(s_ref, own_ref, near_ref, far_ref, mid_ref, *refs):
        for j in range(4):
            sum_a = own_ref[j].astype(F32) + mid_ref[j].astype(F32)
            sum_b = near_ref[j].astype(F32) + far_ref[j].astype(F32)
            refs[-4 + j][...] = (sum_a + sum_b).astype(BF)

    block = pl.BlockSpec((4, 2, 64, span), lambda j, s: (0, 0, 0, j))
    out = pl.BlockSpec((2, 64, span), lambda j, s: (0, 0, start // span + j))
    operands = (parts[0], *got)
    specs = [block] * 4
    aliases = None
    if into is not None:
        operands += tuple(into)
        specs += [pl.BlockSpec(memory_space=pl.ANY)] * 4
        aliases = {5 + j: j for j in range(4)}
    return call(
        body,
        (width // span,),
        specs,
        (out,) * 4,
        (sds((2, 64, total), BF),) * 4,
        scalars,
        operands,
        name,
        stream=True,
        aliases=aliases,
    )


def split_heads(weights, scalars, name, deps=()):
    widths = [w.shape[1] // 2 for w in weights]

    def body(s_ref, *refs):
        mine_ref, theirs_ref = refs[-2:]
        core = s_ref[0]
        for out_ref, head in ((mine_ref, core), (theirs_ref, 1 - core)):
            at = 0
            for ref, width in zip(refs, widths):
                out_ref[:, at : at + width] = ref[:, pl.ds(pl.multiple_of(head * width, width), width)]
                at += width

    total = sum(widths)
    spec = pl.BlockSpec((64, total), lambda i, s: (0, 0))
    return call(
        body,
        (1,),
        [whole(w) for w in weights],
        (spec, spec),
        (sds((64, total), BF),) * 2,
        scalars,
        tuple(weights),
        name,
        deps=deps,
        stream=True,
    )


def join_heads(mine, theirs, widths, scalars, name):
    def body(s_ref, mine_ref, theirs_ref, *outs):
        core = s_ref[0]
        for in_ref, head in ((mine_ref, core), (theirs_ref, 1 - core)):
            at = 0
            for ref, width in zip(outs, widths):
                span = pl.ds(pl.multiple_of(head * width, width), width)
                ref[:, span] = in_ref[:, at : at + width].astype(F32)
                at += width

    shapes = tuple(sds((64, 2 * w), F32) for w in widths)
    return call(
        body,
        (1,),
        [whole(mine), whole(theirs)],
        tuple(whole(s) for s in shapes),
        shapes,
        scalars,
        (mine, theirs),
        name,
    )


def scale_of(values):
    return lax.rsqrt(jnp.mean(values * values, axis=-1, keepdims=True) + 1e-06)


def turned_spec(rows):
    return pl.BlockSpec((rows, D), lambda i, s: (lax.rem(i + s[1], 4), 0))


def plain_spec(rows):
    return pl.BlockSpec((rows, D), lambda i, s: (i, 0))


def enter_rows(tokens, gain, scalars, deps=()):
    rows = tokens.shape[0]
    block = rows // 4

    def body(s_ref, t_ref, g_ref, n_out):
        values = t_ref[...]
        n_out[...] = (values * scale_of(values) * g_ref[...]).astype(BF)

    return call(
        body,
        (4,),
        [turned_spec(block), whole(gain)],
        plain_spec(block),
        sds((rows, D), BF),
        scalars,
        (tokens, gain),
        "enter_rows",
        deps=deps,
    )


def low_rows(cotangent, scalars, deps=()):
    rows = cotangent.shape[0]
    block = rows // 4

    def body(s_ref, c_ref, l_out):
        l_out[...] = c_ref[...].astype(BF)

    return call(
        body,
        (4,),
        [turned_spec(block)],
        plain_spec(block),
        sds((rows, D), BF),
        scalars,
        (cotangent,),
        "low_rows",
        deps=deps,
    )


def each_part(refs, work):
    step = pl.program_id(0)
    for k, ref in enumerate(refs):

        @pl.when(step == k)
        def _(ref=ref):
            work(ref[...].astype(F32))


def second_norm(tokens, parts, gain, scalars, deps=()):
    rows = tokens.shape[0]
    block = rows // 4

    def body(s_ref, t_ref, g_ref, *refs):
        h_out, n_out = refs[4:]

        def work(part):
            values = t_ref[...] + part
            h_out[...] = values
            n_out[...] = (values * scale_of(values) * g_ref[...]).astype(BF)

        each_part(refs[:4], work)

    plain = plain_spec(block)
    return call(
        body,
        (4,),
        [turned_spec(block), whole(gain)] + [whole(p) for p in parts],
        (plain, plain),
        (sds((rows, D), F32), sds((rows, D), BF)),
        scalars,
        (tokens, gain, *parts),
        "second_norm",
        deps=deps,
        stream=True,
    )


def first_gain(own, came, tokens, down_own, down_came, scalars, deps=()):
    rows = own.shape[0]
    block = rows // 4

    def body(s_ref, own_ref, came_ref, t_ref, d_ref, e_ref, *refs):
        total = own_ref[...] + came_ref[...].astype(F32)
        down = d_ref[...] + e_ref[...].astype(F32)
        values = t_ref[...]
        part = jnp.sum(total * (values * scale_of(values)), axis=0, keepdims=True)
        step = pl.program_id(0)
        for k in range(4):

            @pl.when(step == k)
            def _(k=k):
                refs[k][:block] = total.astype(BF)
                refs[k][block:] = down.astype(BF)

        @pl.when(step == 0)
        def _():
            refs[4][...] = part

        @pl.when(step > 0)
        def _():
            refs[4][...] += part

    plain = plain_spec(block)
    shapes = (sds((2 * block, D), BF),) * 4 + (sds((1, D), F32),)
    out = call(
        body,
        (4,),
        [plain, plain, turned_spec(block), plain, plain],
        tuple(whole(s) for s in shapes),
        shapes,
        scalars,
        (own, came, tokens, down_own, down_came),
        "first_gain",
        deps=deps,
        stream=True,
    )
    return out[:4], out[4]


def leave_rows(hidden, tokens, grad_state, parts, gain, scalars, deps=()):
    rows = hidden.shape[0]
    block = rows // 4

    def body(s_ref, h_ref, t_ref, u_ref, g_ref, *refs):
        def work(part):
            refs[4][...] = h_ref[...] + part[block : 2 * block]
            refs[5][...] = u_ref[...] + norm_grad(t_ref[...], part[:block], g_ref[...])

        each_part(refs[:4], work)

    plain, turn = plain_spec(block), turned_spec(block)
    return call(
        body,
        (4,),
        [plain, turn, plain, whole(gain)] + [whole(p) for p in parts],
        (turn, turn),
        (sds((rows, D), F32),) * 2,
        scalars,
        (hidden, tokens, grad_state, gain, *parts),
        "leave_rows",
        deps=deps,
        stream=True,
    )


def gain_part(values, grad, name):
    block = grad.shape[0]

    def body(v_ref, p_ref, out_ref):
        values = v_ref[...]
        out_ref[...] = jnp.sum(
            p_ref[...].astype(F32) * (values * scale_of(values)), axis=0, keepdims=True
        )

    return pl.pallas_call(
        body,
        out_shape=sds((1, D), F32),
        grid=(1,),
        in_specs=[pl.BlockSpec((block, D), lambda i: (0, 0))] * 2,
        out_specs=pl.BlockSpec((1, D), lambda i: (0, 0)),
        name=name,
    )(values, grad)


def norm_grad(values, grad, gain):
    factor = scale_of(values)
    unit = values * factor
    scaled = grad * gain
    return factor * (scaled - unit * jnp.mean(scaled * unit, axis=-1, keepdims=True))


def norm_back(values, upstream, parts, gain, scalars, name, deps=()):
    rows = values.shape[0]
    block = rows // 4

    def body(s_ref, v_ref, u_ref, g_ref, *refs):
        def work(part):
            out = u_ref[...] + norm_grad(v_ref[...], part, g_ref[...])
            refs[4][...] = out
            refs[5][...] = out.astype(BF)

        each_part(refs[:4], work)

    plain = plain_spec(block)
    return call(
        body,
        (4,),
        [plain, turned_spec(block), whole(gain)] + [whole(p) for p in parts],
        (plain, plain),
        (sds((rows, D), F32), sds((rows, D), BF)),
        scalars,
        (values, upstream, gain, *parts),
        name,
        deps=deps,
        stream=True,
    )


def tp_first(blocks):
    got = [shift(blocks[o], "tp", o) for o in (1, 3, 2)]
    near, far, mid = [part.astype(F32) for part in got]
    return (blocks[0].astype(F32) + mid) + (near + far), got


def tp_second(mine):
    near, far, mid = [shift(mine, "tp", -o) for o in (1, 3, 2)]
    return mine, near, mid, far


def tp_total(blocks):
    return tp_second(tp_first(blocks)[0].astype(BF))


def chip_blocks(own, came):
    block = own.shape[0] // 4
    return [
        (own[o * block : (o + 1) * block] + came[o * block : (o + 1) * block].astype(F32)).astype(BF)
        for o in range(4)
    ]


def gate_norm(gate_pre, retained):
    centred = retained - jnp.mean(retained, axis=-1, keepdims=True)
    normed = centred * lax.rsqrt(jnp.mean(centred * centred, axis=-1, keepdims=True) + 1.0 * DK)
    return gate_pre * jax.nn.sigmoid(gate_pre) * normed


def gelu_gate(hidden, linear):
    return jax.nn.gelu(hidden, approximate=True) * linear


def rotate(values, cosine, sine):
    half = DK // 2
    first = values[:, :half]
    second = values[:, half:]
    return jnp.concatenate((first * cosine - second * sine, first * sine + second * cosine), axis=1)


def ein(spec, left, right):
    return jnp.einsum(spec, left, right, preferred_element_type=F32)


def per_device(
    tokens,
    cotangent,
    gain_first,
    gain_second,
    w_query,
    w_key,
    w_value,
    w_gate,
    w_output,
    w_hidden,
    w_linear,
    w_down,
    decay_scale,
    first_length,
):
    rows = tokens.shape[0]
    core = lax.axis_index("core")
    place = lax.axis_index("ctx")
    plane = lax.axis_index("tp")
    scalars = jnp.stack((core, plane, lax.axis_index("x"), place)).astype(jnp.int32)

    w_output = w_output.T
    w_down = w_down.T
    mine, theirs = split_heads((w_value, w_key, w_gate, w_output, w_query), scalars, "split_attn")
    came = swap(theirs)
    block, gathered = stack_attn(mine, came, scalars)
    lengths = jnp.concatenate((first_length, swap(first_length)))
    normed_first = enter_rows(tokens, gain_first.reshape(1, D), scalars, deps=(block,))
    w_kv = stack_blocks(
        spread_near(block), 0, 768, scalars, "stack_kv", deps=(normed_first, lengths)
    )
    w_goq = lax.all_gather(gathered, XY, axis=0, tiled=True).reshape(4, 4, 2, 64, -1)
    mine, theirs = split_heads(
        (w_hidden, w_linear, w_down), scalars, "split_mlp", deps=(gathered,)
    )
    came_mlp = swap(theirs)
    gain_first = gain_first.reshape(1, D)
    gain_second = gain_second.reshape(1, D)
    x_first = (normed_first, swap(normed_first))
    cot_low = low_rows(cotangent, scalars, deps=(x_first[1],))
    g_out = (cot_low, swap(cot_low))
    w_kv = spread_far(w_kv)

    rate = lax.dynamic_index_in_dim(decay_scale, core, 0, False) / 1024.0
    local = (jnp.arange(rows, dtype=jnp.int32) + plane * (rows // 4)) % rows
    index = place * rows + local
    document = (index[None, :] >= lengths[:, None]).astype(jnp.int32)
    carried = (document == 0).astype(F32)
    steps = local.astype(F32)
    offsets = local[:, None] - local[None, :]
    linked = (offsets >= 0)[None] & (document[:, :, None] == document[:, None, :])
    mask = jnp.where(
        linked, jnp.exp(-rate * jnp.maximum(offsets, 0).astype(F32))[None], 0.0
    )
    enter = (carried * jnp.exp(-rate * (steps + 1.0))[None])[:, :, None]
    leave = jnp.exp(-rate * (rows - 1.0 - steps))[None, :, None]
    fade = jnp.exp(-rate * rows)
    half = DK // 2
    frequency = 10000.0 ** (-(jnp.arange(half).astype(F32) / half))
    angles = index.astype(F32)[:, None] * frequency[None, :]
    cosine = jnp.tile(jnp.cos(angles), (2, 1))
    sine = jnp.tile(jnp.sin(angles), (2, 1))

    def carry(came):
        near, mid, far = [part.astype(F32) for part in came]
        return near + fade * (mid + fade * far)

    def spread_state(low, way):
        return [shift_open(low, "ctx", way * o) for o in (1, 2, 3)]

    projected = mm_in(*x_first, [(w_kv, 0, 768)], scalars, "project_kv")
    key = rotate(projected[:, DV:], cosine, sine).astype(BF).reshape(2, rows, DK)
    value = projected[:, :DV].astype(BF).reshape(2, rows, DV)
    key_out = (key.astype(F32) * leave).astype(BF)
    state_out = ein("gjd,gje->gde", key_out, value).astype(BF)
    came = spread_state(state_out, 1)
    w_mlp = lax.all_gather(
        stack_blocks((mine, came_mlp), 0, 1536, scalars, "stack_mlp", deps=came),
        XY,
        axis=0,
        tiled=True,
    ).reshape(4, 4, 2, 64, -1)
    projected = mm_in(
        *x_first, [(w_goq, 0, DV), (w_goq, 1024, DK)], scalars, "project_gq", deps=(state_out, mask, enter)
    )
    state_in = carry(came).astype(BF)
    gate_pre = projected[:, :DV]
    query = rotate(projected[:, DV:], cosine, sine).astype(BF).reshape(2, rows, DK)
    weighted = (ein("gid,gjd->gij", query, key) * mask).astype(BF)
    inner = ein("gij,gje->gie", weighted, value)
    retained = (inner + ein("gid,gde->gie", query, state_in) * enter).reshape(2 * rows, DV)
    mixed_full, gate_back = jax.vjp(gate_norm, gate_pre, retained)
    mixed = mixed_full.astype(BF)
    own, other = mm_back([(mixed, w_goq, DV)], scalars, "project_out")
    parts = tp_total(chip_blocks(own, swap(other)))
    grad_activated = mm_in(
        *g_out, [(w_mlp, 2 * DV, DV)], scalars, "back_down", deps=(other,)
    )
    hidden_state, normed_second = second_norm(tokens, parts, gain_second, scalars)
    x_second = (normed_second, swap(normed_second))
    paired = mm_in(*x_second, [(w_mlp, 0, 2 * DV)], scalars, "project_mlp")
    activated_full, gelu_back = jax.vjp(gelu_gate, paired[:, :DV], paired[:, DV:])
    activated = activated_full.astype(BF)
    grad_pair = jnp.concatenate(gelu_back(grad_activated), axis=1).astype(BF)
    own, other = mm_back([(grad_pair, w_mlp, 0)], scalars, "back_mlp")
    d_mlp = mm_weight(((x_second, grad_pair), (g_out, activated)), scalars, "weight_mlp")
    mine, _ = tp_first(chip_blocks(own, swap(other)))
    (mine,) = tie((mine.astype(BF),), d_mlp[:1])
    parts = tp_second(mine)
    mlp_got = send_far(d_mlp, (), parts[1:])
    down = mm_back([(activated, w_mlp, 2 * DV)], scalars, "project_down", deps=(mine,))
    gain_second_part = gain_part(hidden_state, mine, "gain_second")
    grad_state, grad_state_low = norm_back(
        hidden_state,
        cotangent,
        parts,
        gain_second,
        scalars,
        "second_back",
        deps=(down[1], gain_second_part, *mlp_got[:2]),
    )
    g_state = (grad_state_low, swap(grad_state_low))
    grad_mixed = mm_in(*g_state, [(w_goq, DV, DV)], scalars, "back_out")
    grad_gate, grad_retained = gate_back(grad_mixed)
    grad_low = grad_retained.reshape(2, rows, DV).astype(BF)
    query_in = (query.astype(F32) * enter).astype(BF)
    back_out = ein("gid,gie->gde", query_in, grad_low).astype(BF)
    came = spread_state(tie((back_out,), mlp_got[2:])[0], -1)
    grad_scores = (ein("gie,gje->gij", grad_low, value) * mask).astype(BF)
    grad_query = ein("gij,gjd->gid", grad_scores, key) + enter * ein("gie,gde->gid", grad_low, state_in)
    grad_key = ein("gij,gid->gjd", grad_scores, query)
    grad_value = ein("gij,gie->gje", weighted, grad_low)
    grad_gate = grad_gate.astype(BF)
    grad_query = rotate(grad_query.reshape(2 * rows, DK), cosine, -sine).astype(BF)
    d_og = mm_weight(
        ((g_state, mixed), (x_first, grad_gate)), scalars, "weight_og", deps=(back_out,)
    )
    sums = far_sums(None, d_mlp, mlp_got, 0, 3584, scalars, "sum_mlp")
    og_got = send_far(d_og, came[:1])
    came[0] = tie((came[0],), (d_og[0], sums[0], grad_key, grad_value, grad_query))[0]
    state_back = carry(came).astype(BF)
    grad_key += leave * ein("gje,gde->gjd", value, state_back)
    grad_value += ein("gjd,gde->gje", key_out, state_back)
    grad_key = rotate(grad_key.reshape(2 * rows, DK), cosine, -sine)
    grad_vkq = jnp.concatenate(
        (grad_value.reshape(2 * rows, DV).astype(BF), grad_key.astype(BF), grad_query), axis=1
    )
    own, other = mm_back(
        [(grad_vkq[:, : DV + DK], w_kv, 0), (grad_gate, w_goq, 0), (grad_query, w_goq, 1024)],
        scalars,
        "back_attn",
        deps=og_got[:2],
    )
    d_vkq = mm_weight(((x_first, grad_vkq),), scalars, "weight_vkq", deps=(other,))
    down = (down[0], swap(tie((down[1],), (state_back,))[0]))
    blocks, gain_first_part = first_gain(
        own, swap(other), tokens, *down, scalars, deps=(d_vkq[0], og_got[2])
    )
    mine, _ = tp_first(blocks)
    vkq_got = send_far(d_vkq)
    gains = jnp.concatenate((gain_first_part, gain_second_part))
    for axis, swapped in (
        ("core", (1, 0)),
        ("ctx", (1, 0, 3, 2)),
        ("ctx", (3, 2, 1, 0)),
        ("x", (1, 0, 3, 2)),
        ("x", (3, 2, 1, 0)),
    ):
        gains = gains + lax.ppermute(gains, axis, list(enumerate(swapped)))
    mine = jnp.concatenate((mine, gains, jnp.zeros((14, D), F32))).astype(BF)
    parts = tp_second(tie((mine,), vkq_got)[0])
    sums = far_sums(sums, d_og, og_got, 1536, 3584, scalars, "sum_og")
    sums = far_sums(sums, d_vkq, vkq_got, 2560, 3584, scalars, "sum_vkq")
    got = [hop(sums[j], False, j) for j in (1, 3, 2)]
    gains = [part[128:130].astype(F32) for part in parts]
    gains = (gains[0] + gains[2]) + (gains[1] + gains[3])
    spot = (lax.axis_index("x") * 2 + core) * 4 + place
    gains = lax.dynamic_slice_in_dim(gains, spot * 64, 64, 1)
    layer_out, input_grad = leave_rows(
        hidden_state, tokens, grad_state, parts, gain_first, scalars
    )
    block = sums[0].astype(F32) + got[2].astype(F32) + (got[0].astype(F32) + got[1].astype(F32))
    d_hidden, d_linear, d_down, d_output, d_gate, d_value, d_key, d_query = join_heads(
        block[0].astype(BF),
        swap(block[1].astype(BF)),
        (DV,) * 6 + (DK,) * 2,
        scalars,
        "join_heads",
    )
    return (
        layer_out,
        input_grad,
        gains[0],
        gains[1],
        d_query,
        d_key,
        d_value,
        d_gate,
        d_output.T,
        d_hidden,
        d_linear,
        d_down.T,
    )


def solution(mesh):
    fine = Mesh(np.asarray(mesh.devices).reshape(4, 2, 4, 4), ("x", "core", "ctx", "tp"))
    split = ("x", "core", "ctx")
    row = P(split, None)
    win = P(split, "tp")
    wout = P("tp", split)
    in_specs = (row, row, P(), P(), win, win, win, win, wout, win, win, wout, P("tp"), P(("x", "core")))
    out_specs = (row, row, P(split), P(split), win, win, win, win, wout, win, win, wout)
    return jax.shard_map(
        per_device, mesh=fine, in_specs=in_specs, out_specs=out_specs, check_vma=False
    )
```

```python
import math

import jax
import jax.numpy as jnp
import numpy as np
from jax import lax
from jax.experimental import pallas as pl
from jax.experimental.pallas import tpu as pltpu
from jax.sharding import Mesh, PartitionSpec as P

D = 2048
DK = 256
DV = 512
SLAB = 512
BF = jnp.bfloat16
F32 = jnp.float32
XY = ("x", "ctx")
MIB = 1 << 20


def shift(value, axis, offset):
    n = lax.axis_size(axis)
    return lax.ppermute(value, axis, [(i, (i + offset) % n) for i in range(n)])


def shift_open(value, axis, offset):
    n = lax.axis_size(axis)
    return lax.ppermute(
        value, axis, [(i, i + offset) for i in range(n) if 0 <= i + offset < n]
    )


def swap(value):
    return lax.ppermute(value, "core", [(0, 1), (1, 0)])


def after(value, *earlier):
    return lax.optimization_barrier((value, *earlier))[0]


def call(
    body,
    grid,
    ins,
    outs,
    shapes,
    scalars,
    operands,
    name,
    scratch=(),
    deps=(),
    stream=False,
    aliases=None,
):
    count = len(operands)

    def kernel(s_ref, *refs):
        body(s_ref, *refs[:count], *refs[count + len(deps) :])

    ins = [*ins, *[pl.BlockSpec(memory_space=pl.ANY)] * len(deps)]
    return pl.pallas_call(
        kernel,
        out_shape=shapes,
        grid_spec=pltpu.PrefetchScalarGridSpec(
            num_scalar_prefetch=1, grid=grid, in_specs=ins, out_specs=outs, scratch_shapes=scratch
        ),
        compiler_params=pltpu.CompilerParams(
            vmem_limit_bytes=(60 if stream else 32) * MIB, dimension_semantics=("arbitrary",) * len(grid)
        ),
        cost_estimate=pl.CostEstimate(flops=1, bytes_accessed=1, transcendentals=0),
        input_output_aliases=aliases or {},
        name=name,
    )(scalars, *operands, *deps)


def tie(values, deps):
    count = len(values)
    anywhere = pl.BlockSpec(memory_space=pl.ANY)
    return pl.pallas_call(
        lambda *refs: None,
        out_shape=tuple(sds(v.shape, v.dtype) for v in values),
        in_specs=[anywhere] * (count + len(deps)),
        out_specs=(anywhere,) * count,
        input_output_aliases={i: i for i in range(count)},
        name="tie",
    )(*values, *deps)


def whole(array):
    return pl.BlockSpec(array.shape, lambda *_: (0,) * array.ndim)


def sds(shape, dtype):
    return jax.ShapeDtypeStruct(shape, dtype)


def weight_operands(weight, start, width):
    if not isinstance(weight, tuple):
        spec = pl.BlockSpec((1, 4, 2, 64, width), lambda i, s: (i, 0, 0, 0, start // width))
        return [weight], [spec]
    piece = math.gcd(start, width) if start else width
    operands, specs = [], []
    for at in range(start, start + width, piece):
        for stack in weight:
            operands.append(stack)
            specs.append(pl.BlockSpec((4, 2, 64, piece), lambda i, s, at=at: (0, 0, 0, at // piece)))
    return operands, specs


def load_slab(s_ref, refs, held):
    core = s_ref[0]
    if len(refs) == 1:
        return jnp.concatenate(
            [refs[0][0, y, jnp.bitwise_xor(c, core)] for c in (0, 1) for y in range(4)], axis=0
        )
    x_far = lax.rem(s_ref[2] + 4 - pl.program_id(0), 4)
    at = 0
    for first in range(0, len(refs), 4):
        stacks = refs[first : first + 4]
        width = stacks[0].shape[-1]
        for j in range(4):

            @pl.when((core == 0) & (x_far == j))
            def _(j=j, at=at, width=width, stacks=stacks):
                for i in range(4):
                    y = lax.rem(s_ref[3] + 4 - i, 4)
                    for c in (0, 1):
                        held[c * 4 + y, :, at : at + width] = stacks[j][i, c]

        @pl.when(core == 1)
        def _(at=at, width=width, stacks=stacks):
            for j in range(4):
                y = lax.rem(s_ref[3] + 4 - j, 4)
                for c in (0, 1):
                    held[c * 4 + y, :, at : at + width] = stacks[j][x_far, 1 - c]

        at += width
    return held[...].reshape(SLAB, at)


def hop(value, first, offset):
    pairs = []
    for x in range(4):
        for core in (0, 1):
            for y in range(4):
                to = ((x + offset) % 4, y) if (core == 0) == first else (x, (y + offset) % 4)
                pairs.append(((x * 2 + core) * 4 + y, (to[0] * 2 + core) * 4 + to[1]))
    return lax.ppermute(value, ("x", "core", "ctx"), pairs)


def spread_near(block):
    near, far, mid = [hop(block, False, o) for o in (1, 3, 2)]
    return block, near, mid, far


def stack_blocks(blocks, start, width, scalars, name, deps=()):
    at = start // width if start % width == 0 else None
    span = width if at is not None else blocks[0].shape[1]
    first = 0 if at is not None else start
    height = blocks[0].shape[0]

    def body(s_ref, *refs):
        for k, ref in enumerate(refs[:-1]):
            refs[-1][k * height : (k + 1) * height, :] = ref[:, first : first + width]

    total = sds((height * len(blocks), width), BF)
    return call(
        body,
        (1,),
        [pl.BlockSpec((height, span), lambda i, s: (0, at or 0))] * len(blocks),
        whole(total),
        total,
        scalars,
        tuple(blocks),
        name,
        deps=deps,
    )


def stack_attn(mine, came, scalars):
    height, total = mine.shape

    def body(s_ref, mine_ref, came_ref, first_ref, other_ref):
        for k, ref in enumerate((mine_ref, came_ref)):
            span = slice(k * height, (k + 1) * height)
            first_ref[span, :] = ref[:, :768]
            other_ref[span, :] = ref[:, 768:]

    shapes = (sds((2 * height, 768), BF), sds((2 * height, total - 768), BF))
    return call(
        body,
        (1,),
        [whole(mine), whole(came)],
        tuple(whole(s) for s in shapes),
        shapes,
        scalars,
        (mine, came),
        "stack_attn",
        stream=True,
    )


def spread_far(stack, gate=False):
    stack = stack.reshape(4, 2, 64, -1)
    near, far = hop(stack, True, 1), hop(stack, True, -1)
    mid = hop(tie((stack,), (near, far))[0] if gate else stack, True, 2)
    return stack, near, mid, far


def send_far(parts, near_after=(), mid_after=()):
    near, far = parts[1], parts[3]
    if near_after:
        near, far = tie((near, far), near_after)
    near, far = hop(near, True, 1), hop(far, True, -1)
    (mid,) = tie((parts[2],), (near, far, *mid_after))
    return near, far, hop(mid, True, 2)


def mm_in(left, right, columns, scalars, name, deps=()):
    operands, specs, counts = [], [], []
    for weight, start, width in columns:
        ops, sp = weight_operands(weight, start, width)
        operands += ops
        specs += sp
        counts.append(len(ops))
    total = sum(width for _, _, width in columns)

    def body(s_ref, a_ref, b_ref, *refs):
        out_ref = refs[len(operands)]
        step = pl.program_id(0)
        rows = jnp.concatenate((a_ref[...], b_ref[...]), axis=0)
        at, first = 0, 0
        for k, count in enumerate(counts):
            width = columns[k][2]
            slab = load_slab(s_ref, refs[first : first + count], refs[len(operands) + 1 + k])
            part = jnp.dot(rows, slab, preferred_element_type=F32)
            span = slice(at, at + width)

            @pl.when(step == 0)
            def _(part=part, span=span):
                out_ref[:, span] = part

            @pl.when(step > 0)
            def _(part=part, span=span):
                out_ref[:, span] += part

            at += width
            first += count

    rows = left.shape[0]
    cols = pl.BlockSpec((rows, SLAB), lambda i, s: (0, i))
    return call(
        body,
        (4,),
        [cols, cols, *specs],
        pl.BlockSpec((2 * rows, total), lambda i, s: (0, 0)),
        sds((2 * rows, total), F32),
        scalars,
        (left, right, *operands),
        name,
        scratch=[pltpu.VMEM((8, 64, width), BF) for _, _, width in columns],
        deps=deps,
    )


def mm_back(terms, scalars, name, deps=()):
    rows = terms[0][0].shape[0]
    half = rows // 2
    operands, specs, counts, scratch = [], [], [], []
    for grad, weight, start in terms:
        ops, sp = weight_operands(weight, start, grad.shape[1])
        operands += [grad, *ops]
        specs += [whole(grad), *sp]
        counts.append(len(ops))
        scratch.append(pltpu.VMEM((8, 64, grad.shape[1]), BF))

    def body(s_ref, *refs):
        own_ref, other_ref = refs[len(operands) : len(operands) + 2]
        at, out = 0, 0.0
        for k, count in enumerate(counts):
            slab = load_slab(s_ref, refs[at + 1 : at + 1 + count], refs[len(operands) + 2 + k])
            out += lax.dot_general(
                refs[at][...], slab, (((1,), (1,)), ((), ())), preferred_element_type=F32
            )
            at += count + 1
        own_ref[...] = out[:half]
        other_ref[...] = out[half:].astype(BF)

    cols = pl.BlockSpec((half, SLAB), lambda i, s: (0, i))
    return call(
        body,
        (4,),
        specs,
        (cols, cols),
        (sds((half, D), F32), sds((half, D), BF)),
        scalars,
        tuple(operands),
        name,
        scratch=scratch,
        deps=deps,
    )


def mm_weight(pairs, scalars, name, deps=()):
    widths = [grad.shape[1] for _, grad in pairs]
    rows = pairs[0][0][0].shape[0]
    count = 3 * len(pairs)
    total = sum(widths)

    def body(s_ref, *refs):
        core = s_ref[0]
        outs, held = refs[count:-1], refs[-1]
        at = 0
        for k, width in enumerate(widths):
            a_ref, b_ref, g_ref = refs[3 * k : 3 * k + 3]
            out = lax.dot_general(
                jnp.concatenate((a_ref[...], b_ref[...]), axis=0),
                g_ref[...],
                (((0,), (0,)), ((), ())),
                preferred_element_type=F32,
            ).astype(BF)
            held[:, :, at : at + width] = out.reshape(8, 64, width)
            at += width
        x_far = lax.rem(pl.program_id(0) + 4 - s_ref[2], 4)
        for k in range(4):

            @pl.when((core == 0) & (x_far == k))
            def _(k=k):
                for j in range(4):
                    y = lax.rem(s_ref[3] + j, 4)
                    for rel in (0, 1):
                        outs[k][j, rel] = held[rel * 4 + y]

        @pl.when(core == 1)
        def _():
            for k in range(4):
                y = lax.rem(s_ref[3] + k, 4)
                for rel in (0, 1):
                    outs[k][x_far, rel] = held[(1 - rel) * 4 + y]

    cols = pl.BlockSpec((rows, SLAB), lambda i, s: (0, i))
    specs, operands = [], []
    for (a, b), grad in pairs:
        specs += [cols, cols, whole(grad)]
        operands += [a, b, grad]
    shapes = (sds((4, 2, 64, total), BF),) * 4
    return call(
        body,
        (4,),
        specs,
        tuple(whole(s) for s in shapes),
        shapes,
        scalars,
        tuple(operands),
        name,
        scratch=[pltpu.VMEM((8, 64, total), BF)],
        deps=deps,
    )


def mm_weight_into(into, pairs, start, total, scalars, name, deps=()):
    widths = [grad.shape[1] for _, grad in pairs]
    rows = pairs[0][0][0].shape[0]
    span = sum(widths)

    def body(s_ref, *refs):
        out_ref, mark_ref = refs[-2:]
        at = 0
        for k, width in enumerate(widths):
            a_ref, b_ref, g_ref = refs[3 * k : 3 * k + 3]
            out = lax.dot_general(
                jnp.concatenate((a_ref[...], b_ref[...]), axis=0),
                g_ref[...],
                (((0,), (0,)), ((), ())),
                preferred_element_type=F32,
            ).astype(BF)
            for c in (0, 1):
                for y in range(4):
                    first = (c * 4 + y) * 64
                    out_ref[0, y, jnp.bitwise_xor(c, s_ref[0]), :, at : at + width] = out[
                        first : first + 64
                    ]
            at += width
        mark_ref[...] = jnp.zeros_like(mark_ref)

    cols = pl.BlockSpec((rows, SLAB), lambda i, s: (0, i))
    specs, operands = [], []
    for (a, b), grad in pairs:
        specs += [cols, cols, whole(grad)]
        operands += [a, b, grad]
    aliases = None
    if into is not None:
        aliases = {1 + len(operands): 0}
        specs.append(pl.BlockSpec(memory_space=pl.ANY))
        operands.append(into)
    return call(
        body,
        (4,),
        specs,
        (
            pl.BlockSpec((1, 4, 2, 64, span), lambda i, s: (i, 0, 0, 0, start // span)),
            pl.BlockSpec((8, 128), lambda i, s: (0, 0)),
        ),
        (sds((4, 4, 2, 64, total), BF), sds((8, 128), F32)),
        scalars,
        tuple(operands),
        name,
        deps=deps,
        stream=True,
        aliases=aliases,
    )


def far_sums(parts, got, scalars, name):
    width = parts[0].shape[-1]
    span = 512

    def body(s_ref, own_ref, near_ref, far_ref, mid_ref, *refs):
        for j in range(4):
            sum_a = own_ref[j].astype(F32) + mid_ref[j].astype(F32)
            sum_b = near_ref[j].astype(F32) + far_ref[j].astype(F32)
            refs[j][...] = (sum_a + sum_b).astype(BF)

    return call(
        body,
        (width // span,),
        [pl.BlockSpec((4, 2, 64, span), lambda j, s: (0, 0, 0, j))] * 4,
        (pl.BlockSpec((2, 64, span), lambda j, s: (0, 0, j)),) * 4,
        (sds((2, 64, width), BF),) * 4,
        scalars,
        (parts[0], *got),
        name,
        stream=True,
    )


def split_heads(weights, scalars, name, deps=()):
    widths = [w.shape[1] // 2 for w in weights]

    def body(s_ref, *refs):
        mine_ref, theirs_ref = refs[-2:]
        core = s_ref[0]
        for out_ref, head in ((mine_ref, core), (theirs_ref, 1 - core)):
            at = 0
            for ref, width in zip(refs, widths):
                out_ref[:, at : at + width] = ref[:, pl.ds(pl.multiple_of(head * width, width), width)]
                at += width

    total = sum(widths)
    spec = pl.BlockSpec((64, total), lambda i, s: (0, 0))
    return call(
        body,
        (1,),
        [whole(w) for w in weights],
        (spec, spec),
        (sds((64, total), BF),) * 2,
        scalars,
        tuple(weights),
        name,
        deps=deps,
        stream=True,
    )


def join_heads(mine, theirs, widths, scalars, name):
    def body(s_ref, mine_ref, theirs_ref, *outs):
        core = s_ref[0]
        for in_ref, head in ((mine_ref, core), (theirs_ref, 1 - core)):
            at = 0
            for ref, width in zip(outs, widths):
                span = pl.ds(pl.multiple_of(head * width, width), width)
                ref[:, span] = in_ref[:, at : at + width].astype(F32)
                at += width

    shapes = tuple(sds((64, 2 * w), F32) for w in widths)
    return call(
        body,
        (1,),
        [whole(mine), whole(theirs)],
        tuple(whole(s) for s in shapes),
        shapes,
        scalars,
        (mine, theirs),
        name,
    )


def scale_of(values):
    return lax.rsqrt(jnp.mean(values * values, axis=-1, keepdims=True) + 1e-06)


def turned_spec(rows):
    return pl.BlockSpec((rows, D), lambda i, s: (lax.rem(i + s[1], 4), 0))


def plain_spec(rows):
    return pl.BlockSpec((rows, D), lambda i, s: (i, 0))


def enter_rows(tokens, gain, scalars, deps=()):
    rows = tokens.shape[0]
    block = rows // 4

    def body(s_ref, t_ref, g_ref, n_out):
        values = t_ref[...]
        n_out[...] = (values * scale_of(values) * g_ref[...]).astype(BF)

    return call(
        body,
        (4,),
        [turned_spec(block), whole(gain)],
        plain_spec(block),
        sds((rows, D), BF),
        scalars,
        (tokens, gain),
        "enter_rows",
        deps=deps,
    )


def low_rows(cotangent, scalars, deps=()):
    rows = cotangent.shape[0]
    block = rows // 4

    def body(s_ref, c_ref, l_out):
        l_out[...] = c_ref[...].astype(BF)

    return call(
        body,
        (4,),
        [turned_spec(block)],
        plain_spec(block),
        sds((rows, D), BF),
        scalars,
        (cotangent,),
        "low_rows",
        deps=deps,
    )


def each_part(refs, work):
    step = pl.program_id(0)
    for k, ref in enumerate(refs):

        @pl.when(step == k)
        def _(ref=ref):
            work(ref[...].astype(F32))


def second_norm(tokens, parts, gain, scalars, deps=()):
    rows = tokens.shape[0]
    block = rows // 4

    def body(s_ref, t_ref, g_ref, *refs):
        h_out, n_out = refs[4:]

        def work(part):
            values = t_ref[...] + part
            h_out[...] = values
            n_out[...] = (values * scale_of(values) * g_ref[...]).astype(BF)

        each_part(refs[:4], work)

    plain = plain_spec(block)
    return call(
        body,
        (4,),
        [turned_spec(block), whole(gain)] + [whole(p) for p in parts],
        (plain, plain),
        (sds((rows, D), F32), sds((rows, D), BF)),
        scalars,
        (tokens, gain, *parts),
        "second_norm",
        deps=deps,
        stream=True,
    )


def first_gain(own, came, tokens, down_own, down_came, scalars, deps=()):
    rows = own.shape[0]
    block = rows // 4

    def body(s_ref, own_ref, came_ref, t_ref, d_ref, e_ref, *refs):
        total = own_ref[...] + came_ref[...].astype(F32)
        down = d_ref[...] + e_ref[...].astype(F32)
        values = t_ref[...]
        part = jnp.sum(total * (values * scale_of(values)), axis=0, keepdims=True)
        step = pl.program_id(0)
        for k in range(4):

            @pl.when(step == k)
            def _(k=k):
                refs[k][:block] = total.astype(BF)
                refs[k][block:] = down.astype(BF)

        @pl.when(step == 0)
        def _():
            refs[4][...] = part

        @pl.when(step > 0)
        def _():
            refs[4][...] += part

    plain = plain_spec(block)
    shapes = (sds((2 * block, D), BF),) * 4 + (sds((1, D), F32),)
    out = call(
        body,
        (4,),
        [plain, plain, turned_spec(block), plain, plain],
        tuple(whole(s) for s in shapes),
        shapes,
        scalars,
        (own, came, tokens, down_own, down_came),
        "first_gain",
        deps=deps,
        stream=True,
    )
    return out[:4], out[4]


def leave_rows(hidden, tokens, grad_state, parts, gain, scalars, deps=()):
    rows = hidden.shape[0]
    block = rows // 4

    def body(s_ref, h_ref, t_ref, u_ref, g_ref, *refs):
        def work(part):
            refs[4][...] = h_ref[...] + part[block : 2 * block]
            refs[5][...] = u_ref[...] + norm_grad(t_ref[...], part[:block], g_ref[...])

        each_part(refs[:4], work)

    plain, turn = plain_spec(block), turned_spec(block)
    return call(
        body,
        (4,),
        [plain, turn, plain, whole(gain)] + [whole(p) for p in parts],
        (turn, turn),
        (sds((rows, D), F32),) * 2,
        scalars,
        (hidden, tokens, grad_state, gain, *parts),
        "leave_rows",
        deps=deps,
        stream=True,
    )


def gain_part(values, grad, name):
    block = grad.shape[0]

    def body(v_ref, p_ref, out_ref):
        values = v_ref[...]
        out_ref[...] = jnp.sum(
            p_ref[...].astype(F32) * (values * scale_of(values)), axis=0, keepdims=True
        )

    return pl.pallas_call(
        body,
        out_shape=sds((1, D), F32),
        grid=(1,),
        in_specs=[pl.BlockSpec((block, D), lambda i: (0, 0))] * 2,
        out_specs=pl.BlockSpec((1, D), lambda i: (0, 0)),
        name=name,
    )(values, grad)


def norm_grad(values, grad, gain):
    factor = scale_of(values)
    unit = values * factor
    scaled = grad * gain
    return factor * (scaled - unit * jnp.mean(scaled * unit, axis=-1, keepdims=True))


def norm_back(values, upstream, parts, gain, scalars, name, deps=()):
    rows = values.shape[0]
    block = rows // 4

    def body(s_ref, v_ref, u_ref, g_ref, *refs):
        def work(part):
            out = u_ref[...] + norm_grad(v_ref[...], part, g_ref[...])
            refs[4][...] = out
            refs[5][...] = out.astype(BF)

        each_part(refs[:4], work)

    plain = plain_spec(block)
    return call(
        body,
        (4,),
        [plain, turned_spec(block), whole(gain)] + [whole(p) for p in parts],
        (plain, plain),
        (sds((rows, D), F32), sds((rows, D), BF)),
        scalars,
        (values, upstream, gain, *parts),
        name,
        deps=deps,
        stream=True,
    )


def tp_first(blocks):
    got = [shift(blocks[o], "tp", o) for o in (1, 3, 2)]
    near, far, mid = [part.astype(F32) for part in got]
    return (blocks[0].astype(F32) + mid) + (near + far), got


def tp_second(mine):
    near, far, mid = [shift(mine, "tp", -o) for o in (1, 3, 2)]
    return mine, near, mid, far


def tp_total(blocks):
    return tp_second(tp_first(blocks)[0].astype(BF))


def chip_blocks(own, came):
    block = own.shape[0] // 4
    return [
        (own[o * block : (o + 1) * block] + came[o * block : (o + 1) * block].astype(F32)).astype(BF)
        for o in range(4)
    ]


def gate_norm(gate_pre, retained):
    centred = retained - jnp.mean(retained, axis=-1, keepdims=True)
    normed = centred * lax.rsqrt(jnp.mean(centred * centred, axis=-1, keepdims=True) + 1.0 * DK)
    return gate_pre * jax.nn.sigmoid(gate_pre) * normed


def gelu_gate(hidden, linear):
    return jax.nn.gelu(hidden, approximate=True) * linear


def rotate(values, cosine, sine):
    half = DK // 2
    first = values[:, :half]
    second = values[:, half:]
    return jnp.concatenate((first * cosine - second * sine, first * sine + second * cosine), axis=1)


def ein(spec, left, right):
    return jnp.einsum(spec, left, right, preferred_element_type=F32)


def per_device(
    tokens,
    cotangent,
    gain_first,
    gain_second,
    w_query,
    w_key,
    w_value,
    w_gate,
    w_output,
    w_hidden,
    w_linear,
    w_down,
    decay_scale,
    first_length,
):
    rows = tokens.shape[0]
    core = lax.axis_index("core")
    place = lax.axis_index("ctx")
    plane = lax.axis_index("tp")
    scalars = jnp.stack((core, plane, lax.axis_index("x"), place)).astype(jnp.int32)

    w_output = w_output.T
    w_down = w_down.T
    mine, theirs = split_heads((w_value, w_key, w_gate, w_output, w_query), scalars, "split_attn")
    came = swap(theirs)
    block, gathered = stack_attn(mine, came, scalars)
    lengths = jnp.concatenate((first_length, swap(first_length)))
    normed_first = enter_rows(tokens, gain_first.reshape(1, D), scalars, deps=(block,))
    w_kv = stack_blocks(
        spread_near(block), 0, 768, scalars, "stack_kv", deps=(normed_first, lengths)
    )
    w_goq = lax.all_gather(gathered, XY, axis=0, tiled=True).reshape(4, 4, 2, 64, -1)
    mine, theirs = split_heads(
        (w_hidden, w_linear, w_down), scalars, "split_mlp", deps=(gathered,)
    )
    came_mlp = swap(theirs)
    gain_first = gain_first.reshape(1, D)
    gain_second = gain_second.reshape(1, D)
    x_first = (normed_first, swap(normed_first))
    cot_low = low_rows(cotangent, scalars, deps=(x_first[1],))
    g_out = (cot_low, swap(cot_low))
    w_kv = spread_far(w_kv)

    rate = lax.dynamic_index_in_dim(decay_scale, core, 0, False) / 1024.0
    local = (jnp.arange(rows, dtype=jnp.int32) + plane * (rows // 4)) % rows
    index = place * rows + local
    document = (index[None, :] >= lengths[:, None]).astype(jnp.int32)
    carried = (document == 0).astype(F32)
    steps = local.astype(F32)
    offsets = local[:, None] - local[None, :]
    linked = (offsets >= 0)[None] & (document[:, :, None] == document[:, None, :])
    mask = jnp.where(
        linked, jnp.exp(-rate * jnp.maximum(offsets, 0).astype(F32))[None], 0.0
    )
    enter = (carried * jnp.exp(-rate * (steps + 1.0))[None])[:, :, None]
    leave = jnp.exp(-rate * (rows - 1.0 - steps))[None, :, None]
    fade = jnp.exp(-rate * rows)
    half = DK // 2
    frequency = 10000.0 ** (-(jnp.arange(half).astype(F32) / half))
    angles = index.astype(F32)[:, None] * frequency[None, :]
    cosine = jnp.tile(jnp.cos(angles), (2, 1))
    sine = jnp.tile(jnp.sin(angles), (2, 1))

    def carry(came):
        near, mid, far = [part.astype(F32) for part in came]
        return near + fade * (mid + fade * far)

    def spread_state(low, way):
        return [shift_open(low, "ctx", way * o) for o in (1, 2, 3)]

    projected = mm_in(*x_first, [(w_kv, 0, 768)], scalars, "project_kv")
    key = rotate(projected[:, DV:], cosine, sine).astype(BF).reshape(2, rows, DK)
    value = projected[:, :DV].astype(BF).reshape(2, rows, DV)
    key_out = (key.astype(F32) * leave).astype(BF)
    state_out = ein("gjd,gje->gde", key_out, value).astype(BF)
    came = spread_state(state_out, 1)
    w_mlp = lax.all_gather(
        stack_blocks((mine, came_mlp), 0, 1536, scalars, "stack_mlp", deps=came),
        XY,
        axis=0,
        tiled=True,
    ).reshape(4, 4, 2, 64, -1)
    projected = mm_in(
        *x_first, [(w_goq, 0, DV), (w_goq, 1024, DK)], scalars, "project_gq", deps=(state_out, mask, enter)
    )
    state_in = carry(came).astype(BF)
    gate_pre = projected[:, :DV]
    query = rotate(projected[:, DV:], cosine, sine).astype(BF).reshape(2, rows, DK)
    weighted = (ein("gid,gjd->gij", query, key) * mask).astype(BF)
    inner = ein("gij,gje->gie", weighted, value)
    retained = (inner + ein("gid,gde->gie", query, state_in) * enter).reshape(2 * rows, DV)
    mixed_full, gate_back = jax.vjp(gate_norm, gate_pre, retained)
    mixed = mixed_full.astype(BF)
    own, other = mm_back([(mixed, w_goq, DV)], scalars, "project_out")
    parts = tp_total(chip_blocks(own, swap(other)))
    grad_activated = mm_in(
        *g_out, [(w_mlp, 2 * DV, DV)], scalars, "back_down", deps=(other,)
    )
    hidden_state, normed_second = second_norm(tokens, parts, gain_second, scalars)
    x_second = (normed_second, swap(normed_second))
    paired = mm_in(*x_second, [(w_mlp, 0, 2 * DV)], scalars, "project_mlp")
    activated_full, gelu_back = jax.vjp(gelu_gate, paired[:, :DV], paired[:, DV:])
    activated = activated_full.astype(BF)
    grad_pair = jnp.concatenate(gelu_back(grad_activated), axis=1).astype(BF)
    own, other = mm_back([(grad_pair, w_mlp, 0)], scalars, "back_mlp")
    grads, mark = mm_weight_into(
        None, ((x_second, grad_pair),), 1024, 2560, scalars, "weight_mlp"
    )
    mine, _ = tp_first(chip_blocks(own, swap(other)))
    (mine,) = tie((mine.astype(BF),), (mark,))
    parts = tp_second(mine)
    grads, mark = mm_weight_into(
        grads, ((g_out, activated),), 2048, 2560, scalars, "weight_down", deps=(mine,)
    )
    down = mm_back([(activated, w_mlp, 2 * DV)], scalars, "project_down", deps=(mine,))
    gain_second_part = gain_part(hidden_state, mine, "gain_second")
    grad_state, grad_state_low = norm_back(
        hidden_state,
        cotangent,
        parts,
        gain_second,
        scalars,
        "second_back",
        deps=(down[1], gain_second_part, mark),
    )
    g_state = (grad_state_low, swap(grad_state_low))
    grad_mixed = mm_in(*g_state, [(w_goq, DV, DV)], scalars, "back_out")
    grad_gate, grad_retained = gate_back(grad_mixed)
    grad_low = grad_retained.reshape(2, rows, DV).astype(BF)
    query_in = (query.astype(F32) * enter).astype(BF)
    back_out = ein("gid,gie->gde", query_in, grad_low).astype(BF)
    came = spread_state(back_out, -1)
    grad_scores = (ein("gie,gje->gij", grad_low, value) * mask).astype(BF)
    grad_query = ein("gij,gjd->gid", grad_scores, key) + enter * ein("gie,gde->gid", grad_low, state_in)
    grad_key = ein("gij,gid->gjd", grad_scores, query)
    grad_value = ein("gij,gie->gje", weighted, grad_low)
    grad_gate = grad_gate.astype(BF)
    grad_query = rotate(grad_query.reshape(2 * rows, DK), cosine, -sine).astype(BF)
    grads, mark = mm_weight_into(
        grads,
        ((g_state, mixed), (x_first, grad_gate)),
        0,
        2560,
        scalars,
        "weight_og",
        deps=(back_out,),
    )
    rest = lax.psum_scatter(grads.reshape(2048, -1), XY, scatter_dimension=0, tiled=True)
    came[0] = tie((came[0],), (mark, grad_key, grad_value, grad_query))[0]
    state_back = carry(came).astype(BF)
    grad_key += leave * ein("gje,gde->gjd", value, state_back)
    grad_value += ein("gjd,gde->gje", key_out, state_back)
    grad_key = rotate(grad_key.reshape(2 * rows, DK), cosine, -sine)
    grad_vk = jnp.concatenate(
        (grad_value.reshape(2 * rows, DV).astype(BF), grad_key.astype(BF)), axis=1
    )
    own, other = mm_back(
        [(grad_vk, w_kv, 0), (grad_gate, w_goq, 0), (grad_query, w_goq, 1024)],
        scalars,
        "back_attn",
    )
    d_vkq = mm_weight(
        ((x_first, grad_vk), (x_first, grad_query)), scalars, "weight_vkq", deps=(other,)
    )
    down = (down[0], swap(tie((down[1],), (state_back,))[0]))
    blocks, gain_first_part = first_gain(
        own, swap(other), tokens, *down, scalars, deps=(d_vkq[0],)
    )
    mine, _ = tp_first(blocks)
    vkq_got = send_far(d_vkq, (), (mine,))
    gains = jnp.concatenate((gain_first_part, gain_second_part))
    for axis, swapped in (
        ("core", (1, 0)),
        ("ctx", (1, 0, 3, 2)),
        ("ctx", (3, 2, 1, 0)),
        ("x", (1, 0, 3, 2)),
        ("x", (3, 2, 1, 0)),
    ):
        gains = gains + lax.ppermute(gains, axis, list(enumerate(swapped)))
    mine = jnp.concatenate((mine, gains, jnp.zeros((14, D), F32))).astype(BF)
    parts = tp_second(tie((mine,), vkq_got[:2])[0])
    sums = far_sums(d_vkq, vkq_got, scalars, "sum_vkq")
    got = [hop(sums[j], False, j) for j in (1, 3, 2)]
    gains = [part[128:130].astype(F32) for part in parts]
    gains = (gains[0] + gains[2]) + (gains[1] + gains[3])
    spot = (lax.axis_index("x") * 2 + core) * 4 + place
    gains = lax.dynamic_slice_in_dim(gains, spot * 64, 64, 1)
    layer_out, input_grad = leave_rows(
        hidden_state, tokens, grad_state, parts, gain_first, scalars
    )
    block = sums[0].astype(F32) + got[2].astype(F32) + (got[0].astype(F32) + got[1].astype(F32))
    d_value, d_key, d_query = join_heads(
        block[0].astype(BF), swap(block[1].astype(BF)), (DV, DK, DK), scalars, "join_vkq"
    )
    rest = tie((rest,), (gains, input_grad, d_value))[0].reshape(2, 64, -1)
    d_output, d_gate, d_hidden, d_linear, d_down = join_heads(
        rest[0], swap(rest[1]), (DV,) * 5, scalars, "join_rest"
    )
    return (
        layer_out,
        input_grad,
        gains[0],
        gains[1],
        d_query,
        d_key,
        d_value,
        d_gate,
        d_output.T,
        d_hidden,
        d_linear,
        d_down.T,
    )


def solution(mesh):
    fine = Mesh(np.asarray(mesh.devices).reshape(4, 2, 4, 4), ("x", "core", "ctx", "tp"))
    split = ("x", "core", "ctx")
    row = P(split, None)
    win = P(split, "tp")
    wout = P("tp", split)
    in_specs = (row, row, P(), P(), win, win, win, win, wout, win, win, wout, P("tp"), P(("x", "core")))
    out_specs = (row, row, P(split), P(split), win, win, win, win, wout, win, win, wout)
    return jax.shard_map(
        per_device, mesh=fine, in_specs=in_specs, out_specs=out_specs, check_vma=False
    )
```

```python
import math

import jax
import jax.numpy as jnp
import numpy as np
from jax import lax
from jax.experimental import pallas as pl
from jax.experimental.pallas import tpu as pltpu
from jax.sharding import Mesh, PartitionSpec as P

D = 2048
DK = 256
DV = 512
SLAB = 512
BF = jnp.bfloat16
F32 = jnp.float32
XY = ("x", "ctx")
MIB = 1 << 20


def shift(value, axis, offset):
    n = lax.axis_size(axis)
    return lax.ppermute(value, axis, [(i, (i + offset) % n) for i in range(n)])


def shift_open(value, axis, offset):
    n = lax.axis_size(axis)
    return lax.ppermute(
        value, axis, [(i, i + offset) for i in range(n) if 0 <= i + offset < n]
    )


def swap(value):
    return lax.ppermute(value, "core", [(0, 1), (1, 0)])


def after(value, *earlier):
    return lax.optimization_barrier((value, *earlier))[0]


def call(
    body,
    grid,
    ins,
    outs,
    shapes,
    scalars,
    operands,
    name,
    scratch=(),
    deps=(),
    stream=False,
    aliases=None,
):
    count = len(operands)

    def kernel(s_ref, *refs):
        body(s_ref, *refs[:count], *refs[count + len(deps) :])

    ins = [*ins, *[pl.BlockSpec(memory_space=pl.ANY)] * len(deps)]
    return pl.pallas_call(
        kernel,
        out_shape=shapes,
        grid_spec=pltpu.PrefetchScalarGridSpec(
            num_scalar_prefetch=1, grid=grid, in_specs=ins, out_specs=outs, scratch_shapes=scratch
        ),
        compiler_params=pltpu.CompilerParams(
            vmem_limit_bytes=(60 if stream else 32) * MIB, dimension_semantics=("arbitrary",) * len(grid)
        ),
        cost_estimate=pl.CostEstimate(flops=1, bytes_accessed=1, transcendentals=0),
        input_output_aliases=aliases or {},
        name=name,
    )(scalars, *operands, *deps)


def tie(values, deps):
    count = len(values)
    anywhere = pl.BlockSpec(memory_space=pl.ANY)
    return pl.pallas_call(
        lambda *refs: None,
        out_shape=tuple(sds(v.shape, v.dtype) for v in values),
        in_specs=[anywhere] * (count + len(deps)),
        out_specs=(anywhere,) * count,
        input_output_aliases={i: i for i in range(count)},
        name="tie",
    )(*values, *deps)


def whole(array):
    return pl.BlockSpec(array.shape, lambda *_: (0,) * array.ndim)


def sds(shape, dtype):
    return jax.ShapeDtypeStruct(shape, dtype)


def weight_operands(weight, start, width):
    if not isinstance(weight, tuple):
        spec = pl.BlockSpec((1, 4, 2, 64, width), lambda i, s: (i, 0, 0, 0, start // width))
        return [weight], [spec]
    piece = math.gcd(start, width) if start else width
    operands, specs = [], []
    for at in range(start, start + width, piece):
        for stack in weight:
            operands.append(stack)
            specs.append(pl.BlockSpec((4, 2, 64, piece), lambda i, s, at=at: (0, 0, 0, at // piece)))
    return operands, specs


def load_slab(s_ref, refs, held):
    core = s_ref[0]
    if len(refs) == 1:
        return jnp.concatenate(
            [refs[0][0, y, jnp.bitwise_xor(c, core)] for c in (0, 1) for y in range(4)], axis=0
        )
    x_far = lax.rem(s_ref[2] + 4 - pl.program_id(0), 4)
    at = 0
    for first in range(0, len(refs), 4):
        stacks = refs[first : first + 4]
        width = stacks[0].shape[-1]
        for j in range(4):

            @pl.when((core == 0) & (x_far == j))
            def _(j=j, at=at, width=width, stacks=stacks):
                for i in range(4):
                    y = lax.rem(s_ref[3] + 4 - i, 4)
                    for c in (0, 1):
                        held[c * 4 + y, :, at : at + width] = stacks[j][i, c]

        @pl.when(core == 1)
        def _(at=at, width=width, stacks=stacks):
            for j in range(4):
                y = lax.rem(s_ref[3] + 4 - j, 4)
                for c in (0, 1):
                    held[c * 4 + y, :, at : at + width] = stacks[j][x_far, 1 - c]

        at += width
    return held[...].reshape(SLAB, at)


def hop(value, first, offset):
    pairs = []
    for x in range(4):
        for core in (0, 1):
            for y in range(4):
                to = ((x + offset) % 4, y) if (core == 0) == first else (x, (y + offset) % 4)
                pairs.append(((x * 2 + core) * 4 + y, (to[0] * 2 + core) * 4 + to[1]))
    return lax.ppermute(value, ("x", "core", "ctx"), pairs)


def spread_near(block):
    near, far, mid = [hop(block, False, o) for o in (1, 3, 2)]
    return block, near, mid, far


def stack_blocks(blocks, start, width, scalars, name, deps=()):
    at = start // width if start % width == 0 else None
    span = width if at is not None else blocks[0].shape[1]
    first = 0 if at is not None else start
    height = blocks[0].shape[0]

    def body(s_ref, *refs):
        for k, ref in enumerate(refs[:-1]):
            refs[-1][k * height : (k + 1) * height, :] = ref[:, first : first + width]

    total = sds((height * len(blocks), width), BF)
    return call(
        body,
        (1,),
        [pl.BlockSpec((height, span), lambda i, s: (0, at or 0))] * len(blocks),
        whole(total),
        total,
        scalars,
        tuple(blocks),
        name,
        deps=deps,
    )


def stack_attn(mine, came, scalars):
    height, total = mine.shape

    def body(s_ref, mine_ref, came_ref, first_ref, other_ref):
        for k, ref in enumerate((mine_ref, came_ref)):
            span = slice(k * height, (k + 1) * height)
            first_ref[span, :] = ref[:, :768]
            other_ref[span, :] = ref[:, 768:]

    shapes = (sds((2 * height, 768), BF), sds((2 * height, total - 768), BF))
    return call(
        body,
        (1,),
        [whole(mine), whole(came)],
        tuple(whole(s) for s in shapes),
        shapes,
        scalars,
        (mine, came),
        "stack_attn",
        stream=True,
    )


def spread_far(stack, gate=False):
    stack = stack.reshape(4, 2, 64, -1)
    near, far = hop(stack, True, 1), hop(stack, True, -1)
    mid = hop(tie((stack,), (near, far))[0] if gate else stack, True, 2)
    return stack, near, mid, far


def send_far(parts, near_after=(), mid_after=()):
    near, far = parts[1], parts[3]
    if near_after:
        near, far = tie((near, far), near_after)
    near, far = hop(near, True, 1), hop(far, True, -1)
    (mid,) = tie((parts[2],), (near, far, *mid_after))
    return near, far, hop(mid, True, 2)


def mm_in(left, right, columns, scalars, name, deps=()):
    operands, specs, counts = [], [], []
    for weight, start, width in columns:
        ops, sp = weight_operands(weight, start, width)
        operands += ops
        specs += sp
        counts.append(len(ops))
    total = sum(width for _, _, width in columns)

    def body(s_ref, a_ref, b_ref, *refs):
        out_ref = refs[len(operands)]
        step = pl.program_id(0)
        rows = jnp.concatenate((a_ref[...], b_ref[...]), axis=0)
        at, first = 0, 0
        for k, count in enumerate(counts):
            width = columns[k][2]
            slab = load_slab(s_ref, refs[first : first + count], refs[len(operands) + 1 + k])
            part = jnp.dot(rows, slab, preferred_element_type=F32)
            span = slice(at, at + width)

            @pl.when(step == 0)
            def _(part=part, span=span):
                out_ref[:, span] = part

            @pl.when(step > 0)
            def _(part=part, span=span):
                out_ref[:, span] += part

            at += width
            first += count

    rows = left.shape[0]
    cols = pl.BlockSpec((rows, SLAB), lambda i, s: (0, i))
    return call(
        body,
        (4,),
        [cols, cols, *specs],
        pl.BlockSpec((2 * rows, total), lambda i, s: (0, 0)),
        sds((2 * rows, total), F32),
        scalars,
        (left, right, *operands),
        name,
        scratch=[pltpu.VMEM((8, 64, width), BF) for _, _, width in columns],
        deps=deps,
    )


def mm_back(terms, scalars, name, normed=None, deps=()):
    rows = terms[0][0].shape[0]
    half = rows // 2
    operands, specs, counts, scratch = [], [], [], []
    for grad, weight, start in terms:
        ops, sp = weight_operands(weight, start, grad.shape[1])
        operands += [grad, *ops]
        specs += [whole(grad), *sp]
        counts.append(len(ops))
        scratch.append(pltpu.VMEM((8, 64, grad.shape[1]), BF))
    held = len(operands)
    cols = pl.BlockSpec((half, SLAB), lambda i, s: (0, i))
    outs = [cols, cols]
    shapes = [sds((half, D), F32), sds((half, D), BF)]
    if normed is not None:
        operands += normed
        specs += [cols, cols]
        outs.append(pl.BlockSpec((8, SLAB), lambda i, s: (0, i)))
        shapes.append(sds((8, D), F32))
    total = len(operands)

    def body(s_ref, *refs):
        at, out = 0, 0.0
        for k, count in enumerate(counts):
            slab = load_slab(s_ref, refs[at + 1 : at + 1 + count], refs[total + len(outs) + k])
            out += lax.dot_general(
                refs[at][...], slab, (((1,), (1,)), ((), ())), preferred_element_type=F32
            )
            at += count + 1
        refs[total][...] = out[:half]
        refs[total + 1][...] = out[half:].astype(BF)
        if normed is not None:
            part = out[:half] * refs[held][...].astype(F32) + out[half:] * refs[held + 1][
                ...
            ].astype(F32)
            part = jnp.sum(part, axis=0, keepdims=True)
            refs[total + 2][...] = jnp.broadcast_to(part, (8, SLAB))

    return call(
        body,
        (4,),
        specs,
        tuple(outs),
        tuple(shapes),
        scalars,
        tuple(operands),
        name,
        scratch=scratch,
        deps=deps,
    )


def mm_weight(pairs, extra, scalars, name, deps=()):
    widths = [grad.shape[1] for _, grad in pairs]
    rows = pairs[0][0][0].shape[0]
    count = 3 * len(pairs)
    total = sum(widths) + 128

    def body(s_ref, *refs):
        core = s_ref[0]
        first_ref, second_ref = refs[count : count + 2]
        outs, held = refs[count + 2 : -1], refs[-1]
        at = 0
        for k, width in enumerate(widths):
            a_ref, b_ref, g_ref = refs[3 * k : 3 * k + 3]
            out = lax.dot_general(
                jnp.concatenate((a_ref[...], b_ref[...]), axis=0),
                g_ref[...],
                (((0,), (0,)), ((), ())),
                preferred_element_type=F32,
            ).astype(BF)
            held[:, :, at : at + width] = out.reshape(8, 64, width)
            at += width
        column = jnp.concatenate(
            (first_ref[:1], second_ref[:1], jnp.zeros((126, SLAB), F32)), axis=0
        )
        held[:, :, at:] = column.T.astype(BF).reshape(8, 64, 128)
        x_far = lax.rem(pl.program_id(0) + 4 - s_ref[2], 4)
        for k in range(4):

            @pl.when((core == 0) & (x_far == k))
            def _(k=k):
                for j in range(4):
                    y = lax.rem(s_ref[3] + j, 4)
                    for rel in (0, 1):
                        outs[k][j, rel] = held[rel * 4 + y]

        @pl.when(core == 1)
        def _():
            for k in range(4):
                y = lax.rem(s_ref[3] + k, 4)
                for rel in (0, 1):
                    outs[k][x_far, rel] = held[(1 - rel) * 4 + y]

    cols = pl.BlockSpec((rows, SLAB), lambda i, s: (0, i))
    specs, operands = [], []
    for (a, b), grad in pairs:
        specs += [cols, cols, whole(grad)]
        operands += [a, b, grad]
    specs += [pl.BlockSpec((8, SLAB), lambda i, s: (0, i))] * 2
    operands += extra
    shapes = (sds((4, 2, 64, total), BF),) * 4
    return call(
        body,
        (4,),
        specs,
        tuple(whole(s) for s in shapes),
        shapes,
        scalars,
        tuple(operands),
        name,
        scratch=[pltpu.VMEM((8, 64, total), BF)],
        deps=deps,
        stream=True,
    )


def mm_weight_into(into, pairs, start, total, scalars, name, deps=()):
    widths = [grad.shape[1] for _, grad in pairs]
    rows = pairs[0][0][0].shape[0]
    span = sum(widths)

    def body(s_ref, *refs):
        out_ref, mark_ref = refs[-2:]
        at = 0
        for k, width in enumerate(widths):
            a_ref, b_ref, g_ref = refs[3 * k : 3 * k + 3]
            out = lax.dot_general(
                jnp.concatenate((a_ref[...], b_ref[...]), axis=0),
                g_ref[...],
                (((0,), (0,)), ((), ())),
                preferred_element_type=F32,
            ).astype(BF)
            for c in (0, 1):
                for y in range(4):
                    first = (c * 4 + y) * 64
                    out_ref[0, y, jnp.bitwise_xor(c, s_ref[0]), :, at : at + width] = out[
                        first : first + 64
                    ]
            at += width
        mark_ref[...] = jnp.zeros_like(mark_ref)

    cols = pl.BlockSpec((rows, SLAB), lambda i, s: (0, i))
    specs, operands = [], []
    for (a, b), grad in pairs:
        specs += [cols, cols, whole(grad)]
        operands += [a, b, grad]
    aliases = None
    if into is not None:
        aliases = {1 + len(operands): 0}
        specs.append(pl.BlockSpec(memory_space=pl.ANY))
        operands.append(into)
    return call(
        body,
        (4,),
        specs,
        (
            pl.BlockSpec((1, 4, 2, 64, span), lambda i, s: (i, 0, 0, 0, start // span)),
            pl.BlockSpec((8, 128), lambda i, s: (0, 0)),
        ),
        (sds((4, 4, 2, 64, total), BF), sds((8, 128), F32)),
        scalars,
        tuple(operands),
        name,
        deps=deps,
        stream=True,
        aliases=aliases,
    )


def far_sums(parts, got, scalars, name):
    width = parts[0].shape[-1]

    def body(s_ref, own_ref, near_ref, far_ref, mid_ref, *refs):
        sum_a = own_ref[0].astype(F32) + mid_ref[0].astype(F32)
        sum_b = near_ref[0].astype(F32) + far_ref[0].astype(F32)
        for j in range(4):

            @pl.when(pl.program_id(0) == j)
            def _(j=j):
                refs[j][...] = (sum_a + sum_b).astype(BF)

    shapes = (sds((2, 64, width), BF),) * 4
    return call(
        body,
        (4,),
        [pl.BlockSpec((1, 2, 64, width), lambda j, s: (j, 0, 0, 0))] * 4,
        tuple(whole(s) for s in shapes),
        shapes,
        scalars,
        (parts[0], *got),
        name,
        stream=True,
    )


def split_heads(weights, scalars, name, deps=()):
    widths = [w.shape[1] // 2 for w in weights]

    def body(s_ref, *refs):
        mine_ref, theirs_ref = refs[-2:]
        core = s_ref[0]
        for out_ref, head in ((mine_ref, core), (theirs_ref, 1 - core)):
            at = 0
            for ref, width in zip(refs, widths):
                out_ref[:, at : at + width] = ref[:, pl.ds(pl.multiple_of(head * width, width), width)]
                at += width

    total = sum(widths)
    spec = pl.BlockSpec((64, total), lambda i, s: (0, 0))
    return call(
        body,
        (1,),
        [whole(w) for w in weights],
        (spec, spec),
        (sds((64, total), BF),) * 2,
        scalars,
        tuple(weights),
        name,
        deps=deps,
        stream=True,
    )


def join_heads(mine, theirs, widths, scalars, name):
    def body(s_ref, mine_ref, theirs_ref, *outs):
        core = s_ref[0]
        for in_ref, head in ((mine_ref, core), (theirs_ref, 1 - core)):
            at = 0
            for ref, width in zip(outs, widths):
                span = pl.ds(pl.multiple_of(head * width, width), width)
                ref[:, span] = in_ref[:, at : at + width].astype(F32)
                at += width

    shapes = tuple(sds((64, 2 * w), F32) for w in widths)
    return call(
        body,
        (1,),
        [whole(mine), whole(theirs)],
        tuple(whole(s) for s in shapes),
        shapes,
        scalars,
        (mine, theirs),
        name,
    )


def scale_of(values):
    return lax.rsqrt(jnp.mean(values * values, axis=-1, keepdims=True) + 1e-06)


def turned_spec(rows):
    return pl.BlockSpec((rows, D), lambda i, s: (lax.rem(i + s[1], 4), 0))


def plain_spec(rows):
    return pl.BlockSpec((rows, D), lambda i, s: (i, 0))


def enter_rows(tokens, gain, scalars, deps=()):
    rows = tokens.shape[0]
    block = rows // 4

    def body(s_ref, t_ref, g_ref, n_out):
        values = t_ref[...]
        n_out[...] = (values * scale_of(values) * g_ref[...]).astype(BF)

    return call(
        body,
        (4,),
        [turned_spec(block), whole(gain)],
        plain_spec(block),
        sds((rows, D), BF),
        scalars,
        (tokens, gain),
        "enter_rows",
        deps=deps,
    )


def low_rows(cotangent, scalars, deps=()):
    rows = cotangent.shape[0]
    block = rows // 4

    def body(s_ref, c_ref, l_out):
        l_out[...] = c_ref[...].astype(BF)

    return call(
        body,
        (4,),
        [turned_spec(block)],
        plain_spec(block),
        sds((rows, D), BF),
        scalars,
        (cotangent,),
        "low_rows",
        deps=deps,
    )


def each_part(refs, work):
    step = pl.program_id(0)
    for k, ref in enumerate(refs):

        @pl.when(step == k)
        def _(ref=ref):
            work(ref[...].astype(F32))


def second_norm(tokens, parts, gain, scalars, deps=()):
    rows = tokens.shape[0]
    block = rows // 4

    def body(s_ref, t_ref, g_ref, *refs):
        h_out, n_out = refs[4:]

        def work(part):
            values = t_ref[...] + part
            h_out[...] = values
            n_out[...] = (values * scale_of(values) * g_ref[...]).astype(BF)

        each_part(refs[:4], work)

    plain = plain_spec(block)
    return call(
        body,
        (4,),
        [turned_spec(block), whole(gain)] + [whole(p) for p in parts],
        (plain, plain),
        (sds((rows, D), F32), sds((rows, D), BF)),
        scalars,
        (tokens, gain, *parts),
        "second_norm",
        deps=deps,
        stream=True,
    )


def third_blocks(own, came, down_own, down_came, scalars, deps=()):
    rows = own.shape[0]
    block = rows // 4

    def body(s_ref, own_ref, came_ref, d_ref, e_ref, *refs):
        total = own_ref[...] + came_ref[...].astype(F32)
        down = d_ref[...] + e_ref[...].astype(F32)
        step = pl.program_id(0)
        for k in range(4):

            @pl.when(step == k)
            def _(k=k):
                refs[k][:block] = total.astype(BF)
                refs[k][block:] = down.astype(BF)

    plain = plain_spec(block)
    shapes = (sds((2 * block, D), BF),) * 4
    return call(
        body,
        (4,),
        [plain] * 4,
        tuple(whole(s) for s in shapes),
        shapes,
        scalars,
        (own, came, down_own, down_came),
        "third_blocks",
        deps=deps,
        stream=True,
    )


def leave_rows(hidden, tokens, grad_state, parts, gain, scalars, deps=()):
    rows = hidden.shape[0]
    block = rows // 4

    def body(s_ref, h_ref, t_ref, u_ref, g_ref, *refs):
        def work(part):
            refs[4][...] = h_ref[...] + part[block : 2 * block]
            refs[5][...] = u_ref[...] + norm_grad(t_ref[...], part[:block], g_ref[...])

        each_part(refs[:4], work)

    plain, turn = plain_spec(block), turned_spec(block)
    return call(
        body,
        (4,),
        [plain, turn, plain, whole(gain)] + [whole(p) for p in parts],
        (turn, turn),
        (sds((rows, D), F32),) * 2,
        scalars,
        (hidden, tokens, grad_state, gain, *parts),
        "leave_rows",
        deps=deps,
        stream=True,
    )


def norm_grad(values, grad, gain):
    factor = scale_of(values)
    unit = values * factor
    scaled = grad * gain
    return factor * (scaled - unit * jnp.mean(scaled * unit, axis=-1, keepdims=True))


def norm_back(values, upstream, parts, gain, scalars, name, deps=()):
    rows = values.shape[0]
    block = rows // 4

    def body(s_ref, v_ref, u_ref, g_ref, *refs):
        def work(part):
            out = u_ref[...] + norm_grad(v_ref[...], part, g_ref[...])
            refs[4][...] = out
            refs[5][...] = out.astype(BF)

        each_part(refs[:4], work)

    plain = plain_spec(block)
    return call(
        body,
        (4,),
        [plain, turned_spec(block), whole(gain)] + [whole(p) for p in parts],
        (plain, plain),
        (sds((rows, D), F32), sds((rows, D), BF)),
        scalars,
        (values, upstream, gain, *parts),
        name,
        deps=deps,
        stream=True,
    )


def tp_first(blocks):
    got = [shift(blocks[o], "tp", o) for o in (1, 3, 2)]
    near, far, mid = [part.astype(F32) for part in got]
    return (blocks[0].astype(F32) + mid) + (near + far), got


def tp_second(mine):
    near, far, mid = [shift(mine, "tp", -o) for o in (1, 3, 2)]
    return mine, near, mid, far


def tp_total(blocks):
    return tp_second(tp_first(blocks)[0].astype(BF))


def chip_blocks(own, came):
    block = own.shape[0] // 4
    return [
        (own[o * block : (o + 1) * block] + came[o * block : (o + 1) * block].astype(F32)).astype(BF)
        for o in range(4)
    ]


def gate_norm(gate_pre, retained):
    centred = retained - jnp.mean(retained, axis=-1, keepdims=True)
    normed = centred * lax.rsqrt(jnp.mean(centred * centred, axis=-1, keepdims=True) + 1.0 * DK)
    return gate_pre * jax.nn.sigmoid(gate_pre) * normed


def gelu_gate(hidden, linear):
    return jax.nn.gelu(hidden, approximate=True) * linear


def rotate(values, cosine, sine):
    half = DK // 2
    first = values[:, :half]
    second = values[:, half:]
    return jnp.concatenate((first * cosine - second * sine, first * sine + second * cosine), axis=1)


def ein(spec, left, right):
    return jnp.einsum(spec, left, right, preferred_element_type=F32)


def per_device(
    tokens,
    cotangent,
    gain_first,
    gain_second,
    w_query,
    w_key,
    w_value,
    w_gate,
    w_output,
    w_hidden,
    w_linear,
    w_down,
    decay_scale,
    first_length,
):
    rows = tokens.shape[0]
    core = lax.axis_index("core")
    place = lax.axis_index("ctx")
    plane = lax.axis_index("tp")
    scalars = jnp.stack((core, plane, lax.axis_index("x"), place)).astype(jnp.int32)

    w_output = w_output.T
    w_down = w_down.T
    mine, theirs = split_heads((w_value, w_key, w_gate, w_output, w_query), scalars, "split_attn")
    came = swap(theirs)
    block, gathered = stack_attn(mine, came, scalars)
    lengths = jnp.concatenate((first_length, swap(first_length)))
    normed_first = enter_rows(tokens, gain_first.reshape(1, D), scalars, deps=(block,))
    w_kv = stack_blocks(
        spread_near(block), 0, 768, scalars, "stack_kv", deps=(normed_first, lengths)
    )
    w_goq = lax.all_gather(gathered, XY, axis=0, tiled=True).reshape(4, 4, 2, 64, -1)
    mine, theirs = split_heads(
        (w_hidden, w_linear, w_down), scalars, "split_mlp", deps=(gathered,)
    )
    came_mlp = swap(theirs)
    gain_first = gain_first.reshape(1, D)
    gain_second = gain_second.reshape(1, D)
    x_first = (normed_first, swap(normed_first))
    cot_low = low_rows(cotangent, scalars, deps=(x_first[1],))
    g_out = (cot_low, swap(cot_low))
    w_kv = spread_far(w_kv)

    rate = lax.dynamic_index_in_dim(decay_scale, core, 0, False) / 1024.0
    local = (jnp.arange(rows, dtype=jnp.int32) + plane * (rows // 4)) % rows
    index = place * rows + local
    document = (index[None, :] >= lengths[:, None]).astype(jnp.int32)
    carried = (document == 0).astype(F32)
    steps = local.astype(F32)
    offsets = local[:, None] - local[None, :]
    linked = (offsets >= 0)[None] & (document[:, :, None] == document[:, None, :])
    mask = jnp.where(
        linked, jnp.exp(-rate * jnp.maximum(offsets, 0).astype(F32))[None], 0.0
    )
    enter = (carried * jnp.exp(-rate * (steps + 1.0))[None])[:, :, None]
    leave = jnp.exp(-rate * (rows - 1.0 - steps))[None, :, None]
    fade = jnp.exp(-rate * rows)
    half = DK // 2
    frequency = 10000.0 ** (-(jnp.arange(half).astype(F32) / half))
    angles = index.astype(F32)[:, None] * frequency[None, :]
    cosine = jnp.tile(jnp.cos(angles), (2, 1))
    sine = jnp.tile(jnp.sin(angles), (2, 1))

    def carry(came):
        near, mid, far = [part.astype(F32) for part in came]
        return near + fade * (mid + fade * far)

    def spread_state(low, way):
        return [shift_open(low, "ctx", way * o) for o in (1, 2, 3)]

    projected = mm_in(*x_first, [(w_kv, 0, 768)], scalars, "project_kv")
    key = rotate(projected[:, DV:], cosine, sine).astype(BF).reshape(2, rows, DK)
    value = projected[:, :DV].astype(BF).reshape(2, rows, DV)
    key_out = (key.astype(F32) * leave).astype(BF)
    state_out = ein("gjd,gje->gde", key_out, value).astype(BF)
    came = spread_state(state_out, 1)
    w_mlp = lax.all_gather(
        stack_blocks((mine, came_mlp), 0, 1536, scalars, "stack_mlp", deps=came),
        XY,
        axis=0,
        tiled=True,
    ).reshape(4, 4, 2, 64, -1)
    projected = mm_in(
        *x_first, [(w_goq, 0, DV), (w_goq, 1024, DK)], scalars, "project_gq", deps=(state_out, mask, enter)
    )
    state_in = carry(came).astype(BF)
    gate_pre = projected[:, :DV]
    query = rotate(projected[:, DV:], cosine, sine).astype(BF).reshape(2, rows, DK)
    weighted = (ein("gid,gjd->gij", query, key) * mask).astype(BF)
    inner = ein("gij,gje->gie", weighted, value)
    retained = (inner + ein("gid,gde->gie", query, state_in) * enter).reshape(2 * rows, DV)
    mixed_full, gate_back = jax.vjp(gate_norm, gate_pre, retained)
    mixed = mixed_full.astype(BF)
    own, other = mm_back([(mixed, w_goq, DV)], scalars, "project_out")
    parts = tp_total(chip_blocks(own, swap(other)))
    grad_activated = mm_in(
        *g_out, [(w_mlp, 2 * DV, DV)], scalars, "back_down", deps=(other,)
    )
    hidden_state, normed_second = second_norm(tokens, parts, gain_second, scalars)
    x_second = (normed_second, swap(normed_second))
    paired = mm_in(*x_second, [(w_mlp, 0, 2 * DV)], scalars, "project_mlp")
    activated_full, gelu_back = jax.vjp(gelu_gate, paired[:, :DV], paired[:, DV:])
    activated = activated_full.astype(BF)
    grad_pair = jnp.concatenate(gelu_back(grad_activated), axis=1).astype(BF)
    own, other, gain_second_part = mm_back(
        [(grad_pair, w_mlp, 0)], scalars, "back_mlp", normed=x_second
    )
    grads, mark = mm_weight_into(
        None, ((x_second, grad_pair),), 1024, 2560, scalars, "weight_mlp"
    )
    mine, _ = tp_first(chip_blocks(own, swap(other)))
    (mine,) = tie((mine.astype(BF),), (mark,))
    parts = tp_second(mine)
    grads, mark = mm_weight_into(
        grads, ((g_out, activated),), 2048, 2560, scalars, "weight_down", deps=(mine,)
    )
    down = mm_back([(activated, w_mlp, 2 * DV)], scalars, "project_down", deps=(mine,))
    grad_state, grad_state_low = norm_back(
        hidden_state,
        cotangent,
        parts,
        gain_second,
        scalars,
        "second_back",
        deps=(down[1], mark),
    )
    g_state = (grad_state_low, swap(grad_state_low))
    grad_mixed = mm_in(*g_state, [(w_goq, DV, DV)], scalars, "back_out")
    grad_gate, grad_retained = gate_back(grad_mixed)
    grad_low = grad_retained.reshape(2, rows, DV).astype(BF)
    query_in = (query.astype(F32) * enter).astype(BF)
    back_out = ein("gid,gie->gde", query_in, grad_low).astype(BF)
    came = spread_state(back_out, -1)
    grad_scores = (ein("gie,gje->gij", grad_low, value) * mask).astype(BF)
    grad_query = ein("gij,gjd->gid", grad_scores, key) + enter * ein("gie,gde->gid", grad_low, state_in)
    grad_key = ein("gij,gid->gjd", grad_scores, query)
    grad_value = ein("gij,gie->gje", weighted, grad_low)
    grad_gate = grad_gate.astype(BF)
    grad_query = rotate(grad_query.reshape(2 * rows, DK), cosine, -sine).astype(BF)
    grads, mark = mm_weight_into(
        grads,
        ((g_state, mixed), (x_first, grad_gate)),
        0,
        2560,
        scalars,
        "weight_og",
        deps=(back_out,),
    )
    rest = lax.psum_scatter(grads.reshape(2048, -1), XY, scatter_dimension=0, tiled=True)
    came[0] = tie((came[0],), (mark, grad_key, grad_value, grad_query))[0]
    state_back = carry(came).astype(BF)
    grad_key += leave * ein("gje,gde->gjd", value, state_back)
    grad_value += ein("gjd,gde->gje", key_out, state_back)
    grad_key = rotate(grad_key.reshape(2 * rows, DK), cosine, -sine)
    grad_vk = jnp.concatenate(
        (grad_value.reshape(2 * rows, DV).astype(BF), grad_key.astype(BF)), axis=1
    )
    own, other, gain_first_part = mm_back(
        [(grad_vk, w_kv, 0), (grad_gate, w_goq, 0), (grad_query, w_goq, 1024)],
        scalars,
        "back_attn",
        normed=x_first,
    )
    down = (down[0], swap(tie((down[1],), (state_back,))[0]))
    blocks = third_blocks(own, swap(other), *down, scalars)
    mine, _ = tp_first(blocks)
    d_vkq = mm_weight(
        ((x_first, grad_vk), (x_first, grad_query)),
        (gain_first_part, gain_second_part),
        scalars,
        "weight_vkq",
        deps=blocks[:1],
    )
    vkq_got = send_far(d_vkq, (), (mine,))
    parts = tp_second(tie((mine.astype(BF),), vkq_got[:2])[0])
    sums = far_sums(d_vkq, vkq_got, scalars, "sum_vkq")
    sums = tie(sums, parts[1:])
    got = [hop(sums[j], False, j) for j in (1, 3, 2)]
    block = sums[0].astype(F32) + got[2].astype(F32) + (got[0].astype(F32) + got[1].astype(F32))
    came = swap(block[1].astype(BF))
    gains = block[0, :, 1024:1026] + came[:, 1024:1026].astype(F32)
    near, mid, far = [shift(gains, "tp", o) for o in (1, 2, 3)]
    gains = (gains + mid) + (near + far)
    spot = (lax.axis_index("x") * 2 + core) * 4 + place
    gain_first_grad, gain_second_grad = [
        gains[:, k] / lax.dynamic_slice_in_dim(gain[0], spot * 64, 64, 0)
        for k, gain in ((0, gain_first), (1, gain_second))
    ]
    layer_out, input_grad = leave_rows(
        hidden_state, tokens, grad_state, parts, gain_first, scalars
    )
    d_value, d_key, d_query = join_heads(
        block[0].astype(BF), came, (DV, DK, DK), scalars, "join_vkq"
    )
    rest = tie((rest,), (gains, input_grad, d_value))[0].reshape(2, 64, -1)
    d_output, d_gate, d_hidden, d_linear, d_down = join_heads(
        rest[0], swap(rest[1]), (DV,) * 5, scalars, "join_rest"
    )
    return (
        layer_out,
        input_grad,
        gain_first_grad,
        gain_second_grad,
        d_query,
        d_key,
        d_value,
        d_gate,
        d_output.T,
        d_hidden,
        d_linear,
        d_down.T,
    )


def solution(mesh):
    fine = Mesh(np.asarray(mesh.devices).reshape(4, 2, 4, 4), ("x", "core", "ctx", "tp"))
    split = ("x", "core", "ctx")
    row = P(split, None)
    win = P(split, "tp")
    wout = P("tp", split)
    in_specs = (row, row, P(), P(), win, win, win, win, wout, win, win, wout, P("tp"), P(("x", "core")))
    out_specs = (row, row, P(split), P(split), win, win, win, win, wout, win, win, wout)
    return jax.shard_map(
        per_device, mesh=fine, in_specs=in_specs, out_specs=out_specs, check_vma=False
    )
```

```python
import math

import jax
import jax.numpy as jnp
import numpy as np
from jax import lax
from jax.experimental import pallas as pl
from jax.experimental.pallas import tpu as pltpu
from jax.sharding import Mesh, PartitionSpec as P

D = 2048
DK = 256
DV = 512
SLAB = 512
BF = jnp.bfloat16
F32 = jnp.float32
XY = ("x", "ctx")
MIB = 1 << 20


def shift(value, axis, offset):
    n = lax.axis_size(axis)
    return lax.ppermute(value, axis, [(i, (i + offset) % n) for i in range(n)])


def shift_open(value, axis, offset):
    n = lax.axis_size(axis)
    return lax.ppermute(
        value, axis, [(i, i + offset) for i in range(n) if 0 <= i + offset < n]
    )


def swap(value):
    return lax.ppermute(value, "core", [(0, 1), (1, 0)])


def after(value, *earlier):
    return lax.optimization_barrier((value, *earlier))[0]


def call(
    body,
    grid,
    ins,
    outs,
    shapes,
    scalars,
    operands,
    name,
    scratch=(),
    deps=(),
    stream=False,
    aliases=None,
):
    count = len(operands)

    def kernel(s_ref, *refs):
        body(s_ref, *refs[:count], *refs[count + len(deps) :])

    ins = [*ins, *[pl.BlockSpec(memory_space=pl.ANY)] * len(deps)]
    return pl.pallas_call(
        kernel,
        out_shape=shapes,
        grid_spec=pltpu.PrefetchScalarGridSpec(
            num_scalar_prefetch=1, grid=grid, in_specs=ins, out_specs=outs, scratch_shapes=scratch
        ),
        compiler_params=pltpu.CompilerParams(
            vmem_limit_bytes=(60 if stream else 32) * MIB, dimension_semantics=("arbitrary",) * len(grid)
        ),
        cost_estimate=pl.CostEstimate(flops=1, bytes_accessed=1, transcendentals=0),
        input_output_aliases=aliases or {},
        name=name,
    )(scalars, *operands, *deps)


def tie(values, deps):
    count = len(values)
    anywhere = pl.BlockSpec(memory_space=pl.ANY)
    return pl.pallas_call(
        lambda *refs: None,
        out_shape=tuple(sds(v.shape, v.dtype) for v in values),
        in_specs=[anywhere] * (count + len(deps)),
        out_specs=(anywhere,) * count,
        input_output_aliases={i: i for i in range(count)},
        name="tie",
    )(*values, *deps)


def whole(array):
    return pl.BlockSpec(array.shape, lambda *_: (0,) * array.ndim)


def sds(shape, dtype):
    return jax.ShapeDtypeStruct(shape, dtype)


def weight_operands(weight, start, width):
    if not isinstance(weight, tuple):
        spec = pl.BlockSpec((1, 4, 2, 64, width), lambda i, s: (i, 0, 0, 0, start // width))
        return [weight], [spec]
    piece = math.gcd(start, width) if start else width
    operands, specs = [], []
    for at in range(start, start + width, piece):
        for stack in weight:
            operands.append(stack)
            specs.append(pl.BlockSpec((4, 2, 64, piece), lambda i, s, at=at: (0, 0, 0, at // piece)))
    return operands, specs


def load_slab(s_ref, refs, held):
    core = s_ref[0]
    if len(refs) == 1:
        return jnp.concatenate(
            [refs[0][0, y, jnp.bitwise_xor(c, core)] for c in (0, 1) for y in range(4)], axis=0
        )
    x_far = lax.rem(s_ref[2] + 4 - pl.program_id(0), 4)
    at = 0
    for first in range(0, len(refs), 4):
        stacks = refs[first : first + 4]
        width = stacks[0].shape[-1]
        for j in range(4):

            @pl.when((core == 0) & (x_far == j))
            def _(j=j, at=at, width=width, stacks=stacks):
                for i in range(4):
                    y = lax.rem(s_ref[3] + 4 - i, 4)
                    for c in (0, 1):
                        held[c * 4 + y, :, at : at + width] = stacks[j][i, c]

        @pl.when(core == 1)
        def _(at=at, width=width, stacks=stacks):
            for j in range(4):
                y = lax.rem(s_ref[3] + 4 - j, 4)
                for c in (0, 1):
                    held[c * 4 + y, :, at : at + width] = stacks[j][x_far, 1 - c]

        at += width
    return held[...].reshape(SLAB, at)


def hop(value, first, offset):
    pairs = []
    for x in range(4):
        for core in (0, 1):
            for y in range(4):
                to = ((x + offset) % 4, y) if (core == 0) == first else (x, (y + offset) % 4)
                pairs.append(((x * 2 + core) * 4 + y, (to[0] * 2 + core) * 4 + to[1]))
    return lax.ppermute(value, ("x", "core", "ctx"), pairs)


def spread_near(block):
    near, far, mid = [hop(block, False, o) for o in (1, 3, 2)]
    return block, near, mid, far


def stack_blocks(blocks, start, width, scalars, name, deps=()):
    at = start // width if start % width == 0 else None
    span = width if at is not None else blocks[0].shape[1]
    first = 0 if at is not None else start
    height = blocks[0].shape[0]

    def body(s_ref, *refs):
        for k, ref in enumerate(refs[:-1]):
            refs[-1][k * height : (k + 1) * height, :] = ref[:, first : first + width]

    total = sds((height * len(blocks), width), BF)
    return call(
        body,
        (1,),
        [pl.BlockSpec((height, span), lambda i, s: (0, at or 0))] * len(blocks),
        whole(total),
        total,
        scalars,
        tuple(blocks),
        name,
        deps=deps,
    )


def stack_attn(mine, came, scalars):
    height, total = mine.shape

    def body(s_ref, mine_ref, came_ref, first_ref, other_ref):
        for k, ref in enumerate((mine_ref, came_ref)):
            span = slice(k * height, (k + 1) * height)
            first_ref[span, :] = ref[:, :768]
            other_ref[span, :] = ref[:, 768:]

    shapes = (sds((2 * height, 768), BF), sds((2 * height, total - 768), BF))
    return call(
        body,
        (1,),
        [whole(mine), whole(came)],
        tuple(whole(s) for s in shapes),
        shapes,
        scalars,
        (mine, came),
        "stack_attn",
        stream=True,
    )


def spread_far(stack, gate=False):
    stack = stack.reshape(4, 2, 64, -1)
    near, far = hop(stack, True, 1), hop(stack, True, -1)
    mid = hop(tie((stack,), (near, far))[0] if gate else stack, True, 2)
    return stack, near, mid, far


def mm_in(left, right, columns, scalars, name, deps=()):
    operands, specs, counts = [], [], []
    for weight, start, width in columns:
        ops, sp = weight_operands(weight, start, width)
        operands += ops
        specs += sp
        counts.append(len(ops))
    total = sum(width for _, _, width in columns)

    def body(s_ref, a_ref, b_ref, *refs):
        out_ref = refs[len(operands)]
        step = pl.program_id(0)
        rows = jnp.concatenate((a_ref[...], b_ref[...]), axis=0)
        at, first = 0, 0
        for k, count in enumerate(counts):
            width = columns[k][2]
            slab = load_slab(s_ref, refs[first : first + count], refs[len(operands) + 1 + k])
            part = jnp.dot(rows, slab, preferred_element_type=F32)
            span = slice(at, at + width)

            @pl.when(step == 0)
            def _(part=part, span=span):
                out_ref[:, span] = part

            @pl.when(step > 0)
            def _(part=part, span=span):
                out_ref[:, span] += part

            at += width
            first += count

    rows = left.shape[0]
    cols = pl.BlockSpec((rows, SLAB), lambda i, s: (0, i))
    return call(
        body,
        (4,),
        [cols, cols, *specs],
        pl.BlockSpec((2 * rows, total), lambda i, s: (0, 0)),
        sds((2 * rows, total), F32),
        scalars,
        (left, right, *operands),
        name,
        scratch=[pltpu.VMEM((8, 64, width), BF) for _, _, width in columns],
        deps=deps,
    )


def mm_back(terms, scalars, name, normed=None, deps=()):
    rows = terms[0][0].shape[0]
    half = rows // 2
    operands, specs, counts, scratch = [], [], [], []
    for grad, weight, start in terms:
        ops, sp = weight_operands(weight, start, grad.shape[1])
        operands += [grad, *ops]
        specs += [whole(grad), *sp]
        counts.append(len(ops))
        scratch.append(pltpu.VMEM((8, 64, grad.shape[1]), BF))
    held = len(operands)
    cols = pl.BlockSpec((half, SLAB), lambda i, s: (0, i))
    outs = [cols, cols]
    shapes = [sds((half, D), F32), sds((half, D), BF)]
    if normed is not None:
        operands += normed
        specs += [cols, cols]
        outs.append(pl.BlockSpec((8, SLAB), lambda i, s: (0, i)))
        shapes.append(sds((8, D), F32))
    total = len(operands)

    def body(s_ref, *refs):
        at, out = 0, 0.0
        for k, count in enumerate(counts):
            slab = load_slab(s_ref, refs[at + 1 : at + 1 + count], refs[total + len(outs) + k])
            out += lax.dot_general(
                refs[at][...], slab, (((1,), (1,)), ((), ())), preferred_element_type=F32
            )
            at += count + 1
        refs[total][...] = out[:half]
        refs[total + 1][...] = out[half:].astype(BF)
        if normed is not None:
            part = out[:half] * refs[held][...].astype(F32) + out[half:] * refs[held + 1][
                ...
            ].astype(F32)
            part = jnp.sum(part, axis=0, keepdims=True)
            refs[total + 2][...] = jnp.broadcast_to(part, (8, SLAB))

    return call(
        body,
        (4,),
        specs,
        tuple(outs),
        tuple(shapes),
        scalars,
        tuple(operands),
        name,
        scratch=scratch,
        deps=deps,
    )


def mm_weight_into(into, pairs, start, total, scalars, name, deps=()):
    widths = [grad.shape[1] for _, grad in pairs]
    rows = pairs[0][0][0].shape[0]
    span = sum(widths)

    def body(s_ref, *refs):
        out_ref, mark_ref = refs[-2:]
        at = 0
        for k, width in enumerate(widths):
            a_ref, b_ref, g_ref = refs[3 * k : 3 * k + 3]
            out = lax.dot_general(
                jnp.concatenate((a_ref[...], b_ref[...]), axis=0),
                g_ref[...],
                (((0,), (0,)), ((), ())),
                preferred_element_type=F32,
            ).astype(BF)
            for c in (0, 1):
                for y in range(4):
                    first = (c * 4 + y) * 64
                    out_ref[0, y, jnp.bitwise_xor(c, s_ref[0]), :, at : at + width] = out[
                        first : first + 64
                    ]
            at += width
        mark_ref[...] = jnp.zeros_like(mark_ref)

    cols = pl.BlockSpec((rows, SLAB), lambda i, s: (0, i))
    specs, operands = [], []
    for (a, b), grad in pairs:
        specs += [cols, cols, whole(grad)]
        operands += [a, b, grad]
    aliases = None
    if into is not None:
        aliases = {1 + len(operands): 0}
        specs.append(pl.BlockSpec(memory_space=pl.ANY))
        operands.append(into)
    return call(
        body,
        (4,),
        specs,
        (
            pl.BlockSpec((1, 4, 2, 64, span), lambda i, s: (i, 0, 0, 0, start // span)),
            pl.BlockSpec((8, 128), lambda i, s: (0, 0)),
        ),
        (sds((4, 4, 2, 64, total), BF), sds((8, 128), F32)),
        scalars,
        tuple(operands),
        name,
        deps=deps,
        stream=True,
        aliases=aliases,
    )


def split_heads(weights, scalars, name, deps=()):
    widths = [w.shape[1] // 2 for w in weights]

    def body(s_ref, *refs):
        mine_ref, theirs_ref = refs[-2:]
        core = s_ref[0]
        for out_ref, head in ((mine_ref, core), (theirs_ref, 1 - core)):
            at = 0
            for ref, width in zip(refs, widths):
                out_ref[:, at : at + width] = ref[:, pl.ds(pl.multiple_of(head * width, width), width)]
                at += width

    total = sum(widths)
    spec = pl.BlockSpec((64, total), lambda i, s: (0, 0))
    return call(
        body,
        (1,),
        [whole(w) for w in weights],
        (spec, spec),
        (sds((64, total), BF),) * 2,
        scalars,
        tuple(weights),
        name,
        deps=deps,
        stream=True,
    )


def join_heads(mine, theirs, widths, scalars, name):
    def body(s_ref, mine_ref, theirs_ref, *outs):
        core = s_ref[0]
        for in_ref, head in ((mine_ref, core), (theirs_ref, 1 - core)):
            at = 0
            for ref, width in zip(outs, widths):
                span = pl.ds(pl.multiple_of(head * width, width), width)
                ref[:, span] = in_ref[:, at : at + width].astype(F32)
                at += width

    shapes = tuple(sds((64, 2 * w), F32) for w in widths)
    return call(
        body,
        (1,),
        [whole(mine), whole(theirs)],
        tuple(whole(s) for s in shapes),
        shapes,
        scalars,
        (mine, theirs),
        name,
    )


def scale_of(values):
    return lax.rsqrt(jnp.mean(values * values, axis=-1, keepdims=True) + 1e-06)


def turned_spec(rows):
    return pl.BlockSpec((rows, D), lambda i, s: (lax.rem(i + s[1], 4), 0))


def plain_spec(rows):
    return pl.BlockSpec((rows, D), lambda i, s: (i, 0))


def enter_rows(tokens, gain, scalars, deps=()):
    rows = tokens.shape[0]
    block = rows // 4

    def body(s_ref, t_ref, g_ref, n_out):
        values = t_ref[...]
        n_out[...] = (values * scale_of(values) * g_ref[...]).astype(BF)

    return call(
        body,
        (4,),
        [turned_spec(block), whole(gain)],
        plain_spec(block),
        sds((rows, D), BF),
        scalars,
        (tokens, gain),
        "enter_rows",
        deps=deps,
    )


def low_rows(cotangent, scalars, deps=()):
    rows = cotangent.shape[0]
    block = rows // 4

    def body(s_ref, c_ref, l_out):
        l_out[...] = c_ref[...].astype(BF)

    return call(
        body,
        (4,),
        [turned_spec(block)],
        plain_spec(block),
        sds((rows, D), BF),
        scalars,
        (cotangent,),
        "low_rows",
        deps=deps,
    )


def each_part(refs, work):
    step = pl.program_id(0)
    for k, ref in enumerate(refs):

        @pl.when(step == k)
        def _(ref=ref):
            work(ref[...].astype(F32))


def second_norm(tokens, parts, gain, scalars, deps=()):
    rows = tokens.shape[0]
    block = rows // 4

    def body(s_ref, t_ref, g_ref, *refs):
        h_out, n_out = refs[4:]

        def work(part):
            values = t_ref[...] + part
            h_out[...] = values
            n_out[...] = (values * scale_of(values) * g_ref[...]).astype(BF)

        each_part(refs[:4], work)

    plain = plain_spec(block)
    return call(
        body,
        (4,),
        [turned_spec(block), whole(gain)] + [whole(p) for p in parts],
        (plain, plain),
        (sds((rows, D), F32), sds((rows, D), BF)),
        scalars,
        (tokens, gain, *parts),
        "second_norm",
        deps=deps,
        stream=True,
    )


def third_blocks(own, came, down_own, down_came, scalars, deps=()):
    rows = own.shape[0]
    block = rows // 4

    def body(s_ref, own_ref, came_ref, d_ref, e_ref, *refs):
        total = own_ref[...] + came_ref[...].astype(F32)
        down = d_ref[...] + e_ref[...].astype(F32)
        step = pl.program_id(0)
        for k in range(4):

            @pl.when(step == k)
            def _(k=k):
                refs[k][:block] = total.astype(BF)
                refs[k][block:] = down.astype(BF)

    plain = plain_spec(block)
    shapes = (sds((2 * block, D), BF),) * 4
    return call(
        body,
        (4,),
        [plain] * 4,
        tuple(whole(s) for s in shapes),
        shapes,
        scalars,
        (own, came, down_own, down_came),
        "third_blocks",
        deps=deps,
        stream=True,
    )


def leave_rows(hidden, tokens, grad_state, parts, gain, scalars, deps=()):
    rows = hidden.shape[0]
    block = rows // 4

    def body(s_ref, h_ref, t_ref, u_ref, g_ref, *refs):
        def work(part):
            refs[4][...] = h_ref[...] + part[block : 2 * block]
            refs[5][...] = u_ref[...] + norm_grad(t_ref[...], part[:block], g_ref[...])

        each_part(refs[:4], work)

    plain, turn = plain_spec(block), turned_spec(block)
    return call(
        body,
        (4,),
        [plain, turn, plain, whole(gain)] + [whole(p) for p in parts],
        (turn, turn),
        (sds((rows, D), F32),) * 2,
        scalars,
        (hidden, tokens, grad_state, gain, *parts),
        "leave_rows",
        deps=deps,
        stream=True,
    )


def norm_grad(values, grad, gain):
    factor = scale_of(values)
    unit = values * factor
    scaled = grad * gain
    return factor * (scaled - unit * jnp.mean(scaled * unit, axis=-1, keepdims=True))


def norm_back(values, upstream, parts, gain, scalars, name, deps=()):
    rows = values.shape[0]
    block = rows // 4

    def body(s_ref, v_ref, u_ref, g_ref, *refs):
        def work(part):
            out = u_ref[...] + norm_grad(v_ref[...], part, g_ref[...])
            refs[4][...] = out
            refs[5][...] = out.astype(BF)

        each_part(refs[:4], work)

    plain = plain_spec(block)
    return call(
        body,
        (4,),
        [plain, turned_spec(block), whole(gain)] + [whole(p) for p in parts],
        (plain, plain),
        (sds((rows, D), F32), sds((rows, D), BF)),
        scalars,
        (values, upstream, gain, *parts),
        name,
        deps=deps,
        stream=True,
    )


def tp_first(blocks):
    got = [shift(blocks[o], "tp", o) for o in (1, 3, 2)]
    near, far, mid = [part.astype(F32) for part in got]
    return (blocks[0].astype(F32) + mid) + (near + far), got


def tp_second(mine):
    near, far, mid = [shift(mine, "tp", -o) for o in (1, 3, 2)]
    return mine, near, mid, far


def tp_total(blocks):
    return tp_second(tp_first(blocks)[0].astype(BF))


def chip_blocks(own, came):
    block = own.shape[0] // 4
    return [
        (own[o * block : (o + 1) * block] + came[o * block : (o + 1) * block].astype(F32)).astype(BF)
        for o in range(4)
    ]


def gate_norm(gate_pre, retained):
    centred = retained - jnp.mean(retained, axis=-1, keepdims=True)
    normed = centred * lax.rsqrt(jnp.mean(centred * centred, axis=-1, keepdims=True) + 1.0 * DK)
    return gate_pre * jax.nn.sigmoid(gate_pre) * normed


def gelu_gate(hidden, linear):
    return jax.nn.gelu(hidden, approximate=True) * linear


def rotate(values, cosine, sine):
    half = DK // 2
    first = values[:, :half]
    second = values[:, half:]
    return jnp.concatenate((first * cosine - second * sine, first * sine + second * cosine), axis=1)


def ein(spec, left, right):
    return jnp.einsum(spec, left, right, preferred_element_type=F32)


def per_device(
    tokens,
    cotangent,
    gain_first,
    gain_second,
    w_query,
    w_key,
    w_value,
    w_gate,
    w_output,
    w_hidden,
    w_linear,
    w_down,
    decay_scale,
    first_length,
):
    rows = tokens.shape[0]
    core = lax.axis_index("core")
    place = lax.axis_index("ctx")
    plane = lax.axis_index("tp")
    scalars = jnp.stack((core, plane, lax.axis_index("x"), place)).astype(jnp.int32)

    w_output = w_output.T
    w_down = w_down.T
    mine, theirs = split_heads((w_value, w_key, w_gate, w_output, w_query), scalars, "split_attn")
    came = swap(theirs)
    block, gathered = stack_attn(mine, came, scalars)
    lengths = jnp.concatenate((first_length, swap(first_length)))
    normed_first = enter_rows(tokens, gain_first.reshape(1, D), scalars, deps=(block,))
    w_kv = stack_blocks(
        spread_near(block), 0, 768, scalars, "stack_kv", deps=(normed_first, lengths)
    )
    w_goq = lax.all_gather(gathered, XY, axis=0, tiled=True).reshape(4, 4, 2, 64, -1)
    mine, theirs = split_heads(
        (w_hidden, w_linear, w_down), scalars, "split_mlp", deps=(gathered,)
    )
    came_mlp = swap(theirs)
    gain_first = gain_first.reshape(1, D)
    gain_second = gain_second.reshape(1, D)
    x_first = (normed_first, swap(normed_first))
    cot_low = low_rows(cotangent, scalars, deps=(x_first[1],))
    g_out = (cot_low, swap(cot_low))
    w_kv = spread_far(w_kv)

    rate = lax.dynamic_index_in_dim(decay_scale, core, 0, False) / 1024.0
    local = (jnp.arange(rows, dtype=jnp.int32) + plane * (rows // 4)) % rows
    index = place * rows + local
    document = (index[None, :] >= lengths[:, None]).astype(jnp.int32)
    carried = (document == 0).astype(F32)
    steps = local.astype(F32)
    offsets = local[:, None] - local[None, :]
    linked = (offsets >= 0)[None] & (document[:, :, None] == document[:, None, :])
    mask = jnp.where(
        linked, jnp.exp(-rate * jnp.maximum(offsets, 0).astype(F32))[None], 0.0
    )
    enter = (carried * jnp.exp(-rate * (steps + 1.0))[None])[:, :, None]
    leave = jnp.exp(-rate * (rows - 1.0 - steps))[None, :, None]
    fade = jnp.exp(-rate * rows)
    half = DK // 2
    frequency = 10000.0 ** (-(jnp.arange(half).astype(F32) / half))
    angles = index.astype(F32)[:, None] * frequency[None, :]
    cosine = jnp.tile(jnp.cos(angles), (2, 1))
    sine = jnp.tile(jnp.sin(angles), (2, 1))

    def carry(came):
        near, mid, far = [part.astype(F32) for part in came]
        return near + fade * (mid + fade * far)

    def spread_state(low, way):
        return [shift_open(low, "ctx", way * o) for o in (1, 2, 3)]

    projected = mm_in(*x_first, [(w_kv, 0, 768)], scalars, "project_kv")
    key = rotate(projected[:, DV:], cosine, sine).astype(BF).reshape(2, rows, DK)
    value = projected[:, :DV].astype(BF).reshape(2, rows, DV)
    key_out = (key.astype(F32) * leave).astype(BF)
    state_out = ein("gjd,gje->gde", key_out, value).astype(BF)
    came = spread_state(state_out, 1)
    w_mlp = lax.all_gather(
        stack_blocks((mine, came_mlp), 0, 1536, scalars, "stack_mlp", deps=came),
        XY,
        axis=0,
        tiled=True,
    ).reshape(4, 4, 2, 64, -1)
    projected = mm_in(
        *x_first, [(w_goq, 0, DV), (w_goq, 1024, DK)], scalars, "project_gq", deps=(state_out, mask, enter)
    )
    state_in = carry(came).astype(BF)
    gate_pre = projected[:, :DV]
    query = rotate(projected[:, DV:], cosine, sine).astype(BF).reshape(2, rows, DK)
    weighted = (ein("gid,gjd->gij", query, key) * mask).astype(BF)
    inner = ein("gij,gje->gie", weighted, value)
    retained = (inner + ein("gid,gde->gie", query, state_in) * enter).reshape(2 * rows, DV)
    mixed_full, gate_back = jax.vjp(gate_norm, gate_pre, retained)
    mixed = mixed_full.astype(BF)
    own, other = mm_back([(mixed, w_goq, DV)], scalars, "project_out")
    parts = tp_total(chip_blocks(own, swap(other)))
    grad_activated = mm_in(
        *g_out, [(w_mlp, 2 * DV, DV)], scalars, "back_down", deps=(other,)
    )
    hidden_state, normed_second = second_norm(tokens, parts, gain_second, scalars)
    x_second = (normed_second, swap(normed_second))
    paired = mm_in(*x_second, [(w_mlp, 0, 2 * DV)], scalars, "project_mlp")
    activated_full, gelu_back = jax.vjp(gelu_gate, paired[:, :DV], paired[:, DV:])
    activated = activated_full.astype(BF)
    grad_pair = jnp.concatenate(gelu_back(grad_activated), axis=1).astype(BF)
    own, other, gain_second_part = mm_back(
        [(grad_pair, w_mlp, 0)], scalars, "back_mlp", normed=x_second
    )
    grads, mark = mm_weight_into(
        None, ((x_second, grad_pair),), 1024, 3584, scalars, "weight_mlp"
    )
    mine, _ = tp_first(chip_blocks(own, swap(other)))
    (mine,) = tie((mine.astype(BF),), (mark,))
    parts = tp_second(mine)
    grads, mark = mm_weight_into(
        grads, ((g_out, activated),), 3072, 3584, scalars, "weight_down", deps=(mine,)
    )
    down = mm_back([(activated, w_mlp, 2 * DV)], scalars, "project_down", deps=(mine,))
    grad_state, grad_state_low = norm_back(
        hidden_state,
        cotangent,
        parts,
        gain_second,
        scalars,
        "second_back",
        deps=(down[1], mark),
    )
    g_state = (grad_state_low, swap(grad_state_low))
    grad_mixed = mm_in(*g_state, [(w_goq, DV, DV)], scalars, "back_out")
    grad_gate, grad_retained = gate_back(grad_mixed)
    grad_low = grad_retained.reshape(2, rows, DV).astype(BF)
    query_in = (query.astype(F32) * enter).astype(BF)
    back_out = ein("gid,gie->gde", query_in, grad_low).astype(BF)
    came = spread_state(back_out, -1)
    grad_scores = (ein("gie,gje->gij", grad_low, value) * mask).astype(BF)
    grad_query = ein("gij,gjd->gid", grad_scores, key) + enter * ein("gie,gde->gid", grad_low, state_in)
    grad_key = ein("gij,gid->gjd", grad_scores, query)
    grad_value = ein("gij,gie->gje", weighted, grad_low)
    grad_gate = grad_gate.astype(BF)
    grad_query = rotate(grad_query.reshape(2 * rows, DK), cosine, -sine).astype(BF)
    grads, mark = mm_weight_into(
        grads,
        ((g_state, mixed), (x_first, grad_gate)),
        2048,
        3584,
        scalars,
        "weight_og",
        deps=(back_out,),
    )
    grads, mark = mm_weight_into(
        grads, ((x_first, grad_query),), 768, 3584, scalars, "weight_query"
    )
    came[0] = tie((came[0],), (mark, grad_key, grad_value))[0]
    state_back = carry(came).astype(BF)
    grad_key += leave * ein("gje,gde->gjd", value, state_back)
    grad_value += ein("gjd,gde->gje", key_out, state_back)
    grad_key = rotate(grad_key.reshape(2 * rows, DK), cosine, -sine)
    grad_vk = jnp.concatenate(
        (grad_value.reshape(2 * rows, DV).astype(BF), grad_key.astype(BF)), axis=1
    )
    grads, mark = mm_weight_into(grads, ((x_first, grad_vk),), 0, 3584, scalars, "weight_vk")
    block = lax.psum_scatter(grads.reshape(2048, -1), XY, scatter_dimension=0, tiled=True)
    own, other, gain_first_part = mm_back(
        [(grad_vk, w_kv, 0), (grad_gate, w_goq, 0), (grad_query, w_goq, 1024)],
        scalars,
        "back_attn",
        normed=x_first,
        deps=(mark,),
    )
    down = (down[0], swap(tie((down[1],), (mark,))[0]))
    blocks = third_blocks(own, swap(other), *down, scalars)
    mine, _ = tp_first(blocks)
    gains = jnp.concatenate((gain_first_part[:1], gain_second_part[:1]))
    for axis, swapped in (
        ("core", (1, 0)),
        ("ctx", (1, 0, 3, 2)),
        ("ctx", (3, 2, 1, 0)),
        ("x", (1, 0, 3, 2)),
        ("x", (3, 2, 1, 0)),
    ):
        gains = gains + lax.ppermute(gains, axis, list(enumerate(swapped)))
    mine = jnp.concatenate((mine, gains, jnp.zeros((14, D), F32))).astype(BF)
    parts = tp_second(mine)
    gains = [part[128:130].astype(F32) for part in parts]
    gains = (gains[0] + gains[2]) + (gains[1] + gains[3])
    spot = (lax.axis_index("x") * 2 + core) * 4 + place
    gain_first_grad, gain_second_grad = [
        lax.dynamic_slice_in_dim(gains[k] / gain[0], spot * 64, 64, 0)
        for k, gain in ((0, gain_first), (1, gain_second))
    ]
    layer_out, input_grad = leave_rows(
        hidden_state, tokens, grad_state, parts, gain_first, scalars
    )
    block = tie((block,), (gain_first_grad, gain_second_grad, input_grad))[0].reshape(2, 64, -1)
    d_value, d_key, d_query, d_hidden, d_linear, d_output, d_gate, d_down = join_heads(
        block[0], swap(block[1]), (DV, DK, DK) + (DV,) * 5, scalars, "join_heads"
    )
    return (
        layer_out,
        input_grad,
        gain_first_grad,
        gain_second_grad,
        d_query,
        d_key,
        d_value,
        d_gate,
        d_output.T,
        d_hidden,
        d_linear,
        d_down.T,
    )


def solution(mesh):
    fine = Mesh(np.asarray(mesh.devices).reshape(4, 2, 4, 4), ("x", "core", "ctx", "tp"))
    split = ("x", "core", "ctx")
    row = P(split, None)
    win = P(split, "tp")
    wout = P("tp", split)
    in_specs = (row, row, P(), P(), win, win, win, win, wout, win, win, wout, P("tp"), P(("x", "core")))
    out_specs = (row, row, P(split), P(split), win, win, win, win, wout, win, win, wout)
    return jax.shard_map(
        per_device, mesh=fine, in_specs=in_specs, out_specs=out_specs, check_vma=False
    )
```

```python
import math

import jax
import jax.numpy as jnp
import numpy as np
from jax import lax
from jax.experimental import pallas as pl
from jax.experimental.pallas import tpu as pltpu
from jax.sharding import Mesh, PartitionSpec as P

D = 2048
DK = 256
DV = 512
SLAB = 512
BF = jnp.bfloat16
F32 = jnp.float32
XY = ("x", "ctx")
MIB = 1 << 20


def shift(value, axis, offset):
    n = lax.axis_size(axis)
    return lax.ppermute(value, axis, [(i, (i + offset) % n) for i in range(n)])


def shift_open(value, axis, offset):
    n = lax.axis_size(axis)
    return lax.ppermute(
        value, axis, [(i, i + offset) for i in range(n) if 0 <= i + offset < n]
    )


def swap(value):
    return lax.ppermute(value, "core", [(0, 1), (1, 0)])


def after(value, *earlier):
    return lax.optimization_barrier((value, *earlier))[0]


def call(
    body,
    grid,
    ins,
    outs,
    shapes,
    scalars,
    operands,
    name,
    scratch=(),
    deps=(),
    stream=False,
    aliases=None,
):
    count = len(operands)

    def kernel(s_ref, *refs):
        body(s_ref, *refs[:count], *refs[count + len(deps) :])

    ins = [*ins, *[pl.BlockSpec(memory_space=pl.ANY)] * len(deps)]
    return pl.pallas_call(
        kernel,
        out_shape=shapes,
        grid_spec=pltpu.PrefetchScalarGridSpec(
            num_scalar_prefetch=1, grid=grid, in_specs=ins, out_specs=outs, scratch_shapes=scratch
        ),
        compiler_params=pltpu.CompilerParams(
            vmem_limit_bytes=(60 if stream else 32) * MIB, dimension_semantics=("arbitrary",) * len(grid)
        ),
        cost_estimate=pl.CostEstimate(flops=1, bytes_accessed=1, transcendentals=0),
        input_output_aliases=aliases or {},
        name=name,
    )(scalars, *operands, *deps)


def tie(values, deps):
    count = len(values)
    anywhere = pl.BlockSpec(memory_space=pl.ANY)
    return pl.pallas_call(
        lambda *refs: None,
        out_shape=tuple(sds(v.shape, v.dtype) for v in values),
        in_specs=[anywhere] * (count + len(deps)),
        out_specs=(anywhere,) * count,
        input_output_aliases={i: i for i in range(count)},
        name="tie",
    )(*values, *deps)


def whole(array):
    return pl.BlockSpec(array.shape, lambda *_: (0,) * array.ndim)


def sds(shape, dtype):
    return jax.ShapeDtypeStruct(shape, dtype)


def weight_operands(weight, start, width):
    if not isinstance(weight, tuple):
        spec = pl.BlockSpec((1, 4, 2, 64, width), lambda i, s: (i, 0, 0, 0, start // width))
        return [weight], [spec]
    piece = math.gcd(start, width) if start else width
    operands, specs = [], []
    for at in range(start, start + width, piece):
        for stack in weight:
            operands.append(stack)
            specs.append(pl.BlockSpec((4, 2, 64, piece), lambda i, s, at=at: (0, 0, 0, at // piece)))
    return operands, specs


def load_slab(s_ref, refs, held):
    core = s_ref[0]
    if len(refs) == 1:
        return jnp.concatenate(
            [refs[0][0, y, jnp.bitwise_xor(c, core)] for c in (0, 1) for y in range(4)], axis=0
        )
    x_far = lax.rem(s_ref[2] + 4 - pl.program_id(0), 4)
    at = 0
    for first in range(0, len(refs), 4):
        stacks = refs[first : first + 4]
        width = stacks[0].shape[-1]
        for j in range(4):

            @pl.when((core == 0) & (x_far == j))
            def _(j=j, at=at, width=width, stacks=stacks):
                for i in range(4):
                    y = lax.rem(s_ref[3] + 4 - i, 4)
                    for c in (0, 1):
                        held[c * 4 + y, :, at : at + width] = stacks[j][i, c]

        @pl.when(core == 1)
        def _(at=at, width=width, stacks=stacks):
            for j in range(4):
                y = lax.rem(s_ref[3] + 4 - j, 4)
                for c in (0, 1):
                    held[c * 4 + y, :, at : at + width] = stacks[j][x_far, 1 - c]

        at += width
    return held[...].reshape(SLAB, at)


def hop(value, first, offset):
    pairs = []
    for x in range(4):
        for core in (0, 1):
            for y in range(4):
                to = ((x + offset) % 4, y) if (core == 0) == first else (x, (y + offset) % 4)
                pairs.append(((x * 2 + core) * 4 + y, (to[0] * 2 + core) * 4 + to[1]))
    return lax.ppermute(value, ("x", "core", "ctx"), pairs)


def spread_near(block):
    near, far, mid = [hop(block, False, o) for o in (1, 3, 2)]
    return block, near, mid, far


def stack_blocks(blocks, start, width, scalars, name, deps=()):
    at = start // width if start % width == 0 else None
    span = width if at is not None else blocks[0].shape[1]
    first = 0 if at is not None else start
    height = blocks[0].shape[0]

    def body(s_ref, *refs):
        for k, ref in enumerate(refs[:-1]):
            refs[-1][k * height : (k + 1) * height, :] = ref[:, first : first + width]

    total = sds((height * len(blocks), width), BF)
    return call(
        body,
        (1,),
        [pl.BlockSpec((height, span), lambda i, s: (0, at or 0))] * len(blocks),
        whole(total),
        total,
        scalars,
        tuple(blocks),
        name,
        deps=deps,
    )


def stack_attn(mine, came, scalars):
    height, total = mine.shape

    def body(s_ref, mine_ref, came_ref, first_ref, other_ref):
        for k, ref in enumerate((mine_ref, came_ref)):
            span = slice(k * height, (k + 1) * height)
            first_ref[span, :] = ref[:, :768]
            other_ref[span, :] = ref[:, 768:]

    shapes = (sds((2 * height, 768), BF), sds((2 * height, total - 768), BF))
    return call(
        body,
        (1,),
        [whole(mine), whole(came)],
        tuple(whole(s) for s in shapes),
        shapes,
        scalars,
        (mine, came),
        "stack_attn",
        stream=True,
    )


def spread_far(stack, gate=False):
    stack = stack.reshape(4, 2, 64, -1)
    near, far = hop(stack, True, 1), hop(stack, True, -1)
    mid = hop(tie((stack,), (near, far))[0] if gate else stack, True, 2)
    return stack, near, mid, far


def mm_in(left, right, columns, scalars, name, deps=(), stream=False):
    operands, specs, counts = [], [], []
    for weight, start, width in columns:
        ops, sp = weight_operands(weight, start, width)
        operands += ops
        specs += sp
        counts.append(len(ops))
    total = sum(width for _, _, width in columns)

    def body(s_ref, a_ref, b_ref, *refs):
        out_ref = refs[len(operands)]
        step = pl.program_id(0)
        rows = jnp.concatenate((a_ref[...], b_ref[...]), axis=0)
        at, first = 0, 0
        for k, count in enumerate(counts):
            width = columns[k][2]
            slab = load_slab(s_ref, refs[first : first + count], refs[len(operands) + 1 + k])
            part = jnp.dot(rows, slab, preferred_element_type=F32)
            span = slice(at, at + width)

            @pl.when(step == 0)
            def _(part=part, span=span):
                out_ref[:, span] = part

            @pl.when(step > 0)
            def _(part=part, span=span):
                out_ref[:, span] += part

            at += width
            first += count

    rows = left.shape[0]
    cols = pl.BlockSpec((rows, SLAB), lambda i, s: (0, i))
    return call(
        body,
        (4,),
        [cols, cols, *specs],
        pl.BlockSpec((2 * rows, total), lambda i, s: (0, 0)),
        sds((2 * rows, total), F32),
        scalars,
        (left, right, *operands),
        name,
        scratch=[pltpu.VMEM((8, 64, width), BF) for _, _, width in columns],
        deps=deps,
        stream=stream,
    )


def mm_back(terms, scalars, name, normed=None, deps=()):
    rows = terms[0][0].shape[0]
    half = rows // 2
    operands, specs, counts, scratch = [], [], [], []
    for grad, weight, start in terms:
        ops, sp = weight_operands(weight, start, grad.shape[1])
        operands += [grad, *ops]
        specs += [whole(grad), *sp]
        counts.append(len(ops))
        scratch.append(pltpu.VMEM((8, 64, grad.shape[1]), BF))
    held = len(operands)
    cols = pl.BlockSpec((half, SLAB), lambda i, s: (0, i))
    outs = [cols, cols]
    shapes = [sds((half, D), F32), sds((half, D), BF)]
    if normed is not None:
        operands += normed
        specs += [cols, cols]
        outs.append(pl.BlockSpec((8, SLAB), lambda i, s: (0, i)))
        shapes.append(sds((8, D), F32))
    total = len(operands)

    def body(s_ref, *refs):
        at, out = 0, 0.0
        for k, count in enumerate(counts):
            slab = load_slab(s_ref, refs[at + 1 : at + 1 + count], refs[total + len(outs) + k])
            out += lax.dot_general(
                refs[at][...], slab, (((1,), (1,)), ((), ())), preferred_element_type=F32
            )
            at += count + 1
        refs[total][...] = out[:half]
        refs[total + 1][...] = out[half:].astype(BF)
        if normed is not None:
            part = out[:half] * refs[held][...].astype(F32) + out[half:] * refs[held + 1][
                ...
            ].astype(F32)
            part = jnp.sum(part, axis=0, keepdims=True)
            refs[total + 2][...] = jnp.broadcast_to(part, (8, SLAB))

    return call(
        body,
        (4,),
        specs,
        tuple(outs),
        tuple(shapes),
        scalars,
        tuple(operands),
        name,
        scratch=scratch,
        deps=deps,
    )


def mm_weight_into(into, pairs, start, total, scalars, name, deps=()):
    widths = [grad.shape[1] for _, grad in pairs]
    rows = pairs[0][0][0].shape[0]
    span = sum(widths)

    def body(s_ref, *refs):
        out_ref, mark_ref = refs[-2:]
        at = 0
        for k, width in enumerate(widths):
            a_ref, b_ref, g_ref = refs[3 * k : 3 * k + 3]
            out = lax.dot_general(
                jnp.concatenate((a_ref[...], b_ref[...]), axis=0),
                g_ref[...],
                (((0,), (0,)), ((), ())),
                preferred_element_type=F32,
            ).astype(BF)
            for c in (0, 1):
                for y in range(4):
                    first = (c * 4 + y) * 64
                    out_ref[0, y, jnp.bitwise_xor(c, s_ref[0]), :, at : at + width] = out[
                        first : first + 64
                    ]
            at += width
        mark_ref[...] = jnp.zeros_like(mark_ref)

    cols = pl.BlockSpec((rows, SLAB), lambda i, s: (0, i))
    specs, operands = [], []
    for (a, b), grad in pairs:
        specs += [cols, cols, whole(grad)]
        operands += [a, b, grad]
    aliases = None
    if into is not None:
        aliases = {1 + len(operands): 0}
        specs.append(pl.BlockSpec(memory_space=pl.ANY))
        operands.append(into)
    return call(
        body,
        (4,),
        specs,
        (
            pl.BlockSpec((1, 4, 2, 64, span), lambda i, s: (i, 0, 0, 0, start // span)),
            pl.BlockSpec((8, 128), lambda i, s: (0, 0)),
        ),
        (sds((4, 4, 2, 64, total), BF), sds((8, 128), F32)),
        scalars,
        tuple(operands),
        name,
        deps=deps,
        stream=True,
        aliases=aliases,
    )


def split_heads(weights, scalars, name, deps=()):
    widths = [w.shape[1] // 2 for w in weights]

    def body(s_ref, *refs):
        mine_ref, theirs_ref = refs[-2:]
        core = s_ref[0]
        for out_ref, head in ((mine_ref, core), (theirs_ref, 1 - core)):
            at = 0
            for ref, width in zip(refs, widths):
                out_ref[:, at : at + width] = ref[:, pl.ds(pl.multiple_of(head * width, width), width)]
                at += width

    total = sum(widths)
    spec = pl.BlockSpec((64, total), lambda i, s: (0, 0))
    return call(
        body,
        (1,),
        [whole(w) for w in weights],
        (spec, spec),
        (sds((64, total), BF),) * 2,
        scalars,
        tuple(weights),
        name,
        deps=deps,
        stream=True,
    )


def join_heads(mine, theirs, widths, scalars, name):
    def body(s_ref, mine_ref, theirs_ref, *outs):
        core = s_ref[0]
        for in_ref, head in ((mine_ref, core), (theirs_ref, 1 - core)):
            at = 0
            for ref, width in zip(outs, widths):
                span = pl.ds(pl.multiple_of(head * width, width), width)
                ref[:, span] = in_ref[:, at : at + width].astype(F32)
                at += width

    shapes = tuple(sds((64, 2 * w), F32) for w in widths)
    return call(
        body,
        (1,),
        [whole(mine), whole(theirs)],
        tuple(whole(s) for s in shapes),
        shapes,
        scalars,
        (mine, theirs),
        name,
    )


def scale_of(values):
    return lax.rsqrt(jnp.mean(values * values, axis=-1, keepdims=True) + 1e-06)


def turned_spec(rows):
    return pl.BlockSpec((rows, D), lambda i, s: (lax.rem(i + s[1], 4), 0))


def plain_spec(rows):
    return pl.BlockSpec((rows, D), lambda i, s: (i, 0))


def enter_rows(tokens, gain, scalars, deps=()):
    rows = tokens.shape[0]
    block = rows // 4

    def body(s_ref, t_ref, g_ref, n_out):
        values = t_ref[...]
        n_out[...] = (values * scale_of(values) * g_ref[...]).astype(BF)

    return call(
        body,
        (4,),
        [turned_spec(block), whole(gain)],
        plain_spec(block),
        sds((rows, D), BF),
        scalars,
        (tokens, gain),
        "enter_rows",
        deps=deps,
    )


def low_rows(cotangent, scalars, deps=()):
    rows = cotangent.shape[0]
    block = rows // 4

    def body(s_ref, c_ref, l_out):
        l_out[...] = c_ref[...].astype(BF)

    return call(
        body,
        (4,),
        [turned_spec(block)],
        plain_spec(block),
        sds((rows, D), BF),
        scalars,
        (cotangent,),
        "low_rows",
        deps=deps,
    )


def each_part(refs, work):
    step = pl.program_id(0)
    for k, ref in enumerate(refs):

        @pl.when(step == k)
        def _(ref=ref):
            work(ref[...].astype(F32))


def second_norm(tokens, parts, gain, scalars, deps=()):
    rows = tokens.shape[0]
    block = rows // 4

    def body(s_ref, t_ref, g_ref, *refs):
        h_out, n_out = refs[4:]

        def work(part):
            values = t_ref[...] + part
            h_out[...] = values
            n_out[...] = (values * scale_of(values) * g_ref[...]).astype(BF)

        each_part(refs[:4], work)

    plain = plain_spec(block)
    return call(
        body,
        (4,),
        [turned_spec(block), whole(gain)] + [whole(p) for p in parts],
        (plain, plain),
        (sds((rows, D), F32), sds((rows, D), BF)),
        scalars,
        (tokens, gain, *parts),
        "second_norm",
        deps=deps,
    )


def third_blocks(own, came, down_own, down_came, scalars, deps=()):
    rows = own.shape[0]
    block = rows // 4

    def body(s_ref, own_ref, came_ref, d_ref, e_ref, *refs):
        total = own_ref[...] + came_ref[...].astype(F32)
        down = d_ref[...] + e_ref[...].astype(F32)
        step = pl.program_id(0)
        for k in range(4):

            @pl.when(step == k)
            def _(k=k):
                refs[k][:block] = total.astype(BF)
                refs[k][block:] = down.astype(BF)

    plain = plain_spec(block)
    shapes = (sds((2 * block, D), BF),) * 4
    return call(
        body,
        (4,),
        [plain] * 4,
        tuple(whole(s) for s in shapes),
        shapes,
        scalars,
        (own, came, down_own, down_came),
        "third_blocks",
        deps=deps,
        stream=True,
    )


def leave_rows(hidden, tokens, grad_state, parts, gain, scalars, deps=()):
    rows = hidden.shape[0]
    block = rows // 4

    def body(s_ref, h_ref, t_ref, u_ref, g_ref, *refs):
        def work(part):
            refs[4][...] = h_ref[...] + part[block : 2 * block]
            refs[5][...] = u_ref[...] + norm_grad(t_ref[...], part[:block], g_ref[...])

        each_part(refs[:4], work)

    plain, turn = plain_spec(block), turned_spec(block)
    return call(
        body,
        (4,),
        [plain, turn, plain, whole(gain)] + [whole(p) for p in parts],
        (turn, turn),
        (sds((rows, D), F32),) * 2,
        scalars,
        (hidden, tokens, grad_state, gain, *parts),
        "leave_rows",
        deps=deps,
        stream=True,
    )


def norm_grad(values, grad, gain):
    factor = scale_of(values)
    unit = values * factor
    scaled = grad * gain
    return factor * (scaled - unit * jnp.mean(scaled * unit, axis=-1, keepdims=True))


def norm_back(values, upstream, parts, gain, scalars, name, deps=()):
    rows = values.shape[0]
    block = rows // 4

    def body(s_ref, v_ref, u_ref, g_ref, *refs):
        def work(part):
            out = u_ref[...] + norm_grad(v_ref[...], part, g_ref[...])
            refs[4][...] = out
            refs[5][...] = out.astype(BF)

        each_part(refs[:4], work)

    plain = plain_spec(block)
    return call(
        body,
        (4,),
        [plain, turned_spec(block), whole(gain)] + [whole(p) for p in parts],
        (plain, plain),
        (sds((rows, D), F32), sds((rows, D), BF)),
        scalars,
        (values, upstream, gain, *parts),
        name,
        deps=deps,
        stream=True,
    )


def tp_first(blocks):
    got = [shift(blocks[o], "tp", o) for o in (1, 3, 2)]
    near, far, mid = [part.astype(F32) for part in got]
    return (blocks[0].astype(F32) + mid) + (near + far), got


def tp_second(mine):
    near, far, mid = [shift(mine, "tp", -o) for o in (1, 3, 2)]
    return mine, near, mid, far


def tp_total(blocks):
    return tp_second(tp_first(blocks)[0].astype(BF))


def chip_blocks(own, came):
    block = own.shape[0] // 4
    return [
        (own[o * block : (o + 1) * block] + came[o * block : (o + 1) * block].astype(F32)).astype(BF)
        for o in range(4)
    ]


def gate_norm(gate_pre, retained):
    centred = retained - jnp.mean(retained, axis=-1, keepdims=True)
    normed = centred * lax.rsqrt(jnp.mean(centred * centred, axis=-1, keepdims=True) + 1.0 * DK)
    return gate_pre * jax.nn.sigmoid(gate_pre) * normed


def gelu_gate(hidden, linear):
    return jax.nn.gelu(hidden, approximate=True) * linear


def rotate(values, cosine, sine):
    half = DK // 2
    first = values[:, :half]
    second = values[:, half:]
    return jnp.concatenate((first * cosine - second * sine, first * sine + second * cosine), axis=1)


def ein(spec, left, right):
    return jnp.einsum(spec, left, right, preferred_element_type=F32)


def per_device(
    tokens,
    cotangent,
    gain_first,
    gain_second,
    w_query,
    w_key,
    w_value,
    w_gate,
    w_output,
    w_hidden,
    w_linear,
    w_down,
    decay_scale,
    first_length,
):
    rows = tokens.shape[0]
    core = lax.axis_index("core")
    place = lax.axis_index("ctx")
    plane = lax.axis_index("tp")
    scalars = jnp.stack((core, plane, lax.axis_index("x"), place)).astype(jnp.int32)

    w_output = w_output.T
    w_down = w_down.T
    mine, theirs = split_heads((w_value, w_key, w_gate, w_output, w_query), scalars, "split_attn")
    came = swap(theirs)
    block, gathered = stack_attn(mine, came, scalars)
    lengths = jnp.concatenate((first_length, swap(first_length)))
    blocks = spread_near(block)
    w_kv = stack_blocks(blocks, 0, 768, scalars, "stack_kv", deps=(lengths,))
    normed_first = enter_rows(tokens, gain_first.reshape(1, D), scalars, deps=blocks[1:])
    w_goq = lax.all_gather(gathered, XY, axis=0, tiled=True).reshape(4, 4, 2, 64, -1)
    mine, theirs = split_heads(
        (w_hidden, w_linear, w_down), scalars, "split_mlp", deps=(gathered,)
    )
    came_mlp = swap(theirs)
    gain_first = gain_first.reshape(1, D)
    gain_second = gain_second.reshape(1, D)
    x_first = (normed_first, swap(normed_first))
    cot_low = low_rows(cotangent, scalars, deps=(x_first[1],))
    g_out = (cot_low, swap(cot_low))
    w_kv = spread_far(w_kv)

    rate = lax.dynamic_index_in_dim(decay_scale, core, 0, False) / 1024.0
    local = (jnp.arange(rows, dtype=jnp.int32) + plane * (rows // 4)) % rows
    index = place * rows + local
    document = (index[None, :] >= lengths[:, None]).astype(jnp.int32)
    carried = (document == 0).astype(F32)
    steps = local.astype(F32)
    offsets = local[:, None] - local[None, :]
    linked = (offsets >= 0)[None] & (document[:, :, None] == document[:, None, :])
    mask = jnp.where(
        linked, jnp.exp(-rate * jnp.maximum(offsets, 0).astype(F32))[None], 0.0
    )
    enter = (carried * jnp.exp(-rate * (steps + 1.0))[None])[:, :, None]
    leave = jnp.exp(-rate * (rows - 1.0 - steps))[None, :, None]
    fade = jnp.exp(-rate * rows)
    half = DK // 2
    frequency = 10000.0 ** (-(jnp.arange(half).astype(F32) / half))
    angles = index.astype(F32)[:, None] * frequency[None, :]
    cosine = jnp.tile(jnp.cos(angles), (2, 1))
    sine = jnp.tile(jnp.sin(angles), (2, 1))

    def carry(came):
        near, mid, far = [part.astype(F32) for part in came]
        return near + fade * (mid + fade * far)

    def spread_state(low, way):
        return [shift_open(low, "ctx", way * o) for o in (1, 2, 3)]

    projected = mm_in(*x_first, [(w_kv, 0, 768)], scalars, "project_kv")
    key = rotate(projected[:, DV:], cosine, sine).astype(BF).reshape(2, rows, DK)
    value = projected[:, :DV].astype(BF).reshape(2, rows, DV)
    key_out = (key.astype(F32) * leave).astype(BF)
    state_out = ein("gjd,gje->gde", key_out, value).astype(BF)
    came = spread_state(state_out, 1)
    w_mlp = lax.all_gather(
        stack_blocks((mine, came_mlp), 0, 1536, scalars, "stack_mlp", deps=came),
        XY,
        axis=0,
        tiled=True,
    ).reshape(4, 4, 2, 64, -1)
    projected = mm_in(
        *x_first,
        [(w_goq, 0, DV), (w_goq, 1024, DK)],
        scalars,
        "project_gq",
        deps=(state_out, mask, enter),
        stream=True,
    )
    state_in = carry(came).astype(BF)
    gate_pre = projected[:, :DV]
    query = rotate(projected[:, DV:], cosine, sine).astype(BF).reshape(2, rows, DK)
    weighted = (ein("gid,gjd->gij", query, key) * mask).astype(BF)
    inner = ein("gij,gje->gie", weighted, value)
    retained = (inner + ein("gid,gde->gie", query, state_in) * enter).reshape(2 * rows, DV)
    mixed_full, gate_back = jax.vjp(gate_norm, gate_pre, retained)
    mixed = mixed_full.astype(BF)
    own, other = mm_back([(mixed, w_goq, DV)], scalars, "project_out")
    parts = tp_total(chip_blocks(own, swap(other)))
    grad_activated = mm_in(
        *g_out, [(w_mlp, 2 * DV, DV)], scalars, "back_down", deps=(other,)
    )
    hidden_state, normed_second = second_norm(tokens, parts, gain_second, scalars)
    x_second = (normed_second, swap(normed_second))
    paired = mm_in(*x_second, [(w_mlp, 0, 2 * DV)], scalars, "project_mlp")
    activated_full, gelu_back = jax.vjp(gelu_gate, paired[:, :DV], paired[:, DV:])
    activated = activated_full.astype(BF)
    grad_pair = jnp.concatenate(gelu_back(grad_activated), axis=1).astype(BF)
    own, other, gain_second_part = mm_back(
        [(grad_pair, w_mlp, 0)], scalars, "back_mlp", normed=x_second
    )
    grads, mark = mm_weight_into(
        None, ((x_second, grad_pair),), 1024, 3584, scalars, "weight_mlp"
    )
    mine, _ = tp_first(chip_blocks(own, swap(other)))
    (mine,) = tie((mine.astype(BF),), (mark,))
    parts = tp_second(mine)
    down = mm_back([(activated, w_mlp, 2 * DV)], scalars, "project_down", deps=(mine,))
    grad_state, grad_state_low = norm_back(
        hidden_state,
        cotangent,
        parts,
        gain_second,
        scalars,
        "second_back",
        deps=(down[1],),
    )
    g_state = (grad_state_low, swap(grad_state_low))
    grad_mixed = mm_in(*g_state, [(w_goq, DV, DV)], scalars, "back_out", stream=True)
    grad_gate, grad_retained = gate_back(grad_mixed)
    grad_low = grad_retained.reshape(2, rows, DV).astype(BF)
    query_in = (query.astype(F32) * enter).astype(BF)
    back_out = ein("gid,gie->gde", query_in, grad_low).astype(BF)
    came = spread_state(back_out, -1)
    grad_scores = (ein("gie,gje->gij", grad_low, value) * mask).astype(BF)
    grad_query = ein("gij,gjd->gid", grad_scores, key) + enter * ein("gie,gde->gid", grad_low, state_in)
    grad_key = ein("gij,gid->gjd", grad_scores, query)
    grad_value = ein("gij,gie->gje", weighted, grad_low)
    grad_gate = grad_gate.astype(BF)
    grad_query = rotate(grad_query.reshape(2 * rows, DK), cosine, -sine).astype(BF)
    grads, mark = mm_weight_into(
        grads,
        ((g_state, mixed), (x_first, grad_gate)),
        2048,
        3584,
        scalars,
        "weight_og",
        deps=(back_out,),
    )
    grads, mark = mm_weight_into(
        grads, ((g_out, activated),), 3072, 3584, scalars, "weight_down"
    )
    grads, mark = mm_weight_into(
        grads, ((x_first, grad_query),), 768, 3584, scalars, "weight_query"
    )
    came[0] = tie((came[0],), (mark, grad_key, grad_value))[0]
    state_back = carry(came).astype(BF)
    grad_key += leave * ein("gje,gde->gjd", value, state_back)
    grad_value += ein("gjd,gde->gje", key_out, state_back)
    grad_key = rotate(grad_key.reshape(2 * rows, DK), cosine, -sine)
    grad_vk = jnp.concatenate(
        (grad_value.reshape(2 * rows, DV).astype(BF), grad_key.astype(BF)), axis=1
    )
    grads, mark = mm_weight_into(grads, ((x_first, grad_vk),), 0, 3584, scalars, "weight_vk")
    block = lax.psum_scatter(grads.reshape(2048, -1), XY, scatter_dimension=0, tiled=True)
    own, other, gain_first_part = mm_back(
        [(grad_vk, w_kv, 0), (grad_gate, w_goq, 0), (grad_query, w_goq, 1024)],
        scalars,
        "back_attn",
        normed=x_first,
        deps=(mark,),
    )
    down = (down[0], swap(tie((down[1],), (mark,))[0]))
    blocks = third_blocks(own, swap(other), *down, scalars)
    mine, _ = tp_first(blocks)
    gains = jnp.concatenate((gain_first_part[:1], gain_second_part[:1]))
    for axis, swapped in (
        ("core", (1, 0)),
        ("ctx", (1, 0, 3, 2)),
        ("ctx", (3, 2, 1, 0)),
        ("x", (1, 0, 3, 2)),
        ("x", (3, 2, 1, 0)),
    ):
        gains = gains + lax.ppermute(gains, axis, list(enumerate(swapped)))
    mine = jnp.concatenate((mine, gains, jnp.zeros((14, D), F32))).astype(BF)
    parts = tp_second(mine)
    gains = [part[128:130].astype(F32) for part in parts]
    gains = (gains[0] + gains[2]) + (gains[1] + gains[3])
    spot = (lax.axis_index("x") * 2 + core) * 4 + place
    gain_first_grad, gain_second_grad = [
        lax.dynamic_slice_in_dim(gains[k] / gain[0], spot * 64, 64, 0)
        for k, gain in ((0, gain_first), (1, gain_second))
    ]
    layer_out, input_grad = leave_rows(
        hidden_state, tokens, grad_state, parts, gain_first, scalars
    )
    block = tie((block,), (gain_first_grad, gain_second_grad, input_grad))[0].reshape(2, 64, -1)
    d_value, d_key, d_query, d_hidden, d_linear, d_output, d_gate, d_down = join_heads(
        block[0], swap(block[1]), (DV, DK, DK) + (DV,) * 5, scalars, "join_heads"
    )
    return (
        layer_out,
        input_grad,
        gain_first_grad,
        gain_second_grad,
        d_query,
        d_key,
        d_value,
        d_gate,
        d_output.T,
        d_hidden,
        d_linear,
        d_down.T,
    )


def solution(mesh):
    fine = Mesh(np.asarray(mesh.devices).reshape(4, 2, 4, 4), ("x", "core", "ctx", "tp"))
    split = ("x", "core", "ctx")
    row = P(split, None)
    win = P(split, "tp")
    wout = P("tp", split)
    in_specs = (row, row, P(), P(), win, win, win, win, wout, win, win, wout, P("tp"), P(("x", "core")))
    out_specs = (row, row, P(split), P(split), win, win, win, win, wout, win, win, wout)
    return jax.shard_map(
        per_device, mesh=fine, in_specs=in_specs, out_specs=out_specs, check_vma=False
    )
```

```python
import math

import jax
import jax.numpy as jnp
import numpy as np
from jax import lax
from jax.experimental import pallas as pl
from jax.experimental.pallas import tpu as pltpu
from jax.sharding import Mesh, PartitionSpec as P

D = 2048
DK = 256
DV = 512
SLAB = 512
BF = jnp.bfloat16
F32 = jnp.float32
XY = ("x", "ctx")
MIB = 1 << 20


def shift(value, axis, offset):
    n = lax.axis_size(axis)
    return lax.ppermute(value, axis, [(i, (i + offset) % n) for i in range(n)])


def shift_open(value, axis, offset):
    n = lax.axis_size(axis)
    return lax.ppermute(
        value, axis, [(i, i + offset) for i in range(n) if 0 <= i + offset < n]
    )


def swap(value):
    return lax.ppermute(value, "core", [(0, 1), (1, 0)])


def after(value, *earlier):
    return lax.optimization_barrier((value, *earlier))[0]


def call(
    body,
    grid,
    ins,
    outs,
    shapes,
    scalars,
    operands,
    name,
    scratch=(),
    deps=(),
    stream=False,
    aliases=None,
):
    count = len(operands)

    def kernel(s_ref, *refs):
        body(s_ref, *refs[:count], *refs[count + len(deps) :])

    ins = [*ins, *[pl.BlockSpec(memory_space=pl.ANY)] * len(deps)]
    return pl.pallas_call(
        kernel,
        out_shape=shapes,
        grid_spec=pltpu.PrefetchScalarGridSpec(
            num_scalar_prefetch=1, grid=grid, in_specs=ins, out_specs=outs, scratch_shapes=scratch
        ),
        compiler_params=pltpu.CompilerParams(
            vmem_limit_bytes=(60 if stream else 32) * MIB, dimension_semantics=("arbitrary",) * len(grid)
        ),
        cost_estimate=pl.CostEstimate(flops=1, bytes_accessed=1, transcendentals=0),
        input_output_aliases=aliases or {},
        name=name,
    )(scalars, *operands, *deps)


def tie(values, deps):
    count = len(values)
    anywhere = pl.BlockSpec(memory_space=pl.ANY)
    return pl.pallas_call(
        lambda *refs: None,
        out_shape=tuple(sds(v.shape, v.dtype) for v in values),
        in_specs=[anywhere] * (count + len(deps)),
        out_specs=(anywhere,) * count,
        input_output_aliases={i: i for i in range(count)},
        name="tie",
    )(*values, *deps)


def whole(array):
    return pl.BlockSpec(array.shape, lambda *_: (0,) * array.ndim)


def sds(shape, dtype):
    return jax.ShapeDtypeStruct(shape, dtype)


def weight_operands(weight, start, width):
    if not isinstance(weight, tuple):
        spec = pl.BlockSpec((1, 4, 2, 64, width), lambda i, s: (i, 0, 0, 0, start // width))
        return [weight], [spec]
    piece = math.gcd(start, width) if start else width
    operands, specs = [], []
    for at in range(start, start + width, piece):
        for stack in weight:
            operands.append(stack)
            specs.append(pl.BlockSpec((4, 2, 64, piece), lambda i, s, at=at: (0, 0, 0, at // piece)))
    return operands, specs


def load_slab(s_ref, refs, held):
    core = s_ref[0]
    if len(refs) == 1:
        return jnp.concatenate(
            [refs[0][0, y, jnp.bitwise_xor(c, core)] for c in (0, 1) for y in range(4)], axis=0
        )
    x_far = lax.rem(s_ref[2] + 4 - pl.program_id(0), 4)
    at = 0
    for first in range(0, len(refs), 4):
        stacks = refs[first : first + 4]
        width = stacks[0].shape[-1]
        for j in range(4):

            @pl.when((core == 0) & (x_far == j))
            def _(j=j, at=at, width=width, stacks=stacks):
                for i in range(4):
                    y = lax.rem(s_ref[3] + 4 - i, 4)
                    for c in (0, 1):
                        held[c * 4 + y, :, at : at + width] = stacks[j][i, c]

        @pl.when(core == 1)
        def _(at=at, width=width, stacks=stacks):
            for j in range(4):
                y = lax.rem(s_ref[3] + 4 - j, 4)
                for c in (0, 1):
                    held[c * 4 + y, :, at : at + width] = stacks[j][x_far, 1 - c]

        at += width
    return held[...].reshape(SLAB, at)


def hop(value, first, offset):
    pairs = []
    for x in range(4):
        for core in (0, 1):
            for y in range(4):
                to = ((x + offset) % 4, y) if (core == 0) == first else (x, (y + offset) % 4)
                pairs.append(((x * 2 + core) * 4 + y, (to[0] * 2 + core) * 4 + to[1]))
    return lax.ppermute(value, ("x", "core", "ctx"), pairs)


def spread_near(block):
    near, far, mid = [hop(block, False, o) for o in (1, 3, 2)]
    return block, near, mid, far


def stack_blocks(blocks, start, width, scalars, name, deps=()):
    at = start // width if start % width == 0 else None
    span = width if at is not None else blocks[0].shape[1]
    first = 0 if at is not None else start
    height = blocks[0].shape[0]

    def body(s_ref, *refs):
        for k, ref in enumerate(refs[:-1]):
            refs[-1][k * height : (k + 1) * height, :] = ref[:, first : first + width]

    total = sds((height * len(blocks), width), BF)
    return call(
        body,
        (1,),
        [pl.BlockSpec((height, span), lambda i, s: (0, at or 0))] * len(blocks),
        whole(total),
        total,
        scalars,
        tuple(blocks),
        name,
        deps=deps,
    )


def stack_attn(mine, came, scalars):
    height, total = mine.shape

    def body(s_ref, mine_ref, came_ref, first_ref, other_ref):
        for k, ref in enumerate((mine_ref, came_ref)):
            span = slice(k * height, (k + 1) * height)
            first_ref[span, :] = ref[:, :768]
            other_ref[span, :] = ref[:, 768:]

    shapes = (sds((2 * height, 768), BF), sds((2 * height, total - 768), BF))
    return call(
        body,
        (1,),
        [whole(mine), whole(came)],
        tuple(whole(s) for s in shapes),
        shapes,
        scalars,
        (mine, came),
        "stack_attn",
        stream=True,
    )


def spread_far(stack, gate=False):
    stack = stack.reshape(4, 2, 64, -1)
    near, far = hop(stack, True, 1), hop(stack, True, -1)
    mid = hop(tie((stack,), (near, far))[0] if gate else stack, True, 2)
    return stack, near, mid, far


def mm_in(left, right, columns, scalars, name, deps=(), stream=False):
    operands, specs, counts = [], [], []
    for weight, start, width in columns:
        ops, sp = weight_operands(weight, start, width)
        operands += ops
        specs += sp
        counts.append(len(ops))
    total = sum(width for _, _, width in columns)

    def body(s_ref, a_ref, b_ref, *refs):
        out_ref = refs[len(operands)]
        step = pl.program_id(0)
        rows = jnp.concatenate((a_ref[...], b_ref[...]), axis=0)
        at, first = 0, 0
        for k, count in enumerate(counts):
            width = columns[k][2]
            slab = load_slab(s_ref, refs[first : first + count], refs[len(operands) + 1 + k])
            part = jnp.dot(rows, slab, preferred_element_type=F32)
            span = slice(at, at + width)

            @pl.when(step == 0)
            def _(part=part, span=span):
                out_ref[:, span] = part

            @pl.when(step > 0)
            def _(part=part, span=span):
                out_ref[:, span] += part

            at += width
            first += count

    rows = left.shape[0]
    cols = pl.BlockSpec((rows, SLAB), lambda i, s: (0, i))
    return call(
        body,
        (4,),
        [cols, cols, *specs],
        pl.BlockSpec((2 * rows, total), lambda i, s: (0, 0)),
        sds((2 * rows, total), F32),
        scalars,
        (left, right, *operands),
        name,
        scratch=[pltpu.VMEM((8, 64, width), BF) for _, _, width in columns],
        deps=deps,
        stream=stream,
    )


def mm_back(terms, scalars, name, normed=None, deps=()):
    rows = terms[0][0].shape[0]
    half = rows // 2
    operands, specs, counts, scratch = [], [], [], []
    for grad, weight, start in terms:
        ops, sp = weight_operands(weight, start, grad.shape[1])
        operands += [grad, *ops]
        specs += [whole(grad), *sp]
        counts.append(len(ops))
        scratch.append(pltpu.VMEM((8, 64, grad.shape[1]), BF))
    held = len(operands)
    cols = pl.BlockSpec((half, SLAB), lambda i, s: (0, i))
    outs = [cols, cols]
    shapes = [sds((half, D), F32), sds((half, D), BF)]
    if normed is not None:
        operands += normed
        specs += [cols, cols]
        outs.append(pl.BlockSpec((8, SLAB), lambda i, s: (0, i)))
        shapes.append(sds((8, D), F32))
    total = len(operands)

    def body(s_ref, *refs):
        at, out = 0, 0.0
        for k, count in enumerate(counts):
            slab = load_slab(s_ref, refs[at + 1 : at + 1 + count], refs[total + len(outs) + k])
            out += lax.dot_general(
                refs[at][...], slab, (((1,), (1,)), ((), ())), preferred_element_type=F32
            )
            at += count + 1
        refs[total][...] = out[:half]
        refs[total + 1][...] = out[half:].astype(BF)
        if normed is not None:
            part = out[:half] * refs[held][...].astype(F32) + out[half:] * refs[held + 1][
                ...
            ].astype(F32)
            part = jnp.sum(part, axis=0, keepdims=True)
            refs[total + 2][...] = jnp.broadcast_to(part, (8, SLAB))

    return call(
        body,
        (4,),
        specs,
        tuple(outs),
        tuple(shapes),
        scalars,
        tuple(operands),
        name,
        scratch=scratch,
        deps=deps,
    )


def split_out(out, own_ref, other_ref):
    half = out.shape[0] // 2
    own_ref[...] = out[:half]
    other_ref[...] = out[half:].astype(BF)


def retain(x_pair, weight, key, value, came, fade, mask, enter, cosine, sine, scalars):
    rows = x_pair[0].shape[0]

    def body(
        s_ref, a_ref, b_ref, w_ref, k_ref, v_ref, near_ref, mid_ref, far_ref, f_ref, m_ref, e_ref,
        cos_ref, sin_ref, own_ref, other_ref, query_ref, state_ref, weighted_ref, gate_ref,
        retained_ref, mixed_ref, sums, turned
    ):
        step = pl.program_id(0)

        @pl.when(step < 4)
        def _():
            slab = load_slab(s_ref, (w_ref,), None)
            turned[step] = slab[:, DV : 2 * DV]
            left = jnp.concatenate((a_ref[...], b_ref[...]), axis=0)
            gate = jnp.dot(left, slab[:, :DV], preferred_element_type=F32)
            query = jnp.dot(left, slab[:, 2 * DV :], preferred_element_type=F32)

            @pl.when(step == 0)
            def _():
                gate_ref[...] = gate
                sums[...] = query

            @pl.when(step > 0)
            def _():
                gate_ref[...] += gate
                sums[...] += query

        @pl.when(step == 3)
        def _():
            fade = f_ref[...]
            for g in (0, 1):
                span = slice(g * rows, (g + 1) * rows)
                state = near_ref[g].astype(F32) + fade * (
                    mid_ref[g].astype(F32) + fade * far_ref[g].astype(F32)
                )
                state_ref[g] = state.astype(BF)
                query = rotate(sums[span], cos_ref[span], sin_ref[span]).astype(BF)
                query_ref[span] = query
                scores = lax.dot_general(
                    query, k_ref[g], (((1,), (1,)), ((), ())), preferred_element_type=F32
                )
                weighted = (scores * m_ref[g]).astype(BF)
                weighted_ref[g] = weighted
                retained = jnp.dot(weighted, v_ref[g], preferred_element_type=F32)
                retained += e_ref[span] * jnp.dot(
                    query, state_ref[g], preferred_element_type=F32
                )
                retained_ref[span] = retained
                mixed_ref[span] = gate_norm(gate_ref[span], retained).astype(BF)

        @pl.when(step >= 4)
        def _():
            out = lax.dot_general(
                mixed_ref[...],
                turned[step - 4],
                (((1,), (1,)), ((), ())),
                preferred_element_type=F32,
            )
            split_out(out, own_ref, other_ref)

    cols = pl.BlockSpec((rows, SLAB), lambda i, s: (0, jnp.minimum(i, 3)))
    later = pl.BlockSpec((rows, SLAB), lambda i, s: (0, jnp.maximum(i - 4, 0)))
    operands = (*x_pair, weight, key, value, *came, fade, mask, enter, cosine, sine)
    shapes = (
        sds((rows, D), F32),
        sds((rows, D), BF),
        sds((2 * rows, DK), BF),
        sds((2, DK, DV), BF),
        sds((2, rows, rows), BF),
        sds((2 * rows, DV), F32),
        sds((2 * rows, DV), F32),
        sds((2 * rows, DV), BF),
    )
    block = pl.BlockSpec((1, 4, 2, 64, 1280), lambda i, s: (jnp.minimum(i, 3), 0, 0, 0, 0))
    return call(
        body,
        (8,),
        [cols, cols, block] + [whole(o) for o in operands[3:]],
        (later, later) + tuple(whole(s) for s in shapes[2:]),
        shapes,
        scalars,
        operands,
        "retain",
        scratch=[pltpu.VMEM((2 * rows, DK), F32), pltpu.VMEM((4, SLAB, DV), BF)],
        stream=True,
    )


def mlp(x_pair, g_pair, weight, scalars):
    rows = x_pair[0].shape[0]

    def body(
        s_ref, a_ref, b_ref, c_ref, d_ref, w_ref, own_ref, other_ref, gain_ref, pair_ref, act_ref,
        both, back, kept
    ):
        step = pl.program_id(0)

        @pl.when(step < 4)
        def _():
            slab = load_slab(s_ref, (w_ref,), None)
            kept[step] = slab[:, : 2 * DV]
            left = jnp.concatenate((a_ref[...], b_ref[...]), axis=0)
            grad = jnp.concatenate((c_ref[...], d_ref[...]), axis=0)
            up = jnp.dot(left, slab[:, : 2 * DV], preferred_element_type=F32)
            down = jnp.dot(grad, slab[:, 2 * DV :], preferred_element_type=F32)

            @pl.when(step == 0)
            def _():
                both[...] = up
                back[...] = down

            @pl.when(step > 0)
            def _():
                both[...] += up
                back[...] += down

        @pl.when(step == 3)
        def _():
            def chunk(k, carry):
                span = pl.ds(pl.multiple_of(k * 64, 64), 64)
                hidden, linear, grad = both[span, :DV], both[span, DV:], back[span, :]
                cube = 0.044715 * hidden * hidden
                bent = jnp.tanh(0.7978845608 * hidden * (1.0 + cube))
                half = 0.5 * (1.0 + bent)
                gelu = hidden * half
                slope = half + 0.5 * hidden * (1.0 - bent * bent) * (
                    0.7978845608 * (1.0 + 3.0 * cube)
                )
                act_ref[span, :] = (gelu * linear).astype(BF)
                pair_ref[span, :DV] = (grad * linear * slope).astype(BF)
                pair_ref[span, DV:] = (grad * gelu).astype(BF)
                return carry

            lax.fori_loop(0, 2 * rows // 64, chunk, 0)

        @pl.when(step >= 4)
        def _():
            out = lax.dot_general(
                pair_ref[...], kept[step - 4], (((1,), (1,)), ((), ())), preferred_element_type=F32
            )
            split_out(out, own_ref, other_ref)
            part = out[:rows] * a_ref[...].astype(F32) + out[rows:] * b_ref[...].astype(F32)
            gain_ref[...] = jnp.broadcast_to(jnp.sum(part, axis=0, keepdims=True), (8, SLAB))

    cols = pl.BlockSpec((rows, SLAB), lambda i, s: (0, lax.rem(i, 4)))
    once = pl.BlockSpec((rows, SLAB), lambda i, s: (0, jnp.minimum(i, 3)))
    block = pl.BlockSpec((1, 4, 2, 64, 3 * DV), lambda i, s: (jnp.minimum(i, 3), 0, 0, 0, 0))
    later = pl.BlockSpec((rows, SLAB), lambda i, s: (0, jnp.maximum(i - 4, 0)))
    shapes = (
        sds((rows, D), F32),
        sds((rows, D), BF),
        sds((8, D), F32),
        sds((2 * rows, 2 * DV), BF),
        sds((2 * rows, DV), BF),
    )
    return call(
        body,
        (8,),
        [cols, cols, once, once, block],
        (
            later,
            later,
            pl.BlockSpec((8, SLAB), lambda i, s: (0, jnp.maximum(i - 4, 0))),
            whole(shapes[3]),
            whole(shapes[4]),
        ),
        shapes,
        scalars,
        (*x_pair, *g_pair, weight),
        "mlp",
        scratch=[
            pltpu.VMEM((2 * rows, 2 * DV), F32),
            pltpu.VMEM((2 * rows, DV), F32),
            pltpu.VMEM((4, SLAB, 2 * DV), BF),
        ],
        stream=True,
    )


def mm_weight_into(into, pairs, start, total, scalars, name, deps=()):
    widths = [grad.shape[1] for _, grad in pairs]
    rows = pairs[0][0][0].shape[0]
    span = sum(widths)

    def body(s_ref, *refs):
        out_ref, mark_ref = refs[-2:]
        at = 0
        for k, width in enumerate(widths):
            a_ref, b_ref, g_ref = refs[3 * k : 3 * k + 3]
            out = lax.dot_general(
                jnp.concatenate((a_ref[...], b_ref[...]), axis=0),
                g_ref[...],
                (((0,), (0,)), ((), ())),
                preferred_element_type=F32,
            ).astype(BF)
            for c in (0, 1):
                for y in range(4):
                    first = (c * 4 + y) * 64
                    out_ref[0, y, jnp.bitwise_xor(c, s_ref[0]), :, at : at + width] = out[
                        first : first + 64
                    ]
            at += width
        mark_ref[...] = jnp.zeros_like(mark_ref)

    cols = pl.BlockSpec((rows, SLAB), lambda i, s: (0, i))
    specs, operands = [], []
    for (a, b), grad in pairs:
        specs += [cols, cols, whole(grad)]
        operands += [a, b, grad]
    aliases = None
    if into is not None:
        aliases = {1 + len(operands): 0}
        specs.append(pl.BlockSpec(memory_space=pl.ANY))
        operands.append(into)
    return call(
        body,
        (4,),
        specs,
        (
            pl.BlockSpec((1, 4, 2, 64, span), lambda i, s: (i, 0, 0, 0, start // span)),
            pl.BlockSpec((8, 128), lambda i, s: (0, 0)),
        ),
        (sds((4, 4, 2, 64, total), BF), sds((8, 128), F32)),
        scalars,
        tuple(operands),
        name,
        deps=deps,
        stream=True,
        aliases=aliases,
    )


def split_heads(weights, scalars, name, deps=()):
    widths = [w.shape[1] // 2 for w in weights]

    def body(s_ref, *refs):
        mine_ref, theirs_ref = refs[-2:]
        core = s_ref[0]
        for out_ref, head in ((mine_ref, core), (theirs_ref, 1 - core)):
            at = 0
            for ref, width in zip(refs, widths):
                out_ref[:, at : at + width] = ref[:, pl.ds(pl.multiple_of(head * width, width), width)]
                at += width

    total = sum(widths)
    spec = pl.BlockSpec((64, total), lambda i, s: (0, 0))
    return call(
        body,
        (1,),
        [whole(w) for w in weights],
        (spec, spec),
        (sds((64, total), BF),) * 2,
        scalars,
        tuple(weights),
        name,
        deps=deps,
        stream=True,
    )


def join_heads(mine, theirs, widths, scalars, name):
    def body(s_ref, mine_ref, theirs_ref, *outs):
        core = s_ref[0]
        for in_ref, head in ((mine_ref, core), (theirs_ref, 1 - core)):
            at = 0
            for ref, width in zip(outs, widths):
                span = pl.ds(pl.multiple_of(head * width, width), width)
                ref[:, span] = in_ref[:, at : at + width].astype(F32)
                at += width

    shapes = tuple(sds((64, 2 * w), F32) for w in widths)
    return call(
        body,
        (1,),
        [whole(mine), whole(theirs)],
        tuple(whole(s) for s in shapes),
        shapes,
        scalars,
        (mine, theirs),
        name,
    )


def scale_of(values):
    return lax.rsqrt(jnp.mean(values * values, axis=-1, keepdims=True) + 1e-06)


def turned_spec(rows):
    return pl.BlockSpec((rows, D), lambda i, s: (lax.rem(i + s[1], 4), 0))


def plain_spec(rows):
    return pl.BlockSpec((rows, D), lambda i, s: (i, 0))


def enter_rows(tokens, gain, scalars, deps=()):
    rows = tokens.shape[0]
    block = rows // 4

    def body(s_ref, t_ref, g_ref, n_out):
        values = t_ref[...]
        n_out[...] = (values * scale_of(values) * g_ref[...]).astype(BF)

    return call(
        body,
        (4,),
        [turned_spec(block), whole(gain)],
        plain_spec(block),
        sds((rows, D), BF),
        scalars,
        (tokens, gain),
        "enter_rows",
        deps=deps,
    )


def low_rows(cotangent, scalars, deps=()):
    rows = cotangent.shape[0]
    block = rows // 4

    def body(s_ref, c_ref, l_out):
        l_out[...] = c_ref[...].astype(BF)

    return call(
        body,
        (4,),
        [turned_spec(block)],
        plain_spec(block),
        sds((rows, D), BF),
        scalars,
        (cotangent,),
        "low_rows",
        deps=deps,
    )


def each_part(refs, work):
    step = pl.program_id(0)
    for k, ref in enumerate(refs):

        @pl.when(step == k)
        def _(ref=ref):
            work(ref[...].astype(F32))


def second_norm(tokens, parts, gain, scalars, deps=()):
    rows = tokens.shape[0]
    block = rows // 4

    def body(s_ref, t_ref, g_ref, *refs):
        h_out, n_out = refs[4:]

        def work(part):
            values = t_ref[...] + part
            h_out[...] = values
            n_out[...] = (values * scale_of(values) * g_ref[...]).astype(BF)

        each_part(refs[:4], work)

    plain = plain_spec(block)
    return call(
        body,
        (4,),
        [turned_spec(block), whole(gain)] + [whole(p) for p in parts],
        (plain, plain),
        (sds((rows, D), F32), sds((rows, D), BF)),
        scalars,
        (tokens, gain, *parts),
        "second_norm",
        deps=deps,
    )


def third_blocks(own, came, down_own, down_came, scalars, deps=()):
    rows = own.shape[0]
    block = rows // 4

    def body(s_ref, own_ref, came_ref, d_ref, e_ref, *refs):
        total = own_ref[...] + came_ref[...].astype(F32)
        down = d_ref[...] + e_ref[...].astype(F32)
        step = pl.program_id(0)
        for k in range(4):

            @pl.when(step == k)
            def _(k=k):
                refs[k][:block] = total.astype(BF)
                refs[k][block:] = down.astype(BF)

    plain = plain_spec(block)
    shapes = (sds((2 * block, D), BF),) * 4
    return call(
        body,
        (4,),
        [plain] * 4,
        tuple(whole(s) for s in shapes),
        shapes,
        scalars,
        (own, came, down_own, down_came),
        "third_blocks",
        deps=deps,
        stream=True,
    )


def leave_rows(hidden, tokens, grad_state, parts, gain, scalars, deps=()):
    rows = hidden.shape[0]
    block = rows // 4

    def body(s_ref, h_ref, t_ref, u_ref, g_ref, *refs):
        def work(part):
            refs[4][...] = h_ref[...] + part[block : 2 * block]
            refs[5][...] = u_ref[...] + norm_grad(t_ref[...], part[:block], g_ref[...])

        each_part(refs[:4], work)

    plain, turn = plain_spec(block), turned_spec(block)
    return call(
        body,
        (4,),
        [plain, turn, plain, whole(gain)] + [whole(p) for p in parts],
        (turn, turn),
        (sds((rows, D), F32),) * 2,
        scalars,
        (hidden, tokens, grad_state, gain, *parts),
        "leave_rows",
        deps=deps,
        stream=True,
    )


def norm_grad(values, grad, gain):
    factor = scale_of(values)
    unit = values * factor
    scaled = grad * gain
    return factor * (scaled - unit * jnp.mean(scaled * unit, axis=-1, keepdims=True))


def norm_back(values, upstream, parts, gain, scalars, name, deps=()):
    rows = values.shape[0]
    block = rows // 4

    def body(s_ref, v_ref, u_ref, g_ref, *refs):
        def work(part):
            out = u_ref[...] + norm_grad(v_ref[...], part, g_ref[...])
            refs[4][...] = out
            refs[5][...] = out.astype(BF)

        each_part(refs[:4], work)

    plain = plain_spec(block)
    return call(
        body,
        (4,),
        [plain, turned_spec(block), whole(gain)] + [whole(p) for p in parts],
        (plain, plain),
        (sds((rows, D), F32), sds((rows, D), BF)),
        scalars,
        (values, upstream, gain, *parts),
        name,
        deps=deps,
        stream=True,
    )


def tp_first(blocks):
    got = [shift(blocks[o], "tp", o) for o in (1, 3, 2)]
    near, far, mid = [part.astype(F32) for part in got]
    return (blocks[0].astype(F32) + mid) + (near + far), got


def tp_second(mine):
    near, far, mid = [shift(mine, "tp", -o) for o in (1, 3, 2)]
    return mine, near, mid, far


def tp_total(blocks):
    return tp_second(tp_first(blocks)[0].astype(BF))


def chip_blocks(own, came):
    block = own.shape[0] // 4
    return [
        (own[o * block : (o + 1) * block] + came[o * block : (o + 1) * block].astype(F32)).astype(BF)
        for o in range(4)
    ]


def gate_norm(gate_pre, retained):
    centred = retained - jnp.mean(retained, axis=-1, keepdims=True)
    normed = centred * lax.rsqrt(jnp.mean(centred * centred, axis=-1, keepdims=True) + 1.0 * DK)
    return gate_pre * jax.nn.sigmoid(gate_pre) * normed


def gelu_gate(hidden, linear):
    return jax.nn.gelu(hidden, approximate=True) * linear


def rotate(values, cosine, sine):
    half = DK // 2
    first = values[:, :half]
    second = values[:, half:]
    return jnp.concatenate((first * cosine - second * sine, first * sine + second * cosine), axis=1)


def ein(spec, left, right):
    return jnp.einsum(spec, left, right, preferred_element_type=F32)


def per_device(
    tokens,
    cotangent,
    gain_first,
    gain_second,
    w_query,
    w_key,
    w_value,
    w_gate,
    w_output,
    w_hidden,
    w_linear,
    w_down,
    decay_scale,
    first_length,
):
    rows = tokens.shape[0]
    core = lax.axis_index("core")
    place = lax.axis_index("ctx")
    plane = lax.axis_index("tp")
    scalars = jnp.stack((core, plane, lax.axis_index("x"), place)).astype(jnp.int32)

    w_output = w_output.T
    w_down = w_down.T
    mine, theirs = split_heads((w_value, w_key, w_gate, w_output, w_query), scalars, "split_attn")
    came = swap(theirs)
    block, gathered = stack_attn(mine, came, scalars)
    lengths = jnp.concatenate((first_length, swap(first_length)))
    blocks = spread_near(block)
    w_kv = stack_blocks(blocks, 0, 768, scalars, "stack_kv", deps=(lengths,))
    normed_first = enter_rows(tokens, gain_first.reshape(1, D), scalars, deps=blocks[1:])
    w_goq = lax.all_gather(gathered, XY, axis=0, tiled=True).reshape(4, 4, 2, 64, -1)
    mine, theirs = split_heads(
        (w_hidden, w_linear, w_down), scalars, "split_mlp", deps=(gathered,)
    )
    came_mlp = swap(theirs)
    gain_first = gain_first.reshape(1, D)
    gain_second = gain_second.reshape(1, D)
    x_first = (normed_first, swap(normed_first))
    cot_low = low_rows(cotangent, scalars, deps=(x_first[1],))
    g_out = (cot_low, swap(cot_low))
    w_kv = spread_far(w_kv)

    rate = lax.dynamic_index_in_dim(decay_scale, core, 0, False) / 1024.0
    local = (jnp.arange(rows, dtype=jnp.int32) + plane * (rows // 4)) % rows
    index = place * rows + local
    document = (index[None, :] >= lengths[:, None]).astype(jnp.int32)
    carried = (document == 0).astype(F32)
    steps = local.astype(F32)
    offsets = local[:, None] - local[None, :]
    linked = (offsets >= 0)[None] & (document[:, :, None] == document[:, None, :])
    mask = jnp.where(
        linked, jnp.exp(-rate * jnp.maximum(offsets, 0).astype(F32))[None], 0.0
    )
    enter = (carried * jnp.exp(-rate * (steps + 1.0))[None])[:, :, None]
    leave = jnp.exp(-rate * (rows - 1.0 - steps))[None, :, None]
    fade = jnp.exp(-rate * rows)
    half = DK // 2
    frequency = 10000.0 ** (-(jnp.arange(half).astype(F32) / half))
    angles = index.astype(F32)[:, None] * frequency[None, :]
    cosine = jnp.tile(jnp.cos(angles), (2, 1))
    sine = jnp.tile(jnp.sin(angles), (2, 1))

    def carry(came):
        near, mid, far = [part.astype(F32) for part in came]
        return near + fade * (mid + fade * far)

    def spread_state(low, way):
        return [shift_open(low, "ctx", way * o) for o in (1, 2, 3)]

    projected = mm_in(*x_first, [(w_kv, 0, 768)], scalars, "project_kv")
    key = rotate(projected[:, DV:], cosine, sine).astype(BF).reshape(2, rows, DK)
    value = projected[:, :DV].astype(BF).reshape(2, rows, DV)
    key_out = (key.astype(F32) * leave).astype(BF)
    state_out = ein("gjd,gje->gde", key_out, value).astype(BF)
    came = spread_state(state_out, 1)
    w_mlp = lax.all_gather(
        stack_blocks((mine, came_mlp), 0, 1536, scalars, "stack_mlp", deps=came),
        XY,
        axis=0,
        tiled=True,
    ).reshape(4, 4, 2, 64, -1)
    own, other, query, state_in, weighted, gate_pre, retained, mixed = retain(
        x_first,
        w_goq,
        key,
        value,
        came,
        fade.reshape(1, 1),
        mask,
        enter.reshape(2 * rows, 1),
        cosine,
        sine,
        scalars,
    )
    query = query.reshape(2, rows, DK)
    _, gate_back = jax.vjp(gate_norm, gate_pre, retained)
    parts = tp_total(chip_blocks(own, swap(other)))
    hidden_state, normed_second = second_norm(tokens, parts, gain_second, scalars)
    x_second = (normed_second, swap(normed_second))
    own, other, gain_second_part, grad_pair, activated = mlp(x_second, g_out, w_mlp, scalars)
    grads, mark = mm_weight_into(
        None, ((x_second, grad_pair),), 1024, 3584, scalars, "weight_mlp"
    )
    mine, _ = tp_first(chip_blocks(own, swap(other)))
    (mine,) = tie((mine.astype(BF),), (mark,))
    parts = tp_second(mine)
    down = mm_back([(activated, w_mlp, 2 * DV)], scalars, "project_down", deps=(mine,))
    grad_state, grad_state_low = norm_back(
        hidden_state,
        cotangent,
        parts,
        gain_second,
        scalars,
        "second_back",
        deps=(down[1],),
    )
    g_state = (grad_state_low, swap(grad_state_low))
    grad_mixed = mm_in(*g_state, [(w_goq, DV, DV)], scalars, "back_out", stream=True)
    grad_gate, grad_retained = gate_back(grad_mixed)
    grad_low = grad_retained.reshape(2, rows, DV).astype(BF)
    query_in = (query.astype(F32) * enter).astype(BF)
    back_out = ein("gid,gie->gde", query_in, grad_low).astype(BF)
    came = spread_state(back_out, -1)
    grad_scores = (ein("gie,gje->gij", grad_low, value) * mask).astype(BF)
    grad_query = ein("gij,gjd->gid", grad_scores, key) + enter * ein("gie,gde->gid", grad_low, state_in)
    grad_key = ein("gij,gid->gjd", grad_scores, query)
    grad_value = ein("gij,gie->gje", weighted, grad_low)
    grad_gate = grad_gate.astype(BF)
    grad_query = rotate(grad_query.reshape(2 * rows, DK), cosine, -sine).astype(BF)
    grads, mark = mm_weight_into(
        grads,
        ((g_state, mixed), (x_first, grad_gate)),
        2048,
        3584,
        scalars,
        "weight_og",
        deps=(back_out,),
    )
    grads, mark = mm_weight_into(
        grads, ((g_out, activated),), 3072, 3584, scalars, "weight_down"
    )
    grads, mark = mm_weight_into(
        grads, ((x_first, grad_query),), 768, 3584, scalars, "weight_query"
    )
    came[0] = tie((came[0],), (mark, grad_key, grad_value))[0]
    state_back = carry(came).astype(BF)
    grad_key += leave * ein("gje,gde->gjd", value, state_back)
    grad_value += ein("gjd,gde->gje", key_out, state_back)
    grad_key = rotate(grad_key.reshape(2 * rows, DK), cosine, -sine)
    grad_vk = jnp.concatenate(
        (grad_value.reshape(2 * rows, DV).astype(BF), grad_key.astype(BF)), axis=1
    )
    grads, mark = mm_weight_into(grads, ((x_first, grad_vk),), 0, 3584, scalars, "weight_vk")
    block = lax.psum_scatter(grads.reshape(2048, -1), XY, scatter_dimension=0, tiled=True)
    own, other, gain_first_part = mm_back(
        [(grad_vk, w_kv, 0), (grad_gate, w_goq, 0), (grad_query, w_goq, 1024)],
        scalars,
        "back_attn",
        normed=x_first,
        deps=(mark,),
    )
    down = (down[0], swap(tie((down[1],), (mark,))[0]))
    blocks = third_blocks(own, swap(other), *down, scalars)
    mine, _ = tp_first(blocks)
    gains = jnp.concatenate((gain_first_part[:1], gain_second_part[:1]))
    for axis, swapped in (
        ("core", (1, 0)),
        ("ctx", (1, 0, 3, 2)),
        ("ctx", (3, 2, 1, 0)),
        ("x", (1, 0, 3, 2)),
        ("x", (3, 2, 1, 0)),
    ):
        gains = gains + lax.ppermute(gains, axis, list(enumerate(swapped)))
    mine = jnp.concatenate((mine, gains, jnp.zeros((14, D), F32))).astype(BF)
    parts = tp_second(mine)
    gains = [part[128:130].astype(F32) for part in parts]
    gains = (gains[0] + gains[2]) + (gains[1] + gains[3])
    spot = (lax.axis_index("x") * 2 + core) * 4 + place
    gain_first_grad, gain_second_grad = [
        lax.dynamic_slice_in_dim(gains[k] / gain[0], spot * 64, 64, 0)
        for k, gain in ((0, gain_first), (1, gain_second))
    ]
    layer_out, input_grad = leave_rows(
        hidden_state, tokens, grad_state, parts, gain_first, scalars
    )
    block = tie((block,), (gain_first_grad, gain_second_grad, input_grad))[0].reshape(2, 64, -1)
    d_value, d_key, d_query, d_hidden, d_linear, d_output, d_gate, d_down = join_heads(
        block[0], swap(block[1]), (DV, DK, DK) + (DV,) * 5, scalars, "join_heads"
    )
    return (
        layer_out,
        input_grad,
        gain_first_grad,
        gain_second_grad,
        d_query,
        d_key,
        d_value,
        d_gate,
        d_output.T,
        d_hidden,
        d_linear,
        d_down.T,
    )


def solution(mesh):
    fine = Mesh(np.asarray(mesh.devices).reshape(4, 2, 4, 4), ("x", "core", "ctx", "tp"))
    split = ("x", "core", "ctx")
    row = P(split, None)
    win = P(split, "tp")
    wout = P("tp", split)
    in_specs = (row, row, P(), P(), win, win, win, win, wout, win, win, wout, P("tp"), P(("x", "core")))
    out_specs = (row, row, P(split), P(split), win, win, win, win, wout, win, win, wout)
    return jax.shard_map(
        per_device, mesh=fine, in_specs=in_specs, out_specs=out_specs, check_vma=False
    )
```

```python
import math

import jax
import jax.numpy as jnp
import numpy as np
from jax import lax
from jax.experimental import pallas as pl
from jax.experimental.pallas import tpu as pltpu
from jax.sharding import Mesh, PartitionSpec as P

D = 2048
DK = 256
DV = 512
SLAB = 512
BF = jnp.bfloat16
F32 = jnp.float32
XY = ("x", "ctx")
MIB = 1 << 20


def shift(value, axis, offset):
    n = lax.axis_size(axis)
    return lax.ppermute(value, axis, [(i, (i + offset) % n) for i in range(n)])


def shift_open(value, axis, offset):
    n = lax.axis_size(axis)
    return lax.ppermute(
        value, axis, [(i, i + offset) for i in range(n) if 0 <= i + offset < n]
    )


def swap(value):
    return lax.ppermute(value, "core", [(0, 1), (1, 0)])


def after(value, *earlier):
    return lax.optimization_barrier((value, *earlier))[0]


def call(
    body,
    grid,
    ins,
    outs,
    shapes,
    scalars,
    operands,
    name,
    scratch=(),
    deps=(),
    stream=False,
    aliases=None,
):
    count = len(operands)

    def kernel(s_ref, *refs):
        body(s_ref, *refs[:count], *refs[count + len(deps) :])

    ins = [*ins, *[pl.BlockSpec(memory_space=pl.ANY)] * len(deps)]
    return pl.pallas_call(
        kernel,
        out_shape=shapes,
        grid_spec=pltpu.PrefetchScalarGridSpec(
            num_scalar_prefetch=1, grid=grid, in_specs=ins, out_specs=outs, scratch_shapes=scratch
        ),
        compiler_params=pltpu.CompilerParams(
            vmem_limit_bytes=(60 if stream else 32) * MIB, dimension_semantics=("arbitrary",) * len(grid)
        ),
        cost_estimate=pl.CostEstimate(flops=1, bytes_accessed=1, transcendentals=0),
        input_output_aliases=aliases or {},
        name=name,
    )(scalars, *operands, *deps)


def tie(values, deps):
    count = len(values)
    anywhere = pl.BlockSpec(memory_space=pl.ANY)
    return pl.pallas_call(
        lambda *refs: None,
        out_shape=tuple(sds(v.shape, v.dtype) for v in values),
        in_specs=[anywhere] * (count + len(deps)),
        out_specs=(anywhere,) * count,
        input_output_aliases={i: i for i in range(count)},
        name="tie",
    )(*values, *deps)


def whole(array):
    return pl.BlockSpec(array.shape, lambda *_: (0,) * array.ndim)


def sds(shape, dtype):
    return jax.ShapeDtypeStruct(shape, dtype)


def weight_operands(weight, start, width):
    if not isinstance(weight, tuple):
        spec = pl.BlockSpec((1, 4, 2, 64, width), lambda i, s: (i, 0, 0, 0, start // width))
        return [weight], [spec]
    piece = math.gcd(start, width) if start else width
    operands, specs = [], []
    for at in range(start, start + width, piece):
        for stack in weight:
            operands.append(stack)
            specs.append(pl.BlockSpec((4, 2, 64, piece), lambda i, s, at=at: (0, 0, 0, at // piece)))
    return operands, specs


def load_slab(s_ref, refs, held):
    core = s_ref[0]
    if len(refs) == 1:
        return jnp.concatenate(
            [refs[0][0, y, jnp.bitwise_xor(c, core)] for c in (0, 1) for y in range(4)], axis=0
        )
    x_far = lax.rem(s_ref[2] + 4 - pl.program_id(0), 4)
    at = 0
    for first in range(0, len(refs), 4):
        stacks = refs[first : first + 4]
        width = stacks[0].shape[-1]
        for j in range(4):

            @pl.when((core == 0) & (x_far == j))
            def _(j=j, at=at, width=width, stacks=stacks):
                for i in range(4):
                    y = lax.rem(s_ref[3] + 4 - i, 4)
                    for c in (0, 1):
                        held[c * 4 + y, :, at : at + width] = stacks[j][i, c]

        @pl.when(core == 1)
        def _(at=at, width=width, stacks=stacks):
            for j in range(4):
                y = lax.rem(s_ref[3] + 4 - j, 4)
                for c in (0, 1):
                    held[c * 4 + y, :, at : at + width] = stacks[j][x_far, 1 - c]

        at += width
    return held[...].reshape(SLAB, at)


def hop(value, first, offset):
    pairs = []
    for x in range(4):
        for core in (0, 1):
            for y in range(4):
                to = ((x + offset) % 4, y) if (core == 0) == first else (x, (y + offset) % 4)
                pairs.append(((x * 2 + core) * 4 + y, (to[0] * 2 + core) * 4 + to[1]))
    return lax.ppermute(value, ("x", "core", "ctx"), pairs)


def spread_near(block):
    near, far, mid = [hop(block, False, o) for o in (1, 3, 2)]
    return block, near, mid, far


def stack_blocks(blocks, start, width, scalars, name, deps=()):
    at = start // width if start % width == 0 else None
    span = width if at is not None else blocks[0].shape[1]
    first = 0 if at is not None else start
    height = blocks[0].shape[0]

    def body(s_ref, *refs):
        for k, ref in enumerate(refs[:-1]):
            refs[-1][k * height : (k + 1) * height, :] = ref[:, first : first + width]

    total = sds((height * len(blocks), width), BF)
    return call(
        body,
        (1,),
        [pl.BlockSpec((height, span), lambda i, s: (0, at or 0))] * len(blocks),
        whole(total),
        total,
        scalars,
        tuple(blocks),
        name,
        deps=deps,
    )


def stack_attn(mine, came, scalars):
    height, total = mine.shape

    def body(s_ref, mine_ref, came_ref, first_ref, other_ref):
        for k, ref in enumerate((mine_ref, came_ref)):
            span = slice(k * height, (k + 1) * height)
            first_ref[span, :] = ref[:, :768]
            other_ref[span, :] = ref[:, 768:]

    shapes = (sds((2 * height, 768), BF), sds((2 * height, total - 768), BF))
    return call(
        body,
        (1,),
        [whole(mine), whole(came)],
        tuple(whole(s) for s in shapes),
        shapes,
        scalars,
        (mine, came),
        "stack_attn",
        stream=True,
    )


def spread_far(stack, gate=False):
    stack = stack.reshape(4, 2, 64, -1)
    near, far = hop(stack, True, 1), hop(stack, True, -1)
    mid = hop(tie((stack,), (near, far))[0] if gate else stack, True, 2)
    return stack, near, mid, far


def mm_in(left, right, columns, scalars, name, deps=(), stream=False):
    operands, specs, counts = [], [], []
    for weight, start, width in columns:
        ops, sp = weight_operands(weight, start, width)
        operands += ops
        specs += sp
        counts.append(len(ops))
    total = sum(width for _, _, width in columns)

    def body(s_ref, a_ref, b_ref, *refs):
        out_ref = refs[len(operands)]
        step = pl.program_id(0)
        rows = jnp.concatenate((a_ref[...], b_ref[...]), axis=0)
        at, first = 0, 0
        for k, count in enumerate(counts):
            width = columns[k][2]
            slab = load_slab(s_ref, refs[first : first + count], refs[len(operands) + 1 + k])
            part = jnp.dot(rows, slab, preferred_element_type=F32)
            span = slice(at, at + width)

            @pl.when(step == 0)
            def _(part=part, span=span):
                out_ref[:, span] = part

            @pl.when(step > 0)
            def _(part=part, span=span):
                out_ref[:, span] += part

            at += width
            first += count

    rows = left.shape[0]
    cols = pl.BlockSpec((rows, SLAB), lambda i, s: (0, i))
    return call(
        body,
        (4,),
        [cols, cols, *specs],
        pl.BlockSpec((2 * rows, total), lambda i, s: (0, 0)),
        sds((2 * rows, total), F32),
        scalars,
        (left, right, *operands),
        name,
        scratch=[pltpu.VMEM((8, 64, width), BF) for _, _, width in columns],
        deps=deps,
        stream=stream,
    )


def mm_back(terms, scalars, name, normed=None, deps=()):
    rows = terms[0][0].shape[0]
    half = rows // 2
    operands, specs, counts, scratch = [], [], [], []
    for grad, weight, start in terms:
        ops, sp = weight_operands(weight, start, grad.shape[1])
        operands += [grad, *ops]
        specs += [whole(grad), *sp]
        counts.append(len(ops))
        scratch.append(pltpu.VMEM((8, 64, grad.shape[1]), BF))
    held = len(operands)
    cols = pl.BlockSpec((half, SLAB), lambda i, s: (0, i))
    outs = [cols, cols]
    shapes = [sds((half, D), F32), sds((half, D), BF)]
    if normed is not None:
        operands += normed
        specs += [cols, cols]
        outs.append(pl.BlockSpec((8, SLAB), lambda i, s: (0, i)))
        shapes.append(sds((8, D), F32))
    total = len(operands)

    def body(s_ref, *refs):
        at, out = 0, 0.0
        for k, count in enumerate(counts):
            slab = load_slab(s_ref, refs[at + 1 : at + 1 + count], refs[total + len(outs) + k])
            out += lax.dot_general(
                refs[at][...], slab, (((1,), (1,)), ((), ())), preferred_element_type=F32
            )
            at += count + 1
        refs[total][...] = out[:half]
        refs[total + 1][...] = out[half:].astype(BF)
        if normed is not None:
            part = out[:half] * refs[held][...].astype(F32) + out[half:] * refs[held + 1][
                ...
            ].astype(F32)
            part = jnp.sum(part, axis=0, keepdims=True)
            refs[total + 2][...] = jnp.broadcast_to(part, (8, SLAB))

    return call(
        body,
        (4,),
        specs,
        tuple(outs),
        tuple(shapes),
        scalars,
        tuple(operands),
        name,
        scratch=scratch,
        deps=deps,
    )


def split_out(out, own_ref, other_ref):
    half = out.shape[0] // 2
    own_ref[...] = out[:half]
    other_ref[...] = out[half:].astype(BF)


def retain(x_pair, weight, key, value, came, fade, mask, enter, cosine, sine, scalars):
    rows = x_pair[0].shape[0]

    def body(
        s_ref, a_ref, b_ref, w_ref, k_ref, v_ref, near_ref, mid_ref, far_ref, f_ref, m_ref, e_ref,
        cos_ref, sin_ref, own_ref, other_ref, query_ref, state_ref, weighted_ref, gate_ref,
        retained_ref, mixed_ref, sums, turned
    ):
        step = pl.program_id(0)

        @pl.when(step < 4)
        def _():
            slab = load_slab(s_ref, (w_ref,), None)
            turned[step] = slab[:, DV : 2 * DV]
            left = jnp.concatenate((a_ref[...], b_ref[...]), axis=0)
            gate = jnp.dot(left, slab[:, :DV], preferred_element_type=F32)
            query = jnp.dot(left, slab[:, 2 * DV :], preferred_element_type=F32)

            @pl.when(step == 0)
            def _():
                gate_ref[...] = gate
                sums[...] = query

            @pl.when(step > 0)
            def _():
                gate_ref[...] += gate
                sums[...] += query

        @pl.when(step == 3)
        def _():
            fade = f_ref[...]
            for g in (0, 1):
                span = slice(g * rows, (g + 1) * rows)
                state = near_ref[g].astype(F32) + fade * (
                    mid_ref[g].astype(F32) + fade * far_ref[g].astype(F32)
                )
                state_ref[g] = state.astype(BF)
                query = rotate(sums[span], cos_ref[span], sin_ref[span]).astype(BF)
                query_ref[span] = query
                scores = lax.dot_general(
                    query, k_ref[g], (((1,), (1,)), ((), ())), preferred_element_type=F32
                )
                weighted = (scores * m_ref[g]).astype(BF)
                weighted_ref[g] = weighted
                retained = jnp.dot(weighted, v_ref[g], preferred_element_type=F32)
                retained += e_ref[span] * jnp.dot(
                    query, state_ref[g], preferred_element_type=F32
                )
                retained_ref[span] = retained
                mixed_ref[span] = gate_norm(gate_ref[span], retained).astype(BF)

        @pl.when(step >= 4)
        def _():
            out = lax.dot_general(
                mixed_ref[...],
                turned[step - 4],
                (((1,), (1,)), ((), ())),
                preferred_element_type=F32,
            )
            split_out(out, own_ref, other_ref)

    cols = pl.BlockSpec((rows, SLAB), lambda i, s: (0, jnp.minimum(i, 3)))
    later = pl.BlockSpec((rows, SLAB), lambda i, s: (0, jnp.maximum(i - 4, 0)))
    operands = (*x_pair, weight, key, value, *came, fade, mask, enter, cosine, sine)
    shapes = (
        sds((rows, D), F32),
        sds((rows, D), BF),
        sds((2 * rows, DK), BF),
        sds((2, DK, DV), BF),
        sds((2, rows, rows), BF),
        sds((2 * rows, DV), F32),
        sds((2 * rows, DV), F32),
        sds((2 * rows, DV), BF),
    )
    block = pl.BlockSpec((1, 4, 2, 64, 1280), lambda i, s: (jnp.minimum(i, 3), 0, 0, 0, 0))
    return call(
        body,
        (8,),
        [cols, cols, block] + [whole(o) for o in operands[3:]],
        (later, later) + tuple(whole(s) for s in shapes[2:]),
        shapes,
        scalars,
        operands,
        "retain",
        scratch=[pltpu.VMEM((2 * rows, DK), F32), pltpu.VMEM((4, SLAB, DV), BF)],
        stream=True,
    )


def mlp(x_pair, g_pair, weight, scalars):
    rows = x_pair[0].shape[0]

    def body(
        s_ref, a_ref, b_ref, c_ref, d_ref, w_ref, own_ref, other_ref, gain_ref, pair_ref, act_ref,
        both, back, kept
    ):
        step = pl.program_id(0)

        @pl.when(step < 4)
        def _():
            slab = load_slab(s_ref, (w_ref,), None)
            kept[step] = slab[:, : 2 * DV]
            left = jnp.concatenate((a_ref[...], b_ref[...]), axis=0)
            grad = jnp.concatenate((c_ref[...], d_ref[...]), axis=0)
            up = jnp.dot(left, slab[:, : 2 * DV], preferred_element_type=F32)
            down = jnp.dot(grad, slab[:, 2 * DV :], preferred_element_type=F32)

            @pl.when(step == 0)
            def _():
                both[...] = up
                back[...] = down

            @pl.when(step > 0)
            def _():
                both[...] += up
                back[...] += down

        @pl.when(step == 3)
        def _():
            def chunk(k, carry):
                span = pl.ds(pl.multiple_of(k * 64, 64), 64)
                hidden, linear, grad = both[span, :DV], both[span, DV:], back[span, :]
                cube = 0.044715 * hidden * hidden
                bent = jnp.tanh(0.7978845608 * hidden * (1.0 + cube))
                half = 0.5 * (1.0 + bent)
                gelu = hidden * half
                slope = half + 0.5 * hidden * (1.0 - bent * bent) * (
                    0.7978845608 * (1.0 + 3.0 * cube)
                )
                act_ref[span, :] = (gelu * linear).astype(BF)
                pair_ref[span, :DV] = (grad * linear * slope).astype(BF)
                pair_ref[span, DV:] = (grad * gelu).astype(BF)
                return carry

            lax.fori_loop(0, 2 * rows // 64, chunk, 0)

        @pl.when(step >= 4)
        def _():
            out = lax.dot_general(
                pair_ref[...], kept[step - 4], (((1,), (1,)), ((), ())), preferred_element_type=F32
            )
            split_out(out, own_ref, other_ref)
            part = out[:rows] * a_ref[...].astype(F32) + out[rows:] * b_ref[...].astype(F32)
            gain_ref[...] = jnp.broadcast_to(jnp.sum(part, axis=0, keepdims=True), (8, SLAB))

    cols = pl.BlockSpec((rows, SLAB), lambda i, s: (0, lax.rem(i, 4)))
    once = pl.BlockSpec((rows, SLAB), lambda i, s: (0, jnp.minimum(i, 3)))
    block = pl.BlockSpec((1, 4, 2, 64, 3 * DV), lambda i, s: (jnp.minimum(i, 3), 0, 0, 0, 0))
    later = pl.BlockSpec((rows, SLAB), lambda i, s: (0, jnp.maximum(i - 4, 0)))
    shapes = (
        sds((rows, D), F32),
        sds((rows, D), BF),
        sds((8, D), F32),
        sds((2 * rows, 2 * DV), BF),
        sds((2 * rows, DV), BF),
    )
    return call(
        body,
        (8,),
        [cols, cols, once, once, block],
        (
            later,
            later,
            pl.BlockSpec((8, SLAB), lambda i, s: (0, jnp.maximum(i - 4, 0))),
            whole(shapes[3]),
            whole(shapes[4]),
        ),
        shapes,
        scalars,
        (*x_pair, *g_pair, weight),
        "mlp",
        scratch=[
            pltpu.VMEM((2 * rows, 2 * DV), F32),
            pltpu.VMEM((2 * rows, DV), F32),
            pltpu.VMEM((4, SLAB, 2 * DV), BF),
        ],
        stream=True,
    )


def back_gate(g_pair, weight, gate_pre, retained, query, enter, scalars):
    rows = g_pair[0].shape[0]

    def body(
        s_ref, a_ref, b_ref, w_ref, gate_ref, kept_ref, q_ref, e_ref, dgate_ref, low_ref, state_ref,
        sums
    ):
        step = pl.program_id(0)
        left = jnp.concatenate((a_ref[...], b_ref[...]), axis=0)
        part = jnp.dot(left, load_slab(s_ref, (w_ref,), None), preferred_element_type=F32)

        @pl.when(step == 0)
        def _():
            sums[...] = part

        @pl.when(step > 0)
        def _():
            sums[...] += part

        @pl.when(step == 3)
        def _():
            def chunk(k, carry):
                span = pl.ds(pl.multiple_of(k * 64, 64), 64)
                gate, value, grad = gate_ref[span, :], kept_ref[span, :], sums[span, :]
                value = value - jnp.mean(value, axis=-1, keepdims=True)
                scale = lax.rsqrt(jnp.mean(value * value, axis=-1, keepdims=True) + 1.0 * DK)
                normed = value * scale
                open_part = jax.nn.sigmoid(gate)
                slope = open_part * (1.0 + gate * (1.0 - open_part))
                dgate_ref[span, :] = (grad * normed * slope).astype(BF)
                grad = grad * gate * open_part
                grad = grad - jnp.mean(grad, axis=-1, keepdims=True) - normed * jnp.mean(
                    grad * normed, axis=-1, keepdims=True
                )
                low_ref[span, :] = (grad * scale).astype(BF)
                return carry

            lax.fori_loop(0, 2 * rows // 64, chunk, 0)
            for g in (0, 1):
                span = slice(g * rows, (g + 1) * rows)
                entered = (q_ref[span].astype(F32) * e_ref[span]).astype(BF)
                state_ref[g] = lax.dot_general(
                    entered,
                    low_ref[span],
                    (((0,), (0,)), ((), ())),
                    preferred_element_type=F32,
                ).astype(BF)

    cols = pl.BlockSpec((rows, SLAB), lambda i, s: (0, i))
    operands = (*g_pair, weight, gate_pre, retained, query, enter)
    shapes = (
        sds((2 * rows, DV), BF),
        sds((2 * rows, DV), BF),
        sds((2, DK, DV), BF),
    )
    return call(
        body,
        (4,),
        [cols, cols, pl.BlockSpec((1, 4, 2, 64, DV), lambda i, s: (i, 0, 0, 0, 1))]
        + [whole(o) for o in operands[3:]],
        tuple(whole(s) for s in shapes),
        shapes,
        scalars,
        operands,
        "back_gate",
        scratch=[pltpu.VMEM((2 * rows, DV), F32)],
        stream=True,
    )


def weight_last(into, pair, came, fade, value, key_out, leave, grad_value, grad_key, cosine, sine,
                scalars):
    rows = pair[0].shape[0]

    def body(
        s_ref, a_ref, b_ref, near_ref, mid_ref, far_ref, f_ref, v_ref, k_ref, l_ref, gv_ref, gk_ref,
        cos_ref, sin_ref, into_ref, out_ref, mark_ref, grad_ref
    ):
        @pl.when(pl.program_id(0) == 0)
        def _():
            fade = f_ref[...]
            for g in (0, 1):
                span = slice(g * rows, (g + 1) * rows)
                state = near_ref[g].astype(F32) + fade * (
                    mid_ref[g].astype(F32) + fade * far_ref[g].astype(F32)
                )
                state = state.astype(BF)
                grad_ref[span, :DV] = (
                    gv_ref[g] + jnp.dot(k_ref[g], state, preferred_element_type=F32)
                ).astype(BF)
                grad_key = gk_ref[g] + l_ref[span] * lax.dot_general(
                    v_ref[g], state, (((1,), (1,)), ((), ())), preferred_element_type=F32
                )
                grad_ref[span, DV:] = rotate(grad_key, cos_ref[span], -sin_ref[span]).astype(BF)

        out = lax.dot_general(
            jnp.concatenate((a_ref[...], b_ref[...]), axis=0),
            grad_ref[...],
            (((0,), (0,)), ((), ())),
            preferred_element_type=F32,
        ).astype(BF)
        for c in (0, 1):
            for y in range(4):
                first = (c * 4 + y) * 64
                out_ref[0, y, jnp.bitwise_xor(c, s_ref[0])] = out[first : first + 64]
        mark_ref[...] = jnp.zeros_like(mark_ref)

    cols = pl.BlockSpec((rows, SLAB), lambda i, s: (0, i))
    operands = (*pair, *came, fade, value, key_out, leave, grad_value, grad_key, cosine, sine)
    shapes = (
        sds(into.shape, BF),
        sds((8, 128), F32),
        sds((2 * rows, DV + DK), BF),
    )
    return call(
        body,
        (4,),
        [cols, cols]
        + [whole(o) for o in operands[2:]]
        + [pl.BlockSpec(memory_space=pl.ANY)],
        (
            pl.BlockSpec((1, 4, 2, 64, DV + DK), lambda i, s: (i, 0, 0, 0, 0)),
            whole(shapes[1]),
            whole(shapes[2]),
        ),
        shapes,
        scalars,
        (*operands, into),
        "weight_last",
        stream=True,
        aliases={1 + len(operands): 0},
    )


def mm_weight_into(into, pairs, start, total, scalars, name, deps=()):
    widths = [grad.shape[1] for _, grad in pairs]
    rows = pairs[0][0][0].shape[0]
    span = sum(widths)

    def body(s_ref, *refs):
        out_ref, mark_ref = refs[-2:]
        at = 0
        for k, width in enumerate(widths):
            a_ref, b_ref, g_ref = refs[3 * k : 3 * k + 3]
            out = lax.dot_general(
                jnp.concatenate((a_ref[...], b_ref[...]), axis=0),
                g_ref[...],
                (((0,), (0,)), ((), ())),
                preferred_element_type=F32,
            ).astype(BF)
            for c in (0, 1):
                for y in range(4):
                    first = (c * 4 + y) * 64
                    out_ref[0, y, jnp.bitwise_xor(c, s_ref[0]), :, at : at + width] = out[
                        first : first + 64
                    ]
            at += width
        mark_ref[...] = jnp.zeros_like(mark_ref)

    cols = pl.BlockSpec((rows, SLAB), lambda i, s: (0, i))
    specs, operands = [], []
    for (a, b), grad in pairs:
        specs += [cols, cols, whole(grad)]
        operands += [a, b, grad]
    aliases = None
    if into is not None:
        aliases = {1 + len(operands): 0}
        specs.append(pl.BlockSpec(memory_space=pl.ANY))
        operands.append(into)
    return call(
        body,
        (4,),
        specs,
        (
            pl.BlockSpec((1, 4, 2, 64, span), lambda i, s: (i, 0, 0, 0, start // span)),
            pl.BlockSpec((8, 128), lambda i, s: (0, 0)),
        ),
        (sds((4, 4, 2, 64, total), BF), sds((8, 128), F32)),
        scalars,
        tuple(operands),
        name,
        deps=deps,
        stream=True,
        aliases=aliases,
    )


def split_heads(weights, scalars, name, deps=()):
    widths = [w.shape[1] // 2 for w in weights]

    def body(s_ref, *refs):
        mine_ref, theirs_ref = refs[-2:]
        core = s_ref[0]
        for out_ref, head in ((mine_ref, core), (theirs_ref, 1 - core)):
            at = 0
            for ref, width in zip(refs, widths):
                out_ref[:, at : at + width] = ref[:, pl.ds(pl.multiple_of(head * width, width), width)]
                at += width

    total = sum(widths)
    spec = pl.BlockSpec((64, total), lambda i, s: (0, 0))
    return call(
        body,
        (1,),
        [whole(w) for w in weights],
        (spec, spec),
        (sds((64, total), BF),) * 2,
        scalars,
        tuple(weights),
        name,
        deps=deps,
        stream=True,
    )


def join_heads(mine, theirs, widths, scalars, name):
    def body(s_ref, mine_ref, theirs_ref, *outs):
        core = s_ref[0]
        for in_ref, head in ((mine_ref, core), (theirs_ref, 1 - core)):
            at = 0
            for ref, width in zip(outs, widths):
                span = pl.ds(pl.multiple_of(head * width, width), width)
                ref[:, span] = in_ref[:, at : at + width].astype(F32)
                at += width

    shapes = tuple(sds((64, 2 * w), F32) for w in widths)
    return call(
        body,
        (1,),
        [whole(mine), whole(theirs)],
        tuple(whole(s) for s in shapes),
        shapes,
        scalars,
        (mine, theirs),
        name,
    )


def scale_of(values):
    return lax.rsqrt(jnp.mean(values * values, axis=-1, keepdims=True) + 1e-06)


def turned_spec(rows):
    return pl.BlockSpec((rows, D), lambda i, s: (lax.rem(i + s[1], 4), 0))


def plain_spec(rows):
    return pl.BlockSpec((rows, D), lambda i, s: (i, 0))


def enter_rows(tokens, gain, scalars, deps=()):
    rows = tokens.shape[0]
    block = rows // 4

    def body(s_ref, t_ref, g_ref, n_out):
        values = t_ref[...]
        n_out[...] = (values * scale_of(values) * g_ref[...]).astype(BF)

    return call(
        body,
        (4,),
        [turned_spec(block), whole(gain)],
        plain_spec(block),
        sds((rows, D), BF),
        scalars,
        (tokens, gain),
        "enter_rows",
        deps=deps,
    )


def low_rows(cotangent, scalars, deps=()):
    rows = cotangent.shape[0]
    block = rows // 4

    def body(s_ref, c_ref, l_out):
        l_out[...] = c_ref[...].astype(BF)

    return call(
        body,
        (4,),
        [turned_spec(block)],
        plain_spec(block),
        sds((rows, D), BF),
        scalars,
        (cotangent,),
        "low_rows",
        deps=deps,
    )


def each_part(refs, work):
    step = pl.program_id(0)
    for k, ref in enumerate(refs):

        @pl.when(step == k)
        def _(ref=ref):
            work(ref[...].astype(F32))


def second_norm(tokens, parts, gain, scalars, deps=()):
    rows = tokens.shape[0]
    block = rows // 4

    def body(s_ref, t_ref, g_ref, *refs):
        h_out, n_out = refs[4:]

        def work(part):
            values = t_ref[...] + part
            h_out[...] = values
            n_out[...] = (values * scale_of(values) * g_ref[...]).astype(BF)

        each_part(refs[:4], work)

    plain = plain_spec(block)
    return call(
        body,
        (4,),
        [turned_spec(block), whole(gain)] + [whole(p) for p in parts],
        (plain, plain),
        (sds((rows, D), F32), sds((rows, D), BF)),
        scalars,
        (tokens, gain, *parts),
        "second_norm",
        deps=deps,
    )


def third_blocks(own, came, down_own, down_came, scalars, deps=()):
    rows = own.shape[0]
    block = rows // 4

    def body(s_ref, own_ref, came_ref, d_ref, e_ref, *refs):
        total = own_ref[...] + came_ref[...].astype(F32)
        down = d_ref[...] + e_ref[...].astype(F32)
        step = pl.program_id(0)
        for k in range(4):

            @pl.when(step == k)
            def _(k=k):
                refs[k][:block] = total.astype(BF)
                refs[k][block:] = down.astype(BF)

    plain = plain_spec(block)
    shapes = (sds((2 * block, D), BF),) * 4
    return call(
        body,
        (4,),
        [plain] * 4,
        tuple(whole(s) for s in shapes),
        shapes,
        scalars,
        (own, came, down_own, down_came),
        "third_blocks",
        deps=deps,
        stream=True,
    )


def leave_rows(hidden, tokens, grad_state, parts, gain, scalars, deps=()):
    rows = hidden.shape[0]
    block = rows // 4

    def body(s_ref, h_ref, t_ref, u_ref, g_ref, *refs):
        def work(part):
            refs[4][...] = h_ref[...] + part[block : 2 * block]
            refs[5][...] = u_ref[...] + norm_grad(t_ref[...], part[:block], g_ref[...])

        each_part(refs[:4], work)

    plain, turn = plain_spec(block), turned_spec(block)
    return call(
        body,
        (4,),
        [plain, turn, plain, whole(gain)] + [whole(p) for p in parts],
        (turn, turn),
        (sds((rows, D), F32),) * 2,
        scalars,
        (hidden, tokens, grad_state, gain, *parts),
        "leave_rows",
        deps=deps,
        stream=True,
    )


def norm_grad(values, grad, gain):
    factor = scale_of(values)
    unit = values * factor
    scaled = grad * gain
    return factor * (scaled - unit * jnp.mean(scaled * unit, axis=-1, keepdims=True))


def norm_back(values, upstream, parts, gain, scalars, name, deps=()):
    rows = values.shape[0]
    block = rows // 4

    def body(s_ref, v_ref, u_ref, g_ref, *refs):
        def work(part):
            out = u_ref[...] + norm_grad(v_ref[...], part, g_ref[...])
            refs[4][...] = out
            refs[5][...] = out.astype(BF)

        each_part(refs[:4], work)

    plain = plain_spec(block)
    return call(
        body,
        (4,),
        [plain, turned_spec(block), whole(gain)] + [whole(p) for p in parts],
        (plain, plain),
        (sds((rows, D), F32), sds((rows, D), BF)),
        scalars,
        (values, upstream, gain, *parts),
        name,
        deps=deps,
        stream=True,
    )


def tp_first(blocks):
    got = [shift(blocks[o], "tp", o) for o in (1, 3, 2)]
    near, far, mid = [part.astype(F32) for part in got]
    return (blocks[0].astype(F32) + mid) + (near + far), got


def tp_second(mine):
    near, far, mid = [shift(mine, "tp", -o) for o in (1, 3, 2)]
    return mine, near, mid, far


def tp_total(blocks):
    return tp_second(tp_first(blocks)[0].astype(BF))


def chip_blocks(own, came):
    block = own.shape[0] // 4
    return [
        (own[o * block : (o + 1) * block] + came[o * block : (o + 1) * block].astype(F32)).astype(BF)
        for o in range(4)
    ]


def gate_norm(gate_pre, retained):
    centred = retained - jnp.mean(retained, axis=-1, keepdims=True)
    normed = centred * lax.rsqrt(jnp.mean(centred * centred, axis=-1, keepdims=True) + 1.0 * DK)
    return gate_pre * jax.nn.sigmoid(gate_pre) * normed


def gelu_gate(hidden, linear):
    return jax.nn.gelu(hidden, approximate=True) * linear


def rotate(values, cosine, sine):
    half = DK // 2
    first = values[:, :half]
    second = values[:, half:]
    return jnp.concatenate((first * cosine - second * sine, first * sine + second * cosine), axis=1)


def ein(spec, left, right):
    return jnp.einsum(spec, left, right, preferred_element_type=F32)


def per_device(
    tokens,
    cotangent,
    gain_first,
    gain_second,
    w_query,
    w_key,
    w_value,
    w_gate,
    w_output,
    w_hidden,
    w_linear,
    w_down,
    decay_scale,
    first_length,
):
    rows = tokens.shape[0]
    core = lax.axis_index("core")
    place = lax.axis_index("ctx")
    plane = lax.axis_index("tp")
    scalars = jnp.stack((core, plane, lax.axis_index("x"), place)).astype(jnp.int32)

    w_output = w_output.T
    w_down = w_down.T
    mine, theirs = split_heads((w_value, w_key, w_gate, w_output, w_query), scalars, "split_attn")
    came = swap(theirs)
    block, gathered = stack_attn(mine, came, scalars)
    lengths = jnp.concatenate((first_length, swap(first_length)))
    blocks = spread_near(block)
    w_kv = stack_blocks(blocks, 0, 768, scalars, "stack_kv", deps=(lengths,))
    normed_first = enter_rows(tokens, gain_first.reshape(1, D), scalars, deps=blocks[1:])
    w_goq = lax.all_gather(gathered, XY, axis=0, tiled=True).reshape(4, 4, 2, 64, -1)
    mine, theirs = split_heads(
        (w_hidden, w_linear, w_down), scalars, "split_mlp", deps=(gathered,)
    )
    came_mlp = swap(theirs)
    gain_first = gain_first.reshape(1, D)
    gain_second = gain_second.reshape(1, D)
    x_first = (normed_first, swap(normed_first))
    cot_low = low_rows(cotangent, scalars, deps=(x_first[1],))
    g_out = (cot_low, swap(cot_low))
    w_kv = spread_far(w_kv)

    rate = lax.dynamic_index_in_dim(decay_scale, core, 0, False) / 1024.0
    local = (jnp.arange(rows, dtype=jnp.int32) + plane * (rows // 4)) % rows
    index = place * rows + local
    document = (index[None, :] >= lengths[:, None]).astype(jnp.int32)
    carried = (document == 0).astype(F32)
    steps = local.astype(F32)
    offsets = local[:, None] - local[None, :]
    linked = (offsets >= 0)[None] & (document[:, :, None] == document[:, None, :])
    mask = jnp.where(
        linked, jnp.exp(-rate * jnp.maximum(offsets, 0).astype(F32))[None], 0.0
    )
    enter = (carried * jnp.exp(-rate * (steps + 1.0))[None])[:, :, None]
    leave = jnp.exp(-rate * (rows - 1.0 - steps))[None, :, None]
    fade = jnp.exp(-rate * rows)
    half = DK // 2
    frequency = 10000.0 ** (-(jnp.arange(half).astype(F32) / half))
    angles = index.astype(F32)[:, None] * frequency[None, :]
    cosine = jnp.tile(jnp.cos(angles), (2, 1))
    sine = jnp.tile(jnp.sin(angles), (2, 1))

    def spread_state(low, way):
        return [shift_open(low, "ctx", way * o) for o in (1, 2, 3)]

    enter_rows_in = enter.reshape(2 * rows, 1)
    leave_rows_out = jnp.tile(leave.reshape(rows, 1), (2, 1))
    fade_in = fade.reshape(1, 1)
    projected = mm_in(
        *x_first,
        [(w_kv, 0, 768)],
        scalars,
        "project_kv",
        deps=(mask, enter_rows_in, leave_rows_out, fade_in, cosine, sine),
    )
    key = rotate(projected[:, DV:], cosine, sine).astype(BF).reshape(2, rows, DK)
    value = projected[:, :DV].astype(BF).reshape(2, rows, DV)
    key_out = (key.astype(F32) * leave).astype(BF)
    state_out = ein("gjd,gje->gde", key_out, value).astype(BF)
    came = spread_state(state_out, 1)
    w_mlp = lax.all_gather(
        stack_blocks((mine, came_mlp), 0, 1536, scalars, "stack_mlp", deps=came),
        XY,
        axis=0,
        tiled=True,
    ).reshape(4, 4, 2, 64, -1)
    own, other, query, state_in, weighted, gate_pre, retained, mixed = retain(
        x_first,
        w_goq,
        key,
        value,
        came,
        fade_in,
        mask,
        enter_rows_in,
        cosine,
        sine,
        scalars,
    )
    query = query.reshape(2, rows, DK)
    parts = tp_total(chip_blocks(own, swap(other)))
    hidden_state, normed_second = second_norm(tokens, parts, gain_second, scalars)
    x_second = (normed_second, swap(normed_second))
    own, other, gain_second_part, grad_pair, activated = mlp(x_second, g_out, w_mlp, scalars)
    grads, mark = mm_weight_into(
        None, ((x_second, grad_pair),), 1024, 3584, scalars, "weight_mlp"
    )
    mine, _ = tp_first(chip_blocks(own, swap(other)))
    (mine,) = tie((mine.astype(BF),), (mark,))
    parts = tp_second(mine)
    down = mm_back([(activated, w_mlp, 2 * DV)], scalars, "project_down", deps=(mine,))
    grad_state, grad_state_low = norm_back(
        hidden_state,
        cotangent,
        parts,
        gain_second,
        scalars,
        "second_back",
        deps=(down[1],),
    )
    g_state = (grad_state_low, swap(grad_state_low))
    grad_gate, grad_low, back_out = back_gate(
        g_state, w_goq, gate_pre, retained, query.reshape(2 * rows, DK), enter_rows_in, scalars
    )
    grad_low = grad_low.reshape(2, rows, DV)
    came = spread_state(back_out, -1)
    grad_scores = (ein("gie,gje->gij", grad_low, value) * mask).astype(BF)
    grad_query = ein("gij,gjd->gid", grad_scores, key) + enter * ein("gie,gde->gid", grad_low, state_in)
    grad_key = ein("gij,gid->gjd", grad_scores, query)
    grad_value = ein("gij,gie->gje", weighted, grad_low)
    grad_query = rotate(grad_query.reshape(2 * rows, DK), cosine, -sine).astype(BF)
    grads, mark = mm_weight_into(
        grads,
        ((g_state, mixed), (x_first, grad_gate)),
        2048,
        3584,
        scalars,
        "weight_og",
        deps=(back_out,),
    )
    grads, mark = mm_weight_into(
        grads, ((g_out, activated),), 3072, 3584, scalars, "weight_down"
    )
    grads, mark = mm_weight_into(
        grads, ((x_first, grad_query),), 768, 3584, scalars, "weight_query"
    )
    came[0] = tie((came[0],), (mark, grad_key, grad_value))[0]
    grads, mark, grad_vk = weight_last(
        grads,
        x_first,
        came,
        fade_in,
        value,
        key_out,
        leave_rows_out,
        grad_value,
        grad_key,
        cosine,
        sine,
        scalars,
    )
    block = lax.psum_scatter(grads.reshape(2048, -1), XY, scatter_dimension=0, tiled=True)
    own, other, gain_first_part = mm_back(
        [(grad_vk, w_kv, 0), (grad_gate, w_goq, 0), (grad_query, w_goq, 1024)],
        scalars,
        "back_attn",
        normed=x_first,
        deps=(mark,),
    )
    down = (down[0], swap(tie((down[1],), (mark,))[0]))
    blocks = third_blocks(own, swap(other), *down, scalars)
    mine, _ = tp_first(blocks)
    gains = jnp.concatenate((gain_first_part[:1], gain_second_part[:1]))
    for axis, swapped in (
        ("core", (1, 0)),
        ("ctx", (1, 0, 3, 2)),
        ("ctx", (3, 2, 1, 0)),
        ("x", (1, 0, 3, 2)),
        ("x", (3, 2, 1, 0)),
    ):
        gains = gains + lax.ppermute(gains, axis, list(enumerate(swapped)))
    mine = jnp.concatenate((mine, gains, jnp.zeros((14, D), F32))).astype(BF)
    parts = tp_second(mine)
    gains = [part[128:130].astype(F32) for part in parts]
    gains = (gains[0] + gains[2]) + (gains[1] + gains[3])
    spot = (lax.axis_index("x") * 2 + core) * 4 + place
    gain_first_grad, gain_second_grad = [
        lax.dynamic_slice_in_dim(gains[k] / gain[0], spot * 64, 64, 0)
        for k, gain in ((0, gain_first), (1, gain_second))
    ]
    layer_out, input_grad = leave_rows(
        hidden_state, tokens, grad_state, parts, gain_first, scalars
    )
    block = tie((block,), (gain_first_grad, gain_second_grad, input_grad))[0].reshape(2, 64, -1)
    d_value, d_key, d_query, d_hidden, d_linear, d_output, d_gate, d_down = join_heads(
        block[0], swap(block[1]), (DV, DK, DK) + (DV,) * 5, scalars, "join_heads"
    )
    return (
        layer_out,
        input_grad,
        gain_first_grad,
        gain_second_grad,
        d_query,
        d_key,
        d_value,
        d_gate,
        d_output.T,
        d_hidden,
        d_linear,
        d_down.T,
    )


def solution(mesh):
    fine = Mesh(np.asarray(mesh.devices).reshape(4, 2, 4, 4), ("x", "core", "ctx", "tp"))
    split = ("x", "core", "ctx")
    row = P(split, None)
    win = P(split, "tp")
    wout = P("tp", split)
    in_specs = (row, row, P(), P(), win, win, win, win, wout, win, win, wout, P("tp"), P(("x", "core")))
    out_specs = (row, row, P(split), P(split), win, win, win, win, wout, win, win, wout)
    return jax.shard_map(
        per_device, mesh=fine, in_specs=in_specs, out_specs=out_specs, check_vma=False
    )
```

```python
import math

import jax
import jax.numpy as jnp
import numpy as np
from jax import lax
from jax.experimental import pallas as pl
from jax.experimental.pallas import tpu as pltpu
from jax.sharding import Mesh, PartitionSpec as P

D = 2048
DK = 256
DV = 512
SLAB = 512
BF = jnp.bfloat16
F32 = jnp.float32
XY = ("x", "ctx")
MIB = 1 << 20


def shift(value, axis, offset):
    n = lax.axis_size(axis)
    return lax.ppermute(value, axis, [(i, (i + offset) % n) for i in range(n)])


def shift_open(value, axis, offset):
    n = lax.axis_size(axis)
    return lax.ppermute(
        value, axis, [(i, i + offset) for i in range(n) if 0 <= i + offset < n]
    )


def swap(value):
    return lax.ppermute(value, "core", [(0, 1), (1, 0)])


def after(value, *earlier):
    return lax.optimization_barrier((value, *earlier))[0]


def call(
    body,
    grid,
    ins,
    outs,
    shapes,
    scalars,
    operands,
    name,
    scratch=(),
    deps=(),
    stream=False,
    aliases=None,
):
    count = len(operands)

    def kernel(s_ref, *refs):
        body(s_ref, *refs[:count], *refs[count + len(deps) :])

    ins = [*ins, *[pl.BlockSpec(memory_space=pl.ANY)] * len(deps)]
    return pl.pallas_call(
        kernel,
        out_shape=shapes,
        grid_spec=pltpu.PrefetchScalarGridSpec(
            num_scalar_prefetch=1, grid=grid, in_specs=ins, out_specs=outs, scratch_shapes=scratch
        ),
        compiler_params=pltpu.CompilerParams(
            vmem_limit_bytes=(60 if stream else 32) * MIB, dimension_semantics=("arbitrary",) * len(grid)
        ),
        cost_estimate=pl.CostEstimate(flops=1, bytes_accessed=1, transcendentals=0),
        input_output_aliases=aliases or {},
        name=name,
    )(scalars, *operands, *deps)


def tie(values, deps):
    count = len(values)
    anywhere = pl.BlockSpec(memory_space=pl.ANY)
    return pl.pallas_call(
        lambda *refs: None,
        out_shape=tuple(sds(v.shape, v.dtype) for v in values),
        in_specs=[anywhere] * (count + len(deps)),
        out_specs=(anywhere,) * count,
        input_output_aliases={i: i for i in range(count)},
        name="tie",
    )(*values, *deps)


def whole(array):
    return pl.BlockSpec(array.shape, lambda *_: (0,) * array.ndim)


def sds(shape, dtype):
    return jax.ShapeDtypeStruct(shape, dtype)


def weight_operands(weight, start, width):
    if not isinstance(weight, tuple):
        spec = pl.BlockSpec((1, 4, 2, 64, width), lambda i, s: (i, 0, 0, 0, start // width))
        return [weight], [spec]
    piece = math.gcd(start, width) if start else width
    operands, specs = [], []
    for at in range(start, start + width, piece):
        for stack in weight:
            operands.append(stack)
            specs.append(pl.BlockSpec((4, 2, 64, piece), lambda i, s, at=at: (0, 0, 0, at // piece)))
    return operands, specs


def load_slab(s_ref, refs, held):
    core = s_ref[0]
    if len(refs) == 1:
        return jnp.concatenate(
            [refs[0][0, y, jnp.bitwise_xor(c, core)] for c in (0, 1) for y in range(4)], axis=0
        )
    x_far = lax.rem(s_ref[2] + 4 - pl.program_id(0), 4)
    at = 0
    for first in range(0, len(refs), 4):
        stacks = refs[first : first + 4]
        width = stacks[0].shape[-1]
        for j in range(4):

            @pl.when((core == 0) & (x_far == j))
            def _(j=j, at=at, width=width, stacks=stacks):
                for i in range(4):
                    y = lax.rem(s_ref[3] + 4 - i, 4)
                    for c in (0, 1):
                        held[c * 4 + y, :, at : at + width] = stacks[j][i, c]

        @pl.when(core == 1)
        def _(at=at, width=width, stacks=stacks):
            for j in range(4):
                y = lax.rem(s_ref[3] + 4 - j, 4)
                for c in (0, 1):
                    held[c * 4 + y, :, at : at + width] = stacks[j][x_far, 1 - c]

        at += width
    return held[...].reshape(SLAB, at)


def hop(value, first, offset):
    pairs = []
    for x in range(4):
        for core in (0, 1):
            for y in range(4):
                to = ((x + offset) % 4, y) if (core == 0) == first else (x, (y + offset) % 4)
                pairs.append(((x * 2 + core) * 4 + y, (to[0] * 2 + core) * 4 + to[1]))
    return lax.ppermute(value, ("x", "core", "ctx"), pairs)


def spread_near(block):
    near, far, mid = [hop(block, False, o) for o in (1, 3, 2)]
    return block, near, mid, far


def stack_blocks(blocks, start, width, scalars, name, deps=()):
    at = start // width if start % width == 0 else None
    span = width if at is not None else blocks[0].shape[1]
    first = 0 if at is not None else start
    height = blocks[0].shape[0]

    def body(s_ref, *refs):
        for k, ref in enumerate(refs[:-1]):
            refs[-1][k * height : (k + 1) * height, :] = ref[:, first : first + width]

    total = sds((height * len(blocks), width), BF)
    return call(
        body,
        (1,),
        [pl.BlockSpec((height, span), lambda i, s: (0, at or 0))] * len(blocks),
        whole(total),
        total,
        scalars,
        tuple(blocks),
        name,
        deps=deps,
    )


def stack_attn(mine, came, scalars):
    height, total = mine.shape

    def body(s_ref, mine_ref, came_ref, first_ref, other_ref):
        for k, ref in enumerate((mine_ref, came_ref)):
            span = slice(k * height, (k + 1) * height)
            first_ref[span, :] = ref[:, :768]
            other_ref[span, :] = ref[:, 768:]

    shapes = (sds((2 * height, 768), BF), sds((2 * height, total - 768), BF))
    return call(
        body,
        (1,),
        [whole(mine), whole(came)],
        tuple(whole(s) for s in shapes),
        shapes,
        scalars,
        (mine, came),
        "stack_attn",
        stream=True,
    )


def spread_far(stack, gate=False):
    stack = stack.reshape(4, 2, 64, -1)
    near, far = hop(stack, True, 1), hop(stack, True, -1)
    mid = hop(tie((stack,), (near, far))[0] if gate else stack, True, 2)
    return stack, near, mid, far


def mm_in(left, right, columns, scalars, name, deps=(), stream=False):
    operands, specs, counts = [], [], []
    for weight, start, width in columns:
        ops, sp = weight_operands(weight, start, width)
        operands += ops
        specs += sp
        counts.append(len(ops))
    total = sum(width for _, _, width in columns)

    def body(s_ref, a_ref, b_ref, *refs):
        out_ref = refs[len(operands)]
        step = pl.program_id(0)
        rows = jnp.concatenate((a_ref[...], b_ref[...]), axis=0)
        at, first = 0, 0
        for k, count in enumerate(counts):
            width = columns[k][2]
            slab = load_slab(s_ref, refs[first : first + count], refs[len(operands) + 1 + k])
            part = jnp.dot(rows, slab, preferred_element_type=F32)
            span = slice(at, at + width)

            @pl.when(step == 0)
            def _(part=part, span=span):
                out_ref[:, span] = part

            @pl.when(step > 0)
            def _(part=part, span=span):
                out_ref[:, span] += part

            at += width
            first += count

    rows = left.shape[0]
    cols = pl.BlockSpec((rows, SLAB), lambda i, s: (0, i))
    return call(
        body,
        (4,),
        [cols, cols, *specs],
        pl.BlockSpec((2 * rows, total), lambda i, s: (0, 0)),
        sds((2 * rows, total), F32),
        scalars,
        (left, right, *operands),
        name,
        scratch=[pltpu.VMEM((8, 64, width), BF) for _, _, width in columns],
        deps=deps,
        stream=stream,
    )


def mm_back(terms, scalars, name, normed=None, deps=()):
    rows = terms[0][0].shape[0]
    half = rows // 2
    operands, specs, counts, scratch = [], [], [], []
    for grad, weight, start in terms:
        ops, sp = weight_operands(weight, start, grad.shape[1])
        operands += [grad, *ops]
        specs += [whole(grad), *sp]
        counts.append(len(ops))
        scratch.append(pltpu.VMEM((8, 64, grad.shape[1]), BF))
    held = len(operands)
    cols = pl.BlockSpec((half, SLAB), lambda i, s: (0, i))
    outs = [cols, cols]
    shapes = [sds((half, D), F32), sds((half, D), BF)]
    if normed is not None:
        operands += normed
        specs += [cols, cols]
        outs.append(pl.BlockSpec((8, SLAB), lambda i, s: (0, i)))
        shapes.append(sds((8, D), F32))
    total = len(operands)

    def body(s_ref, *refs):
        at, out = 0, 0.0
        for k, count in enumerate(counts):
            slab = load_slab(s_ref, refs[at + 1 : at + 1 + count], refs[total + len(outs) + k])
            out += lax.dot_general(
                refs[at][...], slab, (((1,), (1,)), ((), ())), preferred_element_type=F32
            )
            at += count + 1
        refs[total][...] = out[:half]
        refs[total + 1][...] = out[half:].astype(BF)
        if normed is not None:
            part = out[:half] * refs[held][...].astype(F32) + out[half:] * refs[held + 1][
                ...
            ].astype(F32)
            part = jnp.sum(part, axis=0, keepdims=True)
            refs[total + 2][...] = jnp.broadcast_to(part, (8, SLAB))

    return call(
        body,
        (4,),
        specs,
        tuple(outs),
        tuple(shapes),
        scalars,
        tuple(operands),
        name,
        scratch=scratch,
        deps=deps,
    )


def split_out(out, own_ref, other_ref):
    half = out.shape[0] // 2
    own_ref[...] = out[:half]
    other_ref[...] = out[half:].astype(BF)


def retain(x_pair, weight, key, value, came, fade, mask, enter, cosine, sine, scalars):
    rows = x_pair[0].shape[0]

    def body(
        s_ref, a_ref, b_ref, w_ref, k_ref, v_ref, near_ref, mid_ref, far_ref, f_ref, m_ref, e_ref,
        cos_ref, sin_ref, own_ref, other_ref, query_ref, state_ref, weighted_ref, gate_ref,
        retained_ref, mixed_ref, sums, turned
    ):
        step = pl.program_id(0)

        @pl.when(step < 4)
        def _():
            slab = load_slab(s_ref, (w_ref,), None)
            turned[step] = slab[:, DV : 2 * DV]
            left = jnp.concatenate((a_ref[...], b_ref[...]), axis=0)
            gate = jnp.dot(left, slab[:, :DV], preferred_element_type=F32)
            query = jnp.dot(left, slab[:, 2 * DV :], preferred_element_type=F32)

            @pl.when(step == 0)
            def _():
                gate_ref[...] = gate
                sums[...] = query

            @pl.when(step > 0)
            def _():
                gate_ref[...] += gate
                sums[...] += query

        @pl.when(step == 3)
        def _():
            fade = f_ref[...]
            for g in (0, 1):
                span = slice(g * rows, (g + 1) * rows)
                state = near_ref[g].astype(F32) + fade * (
                    mid_ref[g].astype(F32) + fade * far_ref[g].astype(F32)
                )
                state_ref[g] = state.astype(BF)
                query = rotate(sums[span], cos_ref[span], sin_ref[span]).astype(BF)
                query_ref[span] = query
                scores = lax.dot_general(
                    query, k_ref[g], (((1,), (1,)), ((), ())), preferred_element_type=F32
                )
                weighted = (scores * m_ref[g]).astype(BF)
                weighted_ref[g] = weighted
                retained = jnp.dot(weighted, v_ref[g], preferred_element_type=F32)
                retained += e_ref[span] * jnp.dot(
                    query, state_ref[g], preferred_element_type=F32
                )
                retained_ref[span] = retained
                mixed_ref[span] = gate_norm(gate_ref[span], retained).astype(BF)

        @pl.when(step >= 4)
        def _():
            out = lax.dot_general(
                mixed_ref[...],
                turned[step - 4],
                (((1,), (1,)), ((), ())),
                preferred_element_type=F32,
            )
            split_out(out, own_ref, other_ref)

    cols = pl.BlockSpec((rows, SLAB), lambda i, s: (0, jnp.minimum(i, 3)))
    later = pl.BlockSpec((rows, SLAB), lambda i, s: (0, jnp.maximum(i - 4, 0)))
    operands = (*x_pair, weight, key, value, *came, fade, mask, enter, cosine, sine)
    shapes = (
        sds((rows, D), F32),
        sds((rows, D), BF),
        sds((2 * rows, DK), BF),
        sds((2, DK, DV), BF),
        sds((2, rows, rows), BF),
        sds((2 * rows, DV), F32),
        sds((2 * rows, DV), F32),
        sds((2 * rows, DV), BF),
    )
    block = pl.BlockSpec((1, 4, 2, 64, 1280), lambda i, s: (jnp.minimum(i, 3), 0, 0, 0, 0))
    return call(
        body,
        (8,),
        [cols, cols, block] + [whole(o) for o in operands[3:]],
        (later, later) + tuple(whole(s) for s in shapes[2:]),
        shapes,
        scalars,
        operands,
        "retain",
        scratch=[pltpu.VMEM((2 * rows, DK), F32), pltpu.VMEM((4, SLAB, DV), BF)],
        stream=True,
    )


def mlp(x_pair, g_pair, weight, scalars):
    rows = x_pair[0].shape[0]

    def body(
        s_ref, a_ref, b_ref, c_ref, d_ref, w_ref, own_ref, other_ref, gain_ref, pair_ref, act_ref,
        both, back, kept
    ):
        step = pl.program_id(0)

        @pl.when(step < 4)
        def _():
            slab = load_slab(s_ref, (w_ref,), None)
            kept[step] = slab[:, : 2 * DV]
            left = jnp.concatenate((a_ref[...], b_ref[...]), axis=0)
            grad = jnp.concatenate((c_ref[...], d_ref[...]), axis=0)
            up = jnp.dot(left, slab[:, : 2 * DV], preferred_element_type=F32)
            down = jnp.dot(grad, slab[:, 2 * DV :], preferred_element_type=F32)

            @pl.when(step == 0)
            def _():
                both[...] = up
                back[...] = down

            @pl.when(step > 0)
            def _():
                both[...] += up
                back[...] += down

        @pl.when(step == 3)
        def _():
            def chunk(k, carry):
                span = pl.ds(pl.multiple_of(k * 64, 64), 64)
                hidden, linear, grad = both[span, :DV], both[span, DV:], back[span, :]
                cube = 0.044715 * hidden * hidden
                bent = jnp.tanh(0.7978845608 * hidden * (1.0 + cube))
                half = 0.5 * (1.0 + bent)
                gelu = hidden * half
                slope = half + 0.5 * hidden * (1.0 - bent * bent) * (
                    0.7978845608 * (1.0 + 3.0 * cube)
                )
                act_ref[span, :] = (gelu * linear).astype(BF)
                pair_ref[span, :DV] = (grad * linear * slope).astype(BF)
                pair_ref[span, DV:] = (grad * gelu).astype(BF)
                return carry

            lax.fori_loop(0, 2 * rows // 64, chunk, 0)

        @pl.when(step >= 4)
        def _():
            out = lax.dot_general(
                pair_ref[...], kept[step - 4], (((1,), (1,)), ((), ())), preferred_element_type=F32
            )
            split_out(out, own_ref, other_ref)
            part = out[:rows] * a_ref[...].astype(F32) + out[rows:] * b_ref[...].astype(F32)
            gain_ref[...] = jnp.broadcast_to(jnp.sum(part, axis=0, keepdims=True), (8, SLAB))

    cols = pl.BlockSpec((rows, SLAB), lambda i, s: (0, lax.rem(i, 4)))
    once = pl.BlockSpec((rows, SLAB), lambda i, s: (0, jnp.minimum(i, 3)))
    block = pl.BlockSpec((1, 4, 2, 64, 3 * DV), lambda i, s: (jnp.minimum(i, 3), 0, 0, 0, 0))
    later = pl.BlockSpec((rows, SLAB), lambda i, s: (0, jnp.maximum(i - 4, 0)))
    shapes = (
        sds((rows, D), F32),
        sds((rows, D), BF),
        sds((8, D), F32),
        sds((2 * rows, 2 * DV), BF),
        sds((2 * rows, DV), BF),
    )
    return call(
        body,
        (8,),
        [cols, cols, once, once, block],
        (
            later,
            later,
            pl.BlockSpec((8, SLAB), lambda i, s: (0, jnp.maximum(i - 4, 0))),
            whole(shapes[3]),
            whole(shapes[4]),
        ),
        shapes,
        scalars,
        (*x_pair, *g_pair, weight),
        "mlp",
        scratch=[
            pltpu.VMEM((2 * rows, 2 * DV), F32),
            pltpu.VMEM((2 * rows, DV), F32),
            pltpu.VMEM((4, SLAB, 2 * DV), BF),
        ],
        stream=True,
    )


def back_gate(g_pair, weight, gate_pre, retained, query, enter, scalars):
    rows = g_pair[0].shape[0]

    def body(
        s_ref, a_ref, b_ref, w_ref, gate_ref, kept_ref, q_ref, e_ref, dgate_ref, low_ref, state_ref,
        sums
    ):
        step = pl.program_id(0)
        left = jnp.concatenate((a_ref[...], b_ref[...]), axis=0)
        part = jnp.dot(left, load_slab(s_ref, (w_ref,), None), preferred_element_type=F32)

        @pl.when(step == 0)
        def _():
            sums[...] = part

        @pl.when(step > 0)
        def _():
            sums[...] += part

        @pl.when(step == 3)
        def _():
            def chunk(k, carry):
                span = pl.ds(pl.multiple_of(k * 64, 64), 64)
                gate, value, grad = gate_ref[span, :], kept_ref[span, :], sums[span, :]
                value = value - jnp.mean(value, axis=-1, keepdims=True)
                scale = lax.rsqrt(jnp.mean(value * value, axis=-1, keepdims=True) + 1.0 * DK)
                normed = value * scale
                open_part = jax.nn.sigmoid(gate)
                slope = open_part * (1.0 + gate * (1.0 - open_part))
                dgate_ref[span, :] = (grad * normed * slope).astype(BF)
                grad = grad * gate * open_part
                grad = grad - jnp.mean(grad, axis=-1, keepdims=True) - normed * jnp.mean(
                    grad * normed, axis=-1, keepdims=True
                )
                low_ref[span, :] = (grad * scale).astype(BF)
                return carry

            lax.fori_loop(0, 2 * rows // 64, chunk, 0)
            for g in (0, 1):
                span = slice(g * rows, (g + 1) * rows)
                entered = (q_ref[span].astype(F32) * e_ref[span]).astype(BF)
                state_ref[g] = lax.dot_general(
                    entered,
                    low_ref[span],
                    (((0,), (0,)), ((), ())),
                    preferred_element_type=F32,
                ).astype(BF)

    cols = pl.BlockSpec((rows, SLAB), lambda i, s: (0, i))
    operands = (*g_pair, weight, gate_pre, retained, query, enter)
    shapes = (
        sds((2 * rows, DV), BF),
        sds((2 * rows, DV), BF),
        sds((2, DK, DV), BF),
    )
    return call(
        body,
        (4,),
        [cols, cols, pl.BlockSpec((1, 4, 2, 64, DV), lambda i, s: (i, 0, 0, 0, 1))]
        + [whole(o) for o in operands[3:]],
        tuple(whole(s) for s in shapes),
        shapes,
        scalars,
        operands,
        "back_gate",
        scratch=[pltpu.VMEM((2 * rows, DV), F32)],
        stream=True,
    )


def weight_last(into, pair, came, fade, value, key_out, leave, grad_value, grad_key, cosine, sine,
                scalars):
    rows = pair[0].shape[0]

    def body(
        s_ref, a_ref, b_ref, near_ref, mid_ref, far_ref, f_ref, v_ref, k_ref, l_ref, gv_ref, gk_ref,
        cos_ref, sin_ref, into_ref, out_ref, mark_ref, grad_ref
    ):
        @pl.when(pl.program_id(0) == 0)
        def _():
            fade = f_ref[...]
            for g in (0, 1):
                span = slice(g * rows, (g + 1) * rows)
                state = near_ref[g].astype(F32) + fade * (
                    mid_ref[g].astype(F32) + fade * far_ref[g].astype(F32)
                )
                state = state.astype(BF)
                grad_ref[span, :DV] = (
                    gv_ref[g] + jnp.dot(k_ref[g], state, preferred_element_type=F32)
                ).astype(BF)
                grad_key = gk_ref[g] + l_ref[span] * lax.dot_general(
                    v_ref[g], state, (((1,), (1,)), ((), ())), preferred_element_type=F32
                )
                grad_ref[span, DV:] = rotate(grad_key, cos_ref[span], -sin_ref[span]).astype(BF)

        out = lax.dot_general(
            jnp.concatenate((a_ref[...], b_ref[...]), axis=0),
            grad_ref[...],
            (((0,), (0,)), ((), ())),
            preferred_element_type=F32,
        ).astype(BF)
        for c in (0, 1):
            for y in range(4):
                first = (c * 4 + y) * 64
                out_ref[0, y, jnp.bitwise_xor(c, s_ref[0])] = out[first : first + 64]
        mark_ref[...] = jnp.zeros_like(mark_ref)

    cols = pl.BlockSpec((rows, SLAB), lambda i, s: (0, i))
    operands = (*pair, *came, fade, value, key_out, leave, grad_value, grad_key, cosine, sine)
    shapes = (
        sds(into.shape, BF),
        sds((8, 128), F32),
        sds((2 * rows, DV + DK), BF),
    )
    return call(
        body,
        (4,),
        [cols, cols]
        + [whole(o) for o in operands[2:]]
        + [pl.BlockSpec(memory_space=pl.ANY)],
        (
            pl.BlockSpec((1, 4, 2, 64, DV + DK), lambda i, s: (i, 0, 0, 0, 0)),
            whole(shapes[1]),
            whole(shapes[2]),
        ),
        shapes,
        scalars,
        (*operands, into),
        "weight_last",
        stream=True,
        aliases={1 + len(operands): 0},
    )


def mm_weight_into(into, pairs, start, total, scalars, name, deps=()):
    widths = [grad.shape[1] for _, grad in pairs]
    rows = pairs[0][0][0].shape[0]
    span = sum(widths)

    def body(s_ref, *refs):
        out_ref, mark_ref = refs[-2:]
        at = 0
        for k, width in enumerate(widths):
            a_ref, b_ref, g_ref = refs[3 * k : 3 * k + 3]
            out = lax.dot_general(
                jnp.concatenate((a_ref[...], b_ref[...]), axis=0),
                g_ref[...],
                (((0,), (0,)), ((), ())),
                preferred_element_type=F32,
            ).astype(BF)
            for c in (0, 1):
                for y in range(4):
                    first = (c * 4 + y) * 64
                    out_ref[0, y, jnp.bitwise_xor(c, s_ref[0]), :, at : at + width] = out[
                        first : first + 64
                    ]
            at += width
        mark_ref[...] = jnp.zeros_like(mark_ref)

    cols = pl.BlockSpec((rows, SLAB), lambda i, s: (0, i))
    specs, operands = [], []
    for (a, b), grad in pairs:
        specs += [cols, cols, whole(grad)]
        operands += [a, b, grad]
    aliases = None
    if into is not None:
        aliases = {1 + len(operands): 0}
        specs.append(pl.BlockSpec(memory_space=pl.ANY))
        operands.append(into)
    return call(
        body,
        (4,),
        specs,
        (
            pl.BlockSpec((1, 4, 2, 64, span), lambda i, s: (i, 0, 0, 0, start // span)),
            pl.BlockSpec((8, 128), lambda i, s: (0, 0)),
        ),
        (sds((4, 4, 2, 64, total), BF), sds((8, 128), F32)),
        scalars,
        tuple(operands),
        name,
        deps=deps,
        stream=True,
        aliases=aliases,
    )


def split_heads(weights, scalars, name, deps=()):
    widths = [w.shape[1] // 2 for w in weights]

    def body(s_ref, *refs):
        mine_ref, theirs_ref = refs[-2:]
        core = s_ref[0]
        for out_ref, head in ((mine_ref, core), (theirs_ref, 1 - core)):
            at = 0
            for ref, width in zip(refs, widths):
                out_ref[:, at : at + width] = ref[:, pl.ds(pl.multiple_of(head * width, width), width)]
                at += width

    total = sum(widths)
    spec = pl.BlockSpec((64, total), lambda i, s: (0, 0))
    return call(
        body,
        (1,),
        [whole(w) for w in weights],
        (spec, spec),
        (sds((64, total), BF),) * 2,
        scalars,
        tuple(weights),
        name,
        deps=deps,
        stream=True,
    )


def join_heads(mine, theirs, widths, scalars, name):
    def body(s_ref, mine_ref, theirs_ref, *outs):
        core = s_ref[0]
        for in_ref, head in ((mine_ref, core), (theirs_ref, 1 - core)):
            at = 0
            for ref, width in zip(outs, widths):
                span = pl.ds(pl.multiple_of(head * width, width), width)
                ref[:, span] = in_ref[:, at : at + width].astype(F32)
                at += width

    shapes = tuple(sds((64, 2 * w), F32) for w in widths)
    return call(
        body,
        (1,),
        [whole(mine), whole(theirs)],
        tuple(whole(s) for s in shapes),
        shapes,
        scalars,
        (mine, theirs),
        name,
    )


def scale_of(values):
    return lax.rsqrt(jnp.mean(values * values, axis=-1, keepdims=True) + 1e-06)


def turned_spec(rows):
    return pl.BlockSpec((rows, D), lambda i, s: (lax.rem(i + s[1], 4), 0))


def plain_spec(rows):
    return pl.BlockSpec((rows, D), lambda i, s: (i, 0))


def enter_rows(tokens, gain, scalars, deps=()):
    rows = tokens.shape[0]
    block = rows // 4

    def body(s_ref, t_ref, g_ref, n_out):
        values = t_ref[...]
        n_out[...] = (values * scale_of(values) * g_ref[...]).astype(BF)

    return call(
        body,
        (4,),
        [turned_spec(block), whole(gain)],
        plain_spec(block),
        sds((rows, D), BF),
        scalars,
        (tokens, gain),
        "enter_rows",
        deps=deps,
    )


def low_rows(cotangent, scalars, deps=()):
    rows = cotangent.shape[0]
    block = rows // 4

    def body(s_ref, c_ref, l_out):
        l_out[...] = c_ref[...].astype(BF)

    return call(
        body,
        (4,),
        [turned_spec(block)],
        plain_spec(block),
        sds((rows, D), BF),
        scalars,
        (cotangent,),
        "low_rows",
        deps=deps,
    )


def each_part(refs, work):
    step = pl.program_id(0)
    for k, ref in enumerate(refs):

        @pl.when(step == k)
        def _(ref=ref):
            work(ref[...].astype(F32))


def second_norm(tokens, parts, gain, scalars, deps=()):
    rows = tokens.shape[0]
    block = rows // 4

    def body(s_ref, t_ref, g_ref, *refs):
        h_out, n_out = refs[4:]

        def work(part):
            values = t_ref[...] + part
            h_out[...] = values
            n_out[...] = (values * scale_of(values) * g_ref[...]).astype(BF)

        each_part(refs[:4], work)

    plain = plain_spec(block)
    return call(
        body,
        (4,),
        [turned_spec(block), whole(gain)] + [whole(p) for p in parts],
        (plain, plain),
        (sds((rows, D), F32), sds((rows, D), BF)),
        scalars,
        (tokens, gain, *parts),
        "second_norm",
        deps=deps,
    )


def third_blocks(own, came, down_own, down_came, scalars, deps=()):
    rows = own.shape[0]
    block = rows // 4

    def body(s_ref, own_ref, came_ref, d_ref, e_ref, *refs):
        total = own_ref[...] + came_ref[...].astype(F32)
        down = d_ref[...] + e_ref[...].astype(F32)
        step = pl.program_id(0)
        for k in range(4):

            @pl.when(step == k)
            def _(k=k):
                refs[k][:block] = total.astype(BF)
                refs[k][block:] = down.astype(BF)

    plain = plain_spec(block)
    shapes = (sds((2 * block, D), BF),) * 4
    return call(
        body,
        (4,),
        [plain] * 4,
        tuple(whole(s) for s in shapes),
        shapes,
        scalars,
        (own, came, down_own, down_came),
        "third_blocks",
        deps=deps,
        stream=True,
    )


def leave_rows(hidden, tokens, grad_state, parts, gain, scalars, deps=()):
    rows = hidden.shape[0]
    block = rows // 4

    def body(s_ref, h_ref, t_ref, u_ref, g_ref, *refs):
        def work(part):
            refs[4][...] = h_ref[...] + part[block : 2 * block]
            refs[5][...] = u_ref[...] + norm_grad(t_ref[...], part[:block], g_ref[...])

        each_part(refs[:4], work)

    plain, turn = plain_spec(block), turned_spec(block)
    return call(
        body,
        (4,),
        [plain, turn, plain, whole(gain)] + [whole(p) for p in parts],
        (turn, turn),
        (sds((rows, D), F32),) * 2,
        scalars,
        (hidden, tokens, grad_state, gain, *parts),
        "leave_rows",
        deps=deps,
        stream=True,
    )


def norm_grad(values, grad, gain):
    factor = scale_of(values)
    unit = values * factor
    scaled = grad * gain
    return factor * (scaled - unit * jnp.mean(scaled * unit, axis=-1, keepdims=True))


def norm_back(values, upstream, parts, gain, scalars, name, deps=()):
    rows = values.shape[0]
    block = rows // 4

    def body(s_ref, v_ref, u_ref, g_ref, *refs):
        def work(part):
            out = u_ref[...] + norm_grad(v_ref[...], part, g_ref[...])
            refs[4][...] = out
            refs[5][...] = out.astype(BF)

        each_part(refs[:4], work)

    plain = plain_spec(block)
    return call(
        body,
        (4,),
        [plain, turned_spec(block), whole(gain)] + [whole(p) for p in parts],
        (plain, plain),
        (sds((rows, D), F32), sds((rows, D), BF)),
        scalars,
        (values, upstream, gain, *parts),
        name,
        deps=deps,
        stream=True,
    )


def tp_first(blocks):
    got = [shift(blocks[o], "tp", o) for o in (1, 3, 2)]
    near, far, mid = [part.astype(F32) for part in got]
    return (blocks[0].astype(F32) + mid) + (near + far), got


def tp_second(mine):
    near, far, mid = [shift(mine, "tp", -o) for o in (1, 3, 2)]
    return mine, near, mid, far


def tp_total(blocks):
    return tp_second(tp_first(blocks)[0].astype(BF))


def chip_blocks(own, came):
    block = own.shape[0] // 4
    return [
        (own[o * block : (o + 1) * block] + came[o * block : (o + 1) * block].astype(F32)).astype(BF)
        for o in range(4)
    ]


def gate_norm(gate_pre, retained):
    centred = retained - jnp.mean(retained, axis=-1, keepdims=True)
    normed = centred * lax.rsqrt(jnp.mean(centred * centred, axis=-1, keepdims=True) + 1.0 * DK)
    return gate_pre * jax.nn.sigmoid(gate_pre) * normed


def gelu_gate(hidden, linear):
    return jax.nn.gelu(hidden, approximate=True) * linear


def rotate(values, cosine, sine):
    half = DK // 2
    first = values[:, :half]
    second = values[:, half:]
    return jnp.concatenate((first * cosine - second * sine, first * sine + second * cosine), axis=1)


def ein(spec, left, right):
    return jnp.einsum(spec, left, right, preferred_element_type=F32)


def per_device(
    tokens,
    cotangent,
    gain_first,
    gain_second,
    w_query,
    w_key,
    w_value,
    w_gate,
    w_output,
    w_hidden,
    w_linear,
    w_down,
    decay_scale,
    first_length,
):
    rows = tokens.shape[0]
    core = lax.axis_index("core")
    place = lax.axis_index("ctx")
    plane = lax.axis_index("tp")
    scalars = jnp.stack((core, plane, lax.axis_index("x"), place)).astype(jnp.int32)

    w_output = w_output.T
    w_down = w_down.T
    mine, theirs = split_heads((w_value, w_key, w_gate, w_output, w_query), scalars, "split_attn")
    came = swap(theirs)
    block, gathered = stack_attn(mine, came, scalars)
    lengths = jnp.concatenate((first_length, swap(first_length)))
    blocks = spread_near(block)
    w_kv = stack_blocks(blocks, 0, 768, scalars, "stack_kv")
    normed_first = enter_rows(tokens, gain_first.reshape(1, D), scalars, deps=(w_kv,))
    (gathered,) = tie((gathered,), blocks[1:])
    w_goq = lax.all_gather(gathered, XY, axis=0, tiled=True).reshape(4, 4, 2, 64, -1)
    mine, theirs = split_heads(
        (w_hidden, w_linear, w_down), scalars, "split_mlp", deps=(normed_first,)
    )
    came_mlp = swap(theirs)
    gain_first = gain_first.reshape(1, D)
    gain_second = gain_second.reshape(1, D)
    x_first = (normed_first, swap(normed_first))
    cot_low = low_rows(cotangent, scalars, deps=(x_first[1],))
    g_out = (cot_low, swap(cot_low))
    w_kv = spread_far(w_kv)

    rate = lax.dynamic_index_in_dim(decay_scale, core, 0, False) / 1024.0
    local = (jnp.arange(rows, dtype=jnp.int32) + plane * (rows // 4)) % rows
    index = place * rows + local
    document = (index[None, :] >= lengths[:, None]).astype(jnp.int32)
    carried = (document == 0).astype(F32)
    steps = local.astype(F32)
    offsets = local[:, None] - local[None, :]
    linked = (offsets >= 0)[None] & (document[:, :, None] == document[:, None, :])
    mask = jnp.where(
        linked, jnp.exp(-rate * jnp.maximum(offsets, 0).astype(F32))[None], 0.0
    )
    enter = (carried * jnp.exp(-rate * (steps + 1.0))[None])[:, :, None]
    leave = jnp.exp(-rate * (rows - 1.0 - steps))[None, :, None]
    fade = jnp.exp(-rate * rows)
    half = DK // 2
    frequency = 10000.0 ** (-(jnp.arange(half).astype(F32) / half))
    angles = index.astype(F32)[:, None] * frequency[None, :]
    cosine = jnp.tile(jnp.cos(angles), (2, 1))
    sine = jnp.tile(jnp.sin(angles), (2, 1))

    def spread_state(low, way):
        return [shift_open(low, "ctx", way * o) for o in (1, 2, 3)]

    enter_rows_in = enter.reshape(2 * rows, 1)
    leave_rows_out = jnp.tile(leave.reshape(rows, 1), (2, 1))
    fade_in = fade.reshape(1, 1)
    projected = mm_in(
        *x_first,
        [(w_kv, 0, 768)],
        scalars,
        "project_kv",
        deps=(mask, enter_rows_in, leave_rows_out, fade_in, cosine, sine, came_mlp),
    )
    key = rotate(projected[:, DV:], cosine, sine).astype(BF).reshape(2, rows, DK)
    value = projected[:, :DV].astype(BF).reshape(2, rows, DV)
    key_out = (key.astype(F32) * leave).astype(BF)
    state_out = ein("gjd,gje->gde", key_out, value).astype(BF)
    came = spread_state(state_out, 1)
    w_mlp = lax.all_gather(
        stack_blocks((mine, came_mlp), 0, 1536, scalars, "stack_mlp", deps=(state_out,)),
        XY,
        axis=0,
        tiled=True,
    ).reshape(4, 4, 2, 64, -1)
    own, other, query, state_in, weighted, gate_pre, retained, mixed = retain(
        x_first,
        w_goq,
        key,
        value,
        came,
        fade_in,
        mask,
        enter_rows_in,
        cosine,
        sine,
        scalars,
    )
    query = query.reshape(2, rows, DK)
    parts = tp_total(chip_blocks(own, swap(other)))
    hidden_state, normed_second = second_norm(tokens, parts, gain_second, scalars)
    x_second = (normed_second, swap(normed_second))
    own, other, gain_second_part, grad_pair, activated = mlp(x_second, g_out, w_mlp, scalars)
    grads, mark = mm_weight_into(
        None, ((x_second, grad_pair),), 1024, 3584, scalars, "weight_mlp"
    )
    mine, _ = tp_first(chip_blocks(own, swap(other)))
    (mine,) = tie((mine.astype(BF),), (mark,))
    parts = tp_second(mine)
    down = mm_back([(activated, w_mlp, 2 * DV)], scalars, "project_down", deps=(mine,))
    grad_state, grad_state_low = norm_back(
        hidden_state,
        cotangent,
        parts,
        gain_second,
        scalars,
        "second_back",
        deps=(down[1],),
    )
    g_state = (grad_state_low, swap(grad_state_low))
    grad_gate, grad_low, back_out = back_gate(
        g_state, w_goq, gate_pre, retained, query.reshape(2 * rows, DK), enter_rows_in, scalars
    )
    grad_low = grad_low.reshape(2, rows, DV)
    came = spread_state(back_out, -1)
    grad_scores = (ein("gie,gje->gij", grad_low, value) * mask).astype(BF)
    grad_query = ein("gij,gjd->gid", grad_scores, key) + enter * ein("gie,gde->gid", grad_low, state_in)
    grad_key = ein("gij,gid->gjd", grad_scores, query)
    grad_value = ein("gij,gie->gje", weighted, grad_low)
    grad_query = rotate(grad_query.reshape(2 * rows, DK), cosine, -sine).astype(BF)
    grads, mark = mm_weight_into(
        grads,
        ((g_state, mixed), (x_first, grad_gate)),
        2048,
        3584,
        scalars,
        "weight_og",
        deps=(back_out,),
    )
    grads, mark = mm_weight_into(
        grads, ((g_out, activated),), 3072, 3584, scalars, "weight_down"
    )
    grads, mark = mm_weight_into(
        grads, ((x_first, grad_query),), 768, 3584, scalars, "weight_query"
    )
    came[0] = tie((came[0],), (mark, grad_key, grad_value))[0]
    grads, mark, grad_vk = weight_last(
        grads,
        x_first,
        came,
        fade_in,
        value,
        key_out,
        leave_rows_out,
        grad_value,
        grad_key,
        cosine,
        sine,
        scalars,
    )
    block = lax.psum_scatter(grads.reshape(2048, -1), XY, scatter_dimension=0, tiled=True)
    own, other, gain_first_part = mm_back(
        [(grad_vk, w_kv, 0), (grad_gate, w_goq, 0), (grad_query, w_goq, 1024)],
        scalars,
        "back_attn",
        normed=x_first,
        deps=(mark,),
    )
    down = (down[0], swap(tie((down[1],), (mark,))[0]))
    blocks = third_blocks(own, swap(other), *down, scalars)
    mine, _ = tp_first(blocks)
    gains = jnp.concatenate((gain_first_part[:1], gain_second_part[:1]))
    for axis, swapped in (
        ("core", (1, 0)),
        ("ctx", (1, 0, 3, 2)),
        ("ctx", (3, 2, 1, 0)),
        ("x", (1, 0, 3, 2)),
        ("x", (3, 2, 1, 0)),
    ):
        gains = gains + lax.ppermute(gains, axis, list(enumerate(swapped)))
    mine = jnp.concatenate((mine, gains, jnp.zeros((14, D), F32))).astype(BF)
    parts = tp_second(mine)
    gains = [part[128:130].astype(F32) for part in parts]
    gains = (gains[0] + gains[2]) + (gains[1] + gains[3])
    spot = (lax.axis_index("x") * 2 + core) * 4 + place
    gain_first_grad, gain_second_grad = [
        lax.dynamic_slice_in_dim(gains[k] / gain[0], spot * 64, 64, 0)
        for k, gain in ((0, gain_first), (1, gain_second))
    ]
    layer_out, input_grad = leave_rows(
        hidden_state, tokens, grad_state, parts, gain_first, scalars
    )
    block = tie((block,), (gain_first_grad, gain_second_grad, input_grad))[0].reshape(2, 64, -1)
    d_value, d_key, d_query, d_hidden, d_linear, d_output, d_gate, d_down = join_heads(
        block[0], swap(block[1]), (DV, DK, DK) + (DV,) * 5, scalars, "join_heads"
    )
    return (
        layer_out,
        input_grad,
        gain_first_grad,
        gain_second_grad,
        d_query,
        d_key,
        d_value,
        d_gate,
        d_output.T,
        d_hidden,
        d_linear,
        d_down.T,
    )


def solution(mesh):
    fine = Mesh(np.asarray(mesh.devices).reshape(4, 2, 4, 4), ("x", "core", "ctx", "tp"))
    split = ("x", "core", "ctx")
    row = P(split, None)
    win = P(split, "tp")
    wout = P("tp", split)
    in_specs = (row, row, P(), P(), win, win, win, win, wout, win, win, wout, P("tp"), P(("x", "core")))
    out_specs = (row, row, P(split), P(split), win, win, win, win, wout, win, win, wout)
    return jax.shard_map(
        per_device, mesh=fine, in_specs=in_specs, out_specs=out_specs, check_vma=False
    )
```

```python
import math

import jax
import jax.numpy as jnp
import numpy as np
from jax import lax
from jax.experimental import pallas as pl
from jax.experimental.pallas import tpu as pltpu
from jax.sharding import Mesh, PartitionSpec as P

D = 2048
DK = 256
DV = 512
SLAB = 512
BF = jnp.bfloat16
F32 = jnp.float32
XY = ("x", "ctx")
MIB = 1 << 20


def shift(value, axis, offset):
    n = lax.axis_size(axis)
    return lax.ppermute(value, axis, [(i, (i + offset) % n) for i in range(n)])


def shift_open(value, axis, offset):
    n = lax.axis_size(axis)
    return lax.ppermute(
        value, axis, [(i, i + offset) for i in range(n) if 0 <= i + offset < n]
    )


def swap(value):
    return lax.ppermute(value, "core", [(0, 1), (1, 0)])


def after(value, *earlier):
    return lax.optimization_barrier((value, *earlier))[0]


def call(
    body,
    grid,
    ins,
    outs,
    shapes,
    scalars,
    operands,
    name,
    scratch=(),
    deps=(),
    stream=False,
    aliases=None,
):
    count = len(operands)

    def kernel(s_ref, *refs):
        body(s_ref, *refs[:count], *refs[count + len(deps) :])

    ins = [*ins, *[pl.BlockSpec(memory_space=pl.ANY)] * len(deps)]
    return pl.pallas_call(
        kernel,
        out_shape=shapes,
        grid_spec=pltpu.PrefetchScalarGridSpec(
            num_scalar_prefetch=1, grid=grid, in_specs=ins, out_specs=outs, scratch_shapes=scratch
        ),
        compiler_params=pltpu.CompilerParams(
            vmem_limit_bytes=(60 if stream else 32) * MIB, dimension_semantics=("arbitrary",) * len(grid)
        ),
        cost_estimate=pl.CostEstimate(flops=1, bytes_accessed=1, transcendentals=0),
        input_output_aliases=aliases or {},
        name=name,
    )(scalars, *operands, *deps)


def tie(values, deps):
    count = len(values)
    anywhere = pl.BlockSpec(memory_space=pl.ANY)
    return pl.pallas_call(
        lambda *refs: None,
        out_shape=tuple(sds(v.shape, v.dtype) for v in values),
        in_specs=[anywhere] * (count + len(deps)),
        out_specs=(anywhere,) * count,
        input_output_aliases={i: i for i in range(count)},
        name="tie",
    )(*values, *deps)


def whole(array):
    return pl.BlockSpec(array.shape, lambda *_: (0,) * array.ndim)


def sds(shape, dtype):
    return jax.ShapeDtypeStruct(shape, dtype)


def weight_operands(weight, start, width):
    if not isinstance(weight, tuple):
        spec = pl.BlockSpec((1, 4, 2, 64, width), lambda i, s: (i, 0, 0, 0, start // width))
        return [weight], [spec]
    piece = math.gcd(start, width) if start else width
    operands, specs = [], []
    for at in range(start, start + width, piece):
        for stack in weight:
            operands.append(stack)
            specs.append(pl.BlockSpec((4, 2, 64, piece), lambda i, s, at=at: (0, 0, 0, at // piece)))
    return operands, specs


def load_slab(s_ref, refs, held):
    core = s_ref[0]
    if len(refs) == 1:
        return jnp.concatenate(
            [refs[0][0, y, jnp.bitwise_xor(c, core)] for c in (0, 1) for y in range(4)], axis=0
        )
    x_far = lax.rem(s_ref[2] + 4 - pl.program_id(0), 4)
    at = 0
    for first in range(0, len(refs), 4):
        stacks = refs[first : first + 4]
        width = stacks[0].shape[-1]
        for j in range(4):

            @pl.when((core == 0) & (x_far == j))
            def _(j=j, at=at, width=width, stacks=stacks):
                for i in range(4):
                    y = lax.rem(s_ref[3] + 4 - i, 4)
                    for c in (0, 1):
                        held[c * 4 + y, :, at : at + width] = stacks[j][i, c]

        @pl.when(core == 1)
        def _(at=at, width=width, stacks=stacks):
            for j in range(4):
                y = lax.rem(s_ref[3] + 4 - j, 4)
                for c in (0, 1):
                    held[c * 4 + y, :, at : at + width] = stacks[j][x_far, 1 - c]

        at += width
    return held[...].reshape(SLAB, at)


def hop(value, first, offset):
    pairs = []
    for x in range(4):
        for core in (0, 1):
            for y in range(4):
                to = ((x + offset) % 4, y) if (core == 0) == first else (x, (y + offset) % 4)
                pairs.append(((x * 2 + core) * 4 + y, (to[0] * 2 + core) * 4 + to[1]))
    return lax.ppermute(value, ("x", "core", "ctx"), pairs)


def spread_near(block):
    near, far, mid = [hop(block, False, o) for o in (1, 3, 2)]
    return block, near, mid, far


def stack_blocks(blocks, start, width, scalars, name, deps=()):
    at = start // width if start % width == 0 else None
    span = width if at is not None else blocks[0].shape[1]
    first = 0 if at is not None else start
    height = blocks[0].shape[0]

    def body(s_ref, *refs):
        for k, ref in enumerate(refs[:-1]):
            refs[-1][k * height : (k + 1) * height, :] = ref[:, first : first + width]

    total = sds((height * len(blocks), width), BF)
    return call(
        body,
        (1,),
        [pl.BlockSpec((height, span), lambda i, s: (0, at or 0))] * len(blocks),
        whole(total),
        total,
        scalars,
        tuple(blocks),
        name,
        deps=deps,
    )


def stack_attn(mine, came, scalars):
    height, total = mine.shape

    def body(s_ref, mine_ref, came_ref, first_ref, other_ref):
        for k, ref in enumerate((mine_ref, came_ref)):
            span = slice(k * height, (k + 1) * height)
            first_ref[span, :] = ref[:, :768]
            other_ref[span, :] = ref[:, 768:]

    shapes = (sds((2 * height, 768), BF), sds((2 * height, total - 768), BF))
    return call(
        body,
        (1,),
        [whole(mine), whole(came)],
        tuple(whole(s) for s in shapes),
        shapes,
        scalars,
        (mine, came),
        "stack_attn",
        stream=True,
    )


def spread_far(stack, gate=False):
    stack = stack.reshape(4, 2, 64, -1)
    near, far = hop(stack, True, 1), hop(stack, True, -1)
    mid = hop(tie((stack,), (near, far))[0] if gate else stack, True, 2)
    return stack, near, mid, far


def mm_in(left, right, columns, scalars, name, deps=(), stream=False):
    operands, specs, counts = [], [], []
    for weight, start, width in columns:
        ops, sp = weight_operands(weight, start, width)
        operands += ops
        specs += sp
        counts.append(len(ops))
    total = sum(width for _, _, width in columns)

    def body(s_ref, a_ref, b_ref, *refs):
        out_ref = refs[len(operands)]
        step = pl.program_id(0)
        rows = jnp.concatenate((a_ref[...], b_ref[...]), axis=0)
        at, first = 0, 0
        for k, count in enumerate(counts):
            width = columns[k][2]
            slab = load_slab(s_ref, refs[first : first + count], refs[len(operands) + 1 + k])
            part = jnp.dot(rows, slab, preferred_element_type=F32)
            span = slice(at, at + width)

            @pl.when(step == 0)
            def _(part=part, span=span):
                out_ref[:, span] = part

            @pl.when(step > 0)
            def _(part=part, span=span):
                out_ref[:, span] += part

            at += width
            first += count

    rows = left.shape[0]
    cols = pl.BlockSpec((rows, SLAB), lambda i, s: (0, i))
    return call(
        body,
        (4,),
        [cols, cols, *specs],
        pl.BlockSpec((2 * rows, total), lambda i, s: (0, 0)),
        sds((2 * rows, total), F32),
        scalars,
        (left, right, *operands),
        name,
        scratch=[pltpu.VMEM((8, 64, width), BF) for _, _, width in columns],
        deps=deps,
        stream=stream,
    )


def mm_back(terms, scalars, name, normed=None, deps=()):
    rows = terms[0][0].shape[0]
    half = rows // 2
    operands, specs, counts, scratch = [], [], [], []
    for grad, weight, start in terms:
        ops, sp = weight_operands(weight, start, grad.shape[1])
        operands += [grad, *ops]
        specs += [whole(grad), *sp]
        counts.append(len(ops))
        scratch.append(pltpu.VMEM((8, 64, grad.shape[1]), BF))
    held = len(operands)
    cols = pl.BlockSpec((half, SLAB), lambda i, s: (0, i))
    outs = [cols, cols]
    shapes = [sds((half, D), F32), sds((half, D), BF)]
    if normed is not None:
        operands += normed
        specs += [cols, cols]
        outs.append(pl.BlockSpec((8, SLAB), lambda i, s: (0, i)))
        shapes.append(sds((8, D), F32))
    total = len(operands)

    def body(s_ref, *refs):
        at, out = 0, 0.0
        for k, count in enumerate(counts):
            slab = load_slab(s_ref, refs[at + 1 : at + 1 + count], refs[total + len(outs) + k])
            out += lax.dot_general(
                refs[at][...], slab, (((1,), (1,)), ((), ())), preferred_element_type=F32
            )
            at += count + 1
        refs[total][...] = out[:half]
        refs[total + 1][...] = out[half:].astype(BF)
        if normed is not None:
            part = out[:half] * refs[held][...].astype(F32) + out[half:] * refs[held + 1][
                ...
            ].astype(F32)
            part = jnp.sum(part, axis=0, keepdims=True)
            refs[total + 2][...] = jnp.broadcast_to(part, (8, SLAB))

    return call(
        body,
        (4,),
        specs,
        tuple(outs),
        tuple(shapes),
        scalars,
        tuple(operands),
        name,
        scratch=scratch,
        deps=deps,
    )


def split_out(out, own_ref, other_ref):
    half = out.shape[0] // 2
    own_ref[...] = out[:half]
    other_ref[...] = out[half:].astype(BF)


def retain(x_pair, weight, key, value, came, fade, mask, enter, cosine, sine, scalars):
    rows = x_pair[0].shape[0]

    def body(
        s_ref, a_ref, b_ref, w_ref, k_ref, v_ref, near_ref, mid_ref, far_ref, f_ref, m_ref, e_ref,
        cos_ref, sin_ref, own_ref, other_ref, query_ref, state_ref, weighted_ref, gate_ref,
        retained_ref, mixed_ref, sums, turned
    ):
        step = pl.program_id(0)

        @pl.when(step < 4)
        def _():
            slab = load_slab(s_ref, (w_ref,), None)
            turned[step] = slab[:, DV : 2 * DV]
            left = jnp.concatenate((a_ref[...], b_ref[...]), axis=0)
            gate = jnp.dot(left, slab[:, :DV], preferred_element_type=F32)
            query = jnp.dot(left, slab[:, 2 * DV :], preferred_element_type=F32)

            @pl.when(step == 0)
            def _():
                gate_ref[...] = gate
                sums[...] = query

            @pl.when(step > 0)
            def _():
                gate_ref[...] += gate
                sums[...] += query

        @pl.when(step == 3)
        def _():
            fade = f_ref[...]
            for g in (0, 1):
                span = slice(g * rows, (g + 1) * rows)
                state = near_ref[g].astype(F32) + fade * (
                    mid_ref[g].astype(F32) + fade * far_ref[g].astype(F32)
                )
                state_ref[g] = state.astype(BF)
                query = rotate(sums[span], cos_ref[span], sin_ref[span]).astype(BF)
                query_ref[span] = query
                scores = lax.dot_general(
                    query, k_ref[g], (((1,), (1,)), ((), ())), preferred_element_type=F32
                )
                weighted = (scores * m_ref[g]).astype(BF)
                weighted_ref[g] = weighted
                retained = jnp.dot(weighted, v_ref[g], preferred_element_type=F32)
                retained += e_ref[span] * jnp.dot(
                    query, state_ref[g], preferred_element_type=F32
                )
                retained_ref[span] = retained
                mixed_ref[span] = gate_norm(gate_ref[span], retained).astype(BF)

        @pl.when(step >= 4)
        def _():
            out = lax.dot_general(
                mixed_ref[...],
                turned[step - 4],
                (((1,), (1,)), ((), ())),
                preferred_element_type=F32,
            )
            split_out(out, own_ref, other_ref)

    cols = pl.BlockSpec((rows, SLAB), lambda i, s: (0, jnp.minimum(i, 3)))
    later = pl.BlockSpec((rows, SLAB), lambda i, s: (0, jnp.maximum(i - 4, 0)))
    operands = (*x_pair, weight, key, value, *came, fade, mask, enter, cosine, sine)
    shapes = (
        sds((rows, D), F32),
        sds((rows, D), BF),
        sds((2 * rows, DK), BF),
        sds((2, DK, DV), BF),
        sds((2, rows, rows), BF),
        sds((2 * rows, DV), F32),
        sds((2 * rows, DV), F32),
        sds((2 * rows, DV), BF),
    )
    block = pl.BlockSpec((1, 4, 2, 64, 1280), lambda i, s: (jnp.minimum(i, 3), 0, 0, 0, 0))
    return call(
        body,
        (8,),
        [cols, cols, block] + [whole(o) for o in operands[3:]],
        (later, later) + tuple(whole(s) for s in shapes[2:]),
        shapes,
        scalars,
        operands,
        "retain",
        scratch=[pltpu.VMEM((2 * rows, DK), F32), pltpu.VMEM((4, SLAB, DV), BF)],
        stream=True,
    )


def mlp(x_pair, g_pair, weight, scalars):
    rows = x_pair[0].shape[0]

    def body(
        s_ref, a_ref, b_ref, c_ref, d_ref, w_ref, own_ref, other_ref, gain_ref, pair_ref, act_ref,
        both, back, kept
    ):
        step = pl.program_id(0)

        @pl.when(step < 4)
        def _():
            slab = load_slab(s_ref, (w_ref,), None)
            kept[step] = slab[:, : 2 * DV]
            left = jnp.concatenate((a_ref[...], b_ref[...]), axis=0)
            grad = jnp.concatenate((c_ref[...], d_ref[...]), axis=0)
            up = jnp.dot(left, slab[:, : 2 * DV], preferred_element_type=F32)
            down = jnp.dot(grad, slab[:, 2 * DV :], preferred_element_type=F32)

            @pl.when(step == 0)
            def _():
                both[...] = up
                back[...] = down

            @pl.when(step > 0)
            def _():
                both[...] += up
                back[...] += down

        @pl.when(step == 3)
        def _():
            def chunk(k, carry):
                span = pl.ds(pl.multiple_of(k * 64, 64), 64)
                hidden, linear, grad = both[span, :DV], both[span, DV:], back[span, :]
                cube = 0.044715 * hidden * hidden
                bent = jnp.tanh(0.7978845608 * hidden * (1.0 + cube))
                half = 0.5 * (1.0 + bent)
                gelu = hidden * half
                slope = half + 0.5 * hidden * (1.0 - bent * bent) * (
                    0.7978845608 * (1.0 + 3.0 * cube)
                )
                act_ref[span, :] = (gelu * linear).astype(BF)
                pair_ref[span, :DV] = (grad * linear * slope).astype(BF)
                pair_ref[span, DV:] = (grad * gelu).astype(BF)
                return carry

            lax.fori_loop(0, 2 * rows // 64, chunk, 0)

        @pl.when(step >= 4)
        def _():
            out = lax.dot_general(
                pair_ref[...], kept[step - 4], (((1,), (1,)), ((), ())), preferred_element_type=F32
            )
            split_out(out, own_ref, other_ref)
            part = out[:rows] * a_ref[...].astype(F32) + out[rows:] * b_ref[...].astype(F32)
            gain_ref[...] = jnp.broadcast_to(jnp.sum(part, axis=0, keepdims=True), (8, SLAB))

    cols = pl.BlockSpec((rows, SLAB), lambda i, s: (0, lax.rem(i, 4)))
    once = pl.BlockSpec((rows, SLAB), lambda i, s: (0, jnp.minimum(i, 3)))
    block = pl.BlockSpec((1, 4, 2, 64, 3 * DV), lambda i, s: (jnp.minimum(i, 3), 0, 0, 0, 0))
    later = pl.BlockSpec((rows, SLAB), lambda i, s: (0, jnp.maximum(i - 4, 0)))
    shapes = (
        sds((rows, D), F32),
        sds((rows, D), BF),
        sds((8, D), F32),
        sds((2 * rows, 2 * DV), BF),
        sds((2 * rows, DV), BF),
    )
    return call(
        body,
        (8,),
        [cols, cols, once, once, block],
        (
            later,
            later,
            pl.BlockSpec((8, SLAB), lambda i, s: (0, jnp.maximum(i - 4, 0))),
            whole(shapes[3]),
            whole(shapes[4]),
        ),
        shapes,
        scalars,
        (*x_pair, *g_pair, weight),
        "mlp",
        scratch=[
            pltpu.VMEM((2 * rows, 2 * DV), F32),
            pltpu.VMEM((2 * rows, DV), F32),
            pltpu.VMEM((4, SLAB, 2 * DV), BF),
        ],
        stream=True,
    )


def back_gate(g_pair, weight, gate_pre, retained, query, enter, scalars):
    rows = g_pair[0].shape[0]

    def body(
        s_ref, a_ref, b_ref, w_ref, gate_ref, kept_ref, q_ref, e_ref, dgate_ref, low_ref, state_ref,
        sums
    ):
        step = pl.program_id(0)
        left = jnp.concatenate((a_ref[...], b_ref[...]), axis=0)
        part = jnp.dot(left, load_slab(s_ref, (w_ref,), None), preferred_element_type=F32)

        @pl.when(step == 0)
        def _():
            sums[...] = part

        @pl.when(step > 0)
        def _():
            sums[...] += part

        @pl.when(step == 3)
        def _():
            def chunk(k, carry):
                span = pl.ds(pl.multiple_of(k * 64, 64), 64)
                gate, value, grad = gate_ref[span, :], kept_ref[span, :], sums[span, :]
                value = value - jnp.mean(value, axis=-1, keepdims=True)
                scale = lax.rsqrt(jnp.mean(value * value, axis=-1, keepdims=True) + 1.0 * DK)
                normed = value * scale
                open_part = jax.nn.sigmoid(gate)
                slope = open_part * (1.0 + gate * (1.0 - open_part))
                dgate_ref[span, :] = (grad * normed * slope).astype(BF)
                grad = grad * gate * open_part
                grad = grad - jnp.mean(grad, axis=-1, keepdims=True) - normed * jnp.mean(
                    grad * normed, axis=-1, keepdims=True
                )
                low_ref[span, :] = (grad * scale).astype(BF)
                return carry

            lax.fori_loop(0, 2 * rows // 64, chunk, 0)
            for g in (0, 1):
                span = slice(g * rows, (g + 1) * rows)
                entered = (q_ref[span].astype(F32) * e_ref[span]).astype(BF)
                state_ref[g] = lax.dot_general(
                    entered,
                    low_ref[span],
                    (((0,), (0,)), ((), ())),
                    preferred_element_type=F32,
                ).astype(BF)

    cols = pl.BlockSpec((rows, SLAB), lambda i, s: (0, i))
    operands = (*g_pair, weight, gate_pre, retained, query, enter)
    shapes = (
        sds((2 * rows, DV), BF),
        sds((2 * rows, DV), BF),
        sds((2, DK, DV), BF),
    )
    return call(
        body,
        (4,),
        [cols, cols, pl.BlockSpec((1, 4, 2, 64, DV), lambda i, s: (i, 0, 0, 0, 1))]
        + [whole(o) for o in operands[3:]],
        tuple(whole(s) for s in shapes),
        shapes,
        scalars,
        operands,
        "back_gate",
        scratch=[pltpu.VMEM((2 * rows, DV), F32)],
        stream=True,
    )


def weight_last(into, pair, came, fade, value, key_out, leave, grad_value, grad_key, cosine, sine,
                scalars):
    rows = pair[0].shape[0]

    def body(
        s_ref, a_ref, b_ref, near_ref, mid_ref, far_ref, f_ref, v_ref, k_ref, l_ref, gv_ref, gk_ref,
        cos_ref, sin_ref, into_ref, out_ref, mark_ref, grad_ref
    ):
        @pl.when(pl.program_id(0) == 0)
        def _():
            fade = f_ref[...]
            for g in (0, 1):
                span = slice(g * rows, (g + 1) * rows)
                state = near_ref[g].astype(F32) + fade * (
                    mid_ref[g].astype(F32) + fade * far_ref[g].astype(F32)
                )
                state = state.astype(BF)
                grad_ref[span, :DV] = (
                    gv_ref[g] + jnp.dot(k_ref[g], state, preferred_element_type=F32)
                ).astype(BF)
                grad_key = gk_ref[g] + l_ref[span] * lax.dot_general(
                    v_ref[g], state, (((1,), (1,)), ((), ())), preferred_element_type=F32
                )
                grad_ref[span, DV:] = rotate(grad_key, cos_ref[span], -sin_ref[span]).astype(BF)

        out = lax.dot_general(
            jnp.concatenate((a_ref[...], b_ref[...]), axis=0),
            grad_ref[...],
            (((0,), (0,)), ((), ())),
            preferred_element_type=F32,
        ).astype(BF)
        for c in (0, 1):
            for y in range(4):
                first = (c * 4 + y) * 64
                out_ref[0, y, jnp.bitwise_xor(c, s_ref[0])] = out[first : first + 64]
        mark_ref[...] = jnp.zeros_like(mark_ref)

    cols = pl.BlockSpec((rows, SLAB), lambda i, s: (0, i))
    operands = (*pair, *came, fade, value, key_out, leave, grad_value, grad_key, cosine, sine)
    shapes = (
        sds(into.shape, BF),
        sds((8, 128), F32),
        sds((2 * rows, DV + DK), BF),
    )
    return call(
        body,
        (4,),
        [cols, cols]
        + [whole(o) for o in operands[2:]]
        + [pl.BlockSpec(memory_space=pl.ANY)],
        (
            pl.BlockSpec((1, 4, 2, 64, DV + DK), lambda i, s: (i, 0, 0, 0, 0)),
            whole(shapes[1]),
            whole(shapes[2]),
        ),
        shapes,
        scalars,
        (*operands, into),
        "weight_last",
        stream=True,
        aliases={1 + len(operands): 0},
    )


def mm_weight_into(into, pairs, start, total, scalars, name, deps=()):
    widths = [grad.shape[1] for _, grad in pairs]
    rows = pairs[0][0][0].shape[0]
    span = sum(widths)

    def body(s_ref, *refs):
        out_ref, mark_ref = refs[-2:]
        at = 0
        for k, width in enumerate(widths):
            a_ref, b_ref, g_ref = refs[3 * k : 3 * k + 3]
            out = lax.dot_general(
                jnp.concatenate((a_ref[...], b_ref[...]), axis=0),
                g_ref[...],
                (((0,), (0,)), ((), ())),
                preferred_element_type=F32,
            ).astype(BF)
            for c in (0, 1):
                for y in range(4):
                    first = (c * 4 + y) * 64
                    out_ref[0, y, jnp.bitwise_xor(c, s_ref[0]), :, at : at + width] = out[
                        first : first + 64
                    ]
            at += width
        mark_ref[...] = jnp.zeros_like(mark_ref)

    cols = pl.BlockSpec((rows, SLAB), lambda i, s: (0, i))
    specs, operands = [], []
    for (a, b), grad in pairs:
        specs += [cols, cols, whole(grad)]
        operands += [a, b, grad]
    aliases = None
    if into is not None:
        aliases = {1 + len(operands): 0}
        specs.append(pl.BlockSpec(memory_space=pl.ANY))
        operands.append(into)
    return call(
        body,
        (4,),
        specs,
        (
            pl.BlockSpec((1, 4, 2, 64, span), lambda i, s: (i, 0, 0, 0, start // span)),
            pl.BlockSpec((8, 128), lambda i, s: (0, 0)),
        ),
        (sds((4, 4, 2, 64, total), BF), sds((8, 128), F32)),
        scalars,
        tuple(operands),
        name,
        deps=deps,
        stream=True,
        aliases=aliases,
    )


def split_heads(weights, scalars, name, deps=()):
    widths = [w.shape[1] // 2 for w in weights]

    def body(s_ref, *refs):
        mine_ref, theirs_ref = refs[-2:]
        core = s_ref[0]
        for out_ref, head in ((mine_ref, core), (theirs_ref, 1 - core)):
            at = 0
            for ref, width in zip(refs, widths):
                out_ref[:, at : at + width] = ref[:, pl.ds(pl.multiple_of(head * width, width), width)]
                at += width

    total = sum(widths)
    spec = pl.BlockSpec((64, total), lambda i, s: (0, 0))
    return call(
        body,
        (1,),
        [whole(w) for w in weights],
        (spec, spec),
        (sds((64, total), BF),) * 2,
        scalars,
        tuple(weights),
        name,
        deps=deps,
        stream=True,
    )


def join_heads(mine, theirs, widths, scalars, name):
    def body(s_ref, mine_ref, theirs_ref, *outs):
        core = s_ref[0]
        for in_ref, head in ((mine_ref, core), (theirs_ref, 1 - core)):
            at = 0
            for ref, width in zip(outs, widths):
                span = pl.ds(pl.multiple_of(head * width, width), width)
                ref[:, span] = in_ref[:, at : at + width].astype(F32)
                at += width

    shapes = tuple(sds((64, 2 * w), F32) for w in widths)
    return call(
        body,
        (1,),
        [whole(mine), whole(theirs)],
        tuple(whole(s) for s in shapes),
        shapes,
        scalars,
        (mine, theirs),
        name,
    )


def scale_of(values):
    return lax.rsqrt(jnp.mean(values * values, axis=-1, keepdims=True) + 1e-06)


def turned_spec(rows):
    return pl.BlockSpec((rows, D), lambda i, s: (lax.rem(i + s[1], 4), 0))


def plain_spec(rows):
    return pl.BlockSpec((rows, D), lambda i, s: (i, 0))


def enter_rows(tokens, gain, scalars, deps=()):
    rows = tokens.shape[0]
    block = rows // 4

    def body(s_ref, t_ref, g_ref, n_out):
        values = t_ref[...]
        n_out[...] = (values * scale_of(values) * g_ref[...]).astype(BF)

    return call(
        body,
        (4,),
        [turned_spec(block), whole(gain)],
        plain_spec(block),
        sds((rows, D), BF),
        scalars,
        (tokens, gain),
        "enter_rows",
        deps=deps,
    )


def low_rows(cotangent, scalars, deps=()):
    rows = cotangent.shape[0]
    block = rows // 4

    def body(s_ref, c_ref, l_out):
        l_out[...] = c_ref[...].astype(BF)

    return call(
        body,
        (4,),
        [turned_spec(block)],
        plain_spec(block),
        sds((rows, D), BF),
        scalars,
        (cotangent,),
        "low_rows",
        deps=deps,
    )


def each_part(refs, work):
    step = pl.program_id(0)
    for k, ref in enumerate(refs):

        @pl.when(step == k)
        def _(ref=ref):
            work(ref[...].astype(F32))


def second_norm(tokens, parts, gain, scalars, deps=()):
    rows = tokens.shape[0]
    block = rows // 4

    def body(s_ref, t_ref, g_ref, *refs):
        h_out, n_out = refs[4:]

        def work(part):
            values = t_ref[...] + part
            h_out[...] = values
            n_out[...] = (values * scale_of(values) * g_ref[...]).astype(BF)

        each_part(refs[:4], work)

    plain = plain_spec(block)
    return call(
        body,
        (4,),
        [turned_spec(block), whole(gain)] + [whole(p) for p in parts],
        (plain, plain),
        (sds((rows, D), F32), sds((rows, D), BF)),
        scalars,
        (tokens, gain, *parts),
        "second_norm",
        deps=deps,
    )


def third_blocks(own, came, down_own, down_came, scalars, deps=()):
    rows = own.shape[0]
    block = rows // 4

    def body(s_ref, own_ref, came_ref, d_ref, e_ref, *refs):
        total = own_ref[...] + came_ref[...].astype(F32)
        down = d_ref[...] + e_ref[...].astype(F32)
        step = pl.program_id(0)
        for k in range(4):

            @pl.when(step == k)
            def _(k=k):
                refs[k][:block] = total.astype(BF)
                refs[k][block:] = down.astype(BF)

    plain = plain_spec(block)
    shapes = (sds((2 * block, D), BF),) * 4
    return call(
        body,
        (4,),
        [plain] * 4,
        tuple(whole(s) for s in shapes),
        shapes,
        scalars,
        (own, came, down_own, down_came),
        "third_blocks",
        deps=deps,
        stream=True,
    )


def leave_rows(hidden, tokens, grad_state, parts, gain, scalars, deps=()):
    rows = hidden.shape[0]
    block = rows // 4

    def body(s_ref, h_ref, t_ref, u_ref, g_ref, *refs):
        def work(part):
            refs[4][...] = h_ref[...] + part[block : 2 * block]
            refs[5][...] = u_ref[...] + norm_grad(t_ref[...], part[:block], g_ref[...])

        each_part(refs[:4], work)

    plain, turn = plain_spec(block), turned_spec(block)
    return call(
        body,
        (4,),
        [plain, turn, plain, whole(gain)] + [whole(p) for p in parts],
        (turn, turn),
        (sds((rows, D), F32),) * 2,
        scalars,
        (hidden, tokens, grad_state, gain, *parts),
        "leave_rows",
        deps=deps,
        stream=True,
    )


def norm_grad(values, grad, gain):
    factor = scale_of(values)
    unit = values * factor
    scaled = grad * gain
    return factor * (scaled - unit * jnp.mean(scaled * unit, axis=-1, keepdims=True))


def norm_back(values, upstream, parts, gain, scalars, name, deps=()):
    rows = values.shape[0]
    block = rows // 4

    def body(s_ref, v_ref, u_ref, g_ref, *refs):
        def work(part):
            out = u_ref[...] + norm_grad(v_ref[...], part, g_ref[...])
            refs[4][...] = out
            refs[5][...] = out.astype(BF)

        each_part(refs[:4], work)

    plain = plain_spec(block)
    return call(
        body,
        (4,),
        [plain, turned_spec(block), whole(gain)] + [whole(p) for p in parts],
        (plain, plain),
        (sds((rows, D), F32), sds((rows, D), BF)),
        scalars,
        (values, upstream, gain, *parts),
        name,
        deps=deps,
        stream=True,
    )


def tp_first(blocks):
    got = [shift(blocks[o], "tp", o) for o in (1, 3, 2)]
    near, far, mid = [part.astype(F32) for part in got]
    return (blocks[0].astype(F32) + mid) + (near + far), got


def tp_second(mine):
    near, far, mid = [shift(mine, "tp", -o) for o in (1, 3, 2)]
    return mine, near, mid, far


def tp_total(blocks):
    return tp_second(tp_first(blocks)[0].astype(BF))


def chip_blocks(own, came):
    block = own.shape[0] // 4
    return [
        (own[o * block : (o + 1) * block] + came[o * block : (o + 1) * block].astype(F32)).astype(BF)
        for o in range(4)
    ]


def gate_norm(gate_pre, retained):
    centred = retained - jnp.mean(retained, axis=-1, keepdims=True)
    normed = centred * lax.rsqrt(jnp.mean(centred * centred, axis=-1, keepdims=True) + 1.0 * DK)
    return gate_pre * jax.nn.sigmoid(gate_pre) * normed


def gelu_gate(hidden, linear):
    return jax.nn.gelu(hidden, approximate=True) * linear


def rotate(values, cosine, sine):
    half = DK // 2
    first = values[:, :half]
    second = values[:, half:]
    return jnp.concatenate((first * cosine - second * sine, first * sine + second * cosine), axis=1)


def ein(spec, left, right):
    return jnp.einsum(spec, left, right, preferred_element_type=F32)


def per_device(
    tokens,
    cotangent,
    gain_first,
    gain_second,
    w_query,
    w_key,
    w_value,
    w_gate,
    w_output,
    w_hidden,
    w_linear,
    w_down,
    decay_scale,
    first_length,
):
    rows = tokens.shape[0]
    core = lax.axis_index("core")
    place = lax.axis_index("ctx")
    plane = lax.axis_index("tp")
    scalars = jnp.stack((core, plane, lax.axis_index("x"), place)).astype(jnp.int32)

    w_output = w_output.T
    w_down = w_down.T
    mine, theirs = split_heads((w_value, w_key, w_gate, w_output, w_query), scalars, "split_attn")
    came = swap(theirs)
    block, gathered = stack_attn(mine, came, scalars)
    lengths = jnp.concatenate((first_length, swap(first_length)))
    blocks = spread_near(block)
    w_kv = stack_blocks(blocks, 0, 768, scalars, "stack_kv", deps=(lengths,))
    normed_first = enter_rows(tokens, gain_first.reshape(1, D), scalars, deps=(w_kv,))
    (gathered,) = tie((gathered,), blocks[1:])
    w_goq = lax.all_gather(gathered, XY, axis=0, tiled=True).reshape(4, 4, 2, 64, -1)
    mine, theirs = split_heads(
        (w_hidden, w_linear, w_down), scalars, "split_mlp", deps=(normed_first,)
    )
    came_mlp = swap(theirs)
    gain_first = gain_first.reshape(1, D)
    gain_second = gain_second.reshape(1, D)
    x_first = (normed_first, swap(normed_first))
    cot_low = low_rows(cotangent, scalars, deps=(x_first[1],))
    g_out = (cot_low, swap(cot_low))
    w_kv = spread_far(w_kv)

    rate = lax.dynamic_index_in_dim(decay_scale, core, 0, False) / 1024.0
    local = (jnp.arange(rows, dtype=jnp.int32) + plane * (rows // 4)) % rows
    index = place * rows + local
    document = (index[None, :] >= lengths[:, None]).astype(jnp.int32)
    carried = (document == 0).astype(F32)
    steps = local.astype(F32)
    offsets = local[:, None] - local[None, :]
    linked = (offsets >= 0)[None] & (document[:, :, None] == document[:, None, :])
    mask = jnp.where(
        linked, jnp.exp(-rate * jnp.maximum(offsets, 0).astype(F32))[None], 0.0
    )
    enter = (carried * jnp.exp(-rate * (steps + 1.0))[None])[:, :, None]
    leave = jnp.exp(-rate * (rows - 1.0 - steps))[None, :, None]
    fade = jnp.exp(-rate * rows)
    half = DK // 2
    frequency = 10000.0 ** (-(jnp.arange(half).astype(F32) / half))
    angles = index.astype(F32)[:, None] * frequency[None, :]
    cosine = jnp.tile(jnp.cos(angles), (2, 1))
    sine = jnp.tile(jnp.sin(angles), (2, 1))

    def spread_state(low, way):
        return [shift_open(low, "ctx", way * o) for o in (1, 2, 3)]

    enter_rows_in = enter.reshape(2 * rows, 1)
    leave_rows_out = jnp.tile(leave.reshape(rows, 1), (2, 1))
    fade_in = fade.reshape(1, 1)
    projected = mm_in(
        *x_first,
        [(w_kv, 0, 768)],
        scalars,
        "project_kv",
        deps=(came_mlp,),
    )
    key = rotate(projected[:, DV:], cosine, sine).astype(BF).reshape(2, rows, DK)
    value = projected[:, :DV].astype(BF).reshape(2, rows, DV)
    key_out = (key.astype(F32) * leave).astype(BF)
    state_out = ein("gjd,gje->gde", key_out, value).astype(BF)
    came = spread_state(state_out, 1)
    w_mlp = lax.all_gather(
        stack_blocks((mine, came_mlp), 0, 1536, scalars, "stack_mlp", deps=(state_out,)),
        XY,
        axis=0,
        tiled=True,
    ).reshape(4, 4, 2, 64, -1)
    own, other, query, state_in, weighted, gate_pre, retained, mixed = retain(
        x_first,
        w_goq,
        key,
        value,
        came,
        fade_in,
        mask,
        enter_rows_in,
        cosine,
        sine,
        scalars,
    )
    query = query.reshape(2, rows, DK)
    parts = tp_total(chip_blocks(own, swap(other)))
    hidden_state, normed_second = second_norm(tokens, parts, gain_second, scalars)
    x_second = (normed_second, swap(normed_second))
    own, other, gain_second_part, grad_pair, activated = mlp(x_second, g_out, w_mlp, scalars)
    grads, mark = mm_weight_into(
        None, ((x_second, grad_pair),), 1024, 3584, scalars, "weight_mlp"
    )
    mine, _ = tp_first(chip_blocks(own, swap(other)))
    (mine,) = tie((mine.astype(BF),), (mark,))
    parts = tp_second(mine)
    down = mm_back([(activated, w_mlp, 2 * DV)], scalars, "project_down", deps=(mine,))
    grad_state, grad_state_low = norm_back(
        hidden_state,
        cotangent,
        parts,
        gain_second,
        scalars,
        "second_back",
        deps=(down[1],),
    )
    g_state = (grad_state_low, swap(grad_state_low))
    grad_gate, grad_low, back_out = back_gate(
        g_state, w_goq, gate_pre, retained, query.reshape(2 * rows, DK), enter_rows_in, scalars
    )
    grad_low = grad_low.reshape(2, rows, DV)
    came = spread_state(back_out, -1)
    grad_scores = (ein("gie,gje->gij", grad_low, value) * mask).astype(BF)
    grad_query = ein("gij,gjd->gid", grad_scores, key) + enter * ein("gie,gde->gid", grad_low, state_in)
    grad_key = ein("gij,gid->gjd", grad_scores, query)
    grad_value = ein("gij,gie->gje", weighted, grad_low)
    grad_query = rotate(grad_query.reshape(2 * rows, DK), cosine, -sine).astype(BF)
    grads, mark = mm_weight_into(
        grads,
        ((g_state, mixed), (x_first, grad_gate)),
        2048,
        3584,
        scalars,
        "weight_og",
        deps=(back_out,),
    )
    grads, mark = mm_weight_into(
        grads, ((g_out, activated),), 3072, 3584, scalars, "weight_down"
    )
    grads, mark = mm_weight_into(
        grads, ((x_first, grad_query),), 768, 3584, scalars, "weight_query"
    )
    came[0] = tie((came[0],), (mark, grad_key, grad_value))[0]
    grads, mark, grad_vk = weight_last(
        grads,
        x_first,
        came,
        fade_in,
        value,
        key_out,
        leave_rows_out,
        grad_value,
        grad_key,
        cosine,
        sine,
        scalars,
    )
    block = lax.psum_scatter(grads.reshape(2048, -1), XY, scatter_dimension=0, tiled=True)
    own, other, gain_first_part = mm_back(
        [(grad_vk, w_kv, 0), (grad_gate, w_goq, 0), (grad_query, w_goq, 1024)],
        scalars,
        "back_attn",
        normed=x_first,
        deps=(mark,),
    )
    down = (down[0], swap(tie((down[1],), (mark,))[0]))
    blocks = third_blocks(own, swap(other), *down, scalars)
    mine, _ = tp_first(blocks)
    gains = jnp.concatenate((gain_first_part[:1], gain_second_part[:1]))
    for axis, swapped in (
        ("core", (1, 0)),
        ("ctx", (1, 0, 3, 2)),
        ("ctx", (3, 2, 1, 0)),
        ("x", (1, 0, 3, 2)),
        ("x", (3, 2, 1, 0)),
    ):
        gains = gains + lax.ppermute(gains, axis, list(enumerate(swapped)))
    mine = jnp.concatenate((mine, gains, jnp.zeros((14, D), F32))).astype(BF)
    parts = tp_second(mine)
    gains = [part[128:130].astype(F32) for part in parts]
    gains = (gains[0] + gains[2]) + (gains[1] + gains[3])
    spot = (lax.axis_index("x") * 2 + core) * 4 + place
    gain_first_grad, gain_second_grad = [
        lax.dynamic_slice_in_dim(gains[k] / gain[0], spot * 64, 64, 0)
        for k, gain in ((0, gain_first), (1, gain_second))
    ]
    layer_out, input_grad = leave_rows(
        hidden_state, tokens, grad_state, parts, gain_first, scalars
    )
    block = tie((block,), (gain_first_grad, gain_second_grad, input_grad))[0].reshape(2, 64, -1)
    d_value, d_key, d_query, d_hidden, d_linear, d_output, d_gate, d_down = join_heads(
        block[0], swap(block[1]), (DV, DK, DK) + (DV,) * 5, scalars, "join_heads"
    )
    return (
        layer_out,
        input_grad,
        gain_first_grad,
        gain_second_grad,
        d_query,
        d_key,
        d_value,
        d_gate,
        d_output.T,
        d_hidden,
        d_linear,
        d_down.T,
    )


def solution(mesh):
    fine = Mesh(np.asarray(mesh.devices).reshape(4, 2, 4, 4), ("x", "core", "ctx", "tp"))
    split = ("x", "core", "ctx")
    row = P(split, None)
    win = P(split, "tp")
    wout = P("tp", split)
    in_specs = (row, row, P(), P(), win, win, win, win, wout, win, win, wout, P("tp"), P(("x", "core")))
    out_specs = (row, row, P(split), P(split), win, win, win, win, wout, win, win, wout)
    return jax.shard_map(
        per_device, mesh=fine, in_specs=in_specs, out_specs=out_specs, check_vma=False
    )
```

```python
import math

import jax
import jax.numpy as jnp
import numpy as np
from jax import lax
from jax.experimental import pallas as pl
from jax.experimental.pallas import tpu as pltpu
from jax.sharding import Mesh, PartitionSpec as P

D = 2048
DK = 256
DV = 512
SLAB = 512
BF = jnp.bfloat16
F32 = jnp.float32
XY = ("x", "ctx")
MIB = 1 << 20


def shift(value, axis, offset):
    n = lax.axis_size(axis)
    return lax.ppermute(value, axis, [(i, (i + offset) % n) for i in range(n)])


def shift_open(value, axis, offset):
    n = lax.axis_size(axis)
    return lax.ppermute(
        value, axis, [(i, i + offset) for i in range(n) if 0 <= i + offset < n]
    )


def swap(value):
    return lax.ppermute(value, "core", [(0, 1), (1, 0)])


def after(value, *earlier):
    return lax.optimization_barrier((value, *earlier))[0]


def call(
    body,
    grid,
    ins,
    outs,
    shapes,
    scalars,
    operands,
    name,
    scratch=(),
    deps=(),
    stream=False,
    aliases=None,
):
    count = len(operands)

    def kernel(s_ref, *refs):
        body(s_ref, *refs[:count], *refs[count + len(deps) :])

    ins = [*ins, *[pl.BlockSpec(memory_space=pl.ANY)] * len(deps)]
    return pl.pallas_call(
        kernel,
        out_shape=shapes,
        grid_spec=pltpu.PrefetchScalarGridSpec(
            num_scalar_prefetch=1, grid=grid, in_specs=ins, out_specs=outs, scratch_shapes=scratch
        ),
        compiler_params=pltpu.CompilerParams(
            vmem_limit_bytes=(60 if stream else 32) * MIB, dimension_semantics=("arbitrary",) * len(grid)
        ),
        cost_estimate=pl.CostEstimate(flops=1, bytes_accessed=1, transcendentals=0),
        input_output_aliases=aliases or {},
        name=name,
    )(scalars, *operands, *deps)


def tie(values, deps):
    count = len(values)
    anywhere = pl.BlockSpec(memory_space=pl.ANY)
    return pl.pallas_call(
        lambda *refs: None,
        out_shape=tuple(sds(v.shape, v.dtype) for v in values),
        in_specs=[anywhere] * (count + len(deps)),
        out_specs=(anywhere,) * count,
        input_output_aliases={i: i for i in range(count)},
        name="tie",
    )(*values, *deps)


def whole(array):
    return pl.BlockSpec(array.shape, lambda *_: (0,) * array.ndim)


def sds(shape, dtype):
    return jax.ShapeDtypeStruct(shape, dtype)


def weight_operands(weight, start, width):
    if not isinstance(weight, tuple):
        spec = pl.BlockSpec((1, 4, 2, 64, width), lambda i, s: (i, 0, 0, 0, start // width))
        return [weight], [spec]
    piece = math.gcd(start, width) if start else width
    operands, specs = [], []
    for at in range(start, start + width, piece):
        for stack in weight:
            operands.append(stack)
            specs.append(pl.BlockSpec((4, 2, 64, piece), lambda i, s, at=at: (0, 0, 0, at // piece)))
    return operands, specs


def load_slab(s_ref, refs, held):
    core = s_ref[0]
    if len(refs) == 1:
        return jnp.concatenate(
            [refs[0][0, y, jnp.bitwise_xor(c, core)] for c in (0, 1) for y in range(4)], axis=0
        )
    x_far = lax.rem(s_ref[2] + 4 - pl.program_id(0), 4)
    at = 0
    for first in range(0, len(refs), 4):
        stacks = refs[first : first + 4]
        width = stacks[0].shape[-1]
        for j in range(4):

            @pl.when((core == 0) & (x_far == j))
            def _(j=j, at=at, width=width, stacks=stacks):
                for i in range(4):
                    y = lax.rem(s_ref[3] + 4 - i, 4)
                    for c in (0, 1):
                        held[c * 4 + y, :, at : at + width] = stacks[j][i, c]

        @pl.when(core == 1)
        def _(at=at, width=width, stacks=stacks):
            for j in range(4):
                y = lax.rem(s_ref[3] + 4 - j, 4)
                for c in (0, 1):
                    held[c * 4 + y, :, at : at + width] = stacks[j][x_far, 1 - c]

        at += width
    return held[...].reshape(SLAB, at)


def hop(value, first, offset):
    pairs = []
    for x in range(4):
        for core in (0, 1):
            for y in range(4):
                to = ((x + offset) % 4, y) if (core == 0) == first else (x, (y + offset) % 4)
                pairs.append(((x * 2 + core) * 4 + y, (to[0] * 2 + core) * 4 + to[1]))
    return lax.ppermute(value, ("x", "core", "ctx"), pairs)


def spread_near(block):
    near, far, mid = [hop(block, False, o) for o in (1, 3, 2)]
    return block, near, mid, far


def stack_blocks(blocks, start, width, scalars, name, deps=()):
    at = start // width if start % width == 0 else None
    span = width if at is not None else blocks[0].shape[1]
    first = 0 if at is not None else start
    height = blocks[0].shape[0]

    def body(s_ref, *refs):
        for k, ref in enumerate(refs[:-1]):
            refs[-1][k * height : (k + 1) * height, :] = ref[:, first : first + width]

    total = sds((height * len(blocks), width), BF)
    return call(
        body,
        (1,),
        [pl.BlockSpec((height, span), lambda i, s: (0, at or 0))] * len(blocks),
        whole(total),
        total,
        scalars,
        tuple(blocks),
        name,
        deps=deps,
    )


def stack_attn(mine, came, scalars):
    height, total = mine.shape

    def body(s_ref, mine_ref, came_ref, first_ref, other_ref):
        for k, ref in enumerate((mine_ref, came_ref)):
            span = slice(k * height, (k + 1) * height)
            first_ref[span, :] = ref[:, :768]
            other_ref[span, :] = ref[:, 768:]

    shapes = (sds((2 * height, 768), BF), sds((2 * height, total - 768), BF))
    return call(
        body,
        (1,),
        [whole(mine), whole(came)],
        tuple(whole(s) for s in shapes),
        shapes,
        scalars,
        (mine, came),
        "stack_attn",
        stream=True,
    )


def spread_far(stack, gate=False):
    stack = stack.reshape(4, 2, 64, -1)
    near, far = hop(stack, True, 1), hop(stack, True, -1)
    mid = hop(tie((stack,), (near, far))[0] if gate else stack, True, 2)
    return stack, near, mid, far


def mm_in(left, right, columns, scalars, name, deps=(), stream=False):
    operands, specs, counts = [], [], []
    for weight, start, width in columns:
        ops, sp = weight_operands(weight, start, width)
        operands += ops
        specs += sp
        counts.append(len(ops))
    total = sum(width for _, _, width in columns)

    def body(s_ref, a_ref, b_ref, *refs):
        out_ref = refs[len(operands)]
        step = pl.program_id(0)
        rows = jnp.concatenate((a_ref[...], b_ref[...]), axis=0)
        at, first = 0, 0
        for k, count in enumerate(counts):
            width = columns[k][2]
            slab = load_slab(s_ref, refs[first : first + count], refs[len(operands) + 1 + k])
            part = jnp.dot(rows, slab, preferred_element_type=F32)
            span = slice(at, at + width)

            @pl.when(step == 0)
            def _(part=part, span=span):
                out_ref[:, span] = part

            @pl.when(step > 0)
            def _(part=part, span=span):
                out_ref[:, span] += part

            at += width
            first += count

    rows = left.shape[0]
    cols = pl.BlockSpec((rows, SLAB), lambda i, s: (0, i))
    return call(
        body,
        (4,),
        [cols, cols, *specs],
        pl.BlockSpec((2 * rows, total), lambda i, s: (0, 0)),
        sds((2 * rows, total), F32),
        scalars,
        (left, right, *operands),
        name,
        scratch=[pltpu.VMEM((8, 64, width), BF) for _, _, width in columns],
        deps=deps,
        stream=stream,
    )


def mm_back(terms, scalars, name, normed=None, deps=()):
    rows = terms[0][0].shape[0]
    half = rows // 2
    operands, specs, counts, scratch = [], [], [], []
    for grad, weight, start in terms:
        ops, sp = weight_operands(weight, start, grad.shape[1])
        operands += [grad, *ops]
        specs += [whole(grad), *sp]
        counts.append(len(ops))
        scratch.append(pltpu.VMEM((8, 64, grad.shape[1]), BF))
    held = len(operands)
    cols = pl.BlockSpec((half, SLAB), lambda i, s: (0, i))
    outs = [cols, cols]
    shapes = [sds((half, D), F32), sds((half, D), BF)]
    if normed is not None:
        operands += normed
        specs += [cols, cols]
        outs.append(pl.BlockSpec((8, SLAB), lambda i, s: (0, i)))
        shapes.append(sds((8, D), F32))
    total = len(operands)

    def body(s_ref, *refs):
        at, out = 0, 0.0
        for k, count in enumerate(counts):
            slab = load_slab(s_ref, refs[at + 1 : at + 1 + count], refs[total + len(outs) + k])
            out += lax.dot_general(
                refs[at][...], slab, (((1,), (1,)), ((), ())), preferred_element_type=F32
            )
            at += count + 1
        refs[total][...] = out[:half]
        refs[total + 1][...] = out[half:].astype(BF)
        if normed is not None:
            part = out[:half] * refs[held][...].astype(F32) + out[half:] * refs[held + 1][
                ...
            ].astype(F32)
            part = jnp.sum(part, axis=0, keepdims=True)
            refs[total + 2][...] = jnp.broadcast_to(part, (8, SLAB))

    return call(
        body,
        (4,),
        specs,
        tuple(outs),
        tuple(shapes),
        scalars,
        tuple(operands),
        name,
        scratch=scratch,
        deps=deps,
    )


def split_out(out, own_ref, other_ref):
    half = out.shape[0] // 2
    own_ref[...] = out[:half]
    other_ref[...] = out[half:].astype(BF)


def retain(x_pair, weight, key, value, came, rate, cosine, sine, scalars):
    rows = x_pair[0].shape[0]

    def body(
        s_ref, a_ref, b_ref, w_ref, k_ref, v_ref, near_ref, mid_ref, far_ref, r_ref, cos_ref,
        sin_ref, own_ref, other_ref, query_ref, state_ref, weighted_ref, gate_ref, retained_ref,
        mixed_ref, m_ref, e_ref, sums, turned
    ):
        step = pl.program_id(0)

        @pl.when(step == 0)
        def _():
            rate = r_ref[...]

            def place_of(shape, dim):
                index = lax.broadcasted_iota(jnp.int32, shape, dim)
                return lax.rem(index + s_ref[1] * (rows // 4), rows)

            left, right = place_of((rows, rows), 0), place_of((rows, rows), 1)
            column = place_of((rows, 1), 0)
            decay = jnp.exp(-rate * jnp.maximum(left - right, 0).astype(F32))
            for g in (0, 1):
                length = s_ref[4 + g] - s_ref[3] * rows
                linked = (left >= right) & ((left >= length) == (right >= length))
                m_ref[g] = jnp.where(linked, decay, 0.0)
                e_ref[g * rows : (g + 1) * rows] = jnp.where(
                    column >= length, 0.0, jnp.exp(-rate * (column.astype(F32) + 1.0))
                )

        @pl.when(step < 4)
        def _():
            slab = load_slab(s_ref, (w_ref,), None)
            turned[step] = slab[:, DV : 2 * DV]
            left = jnp.concatenate((a_ref[...], b_ref[...]), axis=0)
            gate = jnp.dot(left, slab[:, :DV], preferred_element_type=F32)
            query = jnp.dot(left, slab[:, 2 * DV :], preferred_element_type=F32)

            @pl.when(step == 0)
            def _():
                gate_ref[...] = gate
                sums[...] = query

            @pl.when(step > 0)
            def _():
                gate_ref[...] += gate
                sums[...] += query

        @pl.when(step == 3)
        def _():
            fade = jnp.exp(-r_ref[...] * rows)
            for g in (0, 1):
                span = slice(g * rows, (g + 1) * rows)
                state = near_ref[g].astype(F32) + fade * (
                    mid_ref[g].astype(F32) + fade * far_ref[g].astype(F32)
                )
                state_ref[g] = state.astype(BF)
                query = rotate(sums[span], cos_ref[...], sin_ref[...]).astype(BF)
                query_ref[span] = query
                scores = lax.dot_general(
                    query, k_ref[g], (((1,), (1,)), ((), ())), preferred_element_type=F32
                )
                weighted = (scores * m_ref[g]).astype(BF)
                weighted_ref[g] = weighted
                retained = jnp.dot(weighted, v_ref[g], preferred_element_type=F32)
                retained += e_ref[span] * jnp.dot(
                    query, state_ref[g], preferred_element_type=F32
                )
                retained_ref[span] = retained
                mixed_ref[span] = gate_norm(gate_ref[span], retained).astype(BF)

        @pl.when(step >= 4)
        def _():
            out = lax.dot_general(
                mixed_ref[...],
                turned[step - 4],
                (((1,), (1,)), ((), ())),
                preferred_element_type=F32,
            )
            split_out(out, own_ref, other_ref)

    cols = pl.BlockSpec((rows, SLAB), lambda i, s: (0, jnp.minimum(i, 3)))
    later = pl.BlockSpec((rows, SLAB), lambda i, s: (0, jnp.maximum(i - 4, 0)))
    operands = (*x_pair, weight, key, value, *came, rate, cosine, sine)
    shapes = (
        sds((rows, D), F32),
        sds((rows, D), BF),
        sds((2 * rows, DK), BF),
        sds((2, DK, DV), BF),
        sds((2, rows, rows), BF),
        sds((2 * rows, DV), F32),
        sds((2 * rows, DV), F32),
        sds((2 * rows, DV), BF),
        sds((2, rows, rows), F32),
        sds((2 * rows, 1), F32),
    )
    block = pl.BlockSpec((1, 4, 2, 64, 1280), lambda i, s: (jnp.minimum(i, 3), 0, 0, 0, 0))
    return call(
        body,
        (8,),
        [cols, cols, block] + [whole(o) for o in operands[3:]],
        (later, later) + tuple(whole(s) for s in shapes[2:]),
        shapes,
        scalars,
        operands,
        "retain",
        scratch=[pltpu.VMEM((2 * rows, DK), F32), pltpu.VMEM((4, SLAB, DV), BF)],
        stream=True,
    )


def mlp(x_pair, g_pair, weight, scalars):
    rows = x_pair[0].shape[0]

    def body(
        s_ref, a_ref, b_ref, c_ref, d_ref, w_ref, own_ref, other_ref, gain_ref, pair_ref, act_ref,
        both, back, kept
    ):
        step = pl.program_id(0)

        @pl.when(step < 4)
        def _():
            slab = load_slab(s_ref, (w_ref,), None)
            kept[step] = slab[:, : 2 * DV]
            left = jnp.concatenate((a_ref[...], b_ref[...]), axis=0)
            grad = jnp.concatenate((c_ref[...], d_ref[...]), axis=0)
            up = jnp.dot(left, slab[:, : 2 * DV], preferred_element_type=F32)
            down = jnp.dot(grad, slab[:, 2 * DV :], preferred_element_type=F32)

            @pl.when(step == 0)
            def _():
                both[...] = up
                back[...] = down

            @pl.when(step > 0)
            def _():
                both[...] += up
                back[...] += down

        @pl.when(step == 3)
        def _():
            def chunk(k, carry):
                span = pl.ds(pl.multiple_of(k * 64, 64), 64)
                hidden, linear, grad = both[span, :DV], both[span, DV:], back[span, :]
                cube = 0.044715 * hidden * hidden
                bent = jnp.tanh(0.7978845608 * hidden * (1.0 + cube))
                half = 0.5 * (1.0 + bent)
                gelu = hidden * half
                slope = half + 0.5 * hidden * (1.0 - bent * bent) * (
                    0.7978845608 * (1.0 + 3.0 * cube)
                )
                act_ref[span, :] = (gelu * linear).astype(BF)
                pair_ref[span, :DV] = (grad * linear * slope).astype(BF)
                pair_ref[span, DV:] = (grad * gelu).astype(BF)
                return carry

            lax.fori_loop(0, 2 * rows // 64, chunk, 0)

        @pl.when(step >= 4)
        def _():
            out = lax.dot_general(
                pair_ref[...], kept[step - 4], (((1,), (1,)), ((), ())), preferred_element_type=F32
            )
            split_out(out, own_ref, other_ref)
            part = out[:rows] * a_ref[...].astype(F32) + out[rows:] * b_ref[...].astype(F32)
            gain_ref[...] = jnp.broadcast_to(jnp.sum(part, axis=0, keepdims=True), (8, SLAB))

    cols = pl.BlockSpec((rows, SLAB), lambda i, s: (0, lax.rem(i, 4)))
    once = pl.BlockSpec((rows, SLAB), lambda i, s: (0, jnp.minimum(i, 3)))
    block = pl.BlockSpec((1, 4, 2, 64, 3 * DV), lambda i, s: (jnp.minimum(i, 3), 0, 0, 0, 0))
    later = pl.BlockSpec((rows, SLAB), lambda i, s: (0, jnp.maximum(i - 4, 0)))
    shapes = (
        sds((rows, D), F32),
        sds((rows, D), BF),
        sds((8, D), F32),
        sds((2 * rows, 2 * DV), BF),
        sds((2 * rows, DV), BF),
    )
    return call(
        body,
        (8,),
        [cols, cols, once, once, block],
        (
            later,
            later,
            pl.BlockSpec((8, SLAB), lambda i, s: (0, jnp.maximum(i - 4, 0))),
            whole(shapes[3]),
            whole(shapes[4]),
        ),
        shapes,
        scalars,
        (*x_pair, *g_pair, weight),
        "mlp",
        scratch=[
            pltpu.VMEM((2 * rows, 2 * DV), F32),
            pltpu.VMEM((2 * rows, DV), F32),
            pltpu.VMEM((4, SLAB, 2 * DV), BF),
        ],
        stream=True,
    )


def back_gate(g_pair, weight, gate_pre, retained, query, enter, scalars):
    rows = g_pair[0].shape[0]

    def body(
        s_ref, a_ref, b_ref, w_ref, gate_ref, kept_ref, q_ref, e_ref, dgate_ref, low_ref, state_ref,
        sums
    ):
        step = pl.program_id(0)
        left = jnp.concatenate((a_ref[...], b_ref[...]), axis=0)
        part = jnp.dot(left, load_slab(s_ref, (w_ref,), None), preferred_element_type=F32)

        @pl.when(step == 0)
        def _():
            sums[...] = part

        @pl.when(step > 0)
        def _():
            sums[...] += part

        @pl.when(step == 3)
        def _():
            def chunk(k, carry):
                span = pl.ds(pl.multiple_of(k * 64, 64), 64)
                gate, value, grad = gate_ref[span, :], kept_ref[span, :], sums[span, :]
                value = value - jnp.mean(value, axis=-1, keepdims=True)
                scale = lax.rsqrt(jnp.mean(value * value, axis=-1, keepdims=True) + 1.0 * DK)
                normed = value * scale
                open_part = jax.nn.sigmoid(gate)
                slope = open_part * (1.0 + gate * (1.0 - open_part))
                dgate_ref[span, :] = (grad * normed * slope).astype(BF)
                grad = grad * gate * open_part
                grad = grad - jnp.mean(grad, axis=-1, keepdims=True) - normed * jnp.mean(
                    grad * normed, axis=-1, keepdims=True
                )
                low_ref[span, :] = (grad * scale).astype(BF)
                return carry

            lax.fori_loop(0, 2 * rows // 64, chunk, 0)
            for g in (0, 1):
                span = slice(g * rows, (g + 1) * rows)
                entered = (q_ref[span].astype(F32) * e_ref[span]).astype(BF)
                state_ref[g] = lax.dot_general(
                    entered,
                    low_ref[span],
                    (((0,), (0,)), ((), ())),
                    preferred_element_type=F32,
                ).astype(BF)

    cols = pl.BlockSpec((rows, SLAB), lambda i, s: (0, i))
    operands = (*g_pair, weight, gate_pre, retained, query, enter)
    shapes = (
        sds((2 * rows, DV), BF),
        sds((2 * rows, DV), BF),
        sds((2, DK, DV), BF),
    )
    return call(
        body,
        (4,),
        [cols, cols, pl.BlockSpec((1, 4, 2, 64, DV), lambda i, s: (i, 0, 0, 0, 1))]
        + [whole(o) for o in operands[3:]],
        tuple(whole(s) for s in shapes),
        shapes,
        scalars,
        operands,
        "back_gate",
        scratch=[pltpu.VMEM((2 * rows, DV), F32)],
        stream=True,
    )


def weight_last(into, pair, came, fade, value, key_out, leave, grad_value, grad_key, cosine, sine,
                scalars):
    rows = pair[0].shape[0]

    def body(
        s_ref, a_ref, b_ref, near_ref, mid_ref, far_ref, f_ref, v_ref, k_ref, l_ref, gv_ref, gk_ref,
        cos_ref, sin_ref, into_ref, out_ref, mark_ref, grad_ref
    ):
        @pl.when(pl.program_id(0) == 0)
        def _():
            fade = f_ref[...]
            for g in (0, 1):
                span = slice(g * rows, (g + 1) * rows)
                state = near_ref[g].astype(F32) + fade * (
                    mid_ref[g].astype(F32) + fade * far_ref[g].astype(F32)
                )
                state = state.astype(BF)
                grad_ref[span, :DV] = (
                    gv_ref[g] + jnp.dot(k_ref[g], state, preferred_element_type=F32)
                ).astype(BF)
                grad_key = gk_ref[g] + l_ref[...] * lax.dot_general(
                    v_ref[g], state, (((1,), (1,)), ((), ())), preferred_element_type=F32
                )
                grad_ref[span, DV:] = rotate(grad_key, cos_ref[...], -sin_ref[...]).astype(BF)

        out = lax.dot_general(
            jnp.concatenate((a_ref[...], b_ref[...]), axis=0),
            grad_ref[...],
            (((0,), (0,)), ((), ())),
            preferred_element_type=F32,
        ).astype(BF)
        for c in (0, 1):
            for y in range(4):
                first = (c * 4 + y) * 64
                out_ref[0, y, jnp.bitwise_xor(c, s_ref[0])] = out[first : first + 64]
        mark_ref[...] = jnp.zeros_like(mark_ref)

    cols = pl.BlockSpec((rows, SLAB), lambda i, s: (0, i))
    operands = (*pair, *came, fade, value, key_out, leave, grad_value, grad_key, cosine, sine)
    shapes = (
        sds(into.shape, BF),
        sds((8, 128), F32),
        sds((2 * rows, DV + DK), BF),
    )
    return call(
        body,
        (4,),
        [cols, cols]
        + [whole(o) for o in operands[2:]]
        + [pl.BlockSpec(memory_space=pl.ANY)],
        (
            pl.BlockSpec((1, 4, 2, 64, DV + DK), lambda i, s: (i, 0, 0, 0, 0)),
            whole(shapes[1]),
            whole(shapes[2]),
        ),
        shapes,
        scalars,
        (*operands, into),
        "weight_last",
        stream=True,
        aliases={1 + len(operands): 0},
    )


def mm_weight_into(into, pairs, start, total, scalars, name, deps=()):
    widths = [grad.shape[1] for _, grad in pairs]
    rows = pairs[0][0][0].shape[0]
    span = sum(widths)

    def body(s_ref, *refs):
        out_ref, mark_ref = refs[-2:]
        at = 0
        for k, width in enumerate(widths):
            a_ref, b_ref, g_ref = refs[3 * k : 3 * k + 3]
            out = lax.dot_general(
                jnp.concatenate((a_ref[...], b_ref[...]), axis=0),
                g_ref[...],
                (((0,), (0,)), ((), ())),
                preferred_element_type=F32,
            ).astype(BF)
            for c in (0, 1):
                for y in range(4):
                    first = (c * 4 + y) * 64
                    out_ref[0, y, jnp.bitwise_xor(c, s_ref[0]), :, at : at + width] = out[
                        first : first + 64
                    ]
            at += width
        mark_ref[...] = jnp.zeros_like(mark_ref)

    cols = pl.BlockSpec((rows, SLAB), lambda i, s: (0, i))
    specs, operands = [], []
    for (a, b), grad in pairs:
        specs += [cols, cols, whole(grad)]
        operands += [a, b, grad]
    aliases = None
    if into is not None:
        aliases = {1 + len(operands): 0}
        specs.append(pl.BlockSpec(memory_space=pl.ANY))
        operands.append(into)
    return call(
        body,
        (4,),
        specs,
        (
            pl.BlockSpec((1, 4, 2, 64, span), lambda i, s: (i, 0, 0, 0, start // span)),
            pl.BlockSpec((8, 128), lambda i, s: (0, 0)),
        ),
        (sds((4, 4, 2, 64, total), BF), sds((8, 128), F32)),
        scalars,
        tuple(operands),
        name,
        deps=deps,
        stream=True,
        aliases=aliases,
    )


def split_heads(weights, scalars, name, deps=()):
    widths = [w.shape[1] // 2 for w in weights]

    def body(s_ref, *refs):
        mine_ref, theirs_ref = refs[-2:]
        core = s_ref[0]
        for out_ref, head in ((mine_ref, core), (theirs_ref, 1 - core)):
            at = 0
            for ref, width in zip(refs, widths):
                out_ref[:, at : at + width] = ref[:, pl.ds(pl.multiple_of(head * width, width), width)]
                at += width

    total = sum(widths)
    spec = pl.BlockSpec((64, total), lambda i, s: (0, 0))
    return call(
        body,
        (1,),
        [whole(w) for w in weights],
        (spec, spec),
        (sds((64, total), BF),) * 2,
        scalars,
        tuple(weights),
        name,
        deps=deps,
        stream=True,
    )


def join_heads(mine, theirs, widths, scalars, name):
    def body(s_ref, mine_ref, theirs_ref, *outs):
        core = s_ref[0]
        for in_ref, head in ((mine_ref, core), (theirs_ref, 1 - core)):
            at = 0
            for ref, width in zip(outs, widths):
                span = pl.ds(pl.multiple_of(head * width, width), width)
                ref[:, span] = in_ref[:, at : at + width].astype(F32)
                at += width

    shapes = tuple(sds((64, 2 * w), F32) for w in widths)
    return call(
        body,
        (1,),
        [whole(mine), whole(theirs)],
        tuple(whole(s) for s in shapes),
        shapes,
        scalars,
        (mine, theirs),
        name,
    )


def scale_of(values):
    return lax.rsqrt(jnp.mean(values * values, axis=-1, keepdims=True) + 1e-06)


def turned_spec(rows):
    return pl.BlockSpec((rows, D), lambda i, s: (lax.rem(i + s[1], 4), 0))


def plain_spec(rows):
    return pl.BlockSpec((rows, D), lambda i, s: (i, 0))


def enter_rows(tokens, gain, scalars, deps=()):
    rows = tokens.shape[0]
    block = rows // 4

    def body(s_ref, t_ref, g_ref, n_out):
        values = t_ref[...]
        n_out[...] = (values * scale_of(values) * g_ref[...]).astype(BF)

    return call(
        body,
        (4,),
        [turned_spec(block), whole(gain)],
        plain_spec(block),
        sds((rows, D), BF),
        scalars,
        (tokens, gain),
        "enter_rows",
        deps=deps,
    )


def low_rows(cotangent, scalars, deps=()):
    rows = cotangent.shape[0]
    block = rows // 4

    def body(s_ref, c_ref, l_out):
        l_out[...] = c_ref[...].astype(BF)

    return call(
        body,
        (4,),
        [turned_spec(block)],
        plain_spec(block),
        sds((rows, D), BF),
        scalars,
        (cotangent,),
        "low_rows",
        deps=deps,
    )


def each_part(refs, work):
    step = pl.program_id(0)
    for k, ref in enumerate(refs):

        @pl.when(step == k)
        def _(ref=ref):
            work(ref[...].astype(F32))


def second_norm(tokens, parts, gain, scalars, deps=()):
    rows = tokens.shape[0]
    block = rows // 4

    def body(s_ref, t_ref, g_ref, *refs):
        h_out, n_out = refs[4:]

        def work(part):
            values = t_ref[...] + part
            h_out[...] = values
            n_out[...] = (values * scale_of(values) * g_ref[...]).astype(BF)

        each_part(refs[:4], work)

    plain = plain_spec(block)
    return call(
        body,
        (4,),
        [turned_spec(block), whole(gain)] + [whole(p) for p in parts],
        (plain, plain),
        (sds((rows, D), F32), sds((rows, D), BF)),
        scalars,
        (tokens, gain, *parts),
        "second_norm",
        deps=deps,
    )


def third_blocks(own, came, down_own, down_came, scalars, deps=()):
    rows = own.shape[0]
    block = rows // 4

    def body(s_ref, own_ref, came_ref, d_ref, e_ref, *refs):
        total = own_ref[...] + came_ref[...].astype(F32)
        down = d_ref[...] + e_ref[...].astype(F32)
        step = pl.program_id(0)
        for k in range(4):

            @pl.when(step == k)
            def _(k=k):
                refs[k][:block] = total.astype(BF)
                refs[k][block:] = down.astype(BF)

    plain = plain_spec(block)
    shapes = (sds((2 * block, D), BF),) * 4
    return call(
        body,
        (4,),
        [plain] * 4,
        tuple(whole(s) for s in shapes),
        shapes,
        scalars,
        (own, came, down_own, down_came),
        "third_blocks",
        deps=deps,
        stream=True,
    )


def leave_rows(hidden, tokens, grad_state, parts, gain, scalars, deps=()):
    rows = hidden.shape[0]
    block = rows // 4

    def body(s_ref, h_ref, t_ref, u_ref, g_ref, *refs):
        def work(part):
            refs[4][...] = h_ref[...] + part[block : 2 * block]
            refs[5][...] = u_ref[...] + norm_grad(t_ref[...], part[:block], g_ref[...])

        each_part(refs[:4], work)

    plain, turn = plain_spec(block), turned_spec(block)
    return call(
        body,
        (4,),
        [plain, turn, plain, whole(gain)] + [whole(p) for p in parts],
        (turn, turn),
        (sds((rows, D), F32),) * 2,
        scalars,
        (hidden, tokens, grad_state, gain, *parts),
        "leave_rows",
        deps=deps,
        stream=True,
    )


def norm_grad(values, grad, gain):
    factor = scale_of(values)
    unit = values * factor
    scaled = grad * gain
    return factor * (scaled - unit * jnp.mean(scaled * unit, axis=-1, keepdims=True))


def norm_back(values, upstream, parts, gain, scalars, name, deps=()):
    rows = values.shape[0]
    block = rows // 4

    def body(s_ref, v_ref, u_ref, g_ref, *refs):
        def work(part):
            out = u_ref[...] + norm_grad(v_ref[...], part, g_ref[...])
            refs[4][...] = out
            refs[5][...] = out.astype(BF)

        each_part(refs[:4], work)

    plain = plain_spec(block)
    return call(
        body,
        (4,),
        [plain, turned_spec(block), whole(gain)] + [whole(p) for p in parts],
        (plain, plain),
        (sds((rows, D), F32), sds((rows, D), BF)),
        scalars,
        (values, upstream, gain, *parts),
        name,
        deps=deps,
        stream=True,
    )


def tp_first(blocks):
    got = [shift(blocks[o], "tp", o) for o in (1, 3, 2)]
    near, far, mid = [part.astype(F32) for part in got]
    return (blocks[0].astype(F32) + mid) + (near + far), got


def tp_second(mine):
    near, far, mid = [shift(mine, "tp", -o) for o in (1, 3, 2)]
    return mine, near, mid, far


def tp_total(blocks):
    return tp_second(tp_first(blocks)[0].astype(BF))


def chip_blocks(own, came):
    block = own.shape[0] // 4
    return [
        (own[o * block : (o + 1) * block] + came[o * block : (o + 1) * block].astype(F32)).astype(BF)
        for o in range(4)
    ]


def gate_norm(gate_pre, retained):
    centred = retained - jnp.mean(retained, axis=-1, keepdims=True)
    normed = centred * lax.rsqrt(jnp.mean(centred * centred, axis=-1, keepdims=True) + 1.0 * DK)
    return gate_pre * jax.nn.sigmoid(gate_pre) * normed


def gelu_gate(hidden, linear):
    return jax.nn.gelu(hidden, approximate=True) * linear


def rotate(values, cosine, sine):
    half = DK // 2
    first = values[..., :half]
    second = values[..., half:]
    return jnp.concatenate((first * cosine - second * sine, first * sine + second * cosine), axis=-1)


def ein(spec, left, right):
    return jnp.einsum(spec, left, right, preferred_element_type=F32)


def per_device(
    tokens,
    cotangent,
    gain_first,
    gain_second,
    w_query,
    w_key,
    w_value,
    w_gate,
    w_output,
    w_hidden,
    w_linear,
    w_down,
    decay_scale,
    first_length,
):
    rows = tokens.shape[0]
    core = lax.axis_index("core")
    place = lax.axis_index("ctx")
    plane = lax.axis_index("tp")
    scalars = jnp.stack((core, plane, lax.axis_index("x"), place)).astype(jnp.int32)

    w_output = w_output.T
    w_down = w_down.T
    mine, theirs = split_heads((w_value, w_key, w_gate, w_output, w_query), scalars, "split_attn")
    came = swap(theirs)
    block, gathered = stack_attn(mine, came, scalars)
    lengths = jnp.concatenate((first_length, swap(first_length)))
    blocks = spread_near(block)
    w_kv = stack_blocks(blocks, 0, 768, scalars, "stack_kv", deps=(lengths,))
    normed_first = enter_rows(tokens, gain_first.reshape(1, D), scalars, deps=blocks[1:])
    w_goq = lax.all_gather(gathered, XY, axis=0, tiled=True).reshape(4, 4, 2, 64, -1)
    mine, theirs = split_heads(
        (w_hidden, w_linear, w_down), scalars, "split_mlp", deps=(gathered,)
    )
    came_mlp = swap(theirs)
    gain_first = gain_first.reshape(1, D)
    gain_second = gain_second.reshape(1, D)
    x_first = (normed_first, swap(normed_first))
    cot_low = low_rows(cotangent, scalars, deps=(x_first[1],))
    g_out = (cot_low, swap(cot_low))
    w_kv = spread_far(w_kv)

    rate = lax.dynamic_index_in_dim(decay_scale, core, 0, False) / 1024.0
    local = (jnp.arange(rows, dtype=jnp.int32) + plane * (rows // 4)) % rows
    index = place * rows + local
    steps = local.astype(F32)
    leave = jnp.exp(-rate * (rows - 1.0 - steps))[None, :, None]
    fade = jnp.exp(-rate * rows)
    half = DK // 2
    frequency = 10000.0 ** (-(jnp.arange(half).astype(F32) / half))
    angles = index.astype(F32)[:, None] * frequency[None, :]
    cosine = jnp.cos(angles)
    sine = jnp.sin(angles)

    def spread_state(low, way):
        return [shift_open(low, "ctx", way * o) for o in (1, 2, 3)]

    leave_rows_out = leave.reshape(rows, 1)
    fade_in = fade.reshape(1, 1)
    projected = mm_in(*x_first, [(w_kv, 0, 768)], scalars, "project_kv")
    key = rotate(projected[:, DV:].reshape(2, rows, DK), cosine, sine).astype(BF)
    value = projected[:, :DV].astype(BF).reshape(2, rows, DV)
    key_out = (key.astype(F32) * leave).astype(BF)
    state_out = ein("gjd,gje->gde", key_out, value).astype(BF)
    came = spread_state(state_out, 1)
    w_mlp = lax.all_gather(
        stack_blocks((mine, came_mlp), 0, 1536, scalars, "stack_mlp", deps=came),
        XY,
        axis=0,
        tiled=True,
    ).reshape(4, 4, 2, 64, -1)
    own, other, query, state_in, weighted, gate_pre, retained, mixed, mask, enter_rows_in = retain(
        x_first,
        w_goq,
        key,
        value,
        came,
        rate.reshape(1, 1),
        cosine,
        sine,
        jnp.concatenate((scalars, lengths)),
    )
    enter = enter_rows_in.reshape(2, rows, 1)
    query = query.reshape(2, rows, DK)
    parts = tp_total(chip_blocks(own, swap(other)))
    hidden_state, normed_second = second_norm(tokens, parts, gain_second, scalars)
    x_second = (normed_second, swap(normed_second))
    own, other, gain_second_part, grad_pair, activated = mlp(x_second, g_out, w_mlp, scalars)
    grads, mark = mm_weight_into(
        None, ((x_second, grad_pair),), 1024, 3584, scalars, "weight_mlp"
    )
    mine, _ = tp_first(chip_blocks(own, swap(other)))
    (mine,) = tie((mine.astype(BF),), (mark,))
    parts = tp_second(mine)
    down = mm_back([(activated, w_mlp, 2 * DV)], scalars, "project_down", deps=(mine,))
    grad_state, grad_state_low = norm_back(
        hidden_state,
        cotangent,
        parts,
        gain_second,
        scalars,
        "second_back",
        deps=(down[1],),
    )
    g_state = (grad_state_low, swap(grad_state_low))
    grad_gate, grad_low, back_out = back_gate(
        g_state, w_goq, gate_pre, retained, query.reshape(2 * rows, DK), enter_rows_in, scalars
    )
    grad_low = grad_low.reshape(2, rows, DV)
    came = spread_state(back_out, -1)
    grad_scores = (ein("gie,gje->gij", grad_low, value) * mask).astype(BF)
    grad_query = ein("gij,gjd->gid", grad_scores, key) + enter * ein("gie,gde->gid", grad_low, state_in)
    grad_key = ein("gij,gid->gjd", grad_scores, query)
    grad_value = ein("gij,gie->gje", weighted, grad_low)
    grad_query = rotate(grad_query, cosine, -sine).astype(BF).reshape(2 * rows, DK)
    grads, mark = mm_weight_into(
        grads,
        ((g_state, mixed), (x_first, grad_gate)),
        2048,
        3584,
        scalars,
        "weight_og",
        deps=(back_out,),
    )
    grads, mark = mm_weight_into(
        grads, ((g_out, activated),), 3072, 3584, scalars, "weight_down"
    )
    grads, mark = mm_weight_into(
        grads, ((x_first, grad_query),), 768, 3584, scalars, "weight_query"
    )
    came[0] = tie((came[0],), (mark, grad_key, grad_value))[0]
    grads, mark, grad_vk = weight_last(
        grads,
        x_first,
        came,
        fade_in,
        value,
        key_out,
        leave_rows_out,
        grad_value,
        grad_key,
        cosine,
        sine,
        scalars,
    )
    block = lax.psum_scatter(grads.reshape(2048, -1), XY, scatter_dimension=0, tiled=True)
    own, other, gain_first_part = mm_back(
        [(grad_vk, w_kv, 0), (grad_gate, w_goq, 0), (grad_query, w_goq, 1024)],
        scalars,
        "back_attn",
        normed=x_first,
        deps=(mark,),
    )
    down = (down[0], swap(tie((down[1],), (mark,))[0]))
    blocks = third_blocks(own, swap(other), *down, scalars)
    mine, _ = tp_first(blocks)
    gains = jnp.concatenate((gain_first_part[:1], gain_second_part[:1]))
    for axis, swapped in (
        ("core", (1, 0)),
        ("ctx", (1, 0, 3, 2)),
        ("ctx", (3, 2, 1, 0)),
        ("x", (1, 0, 3, 2)),
        ("x", (3, 2, 1, 0)),
    ):
        gains = gains + lax.ppermute(gains, axis, list(enumerate(swapped)))
    mine = jnp.concatenate((mine, gains, jnp.zeros((14, D), F32))).astype(BF)
    parts = tp_second(mine)
    gains = [part[128:130].astype(F32) for part in parts]
    gains = (gains[0] + gains[2]) + (gains[1] + gains[3])
    spot = (lax.axis_index("x") * 2 + core) * 4 + place
    gain_first_grad, gain_second_grad = [
        lax.dynamic_slice_in_dim(gains[k] / gain[0], spot * 64, 64, 0)
        for k, gain in ((0, gain_first), (1, gain_second))
    ]
    layer_out, input_grad = leave_rows(
        hidden_state, tokens, grad_state, parts, gain_first, scalars
    )
    block = tie((block,), (gain_first_grad, gain_second_grad, input_grad))[0].reshape(2, 64, -1)
    d_value, d_key, d_query, d_hidden, d_linear, d_output, d_gate, d_down = join_heads(
        block[0], swap(block[1]), (DV, DK, DK) + (DV,) * 5, scalars, "join_heads"
    )
    return (
        layer_out,
        input_grad,
        gain_first_grad,
        gain_second_grad,
        d_query,
        d_key,
        d_value,
        d_gate,
        d_output.T,
        d_hidden,
        d_linear,
        d_down.T,
    )


def solution(mesh):
    fine = Mesh(np.asarray(mesh.devices).reshape(4, 2, 4, 4), ("x", "core", "ctx", "tp"))
    split = ("x", "core", "ctx")
    row = P(split, None)
    win = P(split, "tp")
    wout = P("tp", split)
    in_specs = (row, row, P(), P(), win, win, win, win, wout, win, win, wout, P("tp"), P(("x", "core")))
    out_specs = (row, row, P(split), P(split), win, win, win, win, wout, win, win, wout)
    return jax.shard_map(
        per_device, mesh=fine, in_specs=in_specs, out_specs=out_specs, check_vma=False
    )
```

```python
import math

import jax
import jax.numpy as jnp
import numpy as np
from jax import lax
from jax.experimental import pallas as pl
from jax.experimental.pallas import tpu as pltpu
from jax.sharding import Mesh, PartitionSpec as P

D = 2048
DK = 256
DV = 512
SLAB = 512
BF = jnp.bfloat16
F32 = jnp.float32
XY = ("x", "ctx")
MIB = 1 << 20


def shift(value, axis, offset):
    n = lax.axis_size(axis)
    return lax.ppermute(value, axis, [(i, (i + offset) % n) for i in range(n)])


def shift_open(value, axis, offset):
    n = lax.axis_size(axis)
    return lax.ppermute(
        value, axis, [(i, i + offset) for i in range(n) if 0 <= i + offset < n]
    )


def swap(value):
    return lax.ppermute(value, "core", [(0, 1), (1, 0)])


def after(value, *earlier):
    return lax.optimization_barrier((value, *earlier))[0]


def call(
    body,
    grid,
    ins,
    outs,
    shapes,
    scalars,
    operands,
    name,
    scratch=(),
    deps=(),
    stream=False,
    aliases=None,
):
    count = len(operands)

    def kernel(s_ref, *refs):
        body(s_ref, *refs[:count], *refs[count + len(deps) :])

    ins = [*ins, *[pl.BlockSpec(memory_space=pl.ANY)] * len(deps)]
    return pl.pallas_call(
        kernel,
        out_shape=shapes,
        grid_spec=pltpu.PrefetchScalarGridSpec(
            num_scalar_prefetch=1, grid=grid, in_specs=ins, out_specs=outs, scratch_shapes=scratch
        ),
        compiler_params=pltpu.CompilerParams(
            vmem_limit_bytes=(60 if stream else 32) * MIB, dimension_semantics=("arbitrary",) * len(grid)
        ),
        cost_estimate=pl.CostEstimate(flops=1, bytes_accessed=1, transcendentals=0),
        input_output_aliases=aliases or {},
        name=name,
    )(scalars, *operands, *deps)


def tie(values, deps):
    count = len(values)
    anywhere = pl.BlockSpec(memory_space=pl.ANY)
    return pl.pallas_call(
        lambda *refs: None,
        out_shape=tuple(sds(v.shape, v.dtype) for v in values),
        in_specs=[anywhere] * (count + len(deps)),
        out_specs=(anywhere,) * count,
        input_output_aliases={i: i for i in range(count)},
        name="tie",
    )(*values, *deps)


def whole(array):
    return pl.BlockSpec(array.shape, lambda *_: (0,) * array.ndim)


def sds(shape, dtype):
    return jax.ShapeDtypeStruct(shape, dtype)


def weight_operands(weight, start, width):
    if not isinstance(weight, tuple):
        spec = pl.BlockSpec((1, 4, 2, 64, width), lambda i, s: (i, 0, 0, 0, start // width))
        return [weight], [spec]
    piece = math.gcd(start, width) if start else width
    operands, specs = [], []
    for at in range(start, start + width, piece):
        for stack in weight:
            operands.append(stack)
            specs.append(pl.BlockSpec((4, 2, 64, piece), lambda i, s, at=at: (0, 0, 0, at // piece)))
    return operands, specs


def load_slab(s_ref, refs, held):
    core = s_ref[0]
    if len(refs) == 1:
        return jnp.concatenate(
            [refs[0][0, y, jnp.bitwise_xor(c, core)] for c in (0, 1) for y in range(4)], axis=0
        )
    x_far = lax.rem(s_ref[2] + 4 - pl.program_id(0), 4)
    at = 0
    for first in range(0, len(refs), 4):
        stacks = refs[first : first + 4]
        width = stacks[0].shape[-1]
        for j in range(4):

            @pl.when((core == 0) & (x_far == j))
            def _(j=j, at=at, width=width, stacks=stacks):
                for i in range(4):
                    y = lax.rem(s_ref[3] + 4 - i, 4)
                    for c in (0, 1):
                        held[c * 4 + y, :, at : at + width] = stacks[j][i, c]

        @pl.when(core == 1)
        def _(at=at, width=width, stacks=stacks):
            for j in range(4):
                y = lax.rem(s_ref[3] + 4 - j, 4)
                for c in (0, 1):
                    held[c * 4 + y, :, at : at + width] = stacks[j][x_far, 1 - c]

        at += width
    return held[...].reshape(SLAB, at)


def hop(value, first, offset):
    pairs = []
    for x in range(4):
        for core in (0, 1):
            for y in range(4):
                to = ((x + offset) % 4, y) if (core == 0) == first else (x, (y + offset) % 4)
                pairs.append(((x * 2 + core) * 4 + y, (to[0] * 2 + core) * 4 + to[1]))
    return lax.ppermute(value, ("x", "core", "ctx"), pairs)


def spread_near(block):
    near, far, mid = [hop(block, False, o) for o in (1, 3, 2)]
    return block, near, mid, far


def stack_blocks(blocks, start, width, scalars, name, deps=()):
    at = start // width if start % width == 0 else None
    span = width if at is not None else blocks[0].shape[1]
    first = 0 if at is not None else start
    height = blocks[0].shape[0]

    def body(s_ref, *refs):
        for k, ref in enumerate(refs[:-1]):
            refs[-1][k * height : (k + 1) * height, :] = ref[:, first : first + width]

    total = sds((height * len(blocks), width), BF)
    return call(
        body,
        (1,),
        [pl.BlockSpec((height, span), lambda i, s: (0, at or 0))] * len(blocks),
        whole(total),
        total,
        scalars,
        tuple(blocks),
        name,
        deps=deps,
    )


def stack_attn(mine, came, scalars):
    height, total = mine.shape

    def body(s_ref, mine_ref, came_ref, first_ref, other_ref):
        for k, ref in enumerate((mine_ref, came_ref)):
            span = slice(k * height, (k + 1) * height)
            first_ref[span, :] = ref[:, :768]
            other_ref[span, :] = ref[:, 768:]

    shapes = (sds((2 * height, 768), BF), sds((2 * height, total - 768), BF))
    return call(
        body,
        (1,),
        [whole(mine), whole(came)],
        tuple(whole(s) for s in shapes),
        shapes,
        scalars,
        (mine, came),
        "stack_attn",
        stream=True,
    )


def spread_far(stack, gate=False):
    stack = stack.reshape(4, 2, 64, -1)
    near, far = hop(stack, True, 1), hop(stack, True, -1)
    mid = hop(tie((stack,), (near, far))[0] if gate else stack, True, 2)
    return stack, near, mid, far


def mm_in(left, right, columns, scalars, name, deps=(), stream=False):
    operands, specs, counts = [], [], []
    for weight, start, width in columns:
        ops, sp = weight_operands(weight, start, width)
        operands += ops
        specs += sp
        counts.append(len(ops))
    total = sum(width for _, _, width in columns)

    def body(s_ref, a_ref, b_ref, *refs):
        out_ref = refs[len(operands)]
        step = pl.program_id(0)
        rows = jnp.concatenate((a_ref[...], b_ref[...]), axis=0)
        at, first = 0, 0
        for k, count in enumerate(counts):
            width = columns[k][2]
            slab = load_slab(s_ref, refs[first : first + count], refs[len(operands) + 1 + k])
            part = jnp.dot(rows, slab, preferred_element_type=F32)
            span = slice(at, at + width)

            @pl.when(step == 0)
            def _(part=part, span=span):
                out_ref[:, span] = part

            @pl.when(step > 0)
            def _(part=part, span=span):
                out_ref[:, span] += part

            at += width
            first += count

    rows = left.shape[0]
    cols = pl.BlockSpec((rows, SLAB), lambda i, s: (0, i))
    return call(
        body,
        (4,),
        [cols, cols, *specs],
        pl.BlockSpec((2 * rows, total), lambda i, s: (0, 0)),
        sds((2 * rows, total), F32),
        scalars,
        (left, right, *operands),
        name,
        scratch=[pltpu.VMEM((8, 64, width), BF) for _, _, width in columns],
        deps=deps,
        stream=stream,
    )


def mm_back(terms, scalars, name, normed=None, deps=()):
    rows = terms[0][0].shape[0]
    half = rows // 2
    operands, specs, counts, scratch = [], [], [], []
    for grad, weight, start in terms:
        ops, sp = weight_operands(weight, start, grad.shape[1])
        operands += [grad, *ops]
        specs += [whole(grad), *sp]
        counts.append(len(ops))
        scratch.append(pltpu.VMEM((8, 64, grad.shape[1]), BF))
    held = len(operands)
    cols = pl.BlockSpec((half, SLAB), lambda i, s: (0, i))
    outs = [cols, cols]
    shapes = [sds((half, D), F32), sds((half, D), BF)]
    if normed is not None:
        operands += normed
        specs += [cols, cols]
        outs.append(pl.BlockSpec((8, SLAB), lambda i, s: (0, i)))
        shapes.append(sds((8, D), F32))
    total = len(operands)

    def body(s_ref, *refs):
        at, out = 0, 0.0
        for k, count in enumerate(counts):
            slab = load_slab(s_ref, refs[at + 1 : at + 1 + count], refs[total + len(outs) + k])
            out += lax.dot_general(
                refs[at][...], slab, (((1,), (1,)), ((), ())), preferred_element_type=F32
            )
            at += count + 1
        refs[total][...] = out[:half]
        refs[total + 1][...] = out[half:].astype(BF)
        if normed is not None:
            part = out[:half] * refs[held][...].astype(F32) + out[half:] * refs[held + 1][
                ...
            ].astype(F32)
            part = jnp.sum(part, axis=0, keepdims=True)
            refs[total + 2][...] = jnp.broadcast_to(part, (8, SLAB))

    return call(
        body,
        (4,),
        specs,
        tuple(outs),
        tuple(shapes),
        scalars,
        tuple(operands),
        name,
        scratch=scratch,
        deps=deps,
    )


def split_out(out, own_ref, other_ref):
    half = out.shape[0] // 2
    own_ref[...] = out[:half]
    other_ref[...] = out[half:].astype(BF)


def retain(x_pair, weight, key, value, came, rate, cosine, sine, scalars):
    rows = x_pair[0].shape[0]

    def body(
        s_ref, a_ref, b_ref, w_ref, k_ref, v_ref, near_ref, mid_ref, far_ref, r_ref, cos_ref,
        sin_ref, own_ref, other_ref, query_ref, state_ref, weighted_ref, gate_ref, retained_ref,
        mixed_ref, m_ref, e_ref, sums, turned
    ):
        step = pl.program_id(0)

        @pl.when(step == 0)
        def _():
            rate = r_ref[...]

            def place_of(shape, dim):
                index = lax.broadcasted_iota(jnp.int32, shape, dim)
                return lax.rem(index + s_ref[1] * (rows // 4), rows)

            left, right = place_of((rows, rows), 0), place_of((rows, rows), 1)
            column = place_of((rows, 1), 0)
            decay = jnp.exp(-rate * jnp.maximum(left - right, 0).astype(F32))
            for g in (0, 1):
                length = s_ref[4 + g] - s_ref[3] * rows
                linked = (left >= right) & ((left >= length) == (right >= length))
                m_ref[g] = jnp.where(linked, decay, 0.0)
                e_ref[g * rows : (g + 1) * rows] = jnp.where(
                    column >= length, 0.0, jnp.exp(-rate * (column.astype(F32) + 1.0))
                )

        @pl.when(step < 4)
        def _():
            slab = load_slab(s_ref, (w_ref,), None)
            turned[step] = slab[:, DV : 2 * DV]
            left = jnp.concatenate((a_ref[...], b_ref[...]), axis=0)
            gate = jnp.dot(left, slab[:, :DV], preferred_element_type=F32)
            query = jnp.dot(left, slab[:, 2 * DV :], preferred_element_type=F32)

            @pl.when(step == 0)
            def _():
                gate_ref[...] = gate
                sums[...] = query

            @pl.when(step > 0)
            def _():
                gate_ref[...] += gate
                sums[...] += query

        @pl.when(step == 3)
        def _():
            fade = jnp.exp(-r_ref[...] * rows)
            for g in (0, 1):
                span = slice(g * rows, (g + 1) * rows)
                state = near_ref[g].astype(F32) + fade * (
                    mid_ref[g].astype(F32) + fade * far_ref[g].astype(F32)
                )
                state_ref[g] = state.astype(BF)
                query = rotate(sums[span], cos_ref[...], sin_ref[...]).astype(BF)
                query_ref[span] = query
                scores = lax.dot_general(
                    query, k_ref[g], (((1,), (1,)), ((), ())), preferred_element_type=F32
                )
                weighted = (scores * m_ref[g]).astype(BF)
                weighted_ref[g] = weighted
                retained = jnp.dot(weighted, v_ref[g], preferred_element_type=F32)
                retained += e_ref[span] * jnp.dot(
                    query, state_ref[g], preferred_element_type=F32
                )
                retained_ref[span] = retained
                mixed_ref[span] = gate_norm(gate_ref[span], retained).astype(BF)

        @pl.when(step >= 4)
        def _():
            out = lax.dot_general(
                mixed_ref[...],
                turned[step - 4],
                (((1,), (1,)), ((), ())),
                preferred_element_type=F32,
            )
            split_out(out, own_ref, other_ref)

    cols = pl.BlockSpec((rows, SLAB), lambda i, s: (0, jnp.minimum(i, 3)))
    later = pl.BlockSpec((rows, SLAB), lambda i, s: (0, jnp.maximum(i - 4, 0)))
    operands = (*x_pair, weight, key, value, *came, rate, cosine, sine)
    shapes = (
        sds((rows, D), F32),
        sds((rows, D), BF),
        sds((2 * rows, DK), BF),
        sds((2, DK, DV), BF),
        sds((2, rows, rows), BF),
        sds((2 * rows, DV), F32),
        sds((2 * rows, DV), F32),
        sds((2 * rows, DV), BF),
        sds((2, rows, rows), F32),
        sds((2 * rows, 1), F32),
    )
    block = pl.BlockSpec((1, 4, 2, 64, 1280), lambda i, s: (jnp.minimum(i, 3), 0, 0, 0, 0))
    return call(
        body,
        (8,),
        [cols, cols, block] + [whole(o) for o in operands[3:]],
        (later, later) + tuple(whole(s) for s in shapes[2:]),
        shapes,
        scalars,
        operands,
        "retain",
        scratch=[pltpu.VMEM((2 * rows, DK), F32), pltpu.VMEM((4, SLAB, DV), BF)],
        stream=True,
    )


def mlp(x_pair, g_pair, weight, scalars):
    rows = x_pair[0].shape[0]

    def body(
        s_ref, a_ref, b_ref, c_ref, d_ref, w_ref, own_ref, other_ref, gain_ref, pair_ref, act_ref,
        both, back, kept
    ):
        step = pl.program_id(0)

        @pl.when(step < 4)
        def _():
            slab = load_slab(s_ref, (w_ref,), None)
            kept[step] = slab[:, : 2 * DV]
            left = jnp.concatenate((a_ref[...], b_ref[...]), axis=0)
            grad = jnp.concatenate((c_ref[...], d_ref[...]), axis=0)
            up = jnp.dot(left, slab[:, : 2 * DV], preferred_element_type=F32)
            down = jnp.dot(grad, slab[:, 2 * DV :], preferred_element_type=F32)

            @pl.when(step == 0)
            def _():
                both[...] = up
                back[...] = down

            @pl.when(step > 0)
            def _():
                both[...] += up
                back[...] += down

        @pl.when(step == 3)
        def _():
            def chunk(k, carry):
                span = pl.ds(pl.multiple_of(k * 64, 64), 64)
                hidden, linear, grad = both[span, :DV], both[span, DV:], back[span, :]
                cube = 0.044715 * hidden * hidden
                bent = jnp.tanh(0.7978845608 * hidden * (1.0 + cube))
                half = 0.5 * (1.0 + bent)
                gelu = hidden * half
                slope = half + 0.5 * hidden * (1.0 - bent * bent) * (
                    0.7978845608 * (1.0 + 3.0 * cube)
                )
                act_ref[span, :] = (gelu * linear).astype(BF)
                pair_ref[span, :DV] = (grad * linear * slope).astype(BF)
                pair_ref[span, DV:] = (grad * gelu).astype(BF)
                return carry

            lax.fori_loop(0, 2 * rows // 64, chunk, 0)

        @pl.when(step >= 4)
        def _():
            out = lax.dot_general(
                pair_ref[...], kept[step - 4], (((1,), (1,)), ((), ())), preferred_element_type=F32
            )
            split_out(out, own_ref, other_ref)
            part = out[:rows] * a_ref[...].astype(F32) + out[rows:] * b_ref[...].astype(F32)
            gain_ref[...] = jnp.broadcast_to(jnp.sum(part, axis=0, keepdims=True), (8, SLAB))

    cols = pl.BlockSpec((rows, SLAB), lambda i, s: (0, lax.rem(i, 4)))
    once = pl.BlockSpec((rows, SLAB), lambda i, s: (0, jnp.minimum(i, 3)))
    block = pl.BlockSpec((1, 4, 2, 64, 3 * DV), lambda i, s: (jnp.minimum(i, 3), 0, 0, 0, 0))
    later = pl.BlockSpec((rows, SLAB), lambda i, s: (0, jnp.maximum(i - 4, 0)))
    shapes = (
        sds((rows, D), F32),
        sds((rows, D), BF),
        sds((8, D), F32),
        sds((2 * rows, 2 * DV), BF),
        sds((2 * rows, DV), BF),
    )
    return call(
        body,
        (8,),
        [cols, cols, once, once, block],
        (
            later,
            later,
            pl.BlockSpec((8, SLAB), lambda i, s: (0, jnp.maximum(i - 4, 0))),
            whole(shapes[3]),
            whole(shapes[4]),
        ),
        shapes,
        scalars,
        (*x_pair, *g_pair, weight),
        "mlp",
        scratch=[
            pltpu.VMEM((2 * rows, 2 * DV), F32),
            pltpu.VMEM((2 * rows, DV), F32),
            pltpu.VMEM((4, SLAB, 2 * DV), BF),
        ],
        stream=True,
    )


def back_gate(g_pair, weight, gate_pre, retained, query, enter, scalars):
    rows = g_pair[0].shape[0]

    def body(
        s_ref, a_ref, b_ref, w_ref, gate_ref, kept_ref, q_ref, e_ref, dgate_ref, low_ref, state_ref,
        sums
    ):
        step = pl.program_id(0)
        left = jnp.concatenate((a_ref[...], b_ref[...]), axis=0)
        part = jnp.dot(left, load_slab(s_ref, (w_ref,), None), preferred_element_type=F32)

        @pl.when(step == 0)
        def _():
            sums[...] = part

        @pl.when(step > 0)
        def _():
            sums[...] += part

        @pl.when(step == 3)
        def _():
            def chunk(k, carry):
                span = pl.ds(pl.multiple_of(k * 64, 64), 64)
                gate, value, grad = gate_ref[span, :], kept_ref[span, :], sums[span, :]
                value = value - jnp.mean(value, axis=-1, keepdims=True)
                scale = lax.rsqrt(jnp.mean(value * value, axis=-1, keepdims=True) + 1.0 * DK)
                normed = value * scale
                open_part = jax.nn.sigmoid(gate)
                slope = open_part * (1.0 + gate * (1.0 - open_part))
                dgate_ref[span, :] = (grad * normed * slope).astype(BF)
                grad = grad * gate * open_part
                grad = grad - jnp.mean(grad, axis=-1, keepdims=True) - normed * jnp.mean(
                    grad * normed, axis=-1, keepdims=True
                )
                low_ref[span, :] = (grad * scale).astype(BF)
                return carry

            lax.fori_loop(0, 2 * rows // 64, chunk, 0)
            for g in (0, 1):
                span = slice(g * rows, (g + 1) * rows)
                entered = (q_ref[span].astype(F32) * e_ref[span]).astype(BF)
                state_ref[g] = lax.dot_general(
                    entered,
                    low_ref[span],
                    (((0,), (0,)), ((), ())),
                    preferred_element_type=F32,
                ).astype(BF)

    cols = pl.BlockSpec((rows, SLAB), lambda i, s: (0, i))
    operands = (*g_pair, weight, gate_pre, retained, query, enter)
    shapes = (
        sds((2 * rows, DV), BF),
        sds((2 * rows, DV), BF),
        sds((2, DK, DV), BF),
    )
    return call(
        body,
        (4,),
        [cols, cols, pl.BlockSpec((1, 4, 2, 64, DV), lambda i, s: (i, 0, 0, 0, 1))]
        + [whole(o) for o in operands[3:]],
        tuple(whole(s) for s in shapes),
        shapes,
        scalars,
        operands,
        "back_gate",
        scratch=[pltpu.VMEM((2 * rows, DV), F32)],
        stream=True,
    )


def weight_last(into, pair, came, fade, value, key_out, leave, grad_value, grad_key, cosine, sine,
                scalars):
    rows = pair[0].shape[0]

    def body(
        s_ref, a_ref, b_ref, near_ref, mid_ref, far_ref, f_ref, v_ref, k_ref, l_ref, gv_ref, gk_ref,
        cos_ref, sin_ref, into_ref, out_ref, mark_ref, grad_ref
    ):
        @pl.when(pl.program_id(0) == 0)
        def _():
            fade = f_ref[...]
            for g in (0, 1):
                span = slice(g * rows, (g + 1) * rows)
                state = near_ref[g].astype(F32) + fade * (
                    mid_ref[g].astype(F32) + fade * far_ref[g].astype(F32)
                )
                state = state.astype(BF)
                grad_ref[span, :DV] = (
                    gv_ref[g] + jnp.dot(k_ref[g], state, preferred_element_type=F32)
                ).astype(BF)
                grad_key = gk_ref[g] + l_ref[...] * lax.dot_general(
                    v_ref[g], state, (((1,), (1,)), ((), ())), preferred_element_type=F32
                )
                grad_ref[span, DV:] = rotate(grad_key, cos_ref[...], -sin_ref[...]).astype(BF)

        out = lax.dot_general(
            jnp.concatenate((a_ref[...], b_ref[...]), axis=0),
            grad_ref[...],
            (((0,), (0,)), ((), ())),
            preferred_element_type=F32,
        ).astype(BF)
        for c in (0, 1):
            for y in range(4):
                first = (c * 4 + y) * 64
                out_ref[0, y, jnp.bitwise_xor(c, s_ref[0])] = out[first : first + 64]
        mark_ref[...] = jnp.zeros_like(mark_ref)

    cols = pl.BlockSpec((rows, SLAB), lambda i, s: (0, i))
    operands = (*pair, *came, fade, value, key_out, leave, grad_value, grad_key, cosine, sine)
    shapes = (
        sds(into.shape, BF),
        sds((8, 128), F32),
        sds((2 * rows, DV + DK), BF),
    )
    return call(
        body,
        (4,),
        [cols, cols]
        + [whole(o) for o in operands[2:]]
        + [pl.BlockSpec(memory_space=pl.ANY)],
        (
            pl.BlockSpec((1, 4, 2, 64, DV + DK), lambda i, s: (i, 0, 0, 0, 0)),
            whole(shapes[1]),
            whole(shapes[2]),
        ),
        shapes,
        scalars,
        (*operands, into),
        "weight_last",
        stream=True,
        aliases={1 + len(operands): 0},
    )


def mm_weight_into(into, pairs, start, total, scalars, name, deps=()):
    widths = [grad.shape[1] for _, grad in pairs]
    rows = pairs[0][0][0].shape[0]
    span = sum(widths)

    def body(s_ref, *refs):
        out_ref, mark_ref = refs[-2:]
        at = 0
        for k, width in enumerate(widths):
            a_ref, b_ref, g_ref = refs[3 * k : 3 * k + 3]
            out = lax.dot_general(
                jnp.concatenate((a_ref[...], b_ref[...]), axis=0),
                g_ref[...],
                (((0,), (0,)), ((), ())),
                preferred_element_type=F32,
            ).astype(BF)
            for c in (0, 1):
                for y in range(4):
                    first = (c * 4 + y) * 64
                    out_ref[0, y, jnp.bitwise_xor(c, s_ref[0]), :, at : at + width] = out[
                        first : first + 64
                    ]
            at += width
        mark_ref[...] = jnp.zeros_like(mark_ref)

    cols = pl.BlockSpec((rows, SLAB), lambda i, s: (0, i))
    specs, operands = [], []
    for (a, b), grad in pairs:
        specs += [cols, cols, whole(grad)]
        operands += [a, b, grad]
    aliases = None
    if into is not None:
        aliases = {1 + len(operands): 0}
        specs.append(pl.BlockSpec(memory_space=pl.ANY))
        operands.append(into)
    return call(
        body,
        (4,),
        specs,
        (
            pl.BlockSpec((1, 4, 2, 64, span), lambda i, s: (i, 0, 0, 0, start // span)),
            pl.BlockSpec((8, 128), lambda i, s: (0, 0)),
        ),
        (sds((4, 4, 2, 64, total), BF), sds((8, 128), F32)),
        scalars,
        tuple(operands),
        name,
        deps=deps,
        stream=True,
        aliases=aliases,
    )


def split_heads(weights, scalars, name, deps=()):
    widths = [w.shape[1] // 2 for w in weights]

    def body(s_ref, *refs):
        mine_ref, theirs_ref = refs[-2:]
        core = s_ref[0]
        for out_ref, head in ((mine_ref, core), (theirs_ref, 1 - core)):
            at = 0
            for ref, width in zip(refs, widths):
                out_ref[:, at : at + width] = ref[:, pl.ds(pl.multiple_of(head * width, width), width)]
                at += width

    total = sum(widths)
    spec = pl.BlockSpec((64, total), lambda i, s: (0, 0))
    return call(
        body,
        (1,),
        [whole(w) for w in weights],
        (spec, spec),
        (sds((64, total), BF),) * 2,
        scalars,
        tuple(weights),
        name,
        deps=deps,
        stream=True,
    )


def join_heads(mine, theirs, widths, scalars, name):
    def body(s_ref, mine_ref, theirs_ref, *outs):
        core = s_ref[0]
        for in_ref, head in ((mine_ref, core), (theirs_ref, 1 - core)):
            at = 0
            for ref, width in zip(outs, widths):
                span = pl.ds(pl.multiple_of(head * width, width), width)
                ref[:, span] = in_ref[:, at : at + width].astype(F32)
                at += width

    shapes = tuple(sds((64, 2 * w), F32) for w in widths)
    return call(
        body,
        (1,),
        [whole(mine), whole(theirs)],
        tuple(whole(s) for s in shapes),
        shapes,
        scalars,
        (mine, theirs),
        name,
    )


def scale_of(values):
    return lax.rsqrt(jnp.mean(values * values, axis=-1, keepdims=True) + 1e-06)


def turned_spec(rows):
    return pl.BlockSpec((rows, D), lambda i, s: (lax.rem(i + s[1], 4), 0))


def plain_spec(rows):
    return pl.BlockSpec((rows, D), lambda i, s: (i, 0))


def enter_rows(tokens, gain, scalars, deps=()):
    rows = tokens.shape[0]
    block = rows // 4

    def body(s_ref, t_ref, g_ref, n_out):
        values = t_ref[...]
        n_out[...] = (values * scale_of(values) * g_ref[...]).astype(BF)

    return call(
        body,
        (4,),
        [turned_spec(block), whole(gain)],
        plain_spec(block),
        sds((rows, D), BF),
        scalars,
        (tokens, gain),
        "enter_rows",
        deps=deps,
    )


def low_rows(cotangent, scalars, deps=()):
    rows = cotangent.shape[0]
    block = rows // 4

    def body(s_ref, c_ref, l_out):
        l_out[...] = c_ref[...].astype(BF)

    return call(
        body,
        (4,),
        [turned_spec(block)],
        plain_spec(block),
        sds((rows, D), BF),
        scalars,
        (cotangent,),
        "low_rows",
        deps=deps,
    )


def each_part(refs, work):
    step = pl.program_id(0)
    for k, ref in enumerate(refs):

        @pl.when(step == k)
        def _(ref=ref):
            work(ref[...].astype(F32))


def second_norm(tokens, parts, gain, scalars, deps=()):
    rows = tokens.shape[0]
    block = rows // 4

    def body(s_ref, t_ref, g_ref, *refs):
        h_out, n_out = refs[4:]

        def work(part):
            values = t_ref[...] + part
            h_out[...] = values
            n_out[...] = (values * scale_of(values) * g_ref[...]).astype(BF)

        each_part(refs[:4], work)

    plain = plain_spec(block)
    return call(
        body,
        (4,),
        [turned_spec(block), whole(gain)] + [whole(p) for p in parts],
        (plain, plain),
        (sds((rows, D), F32), sds((rows, D), BF)),
        scalars,
        (tokens, gain, *parts),
        "second_norm",
        deps=deps,
    )


def third_blocks(own, came, down_own, down_came, scalars, deps=()):
    rows = own.shape[0]
    block = rows // 4

    def body(s_ref, own_ref, came_ref, d_ref, e_ref, *refs):
        total = own_ref[...] + came_ref[...].astype(F32)
        down = d_ref[...] + e_ref[...].astype(F32)
        step = pl.program_id(0)
        for k in range(4):

            @pl.when(step == k)
            def _(k=k):
                refs[k][:block] = total.astype(BF)
                refs[k][block:] = down.astype(BF)

    plain = plain_spec(block)
    shapes = (sds((2 * block, D), BF),) * 4
    return call(
        body,
        (4,),
        [plain] * 4,
        tuple(whole(s) for s in shapes),
        shapes,
        scalars,
        (own, came, down_own, down_came),
        "third_blocks",
        deps=deps,
        stream=True,
    )


def leave_rows(hidden, tokens, grad_state, parts, gain, scalars, deps=()):
    rows = hidden.shape[0]
    block = rows // 4

    def body(s_ref, h_ref, t_ref, u_ref, g_ref, *refs):
        def work(part):
            refs[4][...] = h_ref[...] + part[block : 2 * block]
            refs[5][...] = u_ref[...] + norm_grad(t_ref[...], part[:block], g_ref[...])

        each_part(refs[:4], work)

    plain, turn = plain_spec(block), turned_spec(block)
    return call(
        body,
        (4,),
        [plain, turn, plain, whole(gain)] + [whole(p) for p in parts],
        (turn, turn),
        (sds((rows, D), F32),) * 2,
        scalars,
        (hidden, tokens, grad_state, gain, *parts),
        "leave_rows",
        deps=deps,
        stream=True,
    )


def norm_grad(values, grad, gain):
    factor = scale_of(values)
    unit = values * factor
    scaled = grad * gain
    return factor * (scaled - unit * jnp.mean(scaled * unit, axis=-1, keepdims=True))


def norm_back(values, upstream, parts, gain, scalars, name, deps=()):
    rows = values.shape[0]
    block = rows // 4

    def body(s_ref, v_ref, u_ref, g_ref, *refs):
        def work(part):
            out = u_ref[...] + norm_grad(v_ref[...], part, g_ref[...])
            refs[4][...] = out
            refs[5][...] = out.astype(BF)

        each_part(refs[:4], work)

    plain = plain_spec(block)
    return call(
        body,
        (4,),
        [plain, turned_spec(block), whole(gain)] + [whole(p) for p in parts],
        (plain, plain),
        (sds((rows, D), F32), sds((rows, D), BF)),
        scalars,
        (values, upstream, gain, *parts),
        name,
        deps=deps,
        stream=True,
    )


def tp_first(blocks):
    got = [shift(blocks[o], "tp", o) for o in (1, 3, 2)]
    near, far, mid = [part.astype(F32) for part in got]
    return (blocks[0].astype(F32) + mid) + (near + far), got


def tp_second(mine):
    near, far, mid = [shift(mine, "tp", -o) for o in (1, 3, 2)]
    return mine, near, mid, far


def tp_total(blocks):
    return tp_second(tp_first(blocks)[0].astype(BF))


def chip_blocks(own, came):
    block = own.shape[0] // 4
    return [
        (own[o * block : (o + 1) * block] + came[o * block : (o + 1) * block].astype(F32)).astype(BF)
        for o in range(4)
    ]


def gate_norm(gate_pre, retained):
    centred = retained - jnp.mean(retained, axis=-1, keepdims=True)
    normed = centred * lax.rsqrt(jnp.mean(centred * centred, axis=-1, keepdims=True) + 1.0 * DK)
    return gate_pre * jax.nn.sigmoid(gate_pre) * normed


def gelu_gate(hidden, linear):
    return jax.nn.gelu(hidden, approximate=True) * linear


def rotate(values, cosine, sine):
    half = DK // 2
    first = values[..., :half]
    second = values[..., half:]
    return jnp.concatenate((first * cosine - second * sine, first * sine + second * cosine), axis=-1)


def ein(spec, left, right):
    return jnp.einsum(spec, left, right, preferred_element_type=F32)


def per_device(
    tokens,
    cotangent,
    gain_first,
    gain_second,
    w_query,
    w_key,
    w_value,
    w_gate,
    w_output,
    w_hidden,
    w_linear,
    w_down,
    decay_scale,
    first_length,
):
    rows = tokens.shape[0]
    core = lax.axis_index("core")
    place = lax.axis_index("ctx")
    plane = lax.axis_index("tp")
    scalars = jnp.stack((core, plane, lax.axis_index("x"), place)).astype(jnp.int32)

    w_output = w_output.T
    w_down = w_down.T
    mine, theirs = split_heads((w_value, w_key, w_gate, w_output, w_query), scalars, "split_attn")
    came = swap(theirs)
    block, gathered = stack_attn(mine, came, scalars)
    lengths = jnp.concatenate((first_length, swap(first_length)))
    blocks = spread_near(block)
    w_kv = stack_blocks(blocks, 0, 768, scalars, "stack_kv")
    normed_first = enter_rows(tokens, gain_first.reshape(1, D), scalars, deps=blocks[1:])
    w_goq = lax.all_gather(gathered, XY, axis=0, tiled=True).reshape(4, 4, 2, 64, -1)
    mine, theirs = split_heads(
        (w_hidden, w_linear, w_down), scalars, "split_mlp", deps=(normed_first,)
    )
    came_mlp = swap(theirs)
    gain_first = gain_first.reshape(1, D)
    gain_second = gain_second.reshape(1, D)
    x_first = (normed_first, swap(normed_first))
    cot_low = low_rows(cotangent, scalars, deps=(x_first[1],))
    g_out = (cot_low, swap(cot_low))
    w_kv = spread_far(w_kv)

    rate = lax.dynamic_index_in_dim(decay_scale, core, 0, False) / 1024.0
    local = (jnp.arange(rows, dtype=jnp.int32) + plane * (rows // 4)) % rows
    index = place * rows + local
    steps = local.astype(F32)
    leave = jnp.exp(-rate * (rows - 1.0 - steps))[None, :, None]
    fade = jnp.exp(-rate * rows)
    half = DK // 2
    frequency = 10000.0 ** (-(jnp.arange(half).astype(F32) / half))
    angles = index.astype(F32)[:, None] * frequency[None, :]
    cosine = jnp.cos(angles)
    sine = jnp.sin(angles)

    def spread_state(low, way):
        return [shift_open(low, "ctx", way * o) for o in (1, 2, 3)]

    leave_rows_out = leave.reshape(rows, 1)
    fade_in = fade.reshape(1, 1)
    projected = mm_in(*x_first, [(w_kv, 0, 768)], scalars, "project_kv", deps=(came_mlp,))
    key = rotate(projected[:, DV:].reshape(2, rows, DK), cosine, sine).astype(BF)
    value = projected[:, :DV].astype(BF).reshape(2, rows, DV)
    key_out = (key.astype(F32) * leave).astype(BF)
    state_out = ein("gjd,gje->gde", key_out, value).astype(BF)
    came = spread_state(state_out, 1)
    w_mlp = lax.all_gather(
        stack_blocks((mine, came_mlp), 0, 1536, scalars, "stack_mlp", deps=(state_out,)),
        XY,
        axis=0,
        tiled=True,
    ).reshape(4, 4, 2, 64, -1)
    own, other, query, state_in, weighted, gate_pre, retained, mixed, mask, enter_rows_in = retain(
        x_first,
        w_goq,
        key,
        value,
        came,
        rate.reshape(1, 1),
        cosine,
        sine,
        jnp.concatenate((scalars, lengths)),
    )
    enter = enter_rows_in.reshape(2, rows, 1)
    query = query.reshape(2, rows, DK)
    parts = tp_total(chip_blocks(own, swap(other)))
    hidden_state, normed_second = second_norm(tokens, parts, gain_second, scalars)
    x_second = (normed_second, swap(normed_second))
    own, other, gain_second_part, grad_pair, activated = mlp(x_second, g_out, w_mlp, scalars)
    grads, mark = mm_weight_into(
        None, ((x_second, grad_pair),), 1024, 3584, scalars, "weight_mlp"
    )
    mine, _ = tp_first(chip_blocks(own, swap(other)))
    (mine,) = tie((mine.astype(BF),), (mark,))
    parts = tp_second(mine)
    down = mm_back([(activated, w_mlp, 2 * DV)], scalars, "project_down", deps=(mine,))
    grad_state, grad_state_low = norm_back(
        hidden_state,
        cotangent,
        parts,
        gain_second,
        scalars,
        "second_back",
        deps=(down[1],),
    )
    g_state = (grad_state_low, swap(grad_state_low))
    grad_gate, grad_low, back_out = back_gate(
        g_state, w_goq, gate_pre, retained, query.reshape(2 * rows, DK), enter_rows_in, scalars
    )
    grad_low = grad_low.reshape(2, rows, DV)
    came = spread_state(back_out, -1)
    grad_scores = (ein("gie,gje->gij", grad_low, value) * mask).astype(BF)
    grad_query = ein("gij,gjd->gid", grad_scores, key) + enter * ein("gie,gde->gid", grad_low, state_in)
    grad_key = ein("gij,gid->gjd", grad_scores, query)
    grad_value = ein("gij,gie->gje", weighted, grad_low)
    grad_query = rotate(grad_query, cosine, -sine).astype(BF).reshape(2 * rows, DK)
    grads, mark = mm_weight_into(
        grads,
        ((g_state, mixed), (x_first, grad_gate)),
        2048,
        3584,
        scalars,
        "weight_og",
        deps=(back_out,),
    )
    grads, mark = mm_weight_into(
        grads, ((g_out, activated),), 3072, 3584, scalars, "weight_down"
    )
    grads, mark = mm_weight_into(
        grads, ((x_first, grad_query),), 768, 3584, scalars, "weight_query"
    )
    came[0] = tie((came[0],), (mark, grad_key, grad_value))[0]
    grads, mark, grad_vk = weight_last(
        grads,
        x_first,
        came,
        fade_in,
        value,
        key_out,
        leave_rows_out,
        grad_value,
        grad_key,
        cosine,
        sine,
        scalars,
    )
    block = lax.psum_scatter(grads.reshape(2048, -1), XY, scatter_dimension=0, tiled=True)
    own, other, gain_first_part = mm_back(
        [(grad_vk, w_kv, 0), (grad_gate, w_goq, 0), (grad_query, w_goq, 1024)],
        scalars,
        "back_attn",
        normed=x_first,
        deps=(mark,),
    )
    down = (down[0], swap(tie((down[1],), (mark,))[0]))
    blocks = third_blocks(own, swap(other), *down, scalars)
    mine, _ = tp_first(blocks)
    gains = jnp.concatenate((gain_first_part[:1], gain_second_part[:1]))
    for axis, swapped in (
        ("core", (1, 0)),
        ("ctx", (1, 0, 3, 2)),
        ("ctx", (3, 2, 1, 0)),
        ("x", (1, 0, 3, 2)),
        ("x", (3, 2, 1, 0)),
    ):
        gains = gains + lax.ppermute(gains, axis, list(enumerate(swapped)))
    mine = jnp.concatenate((mine, gains, jnp.zeros((14, D), F32))).astype(BF)
    parts = tp_second(mine)
    gains = [part[128:130].astype(F32) for part in parts]
    gains = (gains[0] + gains[2]) + (gains[1] + gains[3])
    spot = (lax.axis_index("x") * 2 + core) * 4 + place
    gain_first_grad, gain_second_grad = [
        lax.dynamic_slice_in_dim(gains[k] / gain[0], spot * 64, 64, 0)
        for k, gain in ((0, gain_first), (1, gain_second))
    ]
    layer_out, input_grad = leave_rows(
        hidden_state, tokens, grad_state, parts, gain_first, scalars
    )
    block = tie((block,), (gain_first_grad, gain_second_grad, input_grad))[0].reshape(2, 64, -1)
    d_value, d_key, d_query, d_hidden, d_linear, d_output, d_gate, d_down = join_heads(
        block[0], swap(block[1]), (DV, DK, DK) + (DV,) * 5, scalars, "join_heads"
    )
    return (
        layer_out,
        input_grad,
        gain_first_grad,
        gain_second_grad,
        d_query,
        d_key,
        d_value,
        d_gate,
        d_output.T,
        d_hidden,
        d_linear,
        d_down.T,
    )


def solution(mesh):
    fine = Mesh(np.asarray(mesh.devices).reshape(4, 2, 4, 4), ("x", "core", "ctx", "tp"))
    split = ("x", "core", "ctx")
    row = P(split, None)
    win = P(split, "tp")
    wout = P("tp", split)
    in_specs = (row, row, P(), P(), win, win, win, win, wout, win, win, wout, P("tp"), P(("x", "core")))
    out_specs = (row, row, P(split), P(split), win, win, win, win, wout, win, win, wout)
    return jax.shard_map(
        per_device, mesh=fine, in_specs=in_specs, out_specs=out_specs, check_vma=False
    )
```

```python
import math

import jax
import jax.numpy as jnp
import numpy as np
from jax import lax
from jax.experimental import pallas as pl
from jax.experimental.pallas import tpu as pltpu
from jax.sharding import Mesh, PartitionSpec as P

D = 2048
DK = 256
DV = 512
SLAB = 512
BF = jnp.bfloat16
F32 = jnp.float32
XY = ("x", "ctx")
MIB = 1 << 20


def shift(value, axis, offset):
    n = lax.axis_size(axis)
    return lax.ppermute(value, axis, [(i, (i + offset) % n) for i in range(n)])


def shift_open(value, axis, offset):
    n = lax.axis_size(axis)
    return lax.ppermute(
        value, axis, [(i, i + offset) for i in range(n) if 0 <= i + offset < n]
    )


def swap(value):
    return lax.ppermute(value, "core", [(0, 1), (1, 0)])


def after(value, *earlier):
    return lax.optimization_barrier((value, *earlier))[0]


def call(
    body,
    grid,
    ins,
    outs,
    shapes,
    scalars,
    operands,
    name,
    scratch=(),
    deps=(),
    stream=False,
    aliases=None,
):
    count = len(operands)

    def kernel(s_ref, *refs):
        body(s_ref, *refs[:count], *refs[count + len(deps) :])

    ins = [*ins, *[pl.BlockSpec(memory_space=pl.ANY)] * len(deps)]
    return pl.pallas_call(
        kernel,
        out_shape=shapes,
        grid_spec=pltpu.PrefetchScalarGridSpec(
            num_scalar_prefetch=1, grid=grid, in_specs=ins, out_specs=outs, scratch_shapes=scratch
        ),
        compiler_params=pltpu.CompilerParams(
            vmem_limit_bytes=(60 if stream else 32) * MIB, dimension_semantics=("arbitrary",) * len(grid)
        ),
        cost_estimate=pl.CostEstimate(flops=1, bytes_accessed=1, transcendentals=0),
        input_output_aliases=aliases or {},
        name=name,
    )(scalars, *operands, *deps)


def tie(values, deps):
    count = len(values)
    anywhere = pl.BlockSpec(memory_space=pl.ANY)
    return pl.pallas_call(
        lambda *refs: None,
        out_shape=tuple(sds(v.shape, v.dtype) for v in values),
        in_specs=[anywhere] * (count + len(deps)),
        out_specs=(anywhere,) * count,
        input_output_aliases={i: i for i in range(count)},
        name="tie",
    )(*values, *deps)


def whole(array):
    return pl.BlockSpec(array.shape, lambda *_: (0,) * array.ndim)


def sds(shape, dtype):
    return jax.ShapeDtypeStruct(shape, dtype)


def weight_operands(weight, start, width):
    if not isinstance(weight, tuple):
        spec = pl.BlockSpec((1, 4, 2, 64, width), lambda i, s: (i, 0, 0, 0, start // width))
        return [weight], [spec]
    piece = math.gcd(start, width) if start else width
    operands, specs = [], []
    for at in range(start, start + width, piece):
        for stack in weight:
            operands.append(stack)
            specs.append(pl.BlockSpec((4, 2, 64, piece), lambda i, s, at=at: (0, 0, 0, at // piece)))
    return operands, specs


def load_slab(s_ref, refs, held):
    core = s_ref[0]
    if len(refs) == 1:
        return jnp.concatenate(
            [refs[0][0, y, jnp.bitwise_xor(c, core)] for c in (0, 1) for y in range(4)], axis=0
        )
    x_far = lax.rem(s_ref[2] + 4 - pl.program_id(0), 4)
    at = 0
    for first in range(0, len(refs), 4):
        stacks = refs[first : first + 4]
        width = stacks[0].shape[-1]
        for j in range(4):

            @pl.when((core == 0) & (x_far == j))
            def _(j=j, at=at, width=width, stacks=stacks):
                for i in range(4):
                    y = lax.rem(s_ref[3] + 4 - i, 4)
                    for c in (0, 1):
                        held[c * 4 + y, :, at : at + width] = stacks[j][i, c]

        @pl.when(core == 1)
        def _(at=at, width=width, stacks=stacks):
            for j in range(4):
                y = lax.rem(s_ref[3] + 4 - j, 4)
                for c in (0, 1):
                    held[c * 4 + y, :, at : at + width] = stacks[j][x_far, 1 - c]

        at += width
    return held[...].reshape(SLAB, at)


def hop(value, first, offset):
    pairs = []
    for x in range(4):
        for core in (0, 1):
            for y in range(4):
                to = ((x + offset) % 4, y) if (core == 0) == first else (x, (y + offset) % 4)
                pairs.append(((x * 2 + core) * 4 + y, (to[0] * 2 + core) * 4 + to[1]))
    return lax.ppermute(value, ("x", "core", "ctx"), pairs)


def spread_near(block):
    near, far, mid = [hop(block, False, o) for o in (1, 3, 2)]
    return block, near, mid, far


def stack_blocks(blocks, start, width, scalars, name, deps=()):
    at = start // width if start % width == 0 else None
    span = width if at is not None else blocks[0].shape[1]
    first = 0 if at is not None else start
    height = blocks[0].shape[0]

    def body(s_ref, *refs):
        for k, ref in enumerate(refs[:-1]):
            refs[-1][k * height : (k + 1) * height, :] = ref[:, first : first + width]

    total = sds((height * len(blocks), width), BF)
    return call(
        body,
        (1,),
        [pl.BlockSpec((height, span), lambda i, s: (0, at or 0))] * len(blocks),
        whole(total),
        total,
        scalars,
        tuple(blocks),
        name,
        deps=deps,
    )


def stack_attn(mine, came, scalars):
    height, total = mine.shape

    def body(s_ref, mine_ref, came_ref, first_ref, other_ref):
        for k, ref in enumerate((mine_ref, came_ref)):
            span = slice(k * height, (k + 1) * height)
            first_ref[span, :] = ref[:, :768]
            other_ref[span, :] = ref[:, 768:]

    shapes = (sds((2 * height, 768), BF), sds((2 * height, total - 768), BF))
    return call(
        body,
        (1,),
        [whole(mine), whole(came)],
        tuple(whole(s) for s in shapes),
        shapes,
        scalars,
        (mine, came),
        "stack_attn",
        stream=True,
    )


def spread_far(stack, gate=False):
    stack = stack.reshape(4, 2, 64, -1)
    near, far = hop(stack, True, 1), hop(stack, True, -1)
    mid = hop(tie((stack,), (near, far))[0] if gate else stack, True, 2)
    return stack, near, mid, far


def mm_in(left, right, columns, scalars, name, deps=(), stream=False):
    operands, specs, counts = [], [], []
    for weight, start, width in columns:
        ops, sp = weight_operands(weight, start, width)
        operands += ops
        specs += sp
        counts.append(len(ops))
    total = sum(width for _, _, width in columns)

    def body(s_ref, a_ref, b_ref, *refs):
        out_ref = refs[len(operands)]
        step = pl.program_id(0)
        rows = jnp.concatenate((a_ref[...], b_ref[...]), axis=0)
        at, first = 0, 0
        for k, count in enumerate(counts):
            width = columns[k][2]
            slab = load_slab(s_ref, refs[first : first + count], refs[len(operands) + 1 + k])
            part = jnp.dot(rows, slab, preferred_element_type=F32)
            span = slice(at, at + width)

            @pl.when(step == 0)
            def _(part=part, span=span):
                out_ref[:, span] = part

            @pl.when(step > 0)
            def _(part=part, span=span):
                out_ref[:, span] += part

            at += width
            first += count

    rows = left.shape[0]
    cols = pl.BlockSpec((rows, SLAB), lambda i, s: (0, i))
    return call(
        body,
        (4,),
        [cols, cols, *specs],
        pl.BlockSpec((2 * rows, total), lambda i, s: (0, 0)),
        sds((2 * rows, total), F32),
        scalars,
        (left, right, *operands),
        name,
        scratch=[pltpu.VMEM((8, 64, width), BF) for _, _, width in columns],
        deps=deps,
        stream=stream,
    )


def mm_back(terms, scalars, name, normed=None, deps=()):
    rows = terms[0][0].shape[0]
    half = rows // 2
    operands, specs, counts, scratch = [], [], [], []
    for grad, weight, start in terms:
        ops, sp = weight_operands(weight, start, grad.shape[1])
        operands += [grad, *ops]
        specs += [whole(grad), *sp]
        counts.append(len(ops))
        scratch.append(pltpu.VMEM((8, 64, grad.shape[1]), BF))
    held = len(operands)
    cols = pl.BlockSpec((half, SLAB), lambda i, s: (0, i))
    outs = [cols, cols]
    shapes = [sds((half, D), F32), sds((half, D), BF)]
    if normed is not None:
        operands += normed
        specs += [cols, cols]
        outs.append(pl.BlockSpec((8, SLAB), lambda i, s: (0, i)))
        shapes.append(sds((8, D), F32))
    total = len(operands)

    def body(s_ref, *refs):
        at, out = 0, 0.0
        for k, count in enumerate(counts):
            slab = load_slab(s_ref, refs[at + 1 : at + 1 + count], refs[total + len(outs) + k])
            out += lax.dot_general(
                refs[at][...], slab, (((1,), (1,)), ((), ())), preferred_element_type=F32
            )
            at += count + 1
        refs[total][...] = out[:half]
        refs[total + 1][...] = out[half:].astype(BF)
        if normed is not None:
            part = out[:half] * refs[held][...].astype(F32) + out[half:] * refs[held + 1][
                ...
            ].astype(F32)
            part = jnp.sum(part, axis=0, keepdims=True)
            refs[total + 2][...] = jnp.broadcast_to(part, (8, SLAB))

    return call(
        body,
        (4,),
        specs,
        tuple(outs),
        tuple(shapes),
        scalars,
        tuple(operands),
        name,
        scratch=scratch,
        deps=deps,
    )


def split_out(out, own_ref, other_ref):
    half = out.shape[0] // 2
    own_ref[...] = out[:half].astype(BF)
    other_ref[...] = out[half:].astype(BF)


def retain(x_pair, weight, key, value, came, rate, cosine, sine, scalars):
    rows = x_pair[0].shape[0]

    def body(
        s_ref, a_ref, b_ref, w_ref, k_ref, v_ref, near_ref, mid_ref, far_ref, r_ref, cos_ref,
        sin_ref, own_ref, other_ref, query_ref, state_ref, weighted_ref, gate_ref, retained_ref,
        mixed_ref, m_ref, e_ref, sums, turned
    ):
        step = pl.program_id(0)

        @pl.when(step == 0)
        def _():
            rate = r_ref[...]

            def place_of(shape, dim):
                index = lax.broadcasted_iota(jnp.int32, shape, dim)
                return lax.rem(index + s_ref[1] * (rows // 4), rows)

            left, right = place_of((rows, rows), 0), place_of((rows, rows), 1)
            column = place_of((rows, 1), 0)
            decay = jnp.exp(-rate * jnp.maximum(left - right, 0).astype(F32))
            for g in (0, 1):
                length = s_ref[4 + g] - s_ref[3] * rows
                linked = (left >= right) & ((left >= length) == (right >= length))
                m_ref[g] = jnp.where(linked, decay, 0.0)
                e_ref[g * rows : (g + 1) * rows] = jnp.where(
                    column >= length, 0.0, jnp.exp(-rate * (column.astype(F32) + 1.0))
                )

        @pl.when(step < 4)
        def _():
            slab = load_slab(s_ref, (w_ref,), None)
            turned[step] = slab[:, DV : 2 * DV]
            left = jnp.concatenate((a_ref[...], b_ref[...]), axis=0)
            gate = jnp.dot(left, slab[:, :DV], preferred_element_type=F32)
            query = jnp.dot(left, slab[:, 2 * DV :], preferred_element_type=F32)

            @pl.when(step == 0)
            def _():
                gate_ref[...] = gate
                sums[...] = query

            @pl.when(step > 0)
            def _():
                gate_ref[...] += gate
                sums[...] += query

        @pl.when(step == 3)
        def _():
            fade = jnp.exp(-r_ref[...] * rows)
            for g in (0, 1):
                span = slice(g * rows, (g + 1) * rows)
                state = near_ref[g].astype(F32) + fade * (
                    mid_ref[g].astype(F32) + fade * far_ref[g].astype(F32)
                )
                state_ref[g] = state.astype(BF)
                query = rotate(sums[span], cos_ref[...], sin_ref[...]).astype(BF)
                query_ref[span] = query
                scores = lax.dot_general(
                    query, k_ref[g], (((1,), (1,)), ((), ())), preferred_element_type=F32
                )
                weighted = (scores * m_ref[g]).astype(BF)
                weighted_ref[g] = weighted
                retained = jnp.dot(weighted, v_ref[g], preferred_element_type=F32)
                retained += e_ref[span] * jnp.dot(
                    query, state_ref[g], preferred_element_type=F32
                )
                retained_ref[span] = retained
                mixed_ref[span] = gate_norm(gate_ref[span], retained).astype(BF)

        @pl.when(step >= 4)
        def _():
            out = lax.dot_general(
                mixed_ref[...],
                turned[step - 4],
                (((1,), (1,)), ((), ())),
                preferred_element_type=F32,
            )
            split_out(out, own_ref, other_ref)

    cols = pl.BlockSpec((rows, SLAB), lambda i, s: (0, jnp.minimum(i, 3)))
    later = pl.BlockSpec((rows, SLAB), lambda i, s: (0, jnp.maximum(i - 4, 0)))
    operands = (*x_pair, weight, key, value, *came, rate, cosine, sine)
    shapes = (
        sds((rows, D), BF),
        sds((rows, D), BF),
        sds((2 * rows, DK), BF),
        sds((2, DK, DV), BF),
        sds((2, rows, rows), BF),
        sds((2 * rows, DV), F32),
        sds((2 * rows, DV), F32),
        sds((2 * rows, DV), BF),
        sds((2, rows, rows), F32),
        sds((2 * rows, 1), F32),
    )
    block = pl.BlockSpec((1, 4, 2, 64, 1280), lambda i, s: (jnp.minimum(i, 3), 0, 0, 0, 0))
    return call(
        body,
        (8,),
        [cols, cols, block] + [whole(o) for o in operands[3:]],
        (later, later) + tuple(whole(s) for s in shapes[2:]),
        shapes,
        scalars,
        operands,
        "retain",
        scratch=[pltpu.VMEM((2 * rows, DK), F32), pltpu.VMEM((4, SLAB, DV), BF)],
        stream=True,
    )


def mlp(x_pair, g_pair, weight, scalars):
    rows = x_pair[0].shape[0]

    def body(
        s_ref, a_ref, b_ref, c_ref, d_ref, w_ref, own_ref, other_ref, gain_ref, pair_ref, act_ref,
        both, back, kept
    ):
        step = pl.program_id(0)

        @pl.when(step < 4)
        def _():
            slab = load_slab(s_ref, (w_ref,), None)
            kept[step] = slab[:, : 2 * DV]
            left = jnp.concatenate((a_ref[...], b_ref[...]), axis=0)
            grad = jnp.concatenate((c_ref[...], d_ref[...]), axis=0)
            up = jnp.dot(left, slab[:, : 2 * DV], preferred_element_type=F32)
            down = jnp.dot(grad, slab[:, 2 * DV :], preferred_element_type=F32)

            @pl.when(step == 0)
            def _():
                both[...] = up
                back[...] = down

            @pl.when(step > 0)
            def _():
                both[...] += up
                back[...] += down

        @pl.when(step == 3)
        def _():
            def chunk(k, carry):
                span = pl.ds(pl.multiple_of(k * 64, 64), 64)
                hidden, linear, grad = both[span, :DV], both[span, DV:], back[span, :]
                cube = 0.044715 * hidden * hidden
                bent = jnp.tanh(0.7978845608 * hidden * (1.0 + cube))
                half = 0.5 * (1.0 + bent)
                gelu = hidden * half
                slope = half + 0.5 * hidden * (1.0 - bent * bent) * (
                    0.7978845608 * (1.0 + 3.0 * cube)
                )
                act_ref[span, :] = (gelu * linear).astype(BF)
                pair_ref[span, :DV] = (grad * linear * slope).astype(BF)
                pair_ref[span, DV:] = (grad * gelu).astype(BF)
                return carry

            lax.fori_loop(0, 2 * rows // 64, chunk, 0)

        @pl.when(step >= 4)
        def _():
            out = lax.dot_general(
                pair_ref[...], kept[step - 4], (((1,), (1,)), ((), ())), preferred_element_type=F32
            )
            split_out(out, own_ref, other_ref)
            part = out[:rows] * a_ref[...].astype(F32) + out[rows:] * b_ref[...].astype(F32)
            gain_ref[...] = jnp.broadcast_to(jnp.sum(part, axis=0, keepdims=True), (8, SLAB))

    cols = pl.BlockSpec((rows, SLAB), lambda i, s: (0, lax.rem(i, 4)))
    once = pl.BlockSpec((rows, SLAB), lambda i, s: (0, jnp.minimum(i, 3)))
    block = pl.BlockSpec((1, 4, 2, 64, 3 * DV), lambda i, s: (jnp.minimum(i, 3), 0, 0, 0, 0))
    later = pl.BlockSpec((rows, SLAB), lambda i, s: (0, jnp.maximum(i - 4, 0)))
    shapes = (
        sds((rows, D), BF),
        sds((rows, D), BF),
        sds((8, D), F32),
        sds((2 * rows, 2 * DV), BF),
        sds((2 * rows, DV), BF),
    )
    return call(
        body,
        (8,),
        [cols, cols, once, once, block],
        (
            later,
            later,
            pl.BlockSpec((8, SLAB), lambda i, s: (0, jnp.maximum(i - 4, 0))),
            whole(shapes[3]),
            whole(shapes[4]),
        ),
        shapes,
        scalars,
        (*x_pair, *g_pair, weight),
        "mlp",
        scratch=[
            pltpu.VMEM((2 * rows, 2 * DV), F32),
            pltpu.VMEM((2 * rows, DV), F32),
            pltpu.VMEM((4, SLAB, 2 * DV), BF),
        ],
        stream=True,
    )


def back_gate(g_pair, weight, gate_pre, retained, query, enter, scalars):
    rows = g_pair[0].shape[0]

    def body(
        s_ref, a_ref, b_ref, w_ref, gate_ref, kept_ref, q_ref, e_ref, dgate_ref, low_ref, state_ref,
        sums
    ):
        step = pl.program_id(0)
        left = jnp.concatenate((a_ref[...], b_ref[...]), axis=0)
        part = jnp.dot(left, load_slab(s_ref, (w_ref,), None), preferred_element_type=F32)

        @pl.when(step == 0)
        def _():
            sums[...] = part

        @pl.when(step > 0)
        def _():
            sums[...] += part

        @pl.when(step == 3)
        def _():
            def chunk(k, carry):
                span = pl.ds(pl.multiple_of(k * 64, 64), 64)
                gate, value, grad = gate_ref[span, :], kept_ref[span, :], sums[span, :]
                value = value - jnp.mean(value, axis=-1, keepdims=True)
                scale = lax.rsqrt(jnp.mean(value * value, axis=-1, keepdims=True) + 1.0 * DK)
                normed = value * scale
                open_part = jax.nn.sigmoid(gate)
                slope = open_part * (1.0 + gate * (1.0 - open_part))
                dgate_ref[span, :] = (grad * normed * slope).astype(BF)
                grad = grad * gate * open_part
                grad = grad - jnp.mean(grad, axis=-1, keepdims=True) - normed * jnp.mean(
                    grad * normed, axis=-1, keepdims=True
                )
                low_ref[span, :] = (grad * scale).astype(BF)
                return carry

            lax.fori_loop(0, 2 * rows // 64, chunk, 0)
            for g in (0, 1):
                span = slice(g * rows, (g + 1) * rows)
                entered = (q_ref[span].astype(F32) * e_ref[span]).astype(BF)
                state_ref[g] = lax.dot_general(
                    entered,
                    low_ref[span],
                    (((0,), (0,)), ((), ())),
                    preferred_element_type=F32,
                ).astype(BF)

    cols = pl.BlockSpec((rows, SLAB), lambda i, s: (0, i))
    operands = (*g_pair, weight, gate_pre, retained, query, enter)
    shapes = (
        sds((2 * rows, DV), BF),
        sds((2 * rows, DV), BF),
        sds((2, DK, DV), BF),
    )
    return call(
        body,
        (4,),
        [cols, cols, pl.BlockSpec((1, 4, 2, 64, DV), lambda i, s: (i, 0, 0, 0, 1))]
        + [whole(o) for o in operands[3:]],
        tuple(whole(s) for s in shapes),
        shapes,
        scalars,
        operands,
        "back_gate",
        scratch=[pltpu.VMEM((2 * rows, DV), F32)],
        stream=True,
    )


def weight_last(into, pair, came, fade, value, key_out, leave, grad_value, grad_key, cosine, sine,
                scalars):
    rows = pair[0].shape[0]

    def body(
        s_ref, a_ref, b_ref, near_ref, mid_ref, far_ref, f_ref, v_ref, k_ref, l_ref, gv_ref, gk_ref,
        cos_ref, sin_ref, into_ref, out_ref, mark_ref, grad_ref
    ):
        @pl.when(pl.program_id(0) == 0)
        def _():
            fade = f_ref[...]
            for g in (0, 1):
                span = slice(g * rows, (g + 1) * rows)
                state = near_ref[g].astype(F32) + fade * (
                    mid_ref[g].astype(F32) + fade * far_ref[g].astype(F32)
                )
                state = state.astype(BF)
                grad_ref[span, :DV] = (
                    gv_ref[g] + jnp.dot(k_ref[g], state, preferred_element_type=F32)
                ).astype(BF)
                grad_key = gk_ref[g] + l_ref[...] * lax.dot_general(
                    v_ref[g], state, (((1,), (1,)), ((), ())), preferred_element_type=F32
                )
                grad_ref[span, DV:] = rotate(grad_key, cos_ref[...], -sin_ref[...]).astype(BF)

        out = lax.dot_general(
            jnp.concatenate((a_ref[...], b_ref[...]), axis=0),
            grad_ref[...],
            (((0,), (0,)), ((), ())),
            preferred_element_type=F32,
        ).astype(BF)
        for c in (0, 1):
            for y in range(4):
                first = (c * 4 + y) * 64
                out_ref[0, y, jnp.bitwise_xor(c, s_ref[0])] = out[first : first + 64]
        mark_ref[...] = jnp.zeros_like(mark_ref)

    cols = pl.BlockSpec((rows, SLAB), lambda i, s: (0, i))
    operands = (*pair, *came, fade, value, key_out, leave, grad_value, grad_key, cosine, sine)
    shapes = (
        sds(into.shape, BF),
        sds((8, 128), F32),
        sds((2 * rows, DV + DK), BF),
    )
    return call(
        body,
        (4,),
        [cols, cols]
        + [whole(o) for o in operands[2:]]
        + [pl.BlockSpec(memory_space=pl.ANY)],
        (
            pl.BlockSpec((1, 4, 2, 64, DV + DK), lambda i, s: (i, 0, 0, 0, 0)),
            whole(shapes[1]),
            whole(shapes[2]),
        ),
        shapes,
        scalars,
        (*operands, into),
        "weight_last",
        stream=True,
        aliases={1 + len(operands): 0},
    )


def mm_weight_into(into, pairs, start, total, scalars, name, deps=()):
    widths = [grad.shape[1] for _, grad in pairs]
    rows = pairs[0][0][0].shape[0]
    span = sum(widths)

    def body(s_ref, *refs):
        out_ref, mark_ref = refs[-2:]
        at = 0
        for k, width in enumerate(widths):
            a_ref, b_ref, g_ref = refs[3 * k : 3 * k + 3]
            out = lax.dot_general(
                jnp.concatenate((a_ref[...], b_ref[...]), axis=0),
                g_ref[...],
                (((0,), (0,)), ((), ())),
                preferred_element_type=F32,
            ).astype(BF)
            for c in (0, 1):
                for y in range(4):
                    first = (c * 4 + y) * 64
                    out_ref[0, y, jnp.bitwise_xor(c, s_ref[0]), :, at : at + width] = out[
                        first : first + 64
                    ]
            at += width
        mark_ref[...] = jnp.zeros_like(mark_ref)

    cols = pl.BlockSpec((rows, SLAB), lambda i, s: (0, i))
    specs, operands = [], []
    for (a, b), grad in pairs:
        specs += [cols, cols, whole(grad)]
        operands += [a, b, grad]
    aliases = None
    if into is not None:
        aliases = {1 + len(operands): 0}
        specs.append(pl.BlockSpec(memory_space=pl.ANY))
        operands.append(into)
    return call(
        body,
        (4,),
        specs,
        (
            pl.BlockSpec((1, 4, 2, 64, span), lambda i, s: (i, 0, 0, 0, start // span)),
            pl.BlockSpec((8, 128), lambda i, s: (0, 0)),
        ),
        (sds((4, 4, 2, 64, total), BF), sds((8, 128), F32)),
        scalars,
        tuple(operands),
        name,
        deps=deps,
        stream=True,
        aliases=aliases,
    )


def split_heads(weights, scalars, name, deps=()):
    widths = [w.shape[1] // 2 for w in weights]

    def body(s_ref, *refs):
        mine_ref, theirs_ref = refs[-2:]
        core = s_ref[0]
        for out_ref, head in ((mine_ref, core), (theirs_ref, 1 - core)):
            at = 0
            for ref, width in zip(refs, widths):
                out_ref[:, at : at + width] = ref[:, pl.ds(pl.multiple_of(head * width, width), width)]
                at += width

    total = sum(widths)
    spec = pl.BlockSpec((64, total), lambda i, s: (0, 0))
    return call(
        body,
        (1,),
        [whole(w) for w in weights],
        (spec, spec),
        (sds((64, total), BF),) * 2,
        scalars,
        tuple(weights),
        name,
        deps=deps,
        stream=True,
    )


def join_heads(mine, theirs, widths, scalars, name):
    def body(s_ref, mine_ref, theirs_ref, *outs):
        core = s_ref[0]
        for in_ref, head in ((mine_ref, core), (theirs_ref, 1 - core)):
            at = 0
            for ref, width in zip(outs, widths):
                span = pl.ds(pl.multiple_of(head * width, width), width)
                ref[:, span] = in_ref[:, at : at + width].astype(F32)
                at += width

    shapes = tuple(sds((64, 2 * w), F32) for w in widths)
    return call(
        body,
        (1,),
        [whole(mine), whole(theirs)],
        tuple(whole(s) for s in shapes),
        shapes,
        scalars,
        (mine, theirs),
        name,
    )


def scale_of(values):
    return lax.rsqrt(jnp.mean(values * values, axis=-1, keepdims=True) + 1e-06)


def turned_spec(rows):
    return pl.BlockSpec((rows, D), lambda i, s: (lax.rem(i + s[1], 4), 0))


def plain_spec(rows):
    return pl.BlockSpec((rows, D), lambda i, s: (i, 0))


def enter_rows(tokens, gain, scalars, deps=()):
    rows = tokens.shape[0]
    block = rows // 4

    def body(s_ref, t_ref, g_ref, n_out):
        values = t_ref[...]
        n_out[...] = (values * scale_of(values) * g_ref[...]).astype(BF)

    return call(
        body,
        (4,),
        [turned_spec(block), whole(gain)],
        plain_spec(block),
        sds((rows, D), BF),
        scalars,
        (tokens, gain),
        "enter_rows",
        deps=deps,
    )


def low_rows(cotangent, scalars, deps=()):
    rows = cotangent.shape[0]
    block = rows // 4

    def body(s_ref, c_ref, l_out):
        l_out[...] = c_ref[...].astype(BF)

    return call(
        body,
        (4,),
        [turned_spec(block)],
        plain_spec(block),
        sds((rows, D), BF),
        scalars,
        (cotangent,),
        "low_rows",
        deps=deps,
    )


def each_part(refs, work):
    step = pl.program_id(0)
    for k, ref in enumerate(refs):

        @pl.when(step == k)
        def _(ref=ref):
            work(ref[...].astype(F32))


def second_norm(tokens, parts, gain, scalars, deps=()):
    rows = tokens.shape[0]
    block = rows // 4

    def body(s_ref, t_ref, g_ref, *refs):
        h_out, n_out = refs[4:]

        def work(part):
            values = t_ref[...] + part
            h_out[...] = values
            n_out[...] = (values * scale_of(values) * g_ref[...]).astype(BF)

        each_part(refs[:4], work)

    plain = plain_spec(block)
    return call(
        body,
        (4,),
        [turned_spec(block), whole(gain)] + [whole(p) for p in parts],
        (plain, plain),
        (sds((rows, D), F32), sds((rows, D), BF)),
        scalars,
        (tokens, gain, *parts),
        "second_norm",
        deps=deps,
    )


def third_blocks(own, came, down_own, down_came, scalars, deps=()):
    rows = own.shape[0]
    block = rows // 4

    def body(s_ref, own_ref, came_ref, d_ref, e_ref, *refs):
        total = own_ref[...] + came_ref[...].astype(F32)
        down = d_ref[...] + e_ref[...].astype(F32)
        step = pl.program_id(0)
        for k in range(4):

            @pl.when(step == k)
            def _(k=k):
                refs[k][:block] = total.astype(BF)
                refs[k][block:] = down.astype(BF)

    plain = plain_spec(block)
    shapes = (sds((2 * block, D), BF),) * 4
    return call(
        body,
        (4,),
        [plain] * 4,
        tuple(whole(s) for s in shapes),
        shapes,
        scalars,
        (own, came, down_own, down_came),
        "third_blocks",
        deps=deps,
        stream=True,
    )


def leave_rows(hidden, tokens, grad_state, parts, gain, scalars, deps=()):
    rows = hidden.shape[0]
    block = rows // 4

    def body(s_ref, h_ref, t_ref, u_ref, g_ref, *refs):
        def work(part):
            refs[4][...] = h_ref[...] + part[block : 2 * block]
            refs[5][...] = u_ref[...] + norm_grad(t_ref[...], part[:block], g_ref[...])

        each_part(refs[:4], work)

    plain, turn = plain_spec(block), turned_spec(block)
    return call(
        body,
        (4,),
        [plain, turn, plain, whole(gain)] + [whole(p) for p in parts],
        (turn, turn),
        (sds((rows, D), F32),) * 2,
        scalars,
        (hidden, tokens, grad_state, gain, *parts),
        "leave_rows",
        deps=deps,
        stream=True,
    )


def norm_grad(values, grad, gain):
    factor = scale_of(values)
    unit = values * factor
    scaled = grad * gain
    return factor * (scaled - unit * jnp.mean(scaled * unit, axis=-1, keepdims=True))


def norm_back(values, upstream, parts, gain, scalars, name, deps=()):
    rows = values.shape[0]
    block = rows // 4

    def body(s_ref, v_ref, u_ref, g_ref, *refs):
        def work(part):
            out = u_ref[...] + norm_grad(v_ref[...], part, g_ref[...])
            refs[4][...] = out
            refs[5][...] = out.astype(BF)

        each_part(refs[:4], work)

    plain = plain_spec(block)
    return call(
        body,
        (4,),
        [plain, turned_spec(block), whole(gain)] + [whole(p) for p in parts],
        (plain, plain),
        (sds((rows, D), F32), sds((rows, D), BF)),
        scalars,
        (values, upstream, gain, *parts),
        name,
        deps=deps,
        stream=True,
    )


def tp_first(blocks):
    got = [shift(blocks[o], "tp", o) for o in (1, 3, 2)]
    near, far, mid = [part.astype(F32) for part in got]
    return (blocks[0].astype(F32) + mid) + (near + far), got


def tp_second(mine):
    near, far, mid = [shift(mine, "tp", -o) for o in (1, 3, 2)]
    return mine, near, mid, far


def tp_total(blocks):
    return tp_second(tp_first(blocks)[0].astype(BF))


def chip_blocks(own, came):
    block = own.shape[0] // 4
    spans = [slice(o * block, (o + 1) * block) for o in range(4)]
    return [(own[span].astype(F32) + came[span].astype(F32)).astype(BF) for span in spans]


def gate_norm(gate_pre, retained):
    centred = retained - jnp.mean(retained, axis=-1, keepdims=True)
    normed = centred * lax.rsqrt(jnp.mean(centred * centred, axis=-1, keepdims=True) + 1.0 * DK)
    return gate_pre * jax.nn.sigmoid(gate_pre) * normed


def gelu_gate(hidden, linear):
    return jax.nn.gelu(hidden, approximate=True) * linear


def rotate(values, cosine, sine):
    half = DK // 2
    first = values[..., :half]
    second = values[..., half:]
    return jnp.concatenate((first * cosine - second * sine, first * sine + second * cosine), axis=-1)


def ein(spec, left, right):
    return jnp.einsum(spec, left, right, preferred_element_type=F32)


def per_device(
    tokens,
    cotangent,
    gain_first,
    gain_second,
    w_query,
    w_key,
    w_value,
    w_gate,
    w_output,
    w_hidden,
    w_linear,
    w_down,
    decay_scale,
    first_length,
):
    rows = tokens.shape[0]
    core = lax.axis_index("core")
    place = lax.axis_index("ctx")
    plane = lax.axis_index("tp")
    scalars = jnp.stack((core, plane, lax.axis_index("x"), place)).astype(jnp.int32)

    w_output = w_output.T
    w_down = w_down.T
    mine, theirs = split_heads((w_value, w_key, w_gate, w_output, w_query), scalars, "split_attn")
    came = swap(theirs)
    block, gathered = stack_attn(mine, came, scalars)
    lengths = jnp.concatenate((first_length, swap(first_length)))
    blocks = spread_near(block)
    w_kv = stack_blocks(blocks, 0, 768, scalars, "stack_kv")
    normed_first = enter_rows(tokens, gain_first.reshape(1, D), scalars, deps=blocks[1:])
    w_goq = lax.all_gather(gathered, XY, axis=0, tiled=True).reshape(4, 4, 2, 64, -1)
    mine, theirs = split_heads(
        (w_hidden, w_linear, w_down), scalars, "split_mlp", deps=(normed_first,)
    )
    came_mlp = swap(theirs)
    gain_first = gain_first.reshape(1, D)
    gain_second = gain_second.reshape(1, D)
    x_first = (normed_first, swap(normed_first))
    cot_low = low_rows(cotangent, scalars, deps=(x_first[1],))
    g_out = (cot_low, swap(cot_low))
    w_kv = spread_far(w_kv)

    rate = lax.dynamic_index_in_dim(decay_scale, core, 0, False) / 1024.0
    local = (jnp.arange(rows, dtype=jnp.int32) + plane * (rows // 4)) % rows
    index = place * rows + local
    steps = local.astype(F32)
    leave = jnp.exp(-rate * (rows - 1.0 - steps))[None, :, None]
    fade = jnp.exp(-rate * rows)
    half = DK // 2
    frequency = 10000.0 ** (-(jnp.arange(half).astype(F32) / half))
    angles = index.astype(F32)[:, None] * frequency[None, :]
    cosine = jnp.cos(angles)
    sine = jnp.sin(angles)

    def spread_state(low, way):
        return [shift_open(low, "ctx", way * o) for o in (1, 2, 3)]

    leave_rows_out = leave.reshape(rows, 1)
    fade_in = fade.reshape(1, 1)
    projected = mm_in(*x_first, [(w_kv, 0, 768)], scalars, "project_kv", deps=(came_mlp,))
    key = rotate(projected[:, DV:].reshape(2, rows, DK), cosine, sine).astype(BF)
    value = projected[:, :DV].astype(BF).reshape(2, rows, DV)
    key_out = (key.astype(F32) * leave).astype(BF)
    state_out = ein("gjd,gje->gde", key_out, value).astype(BF)
    came = spread_state(state_out, 1)
    w_mlp = lax.all_gather(
        stack_blocks((mine, came_mlp), 0, 1536, scalars, "stack_mlp", deps=(state_out,)),
        XY,
        axis=0,
        tiled=True,
    ).reshape(4, 4, 2, 64, -1)
    own, other, query, state_in, weighted, gate_pre, retained, mixed, mask, enter_rows_in = retain(
        x_first,
        w_goq,
        key,
        value,
        came,
        rate.reshape(1, 1),
        cosine,
        sine,
        jnp.concatenate((scalars, lengths)),
    )
    enter = enter_rows_in.reshape(2, rows, 1)
    query = query.reshape(2, rows, DK)
    parts = tp_total(chip_blocks(own, swap(other)))
    hidden_state, normed_second = second_norm(tokens, parts, gain_second, scalars)
    x_second = (normed_second, swap(normed_second))
    own, other, gain_second_part, grad_pair, activated = mlp(x_second, g_out, w_mlp, scalars)
    grads, mark = mm_weight_into(
        None, ((x_second, grad_pair),), 1024, 3584, scalars, "weight_mlp"
    )
    mine, _ = tp_first(chip_blocks(own, swap(other)))
    (mine,) = tie((mine.astype(BF),), (mark,))
    parts = tp_second(mine)
    down = mm_back([(activated, w_mlp, 2 * DV)], scalars, "project_down", deps=(mine,))
    grad_state, grad_state_low = norm_back(
        hidden_state,
        cotangent,
        parts,
        gain_second,
        scalars,
        "second_back",
        deps=(down[1],),
    )
    g_state = (grad_state_low, swap(grad_state_low))
    grad_gate, grad_low, back_out = back_gate(
        g_state, w_goq, gate_pre, retained, query.reshape(2 * rows, DK), enter_rows_in, scalars
    )
    grad_low = grad_low.reshape(2, rows, DV)
    came = spread_state(back_out, -1)
    grad_scores = (ein("gie,gje->gij", grad_low, value) * mask).astype(BF)
    grad_query = ein("gij,gjd->gid", grad_scores, key) + enter * ein("gie,gde->gid", grad_low, state_in)
    grad_key = ein("gij,gid->gjd", grad_scores, query)
    grad_value = ein("gij,gie->gje", weighted, grad_low)
    grad_query = rotate(grad_query, cosine, -sine).astype(BF).reshape(2 * rows, DK)
    grads, mark = mm_weight_into(
        grads,
        ((g_state, mixed), (x_first, grad_gate)),
        2048,
        3584,
        scalars,
        "weight_og",
        deps=(back_out,),
    )
    grads, mark = mm_weight_into(
        grads, ((g_out, activated),), 3072, 3584, scalars, "weight_down"
    )
    grads, mark = mm_weight_into(
        grads, ((x_first, grad_query),), 768, 3584, scalars, "weight_query"
    )
    came[0] = tie((came[0],), (mark, grad_key, grad_value))[0]
    grads, mark, grad_vk = weight_last(
        grads,
        x_first,
        came,
        fade_in,
        value,
        key_out,
        leave_rows_out,
        grad_value,
        grad_key,
        cosine,
        sine,
        scalars,
    )
    block = lax.psum_scatter(grads.reshape(2048, -1), XY, scatter_dimension=0, tiled=True)
    own, other, gain_first_part = mm_back(
        [(grad_vk, w_kv, 0), (grad_gate, w_goq, 0), (grad_query, w_goq, 1024)],
        scalars,
        "back_attn",
        normed=x_first,
        deps=(mark,),
    )
    down = (down[0], swap(tie((down[1],), (mark,))[0]))
    blocks = third_blocks(own, swap(other), *down, scalars)
    mine, _ = tp_first(blocks)
    gains = jnp.concatenate((gain_first_part[:1], gain_second_part[:1]))
    for axis, swapped in (
        ("core", (1, 0)),
        ("ctx", (1, 0, 3, 2)),
        ("ctx", (3, 2, 1, 0)),
        ("x", (1, 0, 3, 2)),
        ("x", (3, 2, 1, 0)),
    ):
        gains = gains + lax.ppermute(gains, axis, list(enumerate(swapped)))
    mine = jnp.concatenate((mine, gains, jnp.zeros((14, D), F32))).astype(BF)
    parts = tp_second(mine)
    gains = [part[128:130].astype(F32) for part in parts]
    gains = (gains[0] + gains[2]) + (gains[1] + gains[3])
    spot = (lax.axis_index("x") * 2 + core) * 4 + place
    gain_first_grad, gain_second_grad = [
        lax.dynamic_slice_in_dim(gains[k] / gain[0], spot * 64, 64, 0)
        for k, gain in ((0, gain_first), (1, gain_second))
    ]
    layer_out, input_grad = leave_rows(
        hidden_state, tokens, grad_state, parts, gain_first, scalars
    )
    block = tie((block,), (gain_first_grad, gain_second_grad, input_grad))[0].reshape(2, 64, -1)
    d_value, d_key, d_query, d_hidden, d_linear, d_output, d_gate, d_down = join_heads(
        block[0], swap(block[1]), (DV, DK, DK) + (DV,) * 5, scalars, "join_heads"
    )
    return (
        layer_out,
        input_grad,
        gain_first_grad,
        gain_second_grad,
        d_query,
        d_key,
        d_value,
        d_gate,
        d_output.T,
        d_hidden,
        d_linear,
        d_down.T,
    )


def solution(mesh):
    fine = Mesh(np.asarray(mesh.devices).reshape(4, 2, 4, 4), ("x", "core", "ctx", "tp"))
    split = ("x", "core", "ctx")
    row = P(split, None)
    win = P(split, "tp")
    wout = P("tp", split)
    in_specs = (row, row, P(), P(), win, win, win, win, wout, win, win, wout, P("tp"), P(("x", "core")))
    out_specs = (row, row, P(split), P(split), win, win, win, win, wout, win, win, wout)
    return jax.shard_map(
        per_device, mesh=fine, in_specs=in_specs, out_specs=out_specs, check_vma=False
    )
```

```python
import math

import jax
import jax.numpy as jnp
import numpy as np
from jax import lax
from jax.experimental import pallas as pl
from jax.experimental.pallas import tpu as pltpu
from jax.sharding import Mesh, PartitionSpec as P

D = 2048
DK = 256
DV = 512
SLAB = 512
BF = jnp.bfloat16
F32 = jnp.float32
XY = ("x", "ctx")
MIB = 1 << 20


def shift(value, axis, offset):
    n = lax.axis_size(axis)
    return lax.ppermute(value, axis, [(i, (i + offset) % n) for i in range(n)])


def shift_open(value, axis, offset):
    n = lax.axis_size(axis)
    return lax.ppermute(
        value, axis, [(i, i + offset) for i in range(n) if 0 <= i + offset < n]
    )


def swap(value):
    return lax.ppermute(value, "core", [(0, 1), (1, 0)])


def after(value, *earlier):
    return lax.optimization_barrier((value, *earlier))[0]


def call(
    body,
    grid,
    ins,
    outs,
    shapes,
    scalars,
    operands,
    name,
    scratch=(),
    deps=(),
    stream=False,
    aliases=None,
):
    count = len(operands)

    def kernel(s_ref, *refs):
        body(s_ref, *refs[:count], *refs[count + len(deps) :])

    ins = [*ins, *[pl.BlockSpec(memory_space=pl.ANY)] * len(deps)]
    return pl.pallas_call(
        kernel,
        out_shape=shapes,
        grid_spec=pltpu.PrefetchScalarGridSpec(
            num_scalar_prefetch=1, grid=grid, in_specs=ins, out_specs=outs, scratch_shapes=scratch
        ),
        compiler_params=pltpu.CompilerParams(
            vmem_limit_bytes=(60 if stream else 32) * MIB, dimension_semantics=("arbitrary",) * len(grid)
        ),
        cost_estimate=pl.CostEstimate(flops=1, bytes_accessed=1, transcendentals=0),
        input_output_aliases=aliases or {},
        name=name,
    )(scalars, *operands, *deps)


def tie(values, deps):
    count = len(values)
    anywhere = pl.BlockSpec(memory_space=pl.ANY)
    return pl.pallas_call(
        lambda *refs: None,
        out_shape=tuple(sds(v.shape, v.dtype) for v in values),
        in_specs=[anywhere] * (count + len(deps)),
        out_specs=(anywhere,) * count,
        input_output_aliases={i: i for i in range(count)},
        name="tie",
    )(*values, *deps)


def whole(array):
    return pl.BlockSpec(array.shape, lambda *_: (0,) * array.ndim)


def sds(shape, dtype):
    return jax.ShapeDtypeStruct(shape, dtype)


def weight_operands(weight, start, width):
    if not isinstance(weight, tuple):
        spec = pl.BlockSpec((1, 4, 2, 64, width), lambda i, s: (i, 0, 0, 0, start // width))
        return [weight], [spec]
    piece = math.gcd(start, width) if start else width
    operands, specs = [], []
    for at in range(start, start + width, piece):
        for stack in weight:
            operands.append(stack)
            specs.append(pl.BlockSpec((4, 2, 64, piece), lambda i, s, at=at: (0, 0, 0, at // piece)))
    return operands, specs


def load_slab(s_ref, refs, held):
    core = s_ref[0]
    if len(refs) == 1:
        return jnp.concatenate(
            [refs[0][0, y, jnp.bitwise_xor(c, core)] for c in (0, 1) for y in range(4)], axis=0
        )
    x_far = lax.rem(s_ref[2] + 4 - pl.program_id(0), 4)
    at = 0
    for first in range(0, len(refs), 4):
        stacks = refs[first : first + 4]
        width = stacks[0].shape[-1]
        for j in range(4):

            @pl.when((core == 0) & (x_far == j))
            def _(j=j, at=at, width=width, stacks=stacks):
                for i in range(4):
                    y = lax.rem(s_ref[3] + 4 - i, 4)
                    for c in (0, 1):
                        held[c * 4 + y, :, at : at + width] = stacks[j][i, c]

        @pl.when(core == 1)
        def _(at=at, width=width, stacks=stacks):
            for j in range(4):
                y = lax.rem(s_ref[3] + 4 - j, 4)
                for c in (0, 1):
                    held[c * 4 + y, :, at : at + width] = stacks[j][x_far, 1 - c]

        at += width
    return held[...].reshape(SLAB, at)


def hop(value, first, offset):
    pairs = []
    for x in range(4):
        for core in (0, 1):
            for y in range(4):
                to = ((x + offset) % 4, y) if (core == 0) == first else (x, (y + offset) % 4)
                pairs.append(((x * 2 + core) * 4 + y, (to[0] * 2 + core) * 4 + to[1]))
    return lax.ppermute(value, ("x", "core", "ctx"), pairs)


def spread_near(block):
    near, far, mid = [hop(block, False, o) for o in (1, 3, 2)]
    return block, near, mid, far


def stack_blocks(blocks, start, width, scalars, name, deps=()):
    at = start // width if start % width == 0 else None
    span = width if at is not None else blocks[0].shape[1]
    first = 0 if at is not None else start
    height = blocks[0].shape[0]

    def body(s_ref, *refs):
        for k, ref in enumerate(refs[:-1]):
            refs[-1][k * height : (k + 1) * height, :] = ref[:, first : first + width]

    total = sds((height * len(blocks), width), BF)
    return call(
        body,
        (1,),
        [pl.BlockSpec((height, span), lambda i, s: (0, at or 0))] * len(blocks),
        whole(total),
        total,
        scalars,
        tuple(blocks),
        name,
        deps=deps,
    )


def stack_attn(mine, came, scalars):
    height, total = mine.shape

    def body(s_ref, mine_ref, came_ref, first_ref, other_ref):
        for k, ref in enumerate((mine_ref, came_ref)):
            span = slice(k * height, (k + 1) * height)
            first_ref[span, :] = ref[:, :768]
            other_ref[span, :] = ref[:, 768:]

    shapes = (sds((2 * height, 768), BF), sds((2 * height, total - 768), BF))
    return call(
        body,
        (1,),
        [whole(mine), whole(came)],
        tuple(whole(s) for s in shapes),
        shapes,
        scalars,
        (mine, came),
        "stack_attn",
        stream=True,
    )


def spread_far(stack, gate=False):
    stack = stack.reshape(4, 2, 64, -1)
    near, far = hop(stack, True, 1), hop(stack, True, -1)
    mid = hop(tie((stack,), (near, far))[0] if gate else stack, True, 2)
    return stack, near, mid, far


def mm_in(left, right, columns, scalars, name, deps=(), stream=False):
    operands, specs, counts = [], [], []
    for weight, start, width in columns:
        ops, sp = weight_operands(weight, start, width)
        operands += ops
        specs += sp
        counts.append(len(ops))
    total = sum(width for _, _, width in columns)

    def body(s_ref, a_ref, b_ref, *refs):
        out_ref = refs[len(operands)]
        step = pl.program_id(0)
        rows = jnp.concatenate((a_ref[...], b_ref[...]), axis=0)
        at, first = 0, 0
        for k, count in enumerate(counts):
            width = columns[k][2]
            slab = load_slab(s_ref, refs[first : first + count], refs[len(operands) + 1 + k])
            part = jnp.dot(rows, slab, preferred_element_type=F32)
            span = slice(at, at + width)

            @pl.when(step == 0)
            def _(part=part, span=span):
                out_ref[:, span] = part

            @pl.when(step > 0)
            def _(part=part, span=span):
                out_ref[:, span] += part

            at += width
            first += count

    rows = left.shape[0]
    cols = pl.BlockSpec((rows, SLAB), lambda i, s: (0, i))
    return call(
        body,
        (4,),
        [cols, cols, *specs],
        pl.BlockSpec((2 * rows, total), lambda i, s: (0, 0)),
        sds((2 * rows, total), F32),
        scalars,
        (left, right, *operands),
        name,
        scratch=[pltpu.VMEM((8, 64, width), BF) for _, _, width in columns],
        deps=deps,
        stream=stream,
    )


def mm_back(terms, scalars, name, normed=None, deps=()):
    rows = terms[0][0].shape[0]
    half = rows // 2
    operands, specs, counts, scratch = [], [], [], []
    for grad, weight, start in terms:
        ops, sp = weight_operands(weight, start, grad.shape[1])
        operands += [grad, *ops]
        specs += [whole(grad), *sp]
        counts.append(len(ops))
        scratch.append(pltpu.VMEM((8, 64, grad.shape[1]), BF))
    held = len(operands)
    cols = pl.BlockSpec((half, SLAB), lambda i, s: (0, i))
    outs = [cols, cols]
    shapes = [sds((half, D), F32), sds((half, D), BF)]
    if normed is not None:
        operands += normed
        specs += [cols, cols]
        outs.append(pl.BlockSpec((8, SLAB), lambda i, s: (0, i)))
        shapes.append(sds((8, D), F32))
    total = len(operands)

    def body(s_ref, *refs):
        at, out = 0, 0.0
        for k, count in enumerate(counts):
            slab = load_slab(s_ref, refs[at + 1 : at + 1 + count], refs[total + len(outs) + k])
            out += lax.dot_general(
                refs[at][...], slab, (((1,), (1,)), ((), ())), preferred_element_type=F32
            )
            at += count + 1
        refs[total][...] = out[:half]
        refs[total + 1][...] = out[half:].astype(BF)
        if normed is not None:
            part = out[:half] * refs[held][...].astype(F32) + out[half:] * refs[held + 1][
                ...
            ].astype(F32)
            part = jnp.sum(part, axis=0, keepdims=True)
            refs[total + 2][...] = jnp.broadcast_to(part, (8, SLAB))

    return call(
        body,
        (4,),
        specs,
        tuple(outs),
        tuple(shapes),
        scalars,
        tuple(operands),
        name,
        scratch=scratch,
        deps=deps,
    )


def split_out(out, own_ref, other_ref):
    half = out.shape[0] // 2
    own_ref[...] = out[:half].astype(BF)
    other_ref[...] = out[half:].astype(BF)


def retain(x_pair, weight, key, value, came, rate, cosine, sine, scalars):
    rows = x_pair[0].shape[0]

    def body(
        s_ref, a_ref, b_ref, w_ref, k_ref, v_ref, near_ref, mid_ref, far_ref, r_ref, cos_ref,
        sin_ref, own_ref, other_ref, query_ref, state_ref, weighted_ref, gate_ref, retained_ref,
        mixed_ref, m_ref, e_ref, sums, turned
    ):
        step = pl.program_id(0)

        @pl.when(step == 0)
        def _():
            rate = r_ref[...]

            def place_of(shape, dim):
                index = lax.broadcasted_iota(jnp.int32, shape, dim)
                return lax.rem(index + s_ref[1] * (rows // 4), rows)

            left, right = place_of((rows, rows), 0), place_of((rows, rows), 1)
            column = place_of((rows, 1), 0)
            decay = jnp.exp(-rate * jnp.maximum(left - right, 0).astype(F32))
            for g in (0, 1):
                length = s_ref[4 + g] - s_ref[3] * rows
                linked = (left >= right) & ((left >= length) == (right >= length))
                m_ref[g] = jnp.where(linked, decay, 0.0)
                e_ref[g * rows : (g + 1) * rows] = jnp.where(
                    column >= length, 0.0, jnp.exp(-rate * (column.astype(F32) + 1.0))
                )

        @pl.when(step < 4)
        def _():
            slab = load_slab(s_ref, (w_ref,), None)
            turned[step] = slab[:, DV : 2 * DV]
            left = jnp.concatenate((a_ref[...], b_ref[...]), axis=0)
            gate = jnp.dot(left, slab[:, :DV], preferred_element_type=F32)
            query = jnp.dot(left, slab[:, 2 * DV :], preferred_element_type=F32)

            @pl.when(step == 0)
            def _():
                gate_ref[...] = gate
                sums[...] = query

            @pl.when(step > 0)
            def _():
                gate_ref[...] += gate
                sums[...] += query

        @pl.when(step == 3)
        def _():
            fade = jnp.exp(-r_ref[...] * rows)
            for g in (0, 1):
                span = slice(g * rows, (g + 1) * rows)
                state = near_ref[g].astype(F32) + fade * (
                    mid_ref[g].astype(F32) + fade * far_ref[g].astype(F32)
                )
                state_ref[g] = state.astype(BF)
                query = rotate(sums[span], cos_ref[...], sin_ref[...]).astype(BF)
                query_ref[span] = query
                scores = lax.dot_general(
                    query, k_ref[g], (((1,), (1,)), ((), ())), preferred_element_type=F32
                )
                weighted = (scores * m_ref[g]).astype(BF)
                weighted_ref[g] = weighted
                retained = jnp.dot(weighted, v_ref[g], preferred_element_type=F32)
                retained += e_ref[span] * jnp.dot(
                    query, state_ref[g], preferred_element_type=F32
                )
                retained_ref[span] = retained
                mixed_ref[span] = gate_norm(gate_ref[span], retained).astype(BF)

        @pl.when(step >= 4)
        def _():
            out = lax.dot_general(
                mixed_ref[...],
                turned[step - 4],
                (((1,), (1,)), ((), ())),
                preferred_element_type=F32,
            )
            split_out(out, own_ref, other_ref)

    cols = pl.BlockSpec((rows, SLAB), lambda i, s: (0, jnp.minimum(i, 3)))
    later = pl.BlockSpec((rows, SLAB), lambda i, s: (0, jnp.maximum(i - 4, 0)))
    operands = (*x_pair, weight, key, value, *came, rate, cosine, sine)
    shapes = (
        sds((rows, D), BF),
        sds((rows, D), BF),
        sds((2 * rows, DK), BF),
        sds((2, DK, DV), BF),
        sds((2, rows, rows), BF),
        sds((2 * rows, DV), F32),
        sds((2 * rows, DV), F32),
        sds((2 * rows, DV), BF),
        sds((2, rows, rows), F32),
        sds((2 * rows, 1), F32),
    )
    block = pl.BlockSpec((1, 4, 2, 64, 1280), lambda i, s: (jnp.minimum(i, 3), 0, 0, 0, 0))
    return call(
        body,
        (8,),
        [cols, cols, block] + [whole(o) for o in operands[3:]],
        (later, later) + tuple(whole(s) for s in shapes[2:]),
        shapes,
        scalars,
        operands,
        "retain",
        scratch=[pltpu.VMEM((2 * rows, DK), F32), pltpu.VMEM((4, SLAB, DV), BF)],
        stream=True,
    )


def mlp(x_pair, g_pair, weight, scalars):
    rows = x_pair[0].shape[0]

    def body(
        s_ref, a_ref, b_ref, c_ref, d_ref, w_ref, own_ref, other_ref, gain_ref, pair_ref, act_ref,
        both, back, kept
    ):
        step = pl.program_id(0)

        @pl.when(step < 4)
        def _():
            slab = load_slab(s_ref, (w_ref,), None)
            kept[step] = slab[:, : 2 * DV]
            left = jnp.concatenate((a_ref[...], b_ref[...]), axis=0)
            grad = jnp.concatenate((c_ref[...], d_ref[...]), axis=0)
            up = jnp.dot(left, slab[:, : 2 * DV], preferred_element_type=F32)
            down = jnp.dot(grad, slab[:, 2 * DV :], preferred_element_type=F32)

            @pl.when(step == 0)
            def _():
                both[...] = up
                back[...] = down

            @pl.when(step > 0)
            def _():
                both[...] += up
                back[...] += down

        @pl.when(step == 3)
        def _():
            def chunk(k, carry):
                span = pl.ds(pl.multiple_of(k * 64, 64), 64)
                hidden, linear, grad = both[span, :DV], both[span, DV:], back[span, :]
                cube = 0.044715 * hidden * hidden
                bent = jnp.tanh(0.7978845608 * hidden * (1.0 + cube))
                half = 0.5 * (1.0 + bent)
                gelu = hidden * half
                slope = half + 0.5 * hidden * (1.0 - bent * bent) * (
                    0.7978845608 * (1.0 + 3.0 * cube)
                )
                act_ref[span, :] = (gelu * linear).astype(BF)
                pair_ref[span, :DV] = (grad * linear * slope).astype(BF)
                pair_ref[span, DV:] = (grad * gelu).astype(BF)
                return carry

            lax.fori_loop(0, 2 * rows // 64, chunk, 0)

        @pl.when(step >= 4)
        def _():
            out = lax.dot_general(
                pair_ref[...], kept[step - 4], (((1,), (1,)), ((), ())), preferred_element_type=F32
            )
            split_out(out, own_ref, other_ref)
            part = out[:rows] * a_ref[...].astype(F32) + out[rows:] * b_ref[...].astype(F32)
            gain_ref[...] = jnp.broadcast_to(jnp.sum(part, axis=0, keepdims=True), (8, SLAB))

    cols = pl.BlockSpec((rows, SLAB), lambda i, s: (0, lax.rem(i, 4)))
    once = pl.BlockSpec((rows, SLAB), lambda i, s: (0, jnp.minimum(i, 3)))
    block = pl.BlockSpec((1, 4, 2, 64, 3 * DV), lambda i, s: (jnp.minimum(i, 3), 0, 0, 0, 0))
    later = pl.BlockSpec((rows, SLAB), lambda i, s: (0, jnp.maximum(i - 4, 0)))
    shapes = (
        sds((rows, D), BF),
        sds((rows, D), BF),
        sds((8, D), F32),
        sds((2 * rows, 2 * DV), BF),
        sds((2 * rows, DV), BF),
    )
    return call(
        body,
        (8,),
        [cols, cols, once, once, block],
        (
            later,
            later,
            pl.BlockSpec((8, SLAB), lambda i, s: (0, jnp.maximum(i - 4, 0))),
            whole(shapes[3]),
            whole(shapes[4]),
        ),
        shapes,
        scalars,
        (*x_pair, *g_pair, weight),
        "mlp",
        scratch=[
            pltpu.VMEM((2 * rows, 2 * DV), F32),
            pltpu.VMEM((2 * rows, DV), F32),
            pltpu.VMEM((4, SLAB, 2 * DV), BF),
        ],
        stream=True,
    )


def back_gate(g_pair, weight, gate_pre, retained, query, enter, scalars):
    rows = g_pair[0].shape[0]

    def body(
        s_ref, a_ref, b_ref, w_ref, gate_ref, kept_ref, q_ref, e_ref, dgate_ref, low_ref, state_ref,
        sums
    ):
        step = pl.program_id(0)
        left = jnp.concatenate((a_ref[...], b_ref[...]), axis=0)
        part = jnp.dot(left, load_slab(s_ref, (w_ref,), None), preferred_element_type=F32)

        @pl.when(step == 0)
        def _():
            sums[...] = part

        @pl.when(step > 0)
        def _():
            sums[...] += part

        @pl.when(step == 3)
        def _():
            def chunk(k, carry):
                span = pl.ds(pl.multiple_of(k * 64, 64), 64)
                gate, value, grad = gate_ref[span, :], kept_ref[span, :], sums[span, :]
                value = value - jnp.mean(value, axis=-1, keepdims=True)
                scale = lax.rsqrt(jnp.mean(value * value, axis=-1, keepdims=True) + 1.0 * DK)
                normed = value * scale
                open_part = jax.nn.sigmoid(gate)
                slope = open_part * (1.0 + gate * (1.0 - open_part))
                dgate_ref[span, :] = (grad * normed * slope).astype(BF)
                grad = grad * gate * open_part
                grad = grad - jnp.mean(grad, axis=-1, keepdims=True) - normed * jnp.mean(
                    grad * normed, axis=-1, keepdims=True
                )
                low_ref[span, :] = (grad * scale).astype(BF)
                return carry

            lax.fori_loop(0, 2 * rows // 64, chunk, 0)
            for g in (0, 1):
                span = slice(g * rows, (g + 1) * rows)
                entered = (q_ref[span].astype(F32) * e_ref[span]).astype(BF)
                state_ref[g] = lax.dot_general(
                    entered,
                    low_ref[span],
                    (((0,), (0,)), ((), ())),
                    preferred_element_type=F32,
                ).astype(BF)

    cols = pl.BlockSpec((rows, SLAB), lambda i, s: (0, i))
    operands = (*g_pair, weight, gate_pre, retained, query, enter)
    shapes = (
        sds((2 * rows, DV), BF),
        sds((2 * rows, DV), BF),
        sds((2, DK, DV), BF),
    )
    return call(
        body,
        (4,),
        [cols, cols, pl.BlockSpec((1, 4, 2, 64, DV), lambda i, s: (i, 0, 0, 0, 1))]
        + [whole(o) for o in operands[3:]],
        tuple(whole(s) for s in shapes),
        shapes,
        scalars,
        operands,
        "back_gate",
        scratch=[pltpu.VMEM((2 * rows, DV), F32)],
        stream=True,
    )


def weight_last(into, pair, came, fade, value, key_out, leave, grad_value, grad_key, cosine, sine,
                scalars):
    rows = pair[0].shape[0]

    def body(
        s_ref, a_ref, b_ref, near_ref, mid_ref, far_ref, f_ref, v_ref, k_ref, l_ref, gv_ref, gk_ref,
        cos_ref, sin_ref, into_ref, out_ref, mark_ref, grad_ref
    ):
        @pl.when(pl.program_id(0) == 0)
        def _():
            fade = f_ref[...]
            for g in (0, 1):
                span = slice(g * rows, (g + 1) * rows)
                state = near_ref[g].astype(F32) + fade * (
                    mid_ref[g].astype(F32) + fade * far_ref[g].astype(F32)
                )
                state = state.astype(BF)
                grad_ref[span, :DV] = (
                    gv_ref[g] + jnp.dot(k_ref[g], state, preferred_element_type=F32)
                ).astype(BF)
                grad_key = gk_ref[g] + l_ref[...] * lax.dot_general(
                    v_ref[g], state, (((1,), (1,)), ((), ())), preferred_element_type=F32
                )
                grad_ref[span, DV:] = rotate(grad_key, cos_ref[...], -sin_ref[...]).astype(BF)

        out = lax.dot_general(
            jnp.concatenate((a_ref[...], b_ref[...]), axis=0),
            grad_ref[...],
            (((0,), (0,)), ((), ())),
            preferred_element_type=F32,
        ).astype(BF)
        for c in (0, 1):
            for y in range(4):
                first = (c * 4 + y) * 64
                out_ref[0, y, jnp.bitwise_xor(c, s_ref[0])] = out[first : first + 64]
        mark_ref[...] = jnp.zeros_like(mark_ref)

    cols = pl.BlockSpec((rows, SLAB), lambda i, s: (0, i))
    operands = (*pair, *came, fade, value, key_out, leave, grad_value, grad_key, cosine, sine)
    shapes = (
        sds(into.shape, BF),
        sds((8, 128), F32),
        sds((2 * rows, DV + DK), BF),
    )
    return call(
        body,
        (4,),
        [cols, cols]
        + [whole(o) for o in operands[2:]]
        + [pl.BlockSpec(memory_space=pl.ANY)],
        (
            pl.BlockSpec((1, 4, 2, 64, DV + DK), lambda i, s: (i, 0, 0, 0, 0)),
            whole(shapes[1]),
            whole(shapes[2]),
        ),
        shapes,
        scalars,
        (*operands, into),
        "weight_last",
        stream=True,
        aliases={1 + len(operands): 0},
    )


def mm_weight_into(into, pairs, start, total, scalars, name, deps=()):
    widths = [grad.shape[1] for _, grad in pairs]
    rows = pairs[0][0][0].shape[0]
    span = sum(widths)

    def body(s_ref, *refs):
        out_ref, mark_ref = refs[-2:]
        at = 0
        for k, width in enumerate(widths):
            a_ref, b_ref, g_ref = refs[3 * k : 3 * k + 3]
            out = lax.dot_general(
                jnp.concatenate((a_ref[...], b_ref[...]), axis=0),
                g_ref[...],
                (((0,), (0,)), ((), ())),
                preferred_element_type=F32,
            ).astype(BF)
            for c in (0, 1):
                for y in range(4):
                    first = (c * 4 + y) * 64
                    out_ref[0, y, jnp.bitwise_xor(c, s_ref[0]), :, at : at + width] = out[
                        first : first + 64
                    ]
            at += width
        mark_ref[...] = jnp.zeros_like(mark_ref)

    cols = pl.BlockSpec((rows, SLAB), lambda i, s: (0, i))
    specs, operands = [], []
    for (a, b), grad in pairs:
        specs += [cols, cols, whole(grad)]
        operands += [a, b, grad]
    aliases = None
    if into is not None:
        aliases = {1 + len(operands): 0}
        specs.append(pl.BlockSpec(memory_space=pl.ANY))
        operands.append(into)
    return call(
        body,
        (4,),
        specs,
        (
            pl.BlockSpec((1, 4, 2, 64, span), lambda i, s: (i, 0, 0, 0, start // span)),
            pl.BlockSpec((8, 128), lambda i, s: (0, 0)),
        ),
        (sds((4, 4, 2, 64, total), BF), sds((8, 128), F32)),
        scalars,
        tuple(operands),
        name,
        deps=deps,
        stream=True,
        aliases=aliases,
    )


def split_heads(weights, scalars, name, deps=()):
    widths = [w.shape[1] // 2 for w in weights]

    def body(s_ref, *refs):
        mine_ref, theirs_ref = refs[-2:]
        core = s_ref[0]
        for out_ref, head in ((mine_ref, core), (theirs_ref, 1 - core)):
            at = 0
            for ref, width in zip(refs, widths):
                out_ref[:, at : at + width] = ref[:, pl.ds(pl.multiple_of(head * width, width), width)]
                at += width

    total = sum(widths)
    spec = pl.BlockSpec((64, total), lambda i, s: (0, 0))
    return call(
        body,
        (1,),
        [whole(w) for w in weights],
        (spec, spec),
        (sds((64, total), BF),) * 2,
        scalars,
        tuple(weights),
        name,
        deps=deps,
        stream=True,
    )


def join_heads(mine, theirs, widths, scalars, name):
    def body(s_ref, mine_ref, theirs_ref, *outs):
        core = s_ref[0]
        for in_ref, head in ((mine_ref, core), (theirs_ref, 1 - core)):
            at = 0
            for ref, width in zip(outs, widths):
                span = pl.ds(pl.multiple_of(head * width, width), width)
                ref[:, span] = in_ref[:, at : at + width].astype(F32)
                at += width

    shapes = tuple(sds((64, 2 * w), F32) for w in widths)
    return call(
        body,
        (1,),
        [whole(mine), whole(theirs)],
        tuple(whole(s) for s in shapes),
        shapes,
        scalars,
        (mine, theirs),
        name,
    )


def scale_of(values):
    return lax.rsqrt(jnp.mean(values * values, axis=-1, keepdims=True) + 1e-06)


def turned_spec(rows):
    return pl.BlockSpec((rows, D), lambda i, s: (lax.rem(i + s[1], 4), 0))


def plain_spec(rows):
    return pl.BlockSpec((rows, D), lambda i, s: (i, 0))


def enter_rows(tokens, gain, scalars, deps=()):
    rows = tokens.shape[0]
    block = rows // 4

    def body(s_ref, t_ref, g_ref, n_out):
        values = t_ref[...]
        n_out[...] = (values * scale_of(values) * g_ref[...]).astype(BF)

    return call(
        body,
        (4,),
        [turned_spec(block), whole(gain)],
        plain_spec(block),
        sds((rows, D), BF),
        scalars,
        (tokens, gain),
        "enter_rows",
        deps=deps,
    )


def low_rows(cotangent, scalars, deps=()):
    rows = cotangent.shape[0]
    block = rows // 4

    def body(s_ref, c_ref, l_out):
        l_out[...] = c_ref[...].astype(BF)

    return call(
        body,
        (4,),
        [turned_spec(block)],
        plain_spec(block),
        sds((rows, D), BF),
        scalars,
        (cotangent,),
        "low_rows",
        deps=deps,
    )


def each_part(refs, work):
    step = pl.program_id(0)
    for k, ref in enumerate(refs):

        @pl.when(step == k)
        def _(ref=ref):
            work(ref[...].astype(F32))


def second_norm(tokens, parts, gain, scalars, deps=()):
    rows = tokens.shape[0]
    block = rows // 4

    def body(s_ref, t_ref, g_ref, *refs):
        h_out, n_out = refs[4:]

        def work(part):
            values = t_ref[...] + part
            h_out[...] = values
            n_out[...] = (values * scale_of(values) * g_ref[...]).astype(BF)

        each_part(refs[:4], work)

    plain = plain_spec(block)
    return call(
        body,
        (4,),
        [turned_spec(block), whole(gain)] + [whole(p) for p in parts],
        (plain, plain),
        (sds((rows, D), F32), sds((rows, D), BF)),
        scalars,
        (tokens, gain, *parts),
        "second_norm",
        deps=deps,
    )


def third_blocks(own, came, down_own, down_came, scalars, deps=()):
    rows = own.shape[0]
    block = rows // 4

    def body(s_ref, own_ref, came_ref, d_ref, e_ref, *refs):
        total = own_ref[...] + came_ref[...].astype(F32)
        down = d_ref[...] + e_ref[...].astype(F32)
        step = pl.program_id(0)
        for k in range(4):

            @pl.when(step == k)
            def _(k=k):
                refs[k][:block] = total.astype(BF)
                refs[k][block:] = down.astype(BF)

    plain = plain_spec(block)
    shapes = (sds((2 * block, D), BF),) * 4
    return call(
        body,
        (4,),
        [plain] * 4,
        tuple(whole(s) for s in shapes),
        shapes,
        scalars,
        (own, came, down_own, down_came),
        "third_blocks",
        deps=deps,
        stream=True,
    )


def leave_rows(hidden, tokens, grad_state, parts, gain, scalars, deps=()):
    rows = hidden.shape[0]
    block = rows // 4

    def body(s_ref, h_ref, t_ref, u_ref, g_ref, *refs):
        def work(part):
            refs[4][...] = h_ref[...] + part[block : 2 * block]
            refs[5][...] = u_ref[...] + norm_grad(t_ref[...], part[:block], g_ref[...])

        each_part(refs[:4], work)

    plain, turn = plain_spec(block), turned_spec(block)
    return call(
        body,
        (4,),
        [plain, turn, plain, whole(gain)] + [whole(p) for p in parts],
        (turn, turn),
        (sds((rows, D), F32),) * 2,
        scalars,
        (hidden, tokens, grad_state, gain, *parts),
        "leave_rows",
        deps=deps,
        stream=True,
    )


def norm_grad(values, grad, gain):
    factor = scale_of(values)
    unit = values * factor
    scaled = grad * gain
    return factor * (scaled - unit * jnp.mean(scaled * unit, axis=-1, keepdims=True))


def norm_back(values, upstream, parts, gain, scalars, name, deps=()):
    rows = values.shape[0]
    block = rows // 4

    def body(s_ref, v_ref, a_ref, b_ref, g_ref, *refs):
        def work(span, above, part):
            out = above + norm_grad(v_ref[span], part, g_ref[...])
            refs[4][span] = out
            refs[5][span] = out.astype(BF)

        for k in (0, 1):

            @pl.when(pl.program_id(0) == k)
            def _(k=k):
                work(slice(0, block), a_ref[...], refs[2 * k][...].astype(F32))
                work(slice(block, 2 * block), b_ref[...], refs[2 * k + 1][...].astype(F32))

    plain = pl.BlockSpec((2 * block, D), lambda i, s: (i, 0))
    turned = [
        pl.BlockSpec((block, D), lambda i, s, h=h: (lax.rem(2 * i + h + s[1], 4), 0))
        for h in (0, 1)
    ]
    return call(
        body,
        (2,),
        [plain, *turned, whole(gain)] + [whole(p) for p in parts],
        (plain, plain),
        (sds((rows, D), F32), sds((rows, D), BF)),
        scalars,
        (values, upstream, upstream, gain, *parts),
        name,
        deps=deps,
        stream=True,
    )


def tp_first(blocks):
    got = [shift(blocks[o], "tp", o) for o in (1, 3, 2)]
    near, far, mid = [part.astype(F32) for part in got]
    return (blocks[0].astype(F32) + mid) + (near + far), got


def tp_second(mine):
    near, far, mid = [shift(mine, "tp", -o) for o in (1, 3, 2)]
    return mine, near, mid, far


def tp_total(blocks):
    return tp_second(tp_first(blocks)[0].astype(BF))


def chip_blocks(own, came):
    block = own.shape[0] // 4
    spans = [slice(o * block, (o + 1) * block) for o in range(4)]
    return [(own[span].astype(F32) + came[span].astype(F32)).astype(BF) for span in spans]


def gate_norm(gate_pre, retained):
    centred = retained - jnp.mean(retained, axis=-1, keepdims=True)
    normed = centred * lax.rsqrt(jnp.mean(centred * centred, axis=-1, keepdims=True) + 1.0 * DK)
    return gate_pre * jax.nn.sigmoid(gate_pre) * normed


def gelu_gate(hidden, linear):
    return jax.nn.gelu(hidden, approximate=True) * linear


def rotate(values, cosine, sine):
    half = DK // 2
    first = values[..., :half]
    second = values[..., half:]
    return jnp.concatenate((first * cosine - second * sine, first * sine + second * cosine), axis=-1)


def ein(spec, left, right):
    return jnp.einsum(spec, left, right, preferred_element_type=F32)


def per_device(
    tokens,
    cotangent,
    gain_first,
    gain_second,
    w_query,
    w_key,
    w_value,
    w_gate,
    w_output,
    w_hidden,
    w_linear,
    w_down,
    decay_scale,
    first_length,
):
    rows = tokens.shape[0]
    core = lax.axis_index("core")
    place = lax.axis_index("ctx")
    plane = lax.axis_index("tp")
    scalars = jnp.stack((core, plane, lax.axis_index("x"), place)).astype(jnp.int32)

    w_output = w_output.T
    w_down = w_down.T
    mine, theirs = split_heads((w_value, w_key, w_gate, w_output, w_query), scalars, "split_attn")
    came = swap(theirs)
    block, gathered = stack_attn(mine, came, scalars)
    lengths = jnp.concatenate((first_length, swap(first_length)))
    blocks = spread_near(block)
    w_kv = stack_blocks(blocks, 0, 768, scalars, "stack_kv")
    normed_first = enter_rows(tokens, gain_first.reshape(1, D), scalars, deps=blocks[1:])
    w_goq = lax.all_gather(gathered, XY, axis=0, tiled=True).reshape(4, 4, 2, 64, -1)
    mine, theirs = split_heads(
        (w_hidden, w_linear, w_down), scalars, "split_mlp", deps=(normed_first,)
    )
    came_mlp = swap(theirs)
    gain_first = gain_first.reshape(1, D)
    gain_second = gain_second.reshape(1, D)
    x_first = (normed_first, swap(normed_first))
    cot_low = low_rows(cotangent, scalars, deps=(x_first[1],))
    g_out = (cot_low, swap(cot_low))
    w_kv = spread_far(w_kv)

    rate = lax.dynamic_index_in_dim(decay_scale, core, 0, False) / 1024.0
    local = (jnp.arange(rows, dtype=jnp.int32) + plane * (rows // 4)) % rows
    index = place * rows + local
    steps = local.astype(F32)
    leave = jnp.exp(-rate * (rows - 1.0 - steps))[None, :, None]
    fade = jnp.exp(-rate * rows)
    half = DK // 2
    frequency = 10000.0 ** (-(jnp.arange(half).astype(F32) / half))
    angles = index.astype(F32)[:, None] * frequency[None, :]
    cosine = jnp.cos(angles)
    sine = jnp.sin(angles)

    def spread_state(low, way):
        return [shift_open(low, "ctx", way * o) for o in (1, 2, 3)]

    leave_rows_out = leave.reshape(rows, 1)
    fade_in = fade.reshape(1, 1)
    projected = mm_in(*x_first, [(w_kv, 0, 768)], scalars, "project_kv", deps=(came_mlp,))
    key = rotate(projected[:, DV:].reshape(2, rows, DK), cosine, sine).astype(BF)
    value = projected[:, :DV].astype(BF).reshape(2, rows, DV)
    key_out = (key.astype(F32) * leave).astype(BF)
    state_out = ein("gjd,gje->gde", key_out, value).astype(BF)
    came = spread_state(state_out, 1)
    w_mlp = lax.all_gather(
        stack_blocks((mine, came_mlp), 0, 1536, scalars, "stack_mlp", deps=(state_out,)),
        XY,
        axis=0,
        tiled=True,
    ).reshape(4, 4, 2, 64, -1)
    own, other, query, state_in, weighted, gate_pre, retained, mixed, mask, enter_rows_in = retain(
        x_first,
        w_goq,
        key,
        value,
        came,
        rate.reshape(1, 1),
        cosine,
        sine,
        jnp.concatenate((scalars, lengths)),
    )
    enter = enter_rows_in.reshape(2, rows, 1)
    query = query.reshape(2, rows, DK)
    parts = tp_total(chip_blocks(own, swap(other)))
    hidden_state, normed_second = second_norm(tokens, parts, gain_second, scalars)
    x_second = (normed_second, swap(normed_second))
    own, other, gain_second_part, grad_pair, activated = mlp(x_second, g_out, w_mlp, scalars)
    grads, mark = mm_weight_into(
        None, ((x_second, grad_pair),), 1024, 3584, scalars, "weight_mlp"
    )
    mine, _ = tp_first(chip_blocks(own, swap(other)))
    (mine,) = tie((mine.astype(BF),), (mark,))
    parts = tp_second(mine)
    down = mm_back([(activated, w_mlp, 2 * DV)], scalars, "project_down", deps=(mine,))
    grad_state, grad_state_low = norm_back(
        hidden_state,
        cotangent,
        parts,
        gain_second,
        scalars,
        "second_back",
        deps=(down[1],),
    )
    g_state = (grad_state_low, swap(grad_state_low))
    grad_gate, grad_low, back_out = back_gate(
        g_state, w_goq, gate_pre, retained, query.reshape(2 * rows, DK), enter_rows_in, scalars
    )
    grad_low = grad_low.reshape(2, rows, DV)
    came = spread_state(back_out, -1)
    grad_scores = (ein("gie,gje->gij", grad_low, value) * mask).astype(BF)
    grad_query = ein("gij,gjd->gid", grad_scores, key) + enter * ein("gie,gde->gid", grad_low, state_in)
    grad_key = ein("gij,gid->gjd", grad_scores, query)
    grad_value = ein("gij,gie->gje", weighted, grad_low)
    grad_query = rotate(grad_query, cosine, -sine).astype(BF).reshape(2 * rows, DK)
    grads, mark = mm_weight_into(
        grads,
        ((g_state, mixed), (x_first, grad_gate)),
        2048,
        3584,
        scalars,
        "weight_og",
        deps=(back_out,),
    )
    grads, mark = mm_weight_into(
        grads, ((g_out, activated),), 3072, 3584, scalars, "weight_down"
    )
    grads, mark = mm_weight_into(
        grads, ((x_first, grad_query),), 768, 3584, scalars, "weight_query"
    )
    came[0] = tie((came[0],), (mark, grad_key, grad_value))[0]
    grads, mark, grad_vk = weight_last(
        grads,
        x_first,
        came,
        fade_in,
        value,
        key_out,
        leave_rows_out,
        grad_value,
        grad_key,
        cosine,
        sine,
        scalars,
    )
    block = lax.psum_scatter(grads.reshape(2048, -1), XY, scatter_dimension=0, tiled=True)
    own, other, gain_first_part = mm_back(
        [(grad_vk, w_kv, 0), (grad_gate, w_goq, 0), (grad_query, w_goq, 1024)],
        scalars,
        "back_attn",
        normed=x_first,
        deps=(mark,),
    )
    down = (down[0], swap(tie((down[1],), (mark,))[0]))
    blocks = third_blocks(own, swap(other), *down, scalars)
    mine, _ = tp_first(blocks)
    gains = jnp.concatenate((gain_first_part[:1], gain_second_part[:1]))
    for axis, swapped in (
        ("core", (1, 0)),
        ("ctx", (1, 0, 3, 2)),
        ("ctx", (3, 2, 1, 0)),
        ("x", (1, 0, 3, 2)),
        ("x", (3, 2, 1, 0)),
    ):
        gains = gains + lax.ppermute(gains, axis, list(enumerate(swapped)))
    mine = jnp.concatenate((mine, gains, jnp.zeros((14, D), F32))).astype(BF)
    parts = tp_second(mine)
    gains = [part[128:130].astype(F32) for part in parts]
    gains = (gains[0] + gains[2]) + (gains[1] + gains[3])
    spot = (lax.axis_index("x") * 2 + core) * 4 + place
    gain_first_grad, gain_second_grad = [
        lax.dynamic_slice_in_dim(gains[k] / gain[0], spot * 64, 64, 0)
        for k, gain in ((0, gain_first), (1, gain_second))
    ]
    layer_out, input_grad = leave_rows(
        hidden_state, tokens, grad_state, parts, gain_first, scalars
    )
    block = tie((block,), (gain_first_grad, gain_second_grad, input_grad))[0].reshape(2, 64, -1)
    d_value, d_key, d_query, d_hidden, d_linear, d_output, d_gate, d_down = join_heads(
        block[0], swap(block[1]), (DV, DK, DK) + (DV,) * 5, scalars, "join_heads"
    )
    return (
        layer_out,
        input_grad,
        gain_first_grad,
        gain_second_grad,
        d_query,
        d_key,
        d_value,
        d_gate,
        d_output.T,
        d_hidden,
        d_linear,
        d_down.T,
    )


def solution(mesh):
    fine = Mesh(np.asarray(mesh.devices).reshape(4, 2, 4, 4), ("x", "core", "ctx", "tp"))
    split = ("x", "core", "ctx")
    row = P(split, None)
    win = P(split, "tp")
    wout = P("tp", split)
    in_specs = (row, row, P(), P(), win, win, win, win, wout, win, win, wout, P("tp"), P(("x", "core")))
    out_specs = (row, row, P(split), P(split), win, win, win, win, wout, win, win, wout)
    return jax.shard_map(
        per_device, mesh=fine, in_specs=in_specs, out_specs=out_specs, check_vma=False
    )
```
